32 devices in a mesh: ctx: 4 (over y, x), exp: 8 (over z, core).
Axes of the slice: x: 2, y: 2, z: 4, core: 2. Of those that a mesh axis runs over, the one named last changes fastest.
Arguments:
- tokens: bfloat16 [8, 1024, 1536], P('exp', 'ctx'), may hold values from -6 to 6
- routes: int32 [8, 1024, 4], P('exp', 'ctx'), may hold values from 0 to 15, all different within a row; in each aligned block of 256 rows (0 to 255, 256 to 511, ..., all dimensions but the last counted through in order) at most 128 rows name the same one
- gain_attn: bfloat16 [1536], P('exp'), may hold values from 0.5 to 1.5
- w_query: bfloat16 [1536, 1536], P('exp'), may hold values from -0.15625 to 0.15625
- key_value_weight: bfloat16 [1536, 512], P('exp'), may hold values from -0.15625 to 0.15625
- w_out: bfloat16 [1536, 1536], P('exp'), may hold values from -3.5 to 3.5
- gain_ffn: bfloat16 [1536], P('exp'), may hold values from 0.5 to 1.5
- w_router: bfloat16 [1536, 16], P('exp'), may hold values from -0.078125 to 0.078125
- w_gate: bfloat16 [16, 1536, 768], P('exp'), may hold values from -0.15625 to 0.15625
- w_up: bfloat16 [16, 1536, 768], P('exp'), may hold values from -0.15625 to 0.15625
- w_down: bfloat16 [16, 768, 1536], P('exp'), may hold values from -0.4375 to 0.4375
- cotangent: bfloat16 [8, 1024, 1536], P('exp', 'ctx'), may hold values from -6 to 6
Outputs:
- output: bfloat16 [8, 1024, 1536], P('exp', 'ctx')
- grad_tokens: float32 [8, 1024, 1536], P('exp', 'ctx')
- grad_gain_attn: float32 [1536], P('exp')
- grad_query: float32 [1536, 1536], P('exp')
- grad_keyval: float32 [1536, 512], P('exp')
- grad_out: float32 [1536, 1536], P('exp')
- grad_gain_ffn: float32 [1536], P('exp')
- grad_router: float32 [1536, 16], P('exp')
- grad_gate: float32 [16, 1536, 768], P('exp')
- grad_up: float32 [16, 1536, 768], P('exp')
- grad_down: float32 [16, 768, 1536], P('exp')
The draws below stay inside these ranges and needn't reach their ends.
Inputs may be any that keep to these rules, and one draw needn't show every extreme that they name: `routes`: each token names 4 different experts. In the 256 tokens of one device (aligned blocks along a sequence) no expert is named by more than 128 tokens, a bound that some block reaches.
All inputs are finite; a program needn't handle non-finite values.
Results may differ from the reference program's by a relative error of at most 0.025.
Values may be sent and summed in bfloat16 or wider, within the bound.
A program may use at most 192 MiB of HBM per device.

```python
import math
from functools import partial
import jax
import jax.numpy as jnp
import numpy as np
from jax import lax

MODEL_WIDTH = 1536
QUERY_HEADS = 12
KEY_VALUE_HEADS = 2
HEAD_WIDTH = 128
FF = 768
TOP = 4
BLK = 256
EXPERTS = 16
SEQUENCE_TOKENS = 1024
SEQS = 8
CAP = 128
QUERY_BLOCK_ROWS = 256
N_CTX = 4


def shard_levels(key, dims, pieces, smallest, high):
    loudness, own = 1.0, jax.random.fold_in(key, 6)
    for dim, blocks in pieces:
        heights = jnp.exp(jax.random.uniform(jax.random.fold_in(own, dim), (blocks,), jnp.float32, smallest / len(pieces), high / len(pieces)))
        loudness = loudness * jnp.repeat(heights, dims[dim] // blocks).reshape([-1 if axis == dim else 1 for axis in range(len(dims))])
    return loudness


def shared_out(own_key, own, number, rows, count, top, reach, slope):
    order = jax.random.permutation(own_key, count)
    crowded, usual = shares(count, rows * top, reach, slope, True), shares(count, rows * top, reach, slope, False)
    places = jnp.arange(count)

    def named(lengths, rotation):
        used = int((lengths > 0).sum())
        fixed = max(1, used // 4)
        shifted = fixed + (places - fixed + rotation * (used - fixed)) % max(1, count - fixed)
        return jnp.zeros((count,), jnp.int32).at[order[jnp.where(places < fixed, places, shifted)]].set(jnp.asarray(lengths, jnp.int32))

    lengths = jnp.where(number % 4 == 0, named(crowded, number // 4), named(usual, number - number // 4 - 1))
    mixed = jax.random.permutation(jax.random.fold_in(own, 3), count)
    giver, receiver = mixed[0:count // 2 * 2:2], mixed[1:count // 2 * 2:2]
    margin = jnp.minimum(lengths[giver] - 1, reach - lengths[receiver]) // 2
    margin = jnp.where((giver == order[0]) | (receiver == order[0]) | (lengths[receiver] == 0), 0, jnp.maximum(margin, 0))
    shifted = jax.random.randint(jax.random.fold_in(own, 4), (count // 2,), 0, 1 << 20) % (margin + 1)
    lengths = lengths.at[giver].add(-shifted).at[receiver].add(shifted)
    items = jnp.searchsorted(jnp.cumsum(lengths), jnp.arange(rows * top), side="right").astype(jnp.int32)
    grid = items.reshape(top, rows).T
    grid = grid[jax.random.permutation(jax.random.fold_in(own, 1), rows)]
    rotation = jax.random.randint(jax.random.fold_in(own, 2), (rows, 1), 0, top)
    return jnp.take_along_axis(grid, (jnp.arange(top)[None, :] + rotation) % top, axis=1)


def shares(number_of, total, bound, skew, full):
    weights = [(1 << 20) // math.isqrt(rank ** skew) + 1 for rank in range(1, number_of + 1)]
    largest = bound if full else min(bound, max(-(-total // number_of), total * weights[0] // sum(weights)))
    least = 1 if total - largest >= number_of - 1 else 0
    given, surplus = [largest] + [least] * (number_of - 1), total - largest - least * (number_of - 1)
    while surplus > 0:
        candidates = [i for i in range(1, number_of) if given[i] < largest] or [i for i in range(1, number_of) if given[i] < bound]
        mass, left = sum([weights[i] for i in candidates]), surplus
        for i in candidates:
            addition = min(bound - given[i], max(1, left * weights[i] // mass), surplus)
            given[i] = given[i] + addition
            surplus = surplus - addition
    return np.array(given)


def bell_draw(rng, dims, spread, reach, shards=(), held_as=jnp.bfloat16):
    values = jax.random.normal(rng, dims, jnp.float32) * spread
    if len(shards) > 0:
        values = shard_levels(rng, dims, shards, -0.22, 0.18) * values
    return jnp.clip(values, min=-reach, max=reach).astype(held_as)


def setup_inputs(seed: int = 0) -> dict:
    streams_of = jax.random.split(jax.random.key(seed), 13)
    tokens = bell_draw(streams_of[0], (SEQS, SEQUENCE_TOKENS, MODEL_WIDTH), 1.0, 6.0, ((0, 8), (1, 4)))
    routes_keys = jax.random.split(jax.random.fold_in(streams_of[1], 1), SEQS * SEQUENCE_TOKENS // BLK)
    routes_turns = jax.random.permutation(jax.random.fold_in(streams_of[1], 3), SEQS * SEQUENCE_TOKENS // BLK)
    routes = jax.vmap(lambda own, number: shared_out(jax.random.fold_in(streams_of[1], 2), own, number, BLK, EXPERTS, TOP, CAP, 2))(routes_keys, routes_turns).reshape((SEQS, SEQUENCE_TOKENS, TOP))
    gain_attn = jnp.clip(1.0 + 0.1 * jax.random.normal(streams_of[2], (MODEL_WIDTH,), jnp.float32), 0.5, 1.5).astype(jnp.bfloat16)
    w_query = bell_draw(streams_of[3], (MODEL_WIDTH, QUERY_HEADS * HEAD_WIDTH), MODEL_WIDTH ** -0.5, 0.15625, ((0, 8),))
    key_value_weight = bell_draw(streams_of[4], (MODEL_WIDTH, 2 * KEY_VALUE_HEADS * HEAD_WIDTH), MODEL_WIDTH ** -0.5, 0.15625, ((0, 8),))
    w_out = bell_draw(streams_of[5], (QUERY_HEADS * HEAD_WIDTH, MODEL_WIDTH), (max(1, 2 * QUERY_HEADS * HEAD_WIDTH // SEQUENCE_TOKENS)) ** -0.5, 3.5, ((0, 8),))
    gain_ffn = jnp.clip(1.0 + 0.1 * jax.random.normal(streams_of[6], (MODEL_WIDTH,), jnp.float32), 0.5, 1.5).astype(jnp.bfloat16)
    w_router = bell_draw(streams_of[7], (MODEL_WIDTH, EXPERTS), (4 * MODEL_WIDTH) ** -0.5, 0.078125, ((0, 8),))
    w_gate = bell_draw(streams_of[8], (EXPERTS, MODEL_WIDTH, FF), MODEL_WIDTH ** -0.5, 0.15625, ((0, 8),))
    w_up = bell_draw(streams_of[9], (EXPERTS, MODEL_WIDTH, FF), MODEL_WIDTH ** -0.5, 0.15625, ((0, 8),))
    w_down = bell_draw(streams_of[10], (EXPERTS, FF, MODEL_WIDTH), (FF // 4) ** -0.5, 0.4375, ((0, 8),))
    cotangent = bell_draw(streams_of[11], (SEQS, SEQUENCE_TOKENS, MODEL_WIDTH), 1.0, 6.0, ((0, 8), (1, 4)))
    return dict(tokens=tokens, routes=routes, gain_attn=gain_attn, w_query=w_query, key_value_weight=key_value_weight, w_out=w_out, gain_ffn=gain_ffn, w_router=w_router, w_gate=w_gate, w_up=w_up, w_down=w_down, cotangent=cotangent)


EPS = 1e-06
NEG = -1e+30
ROPE_BASE = 1000000.0

@jax.custom_vjp
def lower_bound(v):
    return lax.optimization_barrier(v.astype(jnp.bfloat16)).astype(jnp.float32)

@jax.custom_vjp
def low_back(v):
    return v

def low_keep(v):
    return (lower_bound(v), None)

def low_pass(kept, grad):
    return (grad,)

def back_keep(v):
    return (v, None)

def back_low(kept, grad):
    return (lower_bound(grad),)
lower_bound.defvjp(low_keep, low_pass)
low_back.defvjp(back_keep, back_low)

def rope_tables(first_row, row_count, head_size):
    half_size = head_size // 2
    frequency = ROPE_BASE ** (-jnp.arange(half_size, dtype=jnp.float32) * (2.0 / head_size))
    places = (first_row + jnp.arange(row_count, dtype=jnp.int32)).astype(jnp.float32)
    angles = places[:, None] * frequency[None, :]
    cosine = jnp.cos(angles)
    sine_table = jnp.sin(angles)
    return (jnp.concatenate([cosine, cosine], 1), jnp.concatenate([sine_table, sine_table], 1))

def rotate(vector):
    half_size = vector.shape[-1] // 2
    return jnp.concatenate([-vector[..., half_size:], vector[..., :half_size]], -1)

def rotary_embed(vector, cosine, sine_table):
    return vector * cosine + rotate(vector) * sine_table

def rms_norm(row_block):
    return row_block * lax.rsqrt(lax.optimization_barrier(jnp.mean(row_block * row_block, -1, keepdims=True)) + EPS)

def slot_tables(picked_ids, experts, capacity):
    flat_ids = picked_ids.reshape(-1).astype(jnp.int32)
    hit_table = (flat_ids[:, None] == jnp.arange(experts, dtype=jnp.int32)[None, :]).astype(jnp.int32)
    before = (jnp.cumsum(hit_table, 0) - hit_table).astype(jnp.int32)
    slot_index = lax.optimization_barrier(jnp.sum(before * hit_table, 1)).astype(jnp.int32)
    position = (flat_ids * capacity + slot_index).astype(jnp.int32)
    pair_count = flat_ids.shape[0]
    source_rows = jnp.zeros((experts * capacity,), jnp.int32).at[position].set(jnp.arange(pair_count, dtype=jnp.int32))
    filled = jnp.zeros((experts * capacity,), jnp.int32).at[position].set(1)
    return (position, source_rows, filled)

def take_rows(row_block, row_index):
    return row_block[row_index]

def sequence_forward(packed, params):
    seq_rows, seq_ids, seq_pos, seq_src, seq_fill = packed
    gain_one, query_w, keyval_w, out_w, gain_two, router_w, gate_w, up_w, down_w = params
    highest = lax.Precision.HIGHEST
    scaling = 1.0 / math.sqrt(HEAD_WIDTH)
    hidden_one = lower_bound(rms_norm(seq_rows) * gain_one)
    query_lin = low_back(jnp.dot(hidden_one, query_w, precision=highest))
    key_value_linear = low_back(jnp.dot(hidden_one, keyval_w, precision=highest))
    cosine, sine_table = rope_tables(0, SEQUENCE_TOKENS, HEAD_WIDTH)
    cosine_per_head = cosine[:, None, :]
    sine_per_head = sine_table[:, None, :]
    query_vectors = lower_bound(rotary_embed(query_lin.reshape(SEQUENCE_TOKENS, QUERY_HEADS, HEAD_WIDTH), cosine_per_head, sine_per_head))
    every_key = lower_bound(rotary_embed(key_value_linear[:, :KEY_VALUE_HEADS * HEAD_WIDTH].reshape(SEQUENCE_TOKENS, KEY_VALUE_HEADS, HEAD_WIDTH), cosine_per_head, sine_per_head))
    every_value = lower_bound(key_value_linear[:, KEY_VALUE_HEADS * HEAD_WIDTH:].reshape(SEQUENCE_TOKENS, KEY_VALUE_HEADS, HEAD_WIDTH))
    blocked_queries = query_vectors.reshape(SEQUENCE_TOKENS // QUERY_BLOCK_ROWS, QUERY_BLOCK_ROWS, KEY_VALUE_HEADS, QUERY_HEADS // KEY_VALUE_HEADS, HEAD_WIDTH)
    block_starts = jnp.arange(SEQUENCE_TOKENS // QUERY_BLOCK_ROWS, dtype=jnp.int32) * QUERY_BLOCK_ROWS

    def attend(pair_in):
        block_q, row_start = pair_in
        raw = low_back(jnp.einsum('qhgd,khd->hgqk', block_q, every_key, precision=highest))
        scores = raw * scaling
        allowed = jnp.arange(SEQUENCE_TOKENS, dtype=jnp.int32)[None, :] <= (row_start + jnp.arange(QUERY_BLOCK_ROWS, dtype=jnp.int32))[:, None]
        scores = jnp.where(allowed, scores, NEG)
        weights_now = lower_bound(jax.nn.softmax(scores, -1))
        return lower_bound(low_back(jnp.einsum('hgqk,khd->qhgd', weights_now, every_value, precision=highest)))
    mixed_heads = lax.map(jax.checkpoint(attend), (blocked_queries, block_starts)).reshape(SEQUENCE_TOKENS, QUERY_HEADS * HEAD_WIDTH)
    resid_mid = seq_rows + low_back(jnp.dot(mixed_heads, out_w, precision=highest))
    hidden_two = lower_bound(rms_norm(resid_mid) * gain_two)
    logits = jnp.dot(hidden_two, router_w, precision=highest)
    gate_values = jax.nn.softmax(jnp.take_along_axis(logits, seq_ids, 1), -1)
    blocks = hidden_two.reshape(N_CTX, BLK, MODEL_WIDTH)
    sent = jax.vmap(take_rows)(blocks, seq_src // TOP) * seq_fill.astype(jnp.float32)[..., None]
    sent = low_back(sent).reshape(N_CTX, EXPERTS, CAP, MODEL_WIDTH)
    gate_pre = low_back(jnp.einsum('cerd,edf->cerf', sent, gate_w, precision=highest))
    up_pre = low_back(jnp.einsum('cerd,edf->cerf', sent, up_w, precision=highest))
    activation = lower_bound(jax.nn.silu(gate_pre) * up_pre)
    expert_rows = lower_bound(low_back(jnp.einsum('cerf,efd->cerd', activation, down_w, precision=highest)))
    pair_out = jax.vmap(take_rows)(expert_rows.reshape(N_CTX, EXPERTS * CAP, MODEL_WIDTH), seq_pos).reshape(SEQUENCE_TOKENS, TOP, MODEL_WIDTH)
    return resid_mid + lax.optimization_barrier(jnp.sum(gate_values[:, :, None] * pair_out, 1))

def reference(tokens, routes, gain_attn, w_query, key_value_weight, w_out, gain_ffn, w_router, w_gate, w_up, w_down, cotangent):
    block_ids = routes.reshape(SEQS, N_CTX, BLK, TOP)
    tables = jax.vmap(jax.vmap(partial(slot_tables, experts=EXPERTS, capacity=CAP)))(block_ids)
    position, source_rows, filled = tables

    def forward(rows_in, *params):

        def one_sequence(carried, packed):
            return (carried, jax.checkpoint(sequence_forward)(packed, params))
        start = jnp.zeros((), jnp.float32)
        ignored, result = lax.scan(one_sequence, start, (rows_in, routes, position, source_rows, filled))
        return result
    weights = tuple((w.astype(jnp.float32) for w in (gain_attn, w_query, key_value_weight, w_out, gain_ffn, w_router, w_gate, w_up, w_down)))
    result, pullback = jax.vjp(forward, tokens.astype(jnp.float32), *weights)
    grads = pullback(cotangent.astype(jnp.float32))
    return (result.astype(jnp.bfloat16), grads[0], grads[1], grads[2], grads[3], grads[4], grads[5], grads[6], grads[7], grads[8], grads[9])
```

```python
import functools
import math

import jax
import jax.numpy as jnp
from jax import lax
from jax.experimental import pallas as pl
from jax.experimental.pallas import tpu as pltpu
from jax.sharding import PartitionSpec as P

MESH = pl.DeviceIdType.MESH
ANY = pl.BlockSpec(memory_space=pl.ANY)


def remote(src, dst, send, recv, ctx, exp):
    return pltpu.make_async_remote_copy(
        src_ref=src, dst_ref=dst, send_sem=send, recv_sem=recv, device_id=(ctx, exp), device_id_type=MESH
    )


def greet(pairs):
    barrier = pltpu.get_barrier_semaphore()
    count = 0
    for here, ctx, exp in pairs:
        if here is True:
            pl.semaphore_signal(barrier, inc=1, device_id=(ctx, exp), device_id_type=MESH)
            count = count + 1
        else:
            @pl.when(here)
            def _():
                pl.semaphore_signal(barrier, inc=1, device_id=(ctx, exp), device_id_type=MESH)
            count = count + here.astype(jnp.int32)
    pl.semaphore_wait(barrier, count)


def gather_kernel(line, own, out, local_sem, z_send, z_recv, c_send, c_recv):
    c, e = lax.axis_index("ctx"), lax.axis_index("exp")
    p, k = e // 2, e % 2
    sibling = e + 1 - 2 * k
    greet([(p > 0, c, e - 2), (p < line - 1, c, e + 2), (True, c, sibling)])
    local = pltpu.make_async_copy(own, out.at[e], local_sem)
    local.start()

    def along(q, src, to_right):
        there = e + 2 if to_right else e - 2
        way = 0 if to_right else 1
        return remote(src, out.at[2 * q + k], z_send.at[way, q], z_recv.at[q], c, there)

    def across(q, src):
        return remote(src, out.at[2 * q + k], c_send.at[q], c_recv.at[q], c, sibling)

    @pl.when(p < line - 1)
    def _():
        along(p, own, True).start()

    @pl.when(p > 0)
    def _():
        along(p, own, False).start()

    across(p, own).start()
    for d in range(1, line):
        for to_right in (True, False):
            q = p - d if to_right else p + d
            here = (q >= 0) if to_right else (q < line)
            further = (p < line - 1) if to_right else (p > 0)

            @pl.when(here)
            def _():
                block = out.at[2 * q + k]
                along(q, block, to_right).wait_recv()

                @pl.when(further)
                def _():
                    along(q, block, to_right).start()

                across(q, block).start()

    local.wait()
    for d in range(0, line):
        for to_right in (True, False):
            if d == 0 and not to_right:
                continue
            q = p - d if to_right else p + d
            here = (q >= 0) if to_right else (q < line)

            @pl.when(here)
            def _():
                block = out.at[2 * q + k]
                across(q, block).wait()
    for d in range(0, line):
        for to_right in (True, False):
            q = p - d if to_right else p + d
            here = (q >= 0) if to_right else (q < line)
            further = (p < line - 1) if to_right else (p > 0)

            @pl.when(here & further)
            def _():
                along(q, out.at[2 * q + k], to_right).wait_send()


def gather_rows(own, collective_id):
    n = lax.axis_size("exp")
    line = n // 2
    return pl.pallas_call(
        functools.partial(gather_kernel, line),
        out_shape=jax.ShapeDtypeStruct((n,) + own.shape, own.dtype),
        in_specs=[ANY],
        out_specs=ANY,
        scratch_shapes=[
            pltpu.SemaphoreType.DMA,
            pltpu.SemaphoreType.DMA((2, line)),
            pltpu.SemaphoreType.DMA((line,)),
            pltpu.SemaphoreType.DMA((line,)),
            pltpu.SemaphoreType.DMA((line,)),
        ],
        compiler_params=pltpu.CompilerParams(collective_id=collective_id, has_side_effects=True),
        name="gather_rows",
    )(own)


def add_rows(dst, a, b, rows, step):
    def body(i, carried):
        at = pl.ds(pl.multiple_of(i * step, step), step)
        dst[at, :] = (a[at, :].astype(jnp.float32) + b[at, :].astype(jnp.float32)).astype(dst.dtype)
        return carried

    lax.fori_loop(0, rows // step, body, 0)


def scatter_kernel(line, part, out, mine, other, moving, load_sem, c_send, c_recv, z_send, z_recv):
    c, e = lax.axis_index("ctx"), lax.axis_index("exp")
    p, k = e // 2, e % 2
    sibling = e + 1 - 2 * k
    rows = part.shape[1]
    step = 16
    greet([(p > 0, c, e - 2), (p < line - 1, c, e + 2), (True, c, sibling)])

    def across(q):
        return remote(part.at[2 * q + 1 - k], other.at[q], c_send.at[q], c_recv.at[q], c, sibling)

    def load(q):
        return pltpu.make_async_copy(part.at[2 * q + k], mine.at[q], load_sem.at[q])

    def along(q, to_right):
        way = 0 if to_right else 1
        there = e + 2 if to_right else e - 2
        return remote(mine.at[q], moving.at[way, q], z_send.at[q], z_recv.at[way, q], c, there)

    order = []
    for d in range(line - 1, -1, -1):
        for to_right in (True, False):
            if d == 0 and not to_right:
                continue
            q = p + d if to_right else p - d
            here = (q < line) if to_right else (q >= 0)
            order.append((d, to_right, q, here))
    for d, to_right, q, here in order:
        @pl.when(here)
        def _():
            across(q).start()
            load(q).start()
    for d, to_right, q, here in order:
        @pl.when(here)
        def _():
            load(q).wait()
            across(q).wait()
            add_rows(mine.at[q], mine.at[q], other.at[q], rows, step)
            if d > 0:
                behind = (p > 0) if to_right else (p < line - 1)

                @pl.when(behind)
                def _():
                    along(q, to_right).wait_recv()
                    add_rows(mine.at[q], mine.at[q], moving.at[0 if to_right else 1, q], rows, step)

                along(q, to_right).start()
            else:
                for way, behind in ((0, p > 0), (1, p < line - 1)):
                    @pl.when(behind)
                    def _():
                        along(q, way == 0).wait_recv()
                        add_rows(mine.at[q], mine.at[q], moving.at[way, q], rows, step)

                done = pltpu.make_async_copy(mine.at[q], out, load_sem.at[q])
                done.start()
                done.wait()
    for d, to_right, q, here in order:
        if d > 0:
            @pl.when(here)
            def _():
                along(q, to_right).wait_send()


def scatter_rows(part, collective_id):
    n, rows, width = part.shape
    line = n // 2
    buffers = (line, rows, width)
    return pl.pallas_call(
        functools.partial(scatter_kernel, line),
        out_shape=jax.ShapeDtypeStruct((rows, width), part.dtype),
        in_specs=[ANY],
        out_specs=ANY,
        scratch_shapes=[
            pltpu.VMEM(buffers, part.dtype),
            pltpu.VMEM(buffers, part.dtype),
            pltpu.VMEM((2,) + buffers, part.dtype),
            pltpu.SemaphoreType.DMA((line,)),
            pltpu.SemaphoreType.DMA((line,)),
            pltpu.SemaphoreType.DMA((line,)),
            pltpu.SemaphoreType.DMA((line,)),
            pltpu.SemaphoreType.DMA((2, line)),
        ],
        compiler_params=pltpu.CompilerParams(
            collective_id=collective_id, has_side_effects=True, vmem_limit_bytes=56 << 20
        ),
        name="scatter_rows",
    )(part)


def weights_kernel(line, quarter, *refs):
    count = 3
    own, out = refs[:count], refs[count : 2 * count]
    local_sem, own_send, own_recv, z_send, z_recv, xy_send, xy_recv, d_send, d_recv, c_send, c_recv = refs[2 * count :]
    c, e = lax.axis_index("ctx"), lax.axis_index("exp")
    p, k = e // 2, e % 2
    sibling = e + 1 - 2 * k
    rows = own[0].shape[0]
    nbr = (c + 1 - 2 * (c % 2), (c + 2) % 4)
    opposite = 3 - c
    greet(
        [
            (p > 0, c, e - 2),
            (p < line - 1, c, e + 2),
            (True, c, sibling),
            (True, nbr[0], e),
            (True, nbr[1], e),
        ]
    )

    def whole(a):
        return out[a].at[pl.ds(pl.multiple_of(e * rows, 16), rows), :]

    def piece(a, q, column):
        return out[a].at[pl.ds(pl.multiple_of((2 * q + k) * rows + column * quarter, 16), quarter), :]

    def own_piece(a):
        return own[a].at[pl.ds(pl.multiple_of(c * quarter, 16), quarter), :]

    def local(a):
        return pltpu.make_async_copy(own[a], whole(a), local_sem.at[a])

    def own_across(a):
        return remote(own[a], whole(a), own_send.at[a], own_recv.at[a], c, sibling)

    def along(a, q, src, to_right):
        there = e + 2 if to_right else e - 2
        way = 0 if to_right else 1
        return remote(src, piece(a, q, c), z_send.at[way, q, a], z_recv.at[q, a], c, there)

    def beside(a, q, axis):
        return remote(piece(a, q, c), piece(a, q, c), xy_send.at[axis, q, a], xy_recv.at[axis, q, a], nbr[axis], e)

    def onward(a, q):
        came, goes = (0, 1) if a == 0 else (1, 0)
        block = piece(a, q, nbr[came])
        return remote(block, block, d_send.at[q, a], d_recv.at[q, a], nbr[goes], e)

    def across(a, q, j):
        column = (c, nbr[0], nbr[1], opposite)[j]
        block = piece(a, q, column)
        return remote(block, block, c_send.at[q, j, a], c_recv.at[q, j, a], c, sibling)

    arrays = range(count)
    for a in arrays:
        @pl.when(p < line - 1)
        def _():
            along(a, p, own_piece(a), True).start()

        @pl.when(p > 0)
        def _():
            along(a, p, own_piece(a), False).start()
    for a in arrays:
        own_across(a).start()
        local(a).start()

    def ends(d):
        for to_right in (True, False):
            q = p - d if to_right else p + d
            yield to_right, q, ((q >= 0) if to_right else (q < line))

    for d in range(1, line + 1):
        if d < line:
            for to_right, q, here in ends(d):
                further = (p < line - 1) if to_right else (p > 0)

                @pl.when(here)
                def _():
                    for a in arrays:
                        along(a, q, piece(a, q, c), to_right).wait_recv()

                        @pl.when(further)
                        def _():
                            along(a, q, piece(a, q, c), to_right).start()

                        beside(a, q, 0).start()
                        beside(a, q, 1).start()
                        across(a, q, 0).start()
        if d > 1:
            for to_right, q, here in ends(d - 1):
                @pl.when(here)
                def _():
                    for a in arrays:
                        came = 0 if a == 0 else 1
                        beside(a, q, came).wait_recv()
                        onward(a, q).start()
                        across(a, q, 1 + came).start()
                        beside(a, q, 1 - came).wait_recv()
                        across(a, q, 2 - came).start()
    for d in range(1, line):
        for to_right, q, here in ends(d):
            @pl.when(here)
            def _():
                for a in arrays:
                    onward(a, q).wait_recv()
                    across(a, q, 3).start()
    for a in arrays:
        local(a).wait()
        own_across(a).wait()
    for d in range(0, line):
        for to_right, q, here in ends(d):
            further = (p < line - 1) if to_right else (p > 0)
            for a in arrays:
                @pl.when(here & further)
                def _():
                    along(a, q, piece(a, q, c), to_right).wait_send()
                if d > 0:
                    @pl.when(here)
                    def _():
                        beside(a, q, 0).wait_send()
                        beside(a, q, 1).wait_send()
                        onward(a, q).wait_send()
                        for j in range(4):
                            across(a, q, j).wait()


def gather_weights(shards, collective_id):
    n = lax.axis_size("exp")
    if lax.axis_size("ctx") != 4 or (shards[0].shape[0] // 4) % 16:
        return tuple(lax.all_gather(w, "exp", axis=0, tiled=True) for w in shards)
    line = n // 2
    count = len(shards)
    dma = pltpu.SemaphoreType.DMA
    return pl.pallas_call(
        functools.partial(weights_kernel, line, shards[0].shape[0] // 4),
        out_shape=tuple(jax.ShapeDtypeStruct((n * w.shape[0], w.shape[1]), w.dtype) for w in shards),
        in_specs=[ANY] * count,
        out_specs=(ANY,) * count,
        scratch_shapes=[
            dma((count,)),
            dma((count,)),
            dma((count,)),
            dma((2, line, count)),
            dma((line, count)),
            dma((2, line, count)),
            dma((2, line, count)),
            dma((line, count)),
            dma((line, count)),
            dma((line, 4, count)),
            dma((line, 4, count)),
        ],
        compiler_params=pltpu.CompilerParams(collective_id=collective_id, has_side_effects=True),
        name="gather_weights",
    )(*shards)


def spread_kernel(size, own, out, local_sem, send, recv):
    c, e = lax.axis_index("ctx"), lax.axis_index("exp")
    others = [lax.rem(c + i, size) for i in range(1, size)]
    greet([(True, there, e) for there in others])
    local = pltpu.make_async_copy(own, out.at[c], local_sem)
    local.start()
    for i, there in enumerate(others):
        remote(own, out.at[c], send.at[i], recv.at[i], there, e).start()
    local.wait()
    for i, there in enumerate(others):
        copy = remote(own, out.at[c], send.at[i], recv.at[i], there, e)
        copy.wait_send()
        copy.wait_recv()


def gather_context(own, collective_id):
    size = lax.axis_size("ctx")
    return pl.pallas_call(
        functools.partial(spread_kernel, size),
        out_shape=jax.ShapeDtypeStruct((size,) + own.shape, own.dtype),
        in_specs=[ANY],
        out_specs=ANY,
        scratch_shapes=[
            pltpu.SemaphoreType.DMA,
            pltpu.SemaphoreType.DMA((size - 1,)),
            pltpu.SemaphoreType.DMA((size - 1,)),
        ],
        compiler_params=pltpu.CompilerParams(collective_id=collective_id, has_side_effects=True),
        name="gather_context",
    )(own)


def context_sum_kernel(size, part, out, mine, arrived, local_sem, send, recv):
    c, e = lax.axis_index("ctx"), lax.axis_index("exp")
    others = [lax.rem(c + i, size) for i in range(1, size)]
    greet([(True, there, e) for there in others])
    local = pltpu.make_async_copy(part.at[c], mine, local_sem)
    local.start()
    for i, there in enumerate(others):
        remote(part.at[there], arrived.at[i], send.at[i], recv.at[i], there, e).start()
    local.wait()
    total = mine[...].astype(jnp.float32)
    for i, there in enumerate(others):
        remote(part.at[there], arrived.at[i], send.at[i], recv.at[i], there, e).wait()
        total = total + arrived[i].astype(jnp.float32)
    out[...] = total


def scatter_context(part, collective_id):
    size, rows, width = part.shape
    return pl.pallas_call(
        functools.partial(context_sum_kernel, size),
        out_shape=jax.ShapeDtypeStruct((rows, width), jnp.float32),
        in_specs=[ANY],
        out_specs=pl.BlockSpec(memory_space=pltpu.VMEM),
        scratch_shapes=[
            pltpu.VMEM((rows, width), part.dtype),
            pltpu.VMEM((size - 1, rows, width), part.dtype),
            pltpu.SemaphoreType.DMA,
            pltpu.SemaphoreType.DMA((size - 1,)),
            pltpu.SemaphoreType.DMA((size - 1,)),
        ],
        compiler_params=pltpu.CompilerParams(
            collective_id=collective_id, has_side_effects=True, vmem_limit_bytes=32 << 20
        ),
        name="scatter_context",
    )(part)


def context_total_kernel(size, part, out, mine, arrived, whole, load_sem, a_send, a_recv, b_send, b_recv, out_sem):
    c, e = lax.axis_index("ctx"), lax.axis_index("exp")
    others = [lax.rem(c + i, size) for i in range(1, size)]
    piece = mine.shape[0]
    greet([(True, there, e) for there in others])

    def rows_of(ref, j):
        return ref.at[pl.ds(pl.multiple_of(j * piece, 16), piece), :]

    load = pltpu.make_async_copy(rows_of(part, c), mine, load_sem)
    load.start()
    for i, there in enumerate(others):
        remote(rows_of(part, there), arrived.at[i], a_send.at[i], a_recv.at[i], there, e).start()
    load.wait()
    for i, there in enumerate(others):
        remote(rows_of(part, there), arrived.at[i], a_send.at[i], a_recv.at[i], there, e).wait()
    at_own = pl.ds(pl.multiple_of(c * piece, 16), piece)
    for j in range(piece // 16):
        at = pl.ds(j * 16, 16)
        total = mine[at, :].astype(jnp.float32)
        for i in range(size - 1):
            total = total + arrived[i, at, :].astype(jnp.float32)
        whole[pl.ds(pl.multiple_of(c * piece + j * 16, 16), 16), :] = total.astype(whole.dtype)
    for i, there in enumerate(others):
        remote(whole.at[at_own, :], whole.at[at_own, :], b_send.at[i], b_recv.at[i], there, e).start()
    for i, there in enumerate(others):
        source = lax.rem(c + size - 1 - i, size)
        copy = remote(rows_of(whole, source), rows_of(whole, source), b_send.at[i], b_recv.at[i], there, e)
        copy.wait()
    done = pltpu.make_async_copy(whole, out, out_sem)
    done.start()
    done.wait()


def total_context(part, collective_id):
    size = lax.axis_size("ctx")
    rows, width = part.shape
    if (rows // size) % 16:
        return lax.psum(part, "ctx")
    dma = pltpu.SemaphoreType.DMA
    return pl.pallas_call(
        functools.partial(context_total_kernel, size),
        out_shape=jax.ShapeDtypeStruct((rows, width), part.dtype),
        in_specs=[ANY],
        out_specs=ANY,
        scratch_shapes=[
            pltpu.VMEM((rows // size, width), part.dtype),
            pltpu.VMEM((size - 1, rows // size, width), part.dtype),
            pltpu.VMEM((rows, width), part.dtype),
            dma,
            dma((size - 1,)),
            dma((size - 1,)),
            dma((size - 1,)),
            dma((size - 1,)),
            dma,
        ],
        compiler_params=pltpu.CompilerParams(
            collective_id=collective_id, has_side_effects=True, vmem_limit_bytes=32 << 20
        ),
        name="total_context",
    )(part)


QUERY_HEADS = 12
KEY_VALUE_HEADS = 2
HEAD_WIDTH = 128
EPS = 1e-06
NEG = -1e30
ROPE_BASE = 1000000.0


def rope_tables(first_row, row_count, head_size):
    half_size = head_size // 2
    frequency = ROPE_BASE ** (-jnp.arange(half_size, dtype=jnp.float32) * (2.0 / head_size))
    places = (first_row + jnp.arange(row_count, dtype=jnp.int32)).astype(jnp.float32)
    angles = places[:, None] * frequency[None, :]
    cosine = jnp.cos(angles)
    sine_table = jnp.sin(angles)
    return (jnp.concatenate([cosine, cosine], 1), jnp.concatenate([sine_table, sine_table], 1))


def rotate(vector):
    half_size = vector.shape[-1] // 2
    return jnp.concatenate([-vector[..., half_size:], vector[..., :half_size]], -1)


def rotary_embed(vector, cosine, sine_table):
    return vector * cosine + rotate(vector) * sine_table


def rotary_back(gradient, cosine, sine_table):
    return gradient * cosine - rotate(gradient * sine_table)


def rms_rows(row_block):
    inverse = lax.rsqrt(jnp.mean(row_block * row_block, -1, keepdims=True) + EPS)
    return (row_block * inverse, inverse)


def rms_back(grad_normed, normed, inverse):
    return inverse * (grad_normed - normed * jnp.mean(grad_normed * normed, -1, keepdims=True))


def mm(a, b):
    return jnp.dot(a, b, preferred_element_type=jnp.float32)


def ein(spec, a, b):
    return jnp.einsum(spec, a, b, preferred_element_type=jnp.float32)


def spread_sum(part):
    flat = part.reshape(-1, part.shape[-1])
    piece = lax.psum_scatter(flat, "ctx", scatter_dimension=0, tiled=True)
    return lax.all_gather(piece, "ctx", axis=0, tiled=True).reshape(part.shape)


def shards(
    tokens,
    routes,
    gain_attn,
    w_query,
    key_value_weight,
    w_out,
    gain_ffn,
    w_router,
    w_gate,
    w_up,
    w_down,
    cotangent,
):
    f32 = jnp.float32
    bf16 = jnp.bfloat16
    highest = lax.Precision.HIGHEST
    rows_in = tokens[0]
    rows, width = rows_in.shape
    ctx_size, exp_size = lax.axis_size("ctx"), lax.axis_size("exp")
    ctx_index, exp_index = lax.axis_index("ctx"), lax.axis_index("exp")
    local_experts = w_gate.shape[0]
    experts = local_experts * exp_size
    top = routes.shape[2]
    capacity = 2 * rows * top // experts
    shard_rows = w_query.shape[0]
    heads, kv_heads, head = QUERY_HEADS, KEY_VALUE_HEADS, HEAD_WIDTH
    groups = heads // kv_heads
    q_width, kv_width = heads * head, kv_heads * head
    scaling = 1.0 / math.sqrt(head)
    first_row = ctx_index * rows

    grad_out_all = lax.all_gather(cotangent[0], "exp", axis=0)
    routes_all = lax.all_gather(routes[0], "exp", axis=0)

    small = jnp.concatenate(
        [
            w_router,
            gain_attn[:, None],
            gain_ffn[:, None],
            jnp.zeros((shard_rows, 128 - experts - 2), bf16),
        ],
        1,
    )
    qkv_full, out_full, small_full = gather_weights(
        (jnp.concatenate([w_query, key_value_weight], 1), w_out, small), 1
    )
    router_full = small_full[:, :experts]
    gain_one = small_full[:, experts].astype(f32)
    gain_two = small_full[:, experts + 1].astype(f32)

    cosine, sine_table = rope_tables(first_row, rows, head)
    cosine, sine_table = cosine[:, None, :], sine_table[:, None, :]
    resid_in = rows_in.astype(f32)
    normed_one, inverse_one = rms_rows(resid_in)
    hidden_one = (normed_one * gain_one).astype(bf16)
    qkv = mm(hidden_one, qkv_full)
    queries = rotary_embed(qkv[:, :q_width].reshape(rows, heads, head), cosine, sine_table).astype(bf16)
    keys_own = rotary_embed(
        qkv[:, q_width : q_width + kv_width].reshape(rows, kv_heads, head), cosine, sine_table
    ).astype(bf16)
    keyval_own = jnp.concatenate(
        [keys_own.reshape(rows, kv_width), qkv[:, q_width + kv_width :].astype(bf16)], 1
    )
    keyval = gather_context(keyval_own, 2).reshape(ctx_size * rows, 2 * kv_width)
    keys = keyval[:, :kv_width].reshape(ctx_size * rows, kv_heads, head)
    values = keyval[:, kv_width:].reshape(ctx_size * rows, kv_heads, head)
    grouped = queries.reshape(rows, kv_heads, groups, head)
    allowed = (
        jnp.arange(ctx_size * rows, dtype=jnp.int32)[None, :]
        <= (first_row + jnp.arange(rows, dtype=jnp.int32))[:, None]
    )
    scores = jnp.where(allowed, ein("qhgd,khd->hgqk", grouped, keys) * scaling, NEG)
    peak = jnp.max(scores, -1, keepdims=True)
    weights_now = jnp.exp(scores - peak)
    total = jnp.sum(weights_now, -1, keepdims=True)
    probs = weights_now / total
    probs_low = probs.astype(bf16)
    mixed = (
        ein("hgqk,khd->qhgd", probs_low, values).reshape(rows, q_width).astype(bf16)
    )
    resid_mid = resid_in + mm(mixed, out_full)
    normed_two, inverse_two = rms_rows(resid_mid)
    hidden_two = (normed_two * gain_two).astype(bf16)

    hidden_all = gather_rows(hidden_two, 3)
    named = jnp.any(
        routes_all[:, :, :, None] == jnp.arange(experts, dtype=jnp.int32), axis=2
    )
    logits = mm(hidden_all.reshape(exp_size * rows, width), router_full).reshape(exp_size, rows, experts)
    gates_all = jax.nn.softmax(jnp.where(named, logits, NEG), -1)
    mine = exp_index * local_experts
    named_here = lax.dynamic_slice_in_dim(named, mine, local_experts, 2)
    gates_here = lax.dynamic_slice_in_dim(gates_all, mine, local_experts, 2)
    named_int = named_here.astype(jnp.int32)
    slot = jnp.cumsum(named_int, 1) - named_int
    slot = jnp.where(named_here, slot, -1)
    pick = jnp.transpose(slot, (2, 0, 1))[:, :, None, :] == jnp.arange(capacity, dtype=jnp.int32)[:, None]
    gate_slots = jnp.sum(
        jnp.where(pick, jnp.transpose(gates_here, (2, 0, 1))[:, :, None, :], 0.0), -1
    ).reshape(local_experts, exp_size * capacity, 1)
    pick = pick.astype(bf16)
    slots = exp_size * capacity
    rows_exp = (
        ein("jbst,btd->jbsd", pick, hidden_all).astype(bf16).reshape(local_experts, slots, width)
    )
    grad_exp_rows = (
        ein("jbst,btd->jbsd", pick, grad_out_all).astype(bf16).reshape(local_experts, slots, width)
    )
    gate_pre = ein("erd,edf->erf", rows_exp, w_gate)
    up_pre = ein("erd,edf->erf", rows_exp, w_up)
    sigmoid_gate = jax.nn.sigmoid(gate_pre)
    silu_gate = gate_pre * sigmoid_gate
    activation = (silu_gate * up_pre).astype(bf16)
    grad_exp = (gate_slots * grad_exp_rows.astype(f32)).astype(bf16)
    grad_down = ein("erf,erd->efd", activation, grad_exp).astype(bf16)
    expert_rows = ein("erf,efd->erd", activation, w_down)
    grad_gate_slots = jnp.sum(expert_rows * grad_exp_rows.astype(f32), -1)
    gated_rows = (gate_slots * expert_rows).astype(bf16)
    out_part = ein(
        "jbst,jbsd->btd", pick, gated_rows.reshape(local_experts, exp_size, capacity, width)
    ).astype(bf16)
    grad_activ = ein("erd,efd->erf", grad_exp, w_down)
    grad_gate_pre = (
        grad_activ * up_pre * sigmoid_gate * (1.0 + gate_pre * (1.0 - sigmoid_gate))
    ).astype(bf16)
    grad_up_pre = (grad_activ * silu_gate).astype(bf16)
    grad_gate = ein("erd,erf->edf", rows_exp, grad_gate_pre).astype(bf16)
    grad_up = ein("erd,erf->edf", rows_exp, grad_up_pre).astype(bf16)
    grad_pairs = (
        ein("erf,edf->erd", grad_gate_pre, w_gate) + ein("erf,edf->erd", grad_up_pre, w_up)
    ).astype(bf16)
    grad_rows_part = ein(
        "jbst,jbsd->btd", pick, grad_pairs.reshape(local_experts, exp_size, capacity, width)
    ).astype(bf16)
    grad_gate_part = jnp.sum(
        pick.astype(f32) * grad_gate_slots.reshape(local_experts, exp_size, capacity, 1), 2
    )
    spots = (
        jnp.arange(experts, dtype=jnp.int32)[None, :]
        == mine + jnp.arange(local_experts, dtype=jnp.int32)[:, None]
    ).astype(f32)
    grad_gate_part = jnp.sum(grad_gate_part[..., None] * spots[:, None, None, :], 0)
    coarse = grad_gate_part.astype(bf16)
    fine = (grad_gate_part - coarse.astype(f32)).astype(bf16)
    extra = jnp.concatenate(
        [coarse, fine, jnp.zeros((exp_size, rows, 128 - 2 * experts), bf16)], 2
    )

    total_down = lax.psum(grad_down, "ctx")
    total_gate, total_up = spread_sum(grad_gate), spread_sum(grad_up)

    grad_rows = scatter_rows(jnp.concatenate([grad_rows_part, extra], 2), 4)
    out_sum = scatter_rows(out_part, 5)
    output = (resid_mid + out_sum.astype(f32)).astype(bf16)[None]

    gates_own = lax.dynamic_index_in_dim(gates_all, exp_index, 0, keepdims=False)
    grad_gates = (
        grad_rows[:, width : width + experts].astype(f32)
        + grad_rows[:, width + experts : width + 2 * experts].astype(f32)
    )
    weighted = jnp.sum(gates_own * grad_gates, -1, keepdims=True)
    grad_logits = gates_own * (grad_gates - weighted)
    grad_router_part = jnp.dot(hidden_two.astype(f32).T, grad_logits, precision=highest)
    grad_hidden_two = grad_rows[:, :width].astype(f32) + jnp.dot(
        grad_logits, router_full.astype(f32).T, precision=highest
    )
    grad_gain_two = jnp.sum(grad_hidden_two * normed_two, 0)
    grad_final = cotangent[0].astype(f32)
    grad_mid = grad_final + rms_back(grad_hidden_two * gain_two, normed_two, inverse_two)
    grad_attn = grad_mid.astype(bf16)
    grad_out_part = mm(mixed.T, grad_attn)
    grad_mixed = mm(grad_attn, out_full.T).astype(bf16).reshape(rows, kv_heads, groups, head)
    grad_values = ein("hgqk,qhgd->khd", probs_low, grad_mixed)
    grad_probs = ein("qhgd,khd->hgqk", grad_mixed, values)
    inner = jnp.sum(probs * grad_probs, -1, keepdims=True)
    grad_scores = (probs * (grad_probs - inner) * scaling).astype(bf16)
    grad_queries = ein("hgqk,khd->qhgd", grad_scores, keys).reshape(rows, heads, head)
    grad_keys = ein("hgqk,qhgd->khd", grad_scores, grouped)
    grad_keyval_part = jnp.concatenate(
        [grad_keys.reshape(ctx_size, rows, kv_width), grad_values.reshape(ctx_size, rows, kv_width)], 2
    ).astype(bf16)
    grad_keyval = scatter_context(grad_keyval_part, 6)
    grad_q_rows = rotary_back(grad_queries, cosine, sine_table).reshape(rows, q_width)
    grad_k_rows = rotary_back(
        grad_keyval[:, :kv_width].reshape(rows, kv_heads, head), cosine, sine_table
    ).reshape(rows, kv_width)
    grad_qkv = jnp.concatenate([grad_q_rows, grad_k_rows, grad_keyval[:, kv_width:]], 1).astype(bf16)
    grad_qkv_part = mm(hidden_one.T, grad_qkv)
    grad_hidden_one = mm(grad_qkv, qkv_full.T)
    grad_gain_one = jnp.sum(grad_hidden_one * normed_one, 0)
    grad_input = grad_mid + rms_back(grad_hidden_one * gain_one, normed_one, inverse_one)

    grad_small_part = jnp.concatenate(
        [
            grad_router_part,
            grad_gain_one[:, None],
            grad_gain_two[:, None],
            jnp.zeros((width, 128 - experts - 2), f32),
        ],
        1,
    )
    dense_part = jnp.concatenate(
        [grad_qkv_part.astype(bf16), grad_out_part.astype(bf16), grad_small_part.astype(bf16)], 1
    ).reshape(exp_size, shard_rows, -1)
    dense = scatter_rows(dense_part, 7)
    dense = total_context(dense, 8).astype(f32)
    split = q_width + 2 * kv_width
    small_total = dense[:, split + width :]
    return (
        output,
        grad_input[None],
        small_total[:, experts],
        dense[:, :q_width],
        dense[:, q_width:split],
        dense[:, split : split + width],
        small_total[:, experts + 1],
        small_total[:, :experts],
        total_gate.astype(f32),
        total_up.astype(f32),
        total_down.astype(f32),
    )


def solution(mesh):
    rows, wide, deep = P("exp", "ctx", None), P("exp", None), P("exp", None, None)
    flat = P("exp")
    return jax.shard_map(
        shards,
        mesh=mesh,
        in_specs=(rows, rows, flat, wide, wide, wide, flat, wide, deep, deep, deep, rows),
        out_specs=(rows, rows, flat, wide, wide, wide, flat, wide, deep, deep, deep),
        check_vma=False,
    )
```

```python
import functools
import math

import jax
import jax.numpy as jnp
from jax import lax
from jax.experimental import pallas as pl
from jax.experimental.pallas import tpu as pltpu
from jax.sharding import PartitionSpec as P

MESH = pl.DeviceIdType.MESH
ANY = pl.BlockSpec(memory_space=pl.ANY)


def remote(src, dst, send, recv, ctx, exp):
    return pltpu.make_async_remote_copy(
        src_ref=src, dst_ref=dst, send_sem=send, recv_sem=recv, device_id=(ctx, exp), device_id_type=MESH
    )


def greet(pairs):
    barrier = pltpu.get_barrier_semaphore()
    count = 0
    for here, ctx, exp in pairs:
        if here is True:
            pl.semaphore_signal(barrier, inc=1, device_id=(ctx, exp), device_id_type=MESH)
            count = count + 1
        else:
            @pl.when(here)
            def _():
                pl.semaphore_signal(barrier, inc=1, device_id=(ctx, exp), device_id_type=MESH)
            count = count + here.astype(jnp.int32)
    pl.semaphore_wait(barrier, count)


def gather_kernel(line, own, out, local_sem, z_send, z_recv, c_send, c_recv):
    c, e = lax.axis_index("ctx"), lax.axis_index("exp")
    p, k = e // 2, e % 2
    sibling = e + 1 - 2 * k
    greet([(p > 0, c, e - 2), (p < line - 1, c, e + 2), (True, c, sibling)])
    local = pltpu.make_async_copy(own, out.at[e], local_sem)
    local.start()

    def along(q, src, to_right):
        there = e + 2 if to_right else e - 2
        way = 0 if to_right else 1
        return remote(src, out.at[2 * q + k], z_send.at[way, q], z_recv.at[q], c, there)

    def across(q, src):
        return remote(src, out.at[2 * q + k], c_send.at[q], c_recv.at[q], c, sibling)

    @pl.when(p < line - 1)
    def _():
        along(p, own, True).start()

    @pl.when(p > 0)
    def _():
        along(p, own, False).start()

    across(p, own).start()
    for d in range(1, line):
        for to_right in (True, False):
            q = p - d if to_right else p + d
            here = (q >= 0) if to_right else (q < line)
            further = (p < line - 1) if to_right else (p > 0)

            @pl.when(here)
            def _():
                block = out.at[2 * q + k]
                along(q, block, to_right).wait_recv()

                @pl.when(further)
                def _():
                    along(q, block, to_right).start()

                across(q, block).start()

    local.wait()
    for d in range(0, line):
        for to_right in (True, False):
            if d == 0 and not to_right:
                continue
            q = p - d if to_right else p + d
            here = (q >= 0) if to_right else (q < line)

            @pl.when(here)
            def _():
                block = out.at[2 * q + k]
                across(q, block).wait()
    for d in range(0, line):
        for to_right in (True, False):
            q = p - d if to_right else p + d
            here = (q >= 0) if to_right else (q < line)
            further = (p < line - 1) if to_right else (p > 0)

            @pl.when(here & further)
            def _():
                along(q, out.at[2 * q + k], to_right).wait_send()


def gather_rows(own, collective_id):
    n = lax.axis_size("exp")
    line = n // 2
    return pl.pallas_call(
        functools.partial(gather_kernel, line),
        out_shape=jax.ShapeDtypeStruct((n,) + own.shape, own.dtype),
        in_specs=[ANY],
        out_specs=ANY,
        scratch_shapes=[
            pltpu.SemaphoreType.DMA,
            pltpu.SemaphoreType.DMA((2, line)),
            pltpu.SemaphoreType.DMA((line,)),
            pltpu.SemaphoreType.DMA((line,)),
            pltpu.SemaphoreType.DMA((line,)),
        ],
        compiler_params=pltpu.CompilerParams(collective_id=collective_id, has_side_effects=True),
        name="gather_rows",
    )(own)


def add_rows(dst, a, b, rows, step):
    def body(i, carried):
        at = pl.ds(pl.multiple_of(i * step, step), step)
        dst[at, :] = (a[at, :].astype(jnp.float32) + b[at, :].astype(jnp.float32)).astype(dst.dtype)
        return carried

    lax.fori_loop(0, rows // step, body, 0)


def scatter_kernel(line, part, out, mine, other, moving, load_sem, c_send, c_recv, z_send, z_recv):
    c, e = lax.axis_index("ctx"), lax.axis_index("exp")
    p, k = e // 2, e % 2
    sibling = e + 1 - 2 * k
    rows = part.shape[1]
    step = 16
    greet([(p > 0, c, e - 2), (p < line - 1, c, e + 2), (True, c, sibling)])

    def across(q):
        return remote(part.at[2 * q + 1 - k], other.at[q], c_send.at[q], c_recv.at[q], c, sibling)

    def load(q):
        return pltpu.make_async_copy(part.at[2 * q + k], mine.at[q], load_sem.at[q])

    def along(q, to_right):
        way = 0 if to_right else 1
        there = e + 2 if to_right else e - 2
        return remote(mine.at[q], moving.at[way, q], z_send.at[q], z_recv.at[way, q], c, there)

    order = []
    for d in range(line - 1, -1, -1):
        for to_right in (True, False):
            if d == 0 and not to_right:
                continue
            q = p + d if to_right else p - d
            here = (q < line) if to_right else (q >= 0)
            order.append((d, to_right, q, here))
    for d, to_right, q, here in order:
        @pl.when(here)
        def _():
            across(q).start()
            load(q).start()
    for d, to_right, q, here in order:
        @pl.when(here)
        def _():
            load(q).wait()
            across(q).wait()
            add_rows(mine.at[q], mine.at[q], other.at[q], rows, step)
            if d > 0:
                behind = (p > 0) if to_right else (p < line - 1)

                @pl.when(behind)
                def _():
                    along(q, to_right).wait_recv()
                    add_rows(mine.at[q], mine.at[q], moving.at[0 if to_right else 1, q], rows, step)

                along(q, to_right).start()
            else:
                for way, behind in ((0, p > 0), (1, p < line - 1)):
                    @pl.when(behind)
                    def _():
                        along(q, way == 0).wait_recv()
                        add_rows(mine.at[q], mine.at[q], moving.at[way, q], rows, step)

                done = pltpu.make_async_copy(mine.at[q], out, load_sem.at[q])
                done.start()
                done.wait()
    for d, to_right, q, here in order:
        if d > 0:
            @pl.when(here)
            def _():
                along(q, to_right).wait_send()


def scatter_rows(part, collective_id):
    n, rows, width = part.shape
    line = n // 2
    buffers = (line, rows, width)
    return pl.pallas_call(
        functools.partial(scatter_kernel, line),
        out_shape=jax.ShapeDtypeStruct((rows, width), part.dtype),
        in_specs=[ANY],
        out_specs=ANY,
        scratch_shapes=[
            pltpu.VMEM(buffers, part.dtype),
            pltpu.VMEM(buffers, part.dtype),
            pltpu.VMEM((2,) + buffers, part.dtype),
            pltpu.SemaphoreType.DMA((line,)),
            pltpu.SemaphoreType.DMA((line,)),
            pltpu.SemaphoreType.DMA((line,)),
            pltpu.SemaphoreType.DMA((line,)),
            pltpu.SemaphoreType.DMA((2, line)),
        ],
        compiler_params=pltpu.CompilerParams(
            collective_id=collective_id, has_side_effects=True, vmem_limit_bytes=56 << 20
        ),
        name="scatter_rows",
    )(part)


def weights_kernel(line, quarter, *refs):
    count = 3
    own, out = refs[:count], refs[count : 2 * count]
    local_sem, own_send, own_recv, z_send, z_recv, xy_send, xy_recv, d_send, d_recv, c_send, c_recv = refs[2 * count :]
    c, e = lax.axis_index("ctx"), lax.axis_index("exp")
    p, k = e // 2, e % 2
    sibling = e + 1 - 2 * k
    rows = own[0].shape[0]
    nbr = (c + 1 - 2 * (c % 2), (c + 2) % 4)
    opposite = 3 - c
    greet(
        [
            (p > 0, c, e - 2),
            (p < line - 1, c, e + 2),
            (True, c, sibling),
            (True, nbr[0], e),
            (True, nbr[1], e),
        ]
    )

    def whole(a):
        return out[a].at[pl.ds(pl.multiple_of(e * rows, 16), rows), :]

    def piece(a, q, column):
        return out[a].at[pl.ds(pl.multiple_of((2 * q + k) * rows + column * quarter, 16), quarter), :]

    def own_piece(a):
        return own[a].at[pl.ds(pl.multiple_of(c * quarter, 16), quarter), :]

    def local(a):
        return pltpu.make_async_copy(own[a], whole(a), local_sem.at[a])

    def own_across(a):
        return remote(own[a], whole(a), own_send.at[a], own_recv.at[a], c, sibling)

    def along(a, q, src, to_right):
        there = e + 2 if to_right else e - 2
        way = 0 if to_right else 1
        return remote(src, piece(a, q, c), z_send.at[way, q, a], z_recv.at[q, a], c, there)

    def beside(a, q, axis):
        return remote(piece(a, q, c), piece(a, q, c), xy_send.at[axis, q, a], xy_recv.at[axis, q, a], nbr[axis], e)

    def onward(a, q):
        came, goes = (0, 1) if a == 0 else (1, 0)
        block = piece(a, q, nbr[came])
        return remote(block, block, d_send.at[q, a], d_recv.at[q, a], nbr[goes], e)

    def across(a, q, j):
        column = (c, nbr[0], nbr[1], opposite)[j]
        block = piece(a, q, column)
        return remote(block, block, c_send.at[q, j, a], c_recv.at[q, j, a], c, sibling)

    arrays = range(count)
    for a in arrays:
        @pl.when(p < line - 1)
        def _():
            along(a, p, own_piece(a), True).start()

        @pl.when(p > 0)
        def _():
            along(a, p, own_piece(a), False).start()
    for a in arrays:
        own_across(a).start()
        local(a).start()

    def ends(d):
        for to_right in (True, False):
            q = p - d if to_right else p + d
            yield to_right, q, ((q >= 0) if to_right else (q < line))

    for d in range(1, line + 1):
        if d < line:
            for to_right, q, here in ends(d):
                further = (p < line - 1) if to_right else (p > 0)

                @pl.when(here)
                def _():
                    for a in arrays:
                        along(a, q, piece(a, q, c), to_right).wait_recv()

                        @pl.when(further)
                        def _():
                            along(a, q, piece(a, q, c), to_right).start()

                        beside(a, q, 0).start()
                        beside(a, q, 1).start()
                        across(a, q, 0).start()
        if d > 1:
            for to_right, q, here in ends(d - 1):
                @pl.when(here)
                def _():
                    for a in arrays:
                        came = 0 if a == 0 else 1
                        beside(a, q, came).wait_recv()
                        onward(a, q).start()
                        across(a, q, 1 + came).start()
                        beside(a, q, 1 - came).wait_recv()
                        across(a, q, 2 - came).start()
    for d in range(1, line):
        for to_right, q, here in ends(d):
            @pl.when(here)
            def _():
                for a in arrays:
                    onward(a, q).wait_recv()
                    across(a, q, 3).start()
    for a in arrays:
        local(a).wait()
        own_across(a).wait()
    for d in range(0, line):
        for to_right, q, here in ends(d):
            further = (p < line - 1) if to_right else (p > 0)
            for a in arrays:
                @pl.when(here & further)
                def _():
                    along(a, q, piece(a, q, c), to_right).wait_send()
                if d > 0:
                    @pl.when(here)
                    def _():
                        beside(a, q, 0).wait_send()
                        beside(a, q, 1).wait_send()
                        onward(a, q).wait_send()
                        for j in range(4):
                            across(a, q, j).wait()


def gather_weights(shards, collective_id):
    n = lax.axis_size("exp")
    if lax.axis_size("ctx") != 4 or (shards[0].shape[0] // 4) % 16:
        return tuple(lax.all_gather(w, "exp", axis=0, tiled=True) for w in shards)
    line = n // 2
    count = len(shards)
    dma = pltpu.SemaphoreType.DMA
    return pl.pallas_call(
        functools.partial(weights_kernel, line, shards[0].shape[0] // 4),
        out_shape=tuple(jax.ShapeDtypeStruct((n * w.shape[0], w.shape[1]), w.dtype) for w in shards),
        in_specs=[ANY] * count,
        out_specs=(ANY,) * count,
        scratch_shapes=[
            dma((count,)),
            dma((count,)),
            dma((count,)),
            dma((2, line, count)),
            dma((line, count)),
            dma((2, line, count)),
            dma((2, line, count)),
            dma((line, count)),
            dma((line, count)),
            dma((line, 4, count)),
            dma((line, 4, count)),
        ],
        compiler_params=pltpu.CompilerParams(collective_id=collective_id, has_side_effects=True),
        name="gather_weights",
    )(*shards)


def spread_kernel(size, own, out, local_sem, send, recv):
    c, e = lax.axis_index("ctx"), lax.axis_index("exp")
    others = [lax.rem(c + i, size) for i in range(1, size)]
    greet([(True, there, e) for there in others])
    local = pltpu.make_async_copy(own, out.at[c], local_sem)
    local.start()
    for i, there in enumerate(others):
        remote(own, out.at[c], send.at[i], recv.at[i], there, e).start()
    local.wait()
    for i, there in enumerate(others):
        copy = remote(own, out.at[c], send.at[i], recv.at[i], there, e)
        copy.wait_send()
        copy.wait_recv()


def gather_context(own, collective_id):
    size = lax.axis_size("ctx")
    return pl.pallas_call(
        functools.partial(spread_kernel, size),
        out_shape=jax.ShapeDtypeStruct((size,) + own.shape, own.dtype),
        in_specs=[ANY],
        out_specs=ANY,
        scratch_shapes=[
            pltpu.SemaphoreType.DMA,
            pltpu.SemaphoreType.DMA((size - 1,)),
            pltpu.SemaphoreType.DMA((size - 1,)),
        ],
        compiler_params=pltpu.CompilerParams(collective_id=collective_id, has_side_effects=True),
        name="gather_context",
    )(own)


def context_sum_kernel(size, part, out, mine, arrived, local_sem, send, recv):
    c, e = lax.axis_index("ctx"), lax.axis_index("exp")
    others = [lax.rem(c + i, size) for i in range(1, size)]
    greet([(True, there, e) for there in others])
    local = pltpu.make_async_copy(part.at[c], mine, local_sem)
    local.start()
    for i, there in enumerate(others):
        remote(part.at[there], arrived.at[i], send.at[i], recv.at[i], there, e).start()
    local.wait()
    total = mine[...].astype(jnp.float32)
    for i, there in enumerate(others):
        remote(part.at[there], arrived.at[i], send.at[i], recv.at[i], there, e).wait()
        total = total + arrived[i].astype(jnp.float32)
    out[...] = total


def scatter_context(part, collective_id):
    size, rows, width = part.shape
    return pl.pallas_call(
        functools.partial(context_sum_kernel, size),
        out_shape=jax.ShapeDtypeStruct((rows, width), jnp.float32),
        in_specs=[ANY],
        out_specs=pl.BlockSpec(memory_space=pltpu.VMEM),
        scratch_shapes=[
            pltpu.VMEM((rows, width), part.dtype),
            pltpu.VMEM((size - 1, rows, width), part.dtype),
            pltpu.SemaphoreType.DMA,
            pltpu.SemaphoreType.DMA((size - 1,)),
            pltpu.SemaphoreType.DMA((size - 1,)),
        ],
        compiler_params=pltpu.CompilerParams(
            collective_id=collective_id, has_side_effects=True, vmem_limit_bytes=32 << 20
        ),
        name="scatter_context",
    )(part)


def context_total_kernel(size, part, out, mine, arrived, whole, load_sem, a_send, a_recv, b_send, b_recv, out_sem):
    c, e = lax.axis_index("ctx"), lax.axis_index("exp")
    others = [lax.rem(c + i, size) for i in range(1, size)]
    piece = mine.shape[0]
    greet([(True, there, e) for there in others])

    def rows_of(ref, j):
        return ref.at[pl.ds(pl.multiple_of(j * piece, 16), piece), :]

    load = pltpu.make_async_copy(rows_of(part, c), mine, load_sem)
    load.start()
    for i, there in enumerate(others):
        remote(rows_of(part, there), arrived.at[i], a_send.at[i], a_recv.at[i], there, e).start()
    load.wait()
    for i, there in enumerate(others):
        remote(rows_of(part, there), arrived.at[i], a_send.at[i], a_recv.at[i], there, e).wait()
    at_own = pl.ds(pl.multiple_of(c * piece, 16), piece)
    for j in range(piece // 16):
        at = pl.ds(j * 16, 16)
        total = mine[at, :].astype(jnp.float32)
        for i in range(size - 1):
            total = total + arrived[i, at, :].astype(jnp.float32)
        whole[pl.ds(pl.multiple_of(c * piece + j * 16, 16), 16), :] = total.astype(whole.dtype)
    for i, there in enumerate(others):
        remote(whole.at[at_own, :], whole.at[at_own, :], b_send.at[i], b_recv.at[i], there, e).start()
    for i, there in enumerate(others):
        source = lax.rem(c + size - 1 - i, size)
        copy = remote(rows_of(whole, source), rows_of(whole, source), b_send.at[i], b_recv.at[i], there, e)
        copy.wait()
    done = pltpu.make_async_copy(whole, out, out_sem)
    done.start()
    done.wait()


def total_context(part, collective_id):
    size = lax.axis_size("ctx")
    rows, width = part.shape
    if (rows // size) % 16:
        return lax.psum(part, "ctx")
    dma = pltpu.SemaphoreType.DMA
    return pl.pallas_call(
        functools.partial(context_total_kernel, size),
        out_shape=jax.ShapeDtypeStruct((rows, width), part.dtype),
        in_specs=[ANY],
        out_specs=ANY,
        scratch_shapes=[
            pltpu.VMEM((rows // size, width), part.dtype),
            pltpu.VMEM((size - 1, rows // size, width), part.dtype),
            pltpu.VMEM((rows, width), part.dtype),
            dma,
            dma((size - 1,)),
            dma((size - 1,)),
            dma((size - 1,)),
            dma((size - 1,)),
            dma,
        ],
        compiler_params=pltpu.CompilerParams(
            collective_id=collective_id, has_side_effects=True, vmem_limit_bytes=32 << 20
        ),
        name="total_context",
    )(part)


def dot(a, b):
    return lax.dot_general(a, b, (((1,), (0,)), ((), ())), preferred_element_type=jnp.float32)


def dot_nt(a, b):
    return lax.dot_general(a, b, (((1,), (1,)), ((), ())), preferred_element_type=jnp.float32)


def dot_tn(a, b):
    return lax.dot_general(a, b, (((0,), (0,)), ((), ())), preferred_element_type=jnp.float32)


def visit(p, line, i):
    both = jnp.minimum(p, line - 1 - p)
    d = jnp.where(i <= 2 * both, (i + 1) // 2, i - both)
    left = jnp.where(i <= 2 * both, i % 2 == 1, p > line - 1 - p)
    q = jnp.where(left, p - d, p + d)
    first = (i == 0) | (i > 2 * both) | (i % 2 == 1)
    return q, d, first


def expert_kernel(line, local, cap, hidden, grads_all, picks, bias, router, w_gate, w_up, w_down, *refs):
    hidden_all, out_part, back_part, grad_down, grad_gate, grad_up = refs[:6]
    wg, wu, wd, xs, ds, act, dg, du, es, ys, h_buf, y_buf, out_stage, back_stage, in_stage, down_stage = refs[6:22]
    w_sem, own_sem, z_send, z_recv, c_send, c_recv, h_sem, y_sem, o_sem, b_sem, s_sem = refs[22:]
    f32, bf16 = jnp.float32, jnp.bfloat16
    c, e = lax.axis_index("ctx"), lax.axis_index("exp")
    p, k = e // 2, e % 2
    sibling = e + 1 - 2 * k
    rows, width = hidden.shape
    hidden_units = wg.shape[2]
    slots = 2 * cap
    lanes = router.shape[1]

    loads = [
        pltpu.make_async_copy(src, dst, w_sem.at[i])
        for i, (src, dst) in enumerate(((w_gate, wg), (w_up, wu), (w_down, wd)))
    ]
    for copy in loads:
        copy.start()
    greet([(p > 0, c, e - 2), (p < line - 1, c, e + 2), (True, c, sibling)])
    own = pltpu.make_async_copy(hidden, hidden_all.at[e], own_sem)
    own.start()

    def along(q, src, to_right):
        there = e + 2 if to_right else e - 2
        return remote(src, hidden_all.at[2 * q + k], z_send.at[0 if to_right else 1, q], z_recv.at[q], c, there)

    def across(q, src):
        return remote(src, hidden_all.at[2 * q + k], c_send.at[q], c_recv.at[q], c, sibling)

    def load_hidden(q, slot):
        return pltpu.make_async_copy(hidden_all.at[pl.ds(2 * q, 2)], h_buf.at[slot], h_sem.at[slot])

    def load_grads(q, slot):
        return pltpu.make_async_copy(grads_all.at[pl.ds(2 * q, 2)], y_buf.at[slot], y_sem.at[slot])

    def store_out(q, slot):
        return pltpu.make_async_copy(out_stage.at[slot], out_part.at[pl.ds(2 * q, 2)], o_sem.at[slot])

    def store_back(q, slot):
        return pltpu.make_async_copy(back_stage.at[slot], back_part.at[pl.ds(2 * q, 2)], b_sem.at[slot])

    @pl.when(p < line - 1)
    def _():
        along(p, hidden, True).start()

    @pl.when(p > 0)
    def _():
        along(p, hidden, False).start()

    across(p, hidden).start()
    load_grads(p, 0).start()

    def pump(d):
        for to_right in (True, False):
            q = p - d if to_right else p + d
            here = (q >= 0) if to_right else (q < line)
            further = (p < line - 1) if to_right else (p > 0)

            @pl.when(here)
            def _():
                block = hidden_all.at[2 * q + k]
                along(q, block, to_right).wait_recv()

                @pl.when(further)
                def _():
                    along(q, block, to_right).start()

                across(q, block).start()

    own.wait()
    for copy in loads:
        copy.wait()

    def one_chip(i, carried):
        q, d, first = visit(p, line, i)
        slot = i % 2

        across(q, hidden).wait_recv()
        load_hidden(q, slot).start()

        @pl.when(i < line - 1)
        def _():
            load_grads(visit(p, line, i + 1)[0], 1 - slot).start()

        load_hidden(q, slot).wait()
        load_grads(q, slot).wait()

        @pl.when(i >= 2)
        def _():
            store_out(visit(p, line, i - 2)[0], slot).wait()
            store_back(visit(p, line, i - 2)[0], slot).wait()

        gate_slots = []
        lane = lax.broadcasted_iota(jnp.int32, (local * cap, lanes), 1)
        expert_of_row = lax.broadcasted_iota(jnp.int32, (local * cap, lanes), 0) // cap
        for b in range(2):
            pick = picks[2 * q + b]
            block = h_buf[slot, b]
            picked = dot(pick, block).astype(bf16)
            for j in range(local):
                xs[j, q, b] = picked[j * cap : (j + 1) * cap]
            logits = dot(block, router[...]) + bias[2 * q + b].astype(f32)
            raised = jnp.exp(logits - jnp.max(logits, -1, keepdims=True))
            gates = raised / jnp.sum(raised, -1, keepdims=True)
            coarse = gates.astype(bf16)
            fine = (gates - coarse.astype(f32)).astype(bf16)
            at_slots = dot(pick, coarse) + dot(pick, fine)
            gate_slot = jnp.sum(jnp.where(lane == e * local + expert_of_row, at_slots, 0.0), -1, keepdims=True)
            gate_slots.append(gate_slot)
            grad_rows = dot(pick, y_buf[slot, b])
            grad_pairs = (gate_slot * grad_rows).astype(bf16)
            grad_rows = grad_rows.astype(bf16)
            for j in range(local):
                es[j, b] = grad_rows[j * cap : (j + 1) * cap]
                ds[j, q, b] = grad_pairs[j * cap : (j + 1) * cap]

        tile = 256
        for j in range(local):
            rows_j = xs[j, q].reshape(slots, width)
            grads_j = ds[j, q].reshape(slots, width)

            def units(t, carried):
                at = pl.ds(pl.multiple_of(t * tile, tile), tile)
                gate_pre = dot(rows_j, wg[j, :, at])
                up_pre = dot(rows_j, wu[j, :, at])
                grad_act = dot_nt(grads_j, wd[j, at, :])
                sigmoid = 1.0 / (1.0 + jnp.exp(-gate_pre))
                silu = gate_pre * sigmoid
                act[j, q, :, at] = (silu * up_pre).astype(bf16)
                dg[j, q, :, at] = (grad_act * up_pre * sigmoid * (1.0 + gate_pre * (1.0 - sigmoid))).astype(bf16)
                du[j, q, :, at] = (grad_act * silu).astype(bf16)
                return carried

            lax.fori_loop(0, hidden_units // tile, units, 0)

        wide = 512
        pick_pair = [picks[2 * q + b] for b in range(2)]

        def outputs(t, sums):
            at = pl.ds(pl.multiple_of(t * wide, wide), wide)
            gated, back, new_sums = [], [], []
            for j in range(local):
                y = dot(act[j, q], wd[j, :, at])
                back_j = dot_nt(dg[j, q], wg[j, at, :]) + dot_nt(du[j, q], wu[j, at, :])
                new = []
                for b in range(2):
                    half = slice(b * cap, (b + 1) * cap)
                    y_b = y[half]
                    new.append(sums[j][b] + jnp.sum(y_b * es[j, b, :, at].astype(f32), -1, keepdims=True))
                    gated.append((gate_slots[b][j * cap : (j + 1) * cap] * y_b).astype(bf16))
                    back.append(back_j[half].astype(bf16))
                new_sums.append(tuple(new))
            for b in range(2):
                mine = jnp.concatenate([gated[2 * j + b] for j in range(local)], 0)
                out_stage[slot, b, :, at] = dot_tn(pick_pair[b], mine).astype(bf16)
                mine = jnp.concatenate([back[2 * j + b] for j in range(local)], 0)
                back_stage[slot, b, :, at] = dot_tn(pick_pair[b], mine).astype(bf16)
            return tuple(new_sums)

        nothing = jnp.zeros((cap, 1), f32)
        sums = lax.fori_loop(
            0, width // wide, outputs, tuple((nothing, nothing) for _ in range(local))
        )
        for b in range(2):
            grad_gates = jnp.concatenate([sums[j][b] for j in range(local)], 0)
            coarse = grad_gates.astype(bf16).astype(f32)
            spot = e * local + expert_of_row
            spread = jnp.where(
                lane == spot, coarse, jnp.where(lane == spot + lanes // 2, grad_gates - coarse, 0.0)
            ).astype(bf16)
            back_stage[slot, b, :, width : width + lanes] = dot_tn(pick_pair[b], spread).astype(bf16)
        store_out(q, slot).start()
        store_back(q, slot).start()

        @pl.when(first & (d + 1 < line))
        def _():
            pump(d + 1)

        return carried

    lax.fori_loop(0, line, one_chip, 0)

    def stores(stage, target, sem, j, t, tile):
        return pltpu.make_async_copy(
            stage.at[t % 2], target.at[j, :, pl.ds(pl.multiple_of(t * tile, tile), tile)], sem.at[t % 2]
        )

    def products(left, right, stage, target, sem, j, tile, count):
        deep = line * slots

        def one_tile(t, carried):
            at = pl.ds(pl.multiple_of(t * tile, tile), tile)

            @pl.when(t >= 2)
            def _():
                stores(stage, target, sem, j, t - 2, tile).wait()

            stage[t % 2] = dot_tn(left(), right(at)).astype(bf16)
            stores(stage, target, sem, j, t, tile).start()
            return carried

        lax.fori_loop(0, count, one_tile, 0)
        for t in range(max(0, count - 2), count):
            stores(stage, target, sem, j, t, tile).wait()

    deep = line * slots
    for j in range(local):
        products(
            lambda: act[j].reshape(deep, hidden_units),
            lambda at: ds[j, :, :, :, at].reshape(deep, 512),
            down_stage, grad_down, s_sem, j, 512, width // 512,
        )
    for j in range(local):
        for source, target in ((dg, grad_gate), (du, grad_up)):
            products(
                lambda: xs[j].reshape(deep, width),
                lambda at: source[j, :, :, at].reshape(deep, 256),
                in_stage, target, s_sem, j, 256, hidden_units // 256,
            )

    for i in range(max(0, line - 2), line):
        q = visit(p, line, jnp.int32(i))[0]
        store_out(q, i % 2).wait()
        store_back(q, i % 2).wait()
    for d in range(line):
        for to_right in (True, False):
            if d == 0 and not to_right:
                continue
            q = p - d if to_right else p + d
            here = (q >= 0) if to_right else (q < line)

            @pl.when(here)
            def _():
                across(q, hidden).wait_send()
    for d in range(line):
        for to_right in (True, False):
            q = p - d if to_right else p + d
            here = (q >= 0) if to_right else (q < line)
            further = (p < line - 1) if to_right else (p > 0)

            @pl.when(here & further)
            def _():
                along(q, hidden, to_right).wait_send()


def expert_pass(hidden, grads_all, picks, bias, router, w_gate, w_up, w_down, collective_id):
    n = lax.axis_size("exp")
    line = n // 2
    rows, width = hidden.shape
    local, _, units = w_gate.shape
    cap = picks.shape[1] // local
    bf16 = jnp.bfloat16
    lanes = router.shape[1]
    dma = pltpu.SemaphoreType.DMA
    vmem = pl.BlockSpec(memory_space=pltpu.VMEM)
    slots = n * cap
    return pl.pallas_call(
        functools.partial(expert_kernel, line, local, cap),
        out_shape=(
            jax.ShapeDtypeStruct((n, rows, width), bf16),
            jax.ShapeDtypeStruct((n, rows, width), bf16),
            jax.ShapeDtypeStruct((n, rows, width + lanes), bf16),
            jax.ShapeDtypeStruct((local, units, width), bf16),
            jax.ShapeDtypeStruct((local, width, units), bf16),
            jax.ShapeDtypeStruct((local, width, units), bf16),
        ),
        in_specs=[ANY, ANY, vmem, vmem, vmem, ANY, ANY, ANY],
        out_specs=(ANY,) * 6,
        scratch_shapes=[
            pltpu.VMEM((local, width, units), bf16),
            pltpu.VMEM((local, width, units), bf16),
            pltpu.VMEM((local, units, width), bf16),
            pltpu.VMEM((local, line, 2, cap, width), bf16),
            pltpu.VMEM((local, line, 2, cap, width), bf16),
            pltpu.VMEM((local, line, 2 * cap, units), bf16),
            pltpu.VMEM((local, line, 2 * cap, units), bf16),
            pltpu.VMEM((local, line, 2 * cap, units), bf16),
            pltpu.VMEM((local, 2, cap, width), bf16),
            pltpu.VMEM((8, 128), jnp.float32),
            pltpu.VMEM((2, 2, rows, width), bf16),
            pltpu.VMEM((2, 2, rows, width), bf16),
            pltpu.VMEM((2, 2, rows, width), bf16),
            pltpu.VMEM((2, 2, rows, width + lanes), bf16),
            pltpu.VMEM((2, width, 256), bf16),
            pltpu.VMEM((2, units, 512), bf16),
            dma((3,)),
            dma,
            dma((2, line)),
            dma((line,)),
            dma((line,)),
            dma((line,)),
            dma((2,)),
            dma((2,)),
            dma((2,)),
            dma((2,)),
            dma((2,)),
        ],
        compiler_params=pltpu.CompilerParams(
            collective_id=collective_id, has_side_effects=True, vmem_limit_bytes=62 << 20
        ),
        name="expert_pass",
    )(hidden, grads_all, picks, bias, router, w_gate, w_up, w_down)


QUERY_HEADS = 12
KEY_VALUE_HEADS = 2
HEAD_WIDTH = 128
EPS = 1e-06
NEG = -1e30
ROPE_BASE = 1000000.0


def rope_tables(first_row, row_count, head_size):
    half_size = head_size // 2
    frequency = ROPE_BASE ** (-jnp.arange(half_size, dtype=jnp.float32) * (2.0 / head_size))
    places = (first_row + jnp.arange(row_count, dtype=jnp.int32)).astype(jnp.float32)
    angles = places[:, None] * frequency[None, :]
    cosine = jnp.cos(angles)
    sine_table = jnp.sin(angles)
    return (jnp.concatenate([cosine, cosine], 1), jnp.concatenate([sine_table, sine_table], 1))


def rotate(vector):
    half_size = vector.shape[-1] // 2
    return jnp.concatenate([-vector[..., half_size:], vector[..., :half_size]], -1)


def rotary_embed(vector, cosine, sine_table):
    return vector * cosine + rotate(vector) * sine_table


def rotary_back(gradient, cosine, sine_table):
    return gradient * cosine - rotate(gradient * sine_table)


def rms_rows(row_block):
    inverse = lax.rsqrt(jnp.mean(row_block * row_block, -1, keepdims=True) + EPS)
    return (row_block * inverse, inverse)


def rms_back(grad_normed, normed, inverse):
    return inverse * (grad_normed - normed * jnp.mean(grad_normed * normed, -1, keepdims=True))


def mm(a, b):
    return jnp.dot(a, b, preferred_element_type=jnp.float32)


def ein(spec, a, b):
    return jnp.einsum(spec, a, b, preferred_element_type=jnp.float32)


def spread_sum(part):
    flat = part.reshape(-1, part.shape[-1])
    piece = lax.psum_scatter(flat, "ctx", scatter_dimension=0, tiled=True)
    return lax.all_gather(piece, "ctx", axis=0, tiled=True).reshape(part.shape)


def shards(
    tokens,
    routes,
    gain_attn,
    w_query,
    key_value_weight,
    w_out,
    gain_ffn,
    w_router,
    w_gate,
    w_up,
    w_down,
    cotangent,
):
    f32 = jnp.float32
    bf16 = jnp.bfloat16
    highest = lax.Precision.HIGHEST
    rows_in = tokens[0]
    rows, width = rows_in.shape
    ctx_size, exp_size = lax.axis_size("ctx"), lax.axis_size("exp")
    ctx_index, exp_index = lax.axis_index("ctx"), lax.axis_index("exp")
    local_experts = w_gate.shape[0]
    experts = local_experts * exp_size
    top = routes.shape[2]
    capacity = 2 * rows * top // experts
    shard_rows = w_query.shape[0]
    heads, kv_heads, head = QUERY_HEADS, KEY_VALUE_HEADS, HEAD_WIDTH
    groups = heads // kv_heads
    q_width, kv_width = heads * head, kv_heads * head
    scaling = 1.0 / math.sqrt(head)
    first_row = ctx_index * rows

    grad_out_all = lax.all_gather(cotangent[0], "exp", axis=0)
    routes_all = lax.all_gather(routes[0], "exp", axis=0)

    small = jnp.concatenate(
        [
            w_router,
            gain_attn[:, None],
            gain_ffn[:, None],
            jnp.zeros((shard_rows, 128 - experts - 2), bf16),
        ],
        1,
    )
    qkv_full, out_full, small_full = gather_weights(
        (jnp.concatenate([w_query, key_value_weight], 1), w_out, small), 1
    )
    router_full = small_full[:, :experts]
    gain_one = small_full[:, experts].astype(f32)
    gain_two = small_full[:, experts + 1].astype(f32)

    cosine, sine_table = rope_tables(first_row, rows, head)
    cosine, sine_table = cosine[:, None, :], sine_table[:, None, :]
    resid_in = rows_in.astype(f32)
    normed_one, inverse_one = rms_rows(resid_in)
    hidden_one = (normed_one * gain_one).astype(bf16)
    qkv = mm(hidden_one, qkv_full)
    queries = rotary_embed(qkv[:, :q_width].reshape(rows, heads, head), cosine, sine_table).astype(bf16)
    keys_own = rotary_embed(
        qkv[:, q_width : q_width + kv_width].reshape(rows, kv_heads, head), cosine, sine_table
    ).astype(bf16)
    keyval_own = jnp.concatenate(
        [keys_own.reshape(rows, kv_width), qkv[:, q_width + kv_width :].astype(bf16)], 1
    )
    keyval = gather_context(keyval_own, 2).reshape(ctx_size * rows, 2 * kv_width)
    keys = keyval[:, :kv_width].reshape(ctx_size * rows, kv_heads, head)
    values = keyval[:, kv_width:].reshape(ctx_size * rows, kv_heads, head)
    grouped = queries.reshape(rows, kv_heads, groups, head)
    allowed = (
        jnp.arange(ctx_size * rows, dtype=jnp.int32)[None, :]
        <= (first_row + jnp.arange(rows, dtype=jnp.int32))[:, None]
    )
    scores = jnp.where(allowed, ein("qhgd,khd->hgqk", grouped, keys) * scaling, NEG)
    peak = jnp.max(scores, -1, keepdims=True)
    weights_now = jnp.exp(scores - peak)
    total = jnp.sum(weights_now, -1, keepdims=True)
    probs = weights_now / total
    probs_low = probs.astype(bf16)
    mixed = (
        ein("hgqk,khd->qhgd", probs_low, values).reshape(rows, q_width).astype(bf16)
    )
    resid_mid = resid_in + mm(mixed, out_full)
    normed_two, inverse_two = rms_rows(resid_mid)
    hidden_two = (normed_two * gain_two).astype(bf16)

    named = jnp.any(
        routes_all[:, :, :, None] == jnp.arange(128, dtype=jnp.int32), axis=2
    )
    bias = jnp.where(named, 0.0, NEG).astype(bf16)
    mine = exp_index * local_experts
    named_here = lax.dynamic_slice_in_dim(named, mine, local_experts, 2)
    named_int = named_here.astype(jnp.int32)
    slot = jnp.cumsum(named_int, 1) - named_int
    slot = jnp.transpose(jnp.where(named_here, slot, -1), (0, 2, 1))
    picks = (
        (slot[:, :, None, :] == jnp.arange(capacity, dtype=jnp.int32)[:, None])
        .astype(bf16)
        .reshape(exp_size, local_experts * capacity, rows)
    )
    hidden_all, out_part, back_part, grad_down, grad_gate, grad_up = expert_pass(
        hidden_two, grad_out_all, picks, bias, small_full, w_gate, w_up, w_down, 3
    )
    total_down, total_gate, total_up = lax.psum((grad_down, grad_gate, grad_up), "ctx")
    own_bias = lax.dynamic_index_in_dim(bias, exp_index, 0, keepdims=False)[:, :experts]
    gates_own = jax.nn.softmax(mm(hidden_two, router_full) + own_bias.astype(f32), -1)

    grad_rows = scatter_rows(back_part, 4)
    out_sum = scatter_rows(out_part, 5)
    output = (resid_mid + out_sum.astype(f32)).astype(bf16)[None]

    grad_gates = (
        grad_rows[:, width : width + experts].astype(f32)
        + grad_rows[:, width + 64 : width + 64 + experts].astype(f32)
    )
    weighted = jnp.sum(gates_own * grad_gates, -1, keepdims=True)
    grad_logits = gates_own * (grad_gates - weighted)
    grad_router_part = jnp.dot(hidden_two.astype(f32).T, grad_logits, precision=highest)
    grad_hidden_two = grad_rows[:, :width].astype(f32) + jnp.dot(
        grad_logits, router_full.astype(f32).T, precision=highest
    )
    grad_gain_two = jnp.sum(grad_hidden_two * normed_two, 0)
    grad_final = cotangent[0].astype(f32)
    grad_mid = grad_final + rms_back(grad_hidden_two * gain_two, normed_two, inverse_two)
    grad_attn = grad_mid.astype(bf16)
    grad_out_part = mm(mixed.T, grad_attn)
    grad_mixed = mm(grad_attn, out_full.T).astype(bf16).reshape(rows, kv_heads, groups, head)
    grad_values = ein("hgqk,qhgd->khd", probs_low, grad_mixed)
    grad_probs = ein("qhgd,khd->hgqk", grad_mixed, values)
    inner = jnp.sum(probs * grad_probs, -1, keepdims=True)
    grad_scores = (probs * (grad_probs - inner) * scaling).astype(bf16)
    grad_queries = ein("hgqk,khd->qhgd", grad_scores, keys).reshape(rows, heads, head)
    grad_keys = ein("hgqk,qhgd->khd", grad_scores, grouped)
    grad_keyval_part = jnp.concatenate(
        [grad_keys.reshape(ctx_size, rows, kv_width), grad_values.reshape(ctx_size, rows, kv_width)], 2
    ).astype(bf16)
    grad_keyval = scatter_context(grad_keyval_part, 6)
    grad_q_rows = rotary_back(grad_queries, cosine, sine_table).reshape(rows, q_width)
    grad_k_rows = rotary_back(
        grad_keyval[:, :kv_width].reshape(rows, kv_heads, head), cosine, sine_table
    ).reshape(rows, kv_width)
    grad_qkv = jnp.concatenate([grad_q_rows, grad_k_rows, grad_keyval[:, kv_width:]], 1).astype(bf16)
    grad_qkv_part = mm(hidden_one.T, grad_qkv)
    grad_hidden_one = mm(grad_qkv, qkv_full.T)
    grad_gain_one = jnp.sum(grad_hidden_one * normed_one, 0)
    grad_input = grad_mid + rms_back(grad_hidden_one * gain_one, normed_one, inverse_one)

    grad_small_part = jnp.concatenate(
        [
            grad_router_part,
            grad_gain_one[:, None],
            grad_gain_two[:, None],
            jnp.zeros((width, 128 - experts - 2), f32),
        ],
        1,
    )
    dense_part = jnp.concatenate(
        [grad_qkv_part.astype(bf16), grad_out_part.astype(bf16), grad_small_part.astype(bf16)], 1
    ).reshape(exp_size, shard_rows, -1)
    dense = scatter_rows(dense_part, 7)
    dense = total_context(dense, 8).astype(f32)
    split = q_width + 2 * kv_width
    small_total = dense[:, split + width :]
    return (
        output,
        grad_input[None],
        small_total[:, experts],
        dense[:, :q_width],
        dense[:, q_width:split],
        dense[:, split : split + width],
        small_total[:, experts + 1],
        small_total[:, :experts],
        total_gate.astype(f32),
        total_up.astype(f32),
        total_down.astype(f32),
    )


def solution(mesh):
    rows, wide, deep = P("exp", "ctx", None), P("exp", None), P("exp", None, None)
    flat = P("exp")
    return jax.shard_map(
        shards,
        mesh=mesh,
        in_specs=(rows, rows, flat, wide, wide, wide, flat, wide, deep, deep, deep, rows),
        out_specs=(rows, rows, flat, wide, wide, wide, flat, wide, deep, deep, deep),
        check_vma=False,
    )
```

```python
import functools
import math

import jax
import jax.numpy as jnp
from jax import lax
from jax.experimental import pallas as pl
from jax.experimental.pallas import tpu as pltpu
from jax.sharding import PartitionSpec as P

MESH = pl.DeviceIdType.MESH
ANY = pl.BlockSpec(memory_space=pl.ANY)


def remote(src, dst, send, recv, ctx, exp):
    return pltpu.make_async_remote_copy(
        src_ref=src, dst_ref=dst, send_sem=send, recv_sem=recv, device_id=(ctx, exp), device_id_type=MESH
    )


def greet(pairs):
    barrier = pltpu.get_barrier_semaphore()
    count = 0
    for here, ctx, exp in pairs:
        if here is True:
            pl.semaphore_signal(barrier, inc=1, device_id=(ctx, exp), device_id_type=MESH)
            count = count + 1
        else:
            @pl.when(here)
            def _():
                pl.semaphore_signal(barrier, inc=1, device_id=(ctx, exp), device_id_type=MESH)
            count = count + here.astype(jnp.int32)
    pl.semaphore_wait(barrier, count)


QUERY_HEADS = 12
KEY_VALUE_HEADS = 2
HEAD_WIDTH = 128
EPS = 1e-06
NEG = -1e30
ROPE_BASE = 1000000.0


class Gathering:
    def __init__(self, line, own, out, sems):
        self.line, self.own, self.out = line, own, out
        self.local_sem, self.z_send, self.z_recv, self.c_send, self.c_recv = sems
        self.c, self.e = lax.axis_index("ctx"), lax.axis_index("exp")
        self.p, self.k = self.e // 2, self.e % 2

    def along(self, q, src, to_right):
        there = self.e + 2 if to_right else self.e - 2
        way = 0 if to_right else 1
        return remote(src, self.out.at[2 * q + self.k], self.z_send.at[way, q], self.z_recv.at[q], self.c, there)

    def across(self, q, src):
        there = self.e + 1 - 2 * self.k
        return remote(src, self.out.at[2 * q + self.k], self.c_send.at[q], self.c_recv.at[q], self.c, there)

    def local(self):
        return pltpu.make_async_copy(self.own, self.out.at[self.e], self.local_sem)

    def ends(self, d):
        for to_right in (True, False):
            q = self.p - d if to_right else self.p + d
            here = (q >= 0) if to_right else (q < self.line)
            further = (self.p < self.line - 1) if to_right else (self.p > 0)
            yield to_right, q, here, further

    def begin(self):
        for to_right, q, _, further in self.ends(0):
            @pl.when(further)
            def _():
                self.along(q, self.own, to_right).start()

        self.across(self.p, self.own).start()
        self.local().start()

    def pump(self, d):
        for to_right, q, here, further in self.ends(d):
            @pl.when(here)
            def _():
                block = self.out.at[2 * q + self.k]
                self.along(q, block, to_right).wait_recv()

                @pl.when(further)
                def _():
                    self.along(q, block, to_right).start()

                self.across(q, block).start()

    def end(self):
        self.local().wait()
        for d in range(self.line):
            for to_right, q, here, further in self.ends(d):
                if d > 0 or to_right:
                    @pl.when(here)
                    def _():
                        self.across(q, self.own).wait()

                @pl.when(here & further)
                def _():
                    self.along(q, self.own, to_right).wait_send()

    @staticmethod
    def scratch(line):
        dma = pltpu.SemaphoreType.DMA
        return [dma, dma((2, line)), dma((line,)), dma((line,)), dma((line,))]


def gather_kernel(line, own, out, *sems):
    c, e = lax.axis_index("ctx"), lax.axis_index("exp")
    greet([(e >= 2, c, e - 2), (e < 2 * line - 2, c, e + 2), (True, c, e + 1 - 2 * (e % 2))])
    gathering = Gathering(line, own, out, sems)
    gathering.begin()
    for d in range(1, line):
        gathering.pump(d)
    gathering.end()


def gather_rows(own, collective_id):
    n = lax.axis_size("exp")
    return pl.pallas_call(
        functools.partial(gather_kernel, n // 2),
        out_shape=jax.ShapeDtypeStruct((n,) + own.shape, own.dtype),
        in_specs=[ANY],
        out_specs=ANY,
        scratch_shapes=Gathering.scratch(n // 2),
        compiler_params=pltpu.CompilerParams(collective_id=collective_id, has_side_effects=True),
        name="gather_rows",
    )(own)


def add_rows(dst, a, b, rows, step):
    def body(i, carried):
        at = pl.ds(pl.multiple_of(i * step, step), step)
        dst[at, :] = (a[at, :].astype(jnp.float32) + b[at, :].astype(jnp.float32)).astype(dst.dtype)
        return carried

    lax.fori_loop(0, rows // step, body, 0)


class Summing:
    def __init__(self, line, part, mine, other, moving, sems):
        self.line, self.part, self.mine, self.other, self.moving = line, part, mine, other, moving
        self.load_sem, self.c_send, self.c_recv, self.z_send, self.z_recv = sems
        self.c, self.e = lax.axis_index("ctx"), lax.axis_index("exp")
        self.p, self.k = self.e // 2, self.e % 2
        self.rows = part.shape[1]

    def across(self, q):
        there = self.e + 1 - 2 * self.k
        return remote(
            self.part.at[2 * q + 1 - self.k], self.other.at[q], self.c_send.at[q], self.c_recv.at[q], self.c, there
        )

    def load(self, q):
        return pltpu.make_async_copy(self.part.at[2 * q + self.k], self.mine.at[q], self.load_sem.at[q])

    def along(self, q, to_right):
        there = self.e + 2 if to_right else self.e - 2
        slot = q if to_right else jnp.where(q == self.p - 1, self.line, q)
        return remote(self.mine.at[q], self.moving.at[slot], self.z_send.at[q], self.z_recv.at[slot], self.c, there)

    def arrived(self, q, slot):
        return remote(self.mine.at[q], self.moving.at[slot], self.z_send.at[q], self.z_recv.at[slot], self.c, self.e)

    def ends(self, d):
        for to_right in (True, False):
            if d > 0 or to_right:
                q = self.p + d if to_right else self.p - d
                yield to_right, q, ((q < self.line) if to_right else (q >= 0))

    def begin(self):
        for d in range(self.line - 1, -1, -1):
            for _, q, here in self.ends(d):
                @pl.when(here)
                def _():
                    self.across(q).start()
                    self.load(q).start()

    def step(self, d):
        p, line = self.p, self.line
        for to_right, q, here in self.ends(d):
            @pl.when(here)
            def _():
                self.load(q).wait()
                self.across(q).wait()
                add_rows(self.mine.at[q], self.mine.at[q], self.other.at[q], self.rows, 16)
                if d > 0:
                    @pl.when((p > 0) if to_right else (p < line - 1))
                    def _():
                        self.arrived(q, q).wait_recv()
                        add_rows(self.mine.at[q], self.mine.at[q], self.moving.at[q], self.rows, 16)

                    self.along(q, to_right).start()
                else:
                    for slot, behind in ((p, p > 0), (line, p < line - 1)):
                        @pl.when(behind)
                        def _():
                            self.arrived(q, slot).wait_recv()
                            add_rows(self.mine.at[q], self.mine.at[q], self.moving.at[slot], self.rows, 16)

    def end(self):
        for d in range(1, self.line):
            for to_right, q, here in self.ends(d):
                @pl.when(here)
                def _():
                    self.along(q, to_right).wait_send()

    @staticmethod
    def scratch(line, rows, width):
        dma = pltpu.SemaphoreType.DMA
        return [
            pltpu.VMEM((line, rows, width), jnp.bfloat16),
            pltpu.VMEM((line, rows, width), jnp.bfloat16),
            pltpu.VMEM((line + 1, rows, width), jnp.bfloat16),
            dma((line,)),
            dma((line,)),
            dma((line,)),
            dma((line,)),
            dma((line + 1,)),
        ]


def scatter_kernel(line, part, out, mine, other, moving, out_sem, *sems):
    c, e = lax.axis_index("ctx"), lax.axis_index("exp")
    greet([(e >= 2, c, e - 2), (e < 2 * line - 2, c, e + 2), (True, c, e + 1 - 2 * (e % 2))])
    summing = Summing(line, part, mine, other, moving, sems)
    summing.begin()
    for d in range(line - 1, -1, -1):
        summing.step(d)
    done = pltpu.make_async_copy(mine.at[e // 2], out, out_sem)
    done.start()
    done.wait()
    summing.end()


def scatter_rows(part, collective_id):
    n, rows, width = part.shape
    buffers = Summing.scratch(n // 2, rows, width)
    return pl.pallas_call(
        functools.partial(scatter_kernel, n // 2),
        out_shape=jax.ShapeDtypeStruct((rows, width), part.dtype),
        in_specs=[ANY],
        out_specs=ANY,
        scratch_shapes=buffers[:3] + [pltpu.SemaphoreType.DMA] + buffers[3:],
        compiler_params=pltpu.CompilerParams(
            collective_id=collective_id, has_side_effects=True, vmem_limit_bytes=56 << 20
        ),
        name="scatter_rows",
    )(part)


def weights_kernel(line, quarter, *refs):
    count = 3
    own, own_block = refs[:count], refs[count]
    out, blocks = refs[count + 1 : 2 * count + 1], refs[2 * count + 1]
    local_sem, own_send, own_recv, z_send, z_recv, xy_send, xy_recv, d_send, d_recv, c_send, c_recv = refs[2 * count + 2 : -5]
    c, e = lax.axis_index("ctx"), lax.axis_index("exp")
    p, k = e // 2, e % 2
    sibling = e + 1 - 2 * k
    rows = own[0].shape[0]
    nbr = (c + 1 - 2 * (c % 2), (c + 2) % 4)
    opposite = 3 - c
    greet(
        [
            (p > 0, c, e - 2),
            (p < line - 1, c, e + 2),
            (True, c, sibling),
            (True, nbr[0], e),
            (True, nbr[1], e),
        ]
    )

    def whole(a):
        return out[a].at[pl.ds(pl.multiple_of(e * rows, 16), rows), :]

    def piece(a, q, column):
        return out[a].at[pl.ds(pl.multiple_of((2 * q + k) * rows + column * quarter, 16), quarter), :]

    def own_piece(a):
        return own[a].at[pl.ds(pl.multiple_of(c * quarter, 16), quarter), :]

    def local(a):
        return pltpu.make_async_copy(own[a], whole(a), local_sem.at[a])

    def own_across(a):
        return remote(own[a], whole(a), own_send.at[a], own_recv.at[a], c, sibling)

    def along(a, q, src, to_right):
        there = e + 2 if to_right else e - 2
        way = 0 if to_right else 1
        return remote(src, piece(a, q, c), z_send.at[way, q, a], z_recv.at[q, a], c, there)

    def beside(a, q, axis):
        return remote(piece(a, q, c), piece(a, q, c), xy_send.at[axis, q, a], xy_recv.at[axis, q, a], nbr[axis], e)

    def onward(a, q):
        came, goes = (0, 1) if a == 0 else (1, 0)
        block = piece(a, q, nbr[came])
        return remote(block, block, d_send.at[q, a], d_recv.at[q, a], nbr[goes], e)

    def across(a, q, j):
        column = (c, nbr[0], nbr[1], opposite)[j]
        block = piece(a, q, column)
        return remote(block, block, c_send.at[q, j, a], c_recv.at[q, j, a], c, sibling)

    arrays = range(count)
    gathering = Gathering(line, own_block, blocks, refs[-5:])
    for a in arrays:
        @pl.when(p < line - 1)
        def _():
            along(a, p, own_piece(a), True).start()

        @pl.when(p > 0)
        def _():
            along(a, p, own_piece(a), False).start()
    for a in arrays:
        own_across(a).start()
        local(a).start()

    def ends(d):
        for to_right in (True, False):
            q = p - d if to_right else p + d
            yield to_right, q, ((q >= 0) if to_right else (q < line))

    for d in range(1, line + 1):
        if d < line:
            for to_right, q, here in ends(d):
                further = (p < line - 1) if to_right else (p > 0)

                @pl.when(here)
                def _():
                    for a in arrays:
                        along(a, q, piece(a, q, c), to_right).wait_recv()

                        @pl.when(further)
                        def _():
                            along(a, q, piece(a, q, c), to_right).start()

                        beside(a, q, 0).start()
                        beside(a, q, 1).start()
                        across(a, q, 0).start()
        if d == line - 1:
            gathering.begin()
        if d > 1:
            for to_right, q, here in ends(d - 1):
                @pl.when(here)
                def _():
                    for a in arrays:
                        came = 0 if a == 0 else 1
                        beside(a, q, came).wait_recv()
                        onward(a, q).start()
                        across(a, q, 1 + came).start()
                        beside(a, q, 1 - came).wait_recv()
                        across(a, q, 2 - came).start()
    for d in range(1, line):
        for to_right, q, here in ends(d):
            @pl.when(here)
            def _():
                for a in arrays:
                    onward(a, q).wait_recv()
                    across(a, q, 3).start()
    for d in range(1, line):
        gathering.pump(d)
    gathering.end()
    for a in arrays:
        local(a).wait()
        own_across(a).wait()
    for d in range(0, line):
        for to_right, q, here in ends(d):
            further = (p < line - 1) if to_right else (p > 0)
            for a in arrays:
                @pl.when(here & further)
                def _():
                    along(a, q, piece(a, q, c), to_right).wait_send()
                if d > 0:
                    @pl.when(here)
                    def _():
                        beside(a, q, 0).wait_send()
                        beside(a, q, 1).wait_send()
                        onward(a, q).wait_send()
                        for j in range(4):
                            across(a, q, j).wait()


def gather_weights(shards, block, collective_id):
    n = lax.axis_size("exp")
    if lax.axis_size("ctx") != 4 or (shards[0].shape[0] // 4) % 16:
        whole = tuple(lax.all_gather(w, "exp", axis=0, tiled=True) for w in shards)
        return whole + (gather_rows(block, collective_id),)
    line = n // 2
    count = len(shards)
    dma = pltpu.SemaphoreType.DMA
    return pl.pallas_call(
        functools.partial(weights_kernel, line, shards[0].shape[0] // 4),
        out_shape=tuple(jax.ShapeDtypeStruct((n * w.shape[0], w.shape[1]), w.dtype) for w in shards)
        + (jax.ShapeDtypeStruct((n,) + block.shape, block.dtype),),
        in_specs=[ANY] * (count + 1),
        out_specs=(ANY,) * (count + 1),
        scratch_shapes=[
            dma((count,)),
            dma((count,)),
            dma((count,)),
            dma((2, line, count)),
            dma((line, count)),
            dma((2, line, count)),
            dma((2, line, count)),
            dma((line, count)),
            dma((line, count)),
            dma((line, 4, count)),
            dma((line, 4, count)),
        ]
        + Gathering.scratch(line),
        compiler_params=pltpu.CompilerParams(collective_id=collective_id, has_side_effects=True),
        name="gather_weights",
    )(*shards, block)


def context_total_kernel(size, part, out, mine, arrived, whole, load_sem, a_send, a_recv, b_send, b_recv, out_sem):
    c, e = lax.axis_index("ctx"), lax.axis_index("exp")
    others = [lax.rem(c + i, size) for i in range(1, size)]
    piece = mine.shape[0]
    greet([(True, there, e) for there in others])

    def rows_of(ref, j):
        return ref.at[pl.ds(pl.multiple_of(j * piece, 16), piece), :]

    load = pltpu.make_async_copy(rows_of(part, c), mine, load_sem)
    load.start()
    for i, there in enumerate(others):
        remote(rows_of(part, there), arrived.at[i], a_send.at[i], a_recv.at[i], there, e).start()
    load.wait()
    for i, there in enumerate(others):
        remote(rows_of(part, there), arrived.at[i], a_send.at[i], a_recv.at[i], there, e).wait()
    at_own = pl.ds(pl.multiple_of(c * piece, 16), piece)
    for j in range(piece // 16):
        at = pl.ds(j * 16, 16)
        total = mine[at, :].astype(jnp.float32)
        for i in range(size - 1):
            total = total + arrived[i, at, :].astype(jnp.float32)
        whole[pl.ds(pl.multiple_of(c * piece + j * 16, 16), 16), :] = total.astype(whole.dtype)
    for i, there in enumerate(others):
        remote(whole.at[at_own, :], whole.at[at_own, :], b_send.at[i], b_recv.at[i], there, e).start()
    for i, there in enumerate(others):
        source = lax.rem(c + size - 1 - i, size)
        copy = remote(rows_of(whole, source), rows_of(whole, source), b_send.at[i], b_recv.at[i], there, e)
        copy.wait()
    done = pltpu.make_async_copy(whole, out, out_sem)
    done.start()
    done.wait()


def total_context(part, collective_id):
    size = lax.axis_size("ctx")
    rows, width = part.shape
    if (rows // size) % 16:
        return lax.psum(part, "ctx")
    dma = pltpu.SemaphoreType.DMA
    return pl.pallas_call(
        functools.partial(context_total_kernel, size),
        out_shape=jax.ShapeDtypeStruct((rows, width), part.dtype),
        in_specs=[ANY],
        out_specs=ANY,
        scratch_shapes=[
            pltpu.VMEM((rows // size, width), part.dtype),
            pltpu.VMEM((size - 1, rows // size, width), part.dtype),
            pltpu.VMEM((rows, width), part.dtype),
            dma,
            dma((size - 1,)),
            dma((size - 1,)),
            dma((size - 1,)),
            dma((size - 1,)),
            dma,
        ],
        compiler_params=pltpu.CompilerParams(
            collective_id=collective_id, has_side_effects=True, vmem_limit_bytes=32 << 20
        ),
        name="total_context",
    )(part)


def dot(a, b):
    return lax.dot_general(a, b, (((1,), (0,)), ((), ())), preferred_element_type=jnp.float32)


def dot_nt(a, b):
    return lax.dot_general(a, b, (((1,), (1,)), ((), ())), preferred_element_type=jnp.float32)


def dot_tn(a, b):
    return lax.dot_general(a, b, (((0,), (0,)), ((), ())), preferred_element_type=jnp.float32)


def visit(p, line, i):
    both = jnp.minimum(p, line - 1 - p)
    d = jnp.where(i <= 2 * both, (i + 1) // 2, i - both)
    left = jnp.where(i <= 2 * both, i % 2 == 1, p > line - 1 - p)
    q = jnp.where(left, p - d, p + d)
    first = (i == 0) | (i > 2 * both) | (i % 2 == 1)
    return q, d, first


def expert_kernel(line, local, cap, hidden, grads_all, picks, bias, router, w_gate, w_up, w_down, *refs):
    hidden_all, out_part, back_part, grad_down, grad_gate, grad_up = refs[:6]
    wg, wu, wd, xs, ds, act, dg, du, es, h_buf, y_buf, out_stage, back_stage, in_stage, down_stage = refs[6:21]
    w_sem, own_sem, z_send, z_recv, c_send, c_recv, h_sem, y_sem, o_sem, b_sem, s_sem = refs[21:]
    f32, bf16 = jnp.float32, jnp.bfloat16
    c, e = lax.axis_index("ctx"), lax.axis_index("exp")
    p, k = e // 2, e % 2
    sibling = e + 1 - 2 * k
    rows, width = hidden.shape
    hidden_units = wg.shape[2]
    slots = 2 * cap
    lanes = router.shape[1]

    loads = [
        pltpu.make_async_copy(src, dst, w_sem.at[i])
        for i, (src, dst) in enumerate(((w_gate, wg), (w_up, wu), (w_down, wd)))
    ]
    for copy in loads:
        copy.start()
    greet([(p > 0, c, e - 2), (p < line - 1, c, e + 2), (True, c, sibling)])
    own = pltpu.make_async_copy(hidden, hidden_all.at[e], own_sem)
    own.start()

    def along(q, src, to_right):
        there = e + 2 if to_right else e - 2
        return remote(src, hidden_all.at[2 * q + k], z_send.at[0 if to_right else 1, q], z_recv.at[q], c, there)

    def across(q, src):
        return remote(src, hidden_all.at[2 * q + k], c_send.at[q], c_recv.at[q], c, sibling)

    def load_hidden(q, slot):
        return pltpu.make_async_copy(hidden_all.at[pl.ds(2 * q, 2)], h_buf.at[slot], h_sem.at[slot])

    def load_grads(q, slot):
        return pltpu.make_async_copy(grads_all.at[pl.ds(2 * q, 2), :, 0:width], y_buf.at[slot], y_sem.at[slot])

    def store_out(q, slot):
        return pltpu.make_async_copy(out_stage.at[slot], out_part.at[pl.ds(2 * q, 2)], o_sem.at[slot])

    def store_back(q, slot):
        return pltpu.make_async_copy(back_stage.at[slot], back_part.at[pl.ds(2 * q, 2)], b_sem.at[slot])

    @pl.when(p < line - 1)
    def _():
        along(p, hidden, True).start()

    @pl.when(p > 0)
    def _():
        along(p, hidden, False).start()

    across(p, hidden).start()
    load_grads(p, 0).start()

    def pump(d):
        for to_right in (True, False):
            q = p - d if to_right else p + d
            here = (q >= 0) if to_right else (q < line)
            further = (p < line - 1) if to_right else (p > 0)

            @pl.when(here)
            def _():
                block = hidden_all.at[2 * q + k]
                along(q, block, to_right).wait_recv()

                @pl.when(further)
                def _():
                    along(q, block, to_right).start()

                across(q, block).start()

    own.wait()
    for copy in loads:
        copy.wait()

    def one_chip(i, carried):
        q, d, first = visit(p, line, i)
        slot = i % 2

        across(q, hidden).wait_recv()
        load_hidden(q, slot).start()

        @pl.when(i < line - 1)
        def _():
            load_grads(visit(p, line, i + 1)[0], 1 - slot).start()

        load_hidden(q, slot).wait()
        load_grads(q, slot).wait()

        @pl.when(i >= 2)
        def _():
            store_out(visit(p, line, i - 2)[0], slot).wait()
            store_back(visit(p, line, i - 2)[0], slot).wait()

        gate_slots = []
        lane = lax.broadcasted_iota(jnp.int32, (local * cap, lanes), 1)
        expert_of_row = lax.broadcasted_iota(jnp.int32, (local * cap, lanes), 0) // cap
        for b in range(2):
            pick = picks[2 * q + b]
            block = h_buf[slot, b]
            picked = dot(pick, block).astype(bf16)
            for j in range(local):
                xs[j, q, b] = picked[j * cap : (j + 1) * cap]
            logits = dot(block, router[...]) + bias[2 * q + b].astype(f32)
            raised = jnp.exp(logits - jnp.max(logits, -1, keepdims=True))
            gates = raised / jnp.sum(raised, -1, keepdims=True)
            coarse = gates.astype(bf16)
            fine = (gates - coarse.astype(f32)).astype(bf16)
            at_slots = dot(pick, coarse) + dot(pick, fine)
            gate_slot = jnp.sum(jnp.where(lane == e * local + expert_of_row, at_slots, 0.0), -1, keepdims=True)
            gate_slots.append(gate_slot)
            grad_rows = dot(pick, y_buf[slot, b])
            grad_pairs = (gate_slot * grad_rows).astype(bf16)
            grad_rows = grad_rows.astype(bf16)
            for j in range(local):
                es[j, b] = grad_rows[j * cap : (j + 1) * cap]
                ds[j, q, b] = grad_pairs[j * cap : (j + 1) * cap]

        tile = 256
        for j in range(local):
            rows_j = xs[j, q].reshape(slots, width)
            grads_j = ds[j, q].reshape(slots, width)

            def units(t, carried):
                at = pl.ds(pl.multiple_of(t * tile, tile), tile)
                gate_pre = dot(rows_j, wg[j, :, at])
                up_pre = dot(rows_j, wu[j, :, at])
                grad_act = dot_nt(grads_j, wd[j, at, :])
                sigmoid = 1.0 / (1.0 + jnp.exp(-gate_pre))
                silu = gate_pre * sigmoid
                act[j, q, :, at] = (silu * up_pre).astype(bf16)
                dg[j, q, :, at] = (grad_act * up_pre * sigmoid * (1.0 + gate_pre * (1.0 - sigmoid))).astype(bf16)
                du[j, q, :, at] = (grad_act * silu).astype(bf16)
                return carried

            lax.fori_loop(0, hidden_units // tile, units, 0)

        wide = 512
        pick_pair = [picks[2 * q + b] for b in range(2)]

        def outputs(t, sums):
            at = pl.ds(pl.multiple_of(t * wide, wide), wide)
            gated, back, new_sums = [], [], []
            for j in range(local):
                y = dot(act[j, q], wd[j, :, at])
                back_j = dot_nt(dg[j, q], wg[j, at, :]) + dot_nt(du[j, q], wu[j, at, :])
                new = []
                for b in range(2):
                    half = slice(b * cap, (b + 1) * cap)
                    y_b = y[half]
                    new.append(sums[j][b] + jnp.sum(y_b * es[j, b, :, at].astype(f32), -1, keepdims=True))
                    gated.append((gate_slots[b][j * cap : (j + 1) * cap] * y_b).astype(bf16))
                    back.append(back_j[half].astype(bf16))
                new_sums.append(tuple(new))
            for b in range(2):
                mine = jnp.concatenate([gated[2 * j + b] for j in range(local)], 0)
                out_stage[slot, b, :, at] = dot_tn(pick_pair[b], mine).astype(bf16)
                mine = jnp.concatenate([back[2 * j + b] for j in range(local)], 0)
                back_stage[slot, b, :, at] = dot_tn(pick_pair[b], mine).astype(bf16)
            return tuple(new_sums)

        nothing = jnp.zeros((cap, 1), f32)
        sums = lax.fori_loop(
            0, width // wide, outputs, tuple((nothing, nothing) for _ in range(local))
        )
        for b in range(2):
            grad_gates = jnp.concatenate([sums[j][b] for j in range(local)], 0)
            coarse = grad_gates.astype(bf16).astype(f32)
            spot = e * local + expert_of_row
            spread = jnp.where(
                lane == spot, coarse, jnp.where(lane == spot + lanes // 2, grad_gates - coarse, 0.0)
            ).astype(bf16)
            back_stage[slot, b, :, width : width + lanes] = dot_tn(pick_pair[b], spread).astype(bf16)
        store_out(q, slot).start()
        store_back(q, slot).start()

        @pl.when(first & (d + 1 < line))
        def _():
            pump(d + 1)

        return carried

    lax.fori_loop(0, line, one_chip, 0)

    def stores(stage, target, sem, j, t, tile):
        return pltpu.make_async_copy(
            stage.at[t % 2], target.at[j, :, pl.ds(pl.multiple_of(t * tile, tile), tile)], sem.at[t % 2]
        )

    def products(left, right, stage, target, sem, j, tile, count):
        deep = line * slots

        def one_tile(t, carried):
            at = pl.ds(pl.multiple_of(t * tile, tile), tile)

            @pl.when(t >= 2)
            def _():
                stores(stage, target, sem, j, t - 2, tile).wait()

            stage[t % 2] = dot_tn(left(), right(at)).astype(bf16)
            stores(stage, target, sem, j, t, tile).start()
            return carried

        lax.fori_loop(0, count, one_tile, 0)
        for t in range(max(0, count - 2), count):
            stores(stage, target, sem, j, t, tile).wait()

    deep = line * slots
    for j in range(local):
        products(
            lambda: act[j].reshape(deep, hidden_units),
            lambda at: ds[j, :, :, :, at].reshape(deep, 512),
            down_stage, grad_down, s_sem, j, 512, width // 512,
        )
    for j in range(local):
        for source, target in ((dg, grad_gate), (du, grad_up)):
            products(
                lambda: xs[j].reshape(deep, width),
                lambda at: source[j, :, :, at].reshape(deep, 256),
                in_stage, target, s_sem, j, 256, hidden_units // 256,
            )

    for i in range(max(0, line - 2), line):
        q = visit(p, line, jnp.int32(i))[0]
        store_out(q, i % 2).wait()
        store_back(q, i % 2).wait()
    for d in range(line):
        for to_right in (True, False):
            if d == 0 and not to_right:
                continue
            q = p - d if to_right else p + d
            here = (q >= 0) if to_right else (q < line)

            @pl.when(here)
            def _():
                across(q, hidden).wait_send()
    for d in range(line):
        for to_right in (True, False):
            q = p - d if to_right else p + d
            here = (q >= 0) if to_right else (q < line)
            further = (p < line - 1) if to_right else (p > 0)

            @pl.when(here & further)
            def _():
                along(q, hidden, to_right).wait_send()


def expert_pass(hidden, grads_all, picks, bias, router, w_gate, w_up, w_down, collective_id):
    n = lax.axis_size("exp")
    line = n // 2
    rows, width = hidden.shape
    local, _, units = w_gate.shape
    cap = picks.shape[1] // local
    bf16 = jnp.bfloat16
    lanes = router.shape[1]
    dma = pltpu.SemaphoreType.DMA
    vmem = pl.BlockSpec(memory_space=pltpu.VMEM)
    slots = n * cap
    return pl.pallas_call(
        functools.partial(expert_kernel, line, local, cap),
        out_shape=(
            jax.ShapeDtypeStruct((n, rows, width), bf16),
            jax.ShapeDtypeStruct((n, rows, width), bf16),
            jax.ShapeDtypeStruct((n, rows, width + lanes), bf16),
            jax.ShapeDtypeStruct((local, units, width), bf16),
            jax.ShapeDtypeStruct((local, width, units), bf16),
            jax.ShapeDtypeStruct((local, width, units), bf16),
        ),
        in_specs=[ANY, ANY, vmem, vmem, vmem, ANY, ANY, ANY],
        out_specs=(ANY,) * 6,
        scratch_shapes=[
            pltpu.VMEM((local, width, units), bf16),
            pltpu.VMEM((local, width, units), bf16),
            pltpu.VMEM((local, units, width), bf16),
            pltpu.VMEM((local, line, 2, cap, width), bf16),
            pltpu.VMEM((local, line, 2, cap, width), bf16),
            pltpu.VMEM((local, line, 2 * cap, units), bf16),
            pltpu.VMEM((local, line, 2 * cap, units), bf16),
            pltpu.VMEM((local, line, 2 * cap, units), bf16),
            pltpu.VMEM((local, 2, cap, width), bf16),
            pltpu.VMEM((2, 2, rows, width), bf16),
            pltpu.VMEM((2, 2, rows, width), bf16),
            pltpu.VMEM((2, 2, rows, width), bf16),
            pltpu.VMEM((2, 2, rows, width + lanes), bf16),
            pltpu.VMEM((2, width, 256), bf16),
            pltpu.VMEM((2, units, 512), bf16),
            dma((3,)),
            dma,
            dma((2, line)),
            dma((line,)),
            dma((line,)),
            dma((line,)),
            dma((2,)),
            dma((2,)),
            dma((2,)),
            dma((2,)),
            dma((2,)),
        ],
        compiler_params=pltpu.CompilerParams(
            collective_id=collective_id, has_side_effects=True, vmem_limit_bytes=62 << 20
        ),
        name="expert_pass",
    )(hidden, grads_all, picks, bias, router, w_gate, w_up, w_down)


def turn(block, cosine, signed_sine):
    return block * cosine + pltpu.roll(block, block.shape[1] // 2, 1) * signed_sine


def row_norm(block):
    inverse = lax.rsqrt(jnp.mean(block * block, -1, keepdims=True) + EPS)
    return block * inverse, inverse


def attend_kernel(size, heads, kv_heads, tokens, gains, cosine, sine, qkv_hbm, out_hbm, *refs):
    queries, keyval, mixed, lse, mid, hidden = refs[:6]
    wqkv, wout, h1, w_sem, send, recv = refs[6:]
    f32, bf16 = jnp.float32, jnp.bfloat16
    c, e = lax.axis_index("ctx"), lax.axis_index("exp")
    rows, width = tokens.shape
    head = HEAD_WIDTH
    groups = heads // kv_heads
    q_width, kv_width = heads * head, kv_heads * head
    loads = [
        pltpu.make_async_copy(qkv_hbm, wqkv, w_sem.at[0]),
        pltpu.make_async_copy(out_hbm, wout, w_sem.at[1]),
    ]
    for copy in loads:
        copy.start()
    others = [lax.rem(c + i, size) for i in range(1, size)]
    greet([(True, there, e) for there in others])

    def step(t, carried):
        at = pl.ds(pl.multiple_of(t * 64, 64), 64)
        normed, _ = row_norm(tokens[at, :].astype(f32))
        h1[at, :] = (normed * gains[0:1, :]).astype(bf16)
        return carried

    lax.fori_loop(0, rows // 64, step, 0)
    loads[0].wait()
    kv = dot(h1[...], wqkv[:, q_width:])
    for j in range(kv_heads):
        at = slice(j * head, (j + 1) * head)
        keyval[c, :, at] = turn(kv[:, at], cosine[...], sine[...]).astype(bf16)
    keyval[c, :, kv_width:] = kv[:, kv_width:].astype(bf16)

    def give(i):
        return remote(keyval.at[c], keyval.at[c], send.at[i - 1], recv.at[i - 1], others[i - 1], e)

    for i in range(1, size):
        @pl.when(c + i < size)
        def _():
            give(i).start()

    for j in range(1, size):
        @pl.when(j > c)
        def _():
            keyval[j] = jnp.zeros((rows, 2 * kv_width), bf16)

    pair = 2 * head

    def project(t, carried):
        at = pl.ds(pl.multiple_of(t * pair, pair), pair)
        q = dot(h1[...], wqkv[:, at])
        for j in range(2):
            queries[2 * t + j] = turn(q[:, j * head : (j + 1) * head], cosine[...], sine[...]).astype(bf16)
        return carried

    lax.fori_loop(0, heads // 2, project, 0)
    for i in range(1, size):
        @pl.when(c - i >= 0)
        def _():
            give(i).wait_recv()

    keys_count = size * rows
    scaling = 1.0 / math.sqrt(head)
    lane = lax.broadcasted_iota(jnp.int32, (rows, 128), 1)

    def one_head(j):
        h = j // groups
        keys = keyval[:, :, pl.ds(pl.multiple_of(h * head, head), head)].reshape(keys_count, head)
        values = keyval[:, :, pl.ds(pl.multiple_of(kv_width + h * head, head), head)].reshape(keys_count, head)
        place = lax.broadcasted_iota(jnp.int32, (rows, keys_count), 1)
        row = c * rows + lax.broadcasted_iota(jnp.int32, (rows, keys_count), 0)
        scores = jnp.where(place <= row, dot_nt(queries[j], keys) * scaling, NEG)
        peak = jnp.max(scores, -1, keepdims=True)
        raised = jnp.exp(scores - peak)
        total = jnp.sum(raised, -1, keepdims=True)
        probs = (raised * (1.0 / total)).astype(bf16)
        return dot(probs, values), peak + jnp.log(total)

    def two_heads(t, stats):
        found = [one_head(2 * t + i) for i in range(2)]
        mixed[:, pl.ds(pl.multiple_of(t * pair, pair), pair)] = jnp.concatenate(
            [block for block, _ in found], 1
        ).astype(bf16)
        for i, (_, value) in enumerate(found):
            stats = jnp.where(lane == 2 * t + i, value, stats)
        return stats

    lse[...] = lax.fori_loop(0, heads // 2, two_heads, jnp.zeros((rows, 128), f32))
    loads[1].wait()

    def outward(t, carried):
        at = pl.ds(pl.multiple_of(t * 256, 256), 256)
        mid[:, at] = tokens[:, at].astype(f32) + dot(mixed[...], wout[:, at])
        return carried

    lax.fori_loop(0, width // 256, outward, 0)

    def last(t, carried):
        at = pl.ds(pl.multiple_of(t * 64, 64), 64)
        normed, _ = row_norm(mid[at, :])
        hidden[at, :] = (normed * gains[1:2, :]).astype(bf16)
        return carried

    lax.fori_loop(0, rows // 64, last, 0)
    for i in range(1, size):
        @pl.when(c + i < size)
        def _():
            give(i).wait_send()


def attend(tokens, gains, cosine, sine, qkv_full, out_full, collective_id):
    size = lax.axis_size("ctx")
    rows, width = tokens.shape
    f32, bf16 = jnp.float32, jnp.bfloat16
    dma = pltpu.SemaphoreType.DMA
    vmem = pl.BlockSpec(memory_space=pltpu.VMEM)
    shape = jax.ShapeDtypeStruct
    return pl.pallas_call(
        functools.partial(attend_kernel, size, QUERY_HEADS, KEY_VALUE_HEADS),
        out_shape=(
            shape((QUERY_HEADS, rows, HEAD_WIDTH), bf16),
            shape((size, rows, 2 * KEY_VALUE_HEADS * HEAD_WIDTH), bf16),
            shape((rows, QUERY_HEADS * HEAD_WIDTH), bf16),
            shape((rows, 128), f32),
            shape((rows, width), f32),
            shape((rows, width), bf16),
        ),
        in_specs=[vmem] * 4 + [ANY] * 2,
        out_specs=(vmem,) * 6,
        scratch_shapes=[
            pltpu.VMEM(qkv_full.shape, bf16),
            pltpu.VMEM(out_full.shape, bf16),
            pltpu.VMEM((rows, width), bf16),
            dma((2,)),
            dma((size - 1,)),
            dma((size - 1,)),
        ],
        compiler_params=pltpu.CompilerParams(
            collective_id=collective_id, has_side_effects=True, vmem_limit_bytes=48 << 20
        ),
        name="attend",
    )(tokens, gains, cosine, sine, qkv_full, out_full)


def halves(values):
    coarse = values.astype(jnp.bfloat16)
    return coarse, (values - coarse.astype(jnp.float32)).astype(jnp.bfloat16)


def backward_kernel(size, line, heads, kv_heads, experts, fused, *refs):
    back_part, out_part, tokens, mid, final, bias, small, gains, queries, keyval, mixed, lse, cosine, sine = refs[:14]
    qkv_hbm, out_hbm, output, grad_tokens, dense = refs[14:19]
    refs = refs[19:]
    if fused:
        sum_back, sum_out, refs = refs[:8], refs[8:16], refs[16:]
    wqkv, wout, probs, d_scores, d_mixed, d_att, d_mid, h1, h2, dq, dkv, kv_part, kv_other, stage = refs[:14]
    w_sem, kv_send, kv_recv, s_sem = refs[14:]
    f32, bf16 = jnp.float32, jnp.bfloat16
    c, e = lax.axis_index("ctx"), lax.axis_index("exp")
    p, k = e // 2, e % 2
    rows, width = tokens.shape
    head = HEAD_WIDTH
    groups = heads // kv_heads
    q_width, kv_width = heads * head, kv_heads * head
    scaling = 1.0 / math.sqrt(head)
    keys_count = size * rows
    n = 2 * line
    shard = dense.shape[1]

    loads = [
        pltpu.make_async_copy(qkv_hbm, wqkv, w_sem.at[0]),
        pltpu.make_async_copy(out_hbm, wout, w_sem.at[1]),
    ]
    others = [lax.rem(c + i, size) for i in range(1, size)]
    column = [(p > 0, c, e - 2), (p < line - 1, c, e + 2), (True, c, e + 1 - 2 * k)]
    greet((column if fused else []) + [(True, there, e) for there in others])
    if fused:
        back = Summing(line, back_part, *sum_back[:3], sum_back[3:])
        outs = Summing(line, out_part, *sum_out[:3], sum_out[3:])
        back.begin()
    for copy in loads:
        copy.start()

    lane = lax.broadcasted_iota(jnp.int32, (rows, 128), 1)

    def keys_of(h):
        return keyval[:, :, pl.ds(pl.multiple_of(h * head, head), head)].reshape(keys_count, head)

    def values_of(h):
        return keyval[:, :, pl.ds(pl.multiple_of(kv_width + h * head, head), head)].reshape(keys_count, head)

    def again(j, carried):
        place = lax.broadcasted_iota(jnp.int32, (rows, keys_count), 1)
        row = c * rows + lax.broadcasted_iota(jnp.int32, (rows, keys_count), 0)
        scores = dot_nt(queries[j], keys_of(j // groups)) * scaling
        level = jnp.sum(jnp.where(lane == j, lse[...], 0.0), -1, keepdims=True)
        probs[j] = jnp.exp(jnp.where(place <= row, scores - level, NEG)).astype(bf16)
        return carried

    def norms(t, carried):
        at = pl.ds(pl.multiple_of(t * 64, 64), 64)
        normed, _ = row_norm(mid[at, :])
        h2[at, :] = (normed * gains[1:2, :]).astype(bf16)
        normed, _ = row_norm(tokens[at, :].astype(f32))
        h1[at, :] = (normed * gains[0:1, :]).astype(bf16)
        return carried

    bounds = [heads * i // max(1, line - 1) for i in range(line)]
    for i, d in enumerate(range(line - 1, 0, -1)):
        if fused:
            back.step(d)
        if i == 0:
            lax.fori_loop(0, rows // 64, norms, 0)
        lax.fori_loop(bounds[i], bounds[i + 1], again, 0)
    if fused:
        back.step(0)
        outs.begin()
        outs.step(line - 1)

    logits = dot(h2[...], small[...]) + bias[...].astype(f32)
    raised = jnp.exp(logits - jnp.max(logits, -1, keepdims=True))
    gates = raised / jnp.sum(raised, -1, keepdims=True)
    came = sum_back[0].at[p] if fused else back_part
    extra = came[:, width:].astype(f32)
    grad_gates = extra + pltpu.roll(extra, extra.shape[1] // 2, 1)
    grad_logits = gates * (grad_gates - jnp.sum(gates * grad_gates, -1, keepdims=True))
    logits_hi, logits_lo = halves(grad_logits)
    grad_small = dot_tn(h2[...], logits_hi) + dot_tn(h2[...], logits_lo)

    def second_norm(t, total):
        at = pl.ds(pl.multiple_of(t * 32, 32), 32)
        normed, inverse = row_norm(mid[at, :])
        low, high = halves(grad_logits_ref[at, :])
        grad_h2 = came[at, :width].astype(f32) + dot_nt(low, small[...]) + dot_nt(high, small[...])
        total = total + jnp.sum(grad_h2 * normed, 0, keepdims=True)
        scaled = grad_h2 * gains[1:2, :]
        grad = final[at, :].astype(f32) + inverse * (scaled - normed * jnp.mean(scaled * normed, -1, keepdims=True))
        d_mid[at, :] = grad
        d_att[at, :] = grad.astype(bf16)
        return total

    grad_logits_ref = dkv.at[:, 0:128]
    dkv[:, 0:128] = grad_logits
    gain_two = lax.fori_loop(0, rows // 32, second_norm, jnp.zeros((1, width), f32))

    loads[1].wait()

    def mixing(t, carried):
        at = pl.ds(pl.multiple_of(t * 256, 256), 256)
        block = dot_nt(d_att[...], wout[at, :]).astype(bf16)
        for i in range(2):
            d_mixed[2 * t + i] = block[:, i * head : (i + 1) * head]
        return carried

    lax.fori_loop(0, q_width // 256, mixing, 0)

    def per_head(j, carried):
        grad_probs = dot_nt(d_mixed[j], values_of(j // groups))
        weights_now = probs[j].astype(f32)
        inner = jnp.sum(weights_now * grad_probs, -1, keepdims=True)
        grad = (weights_now * (grad_probs - inner) * scaling).astype(bf16)
        d_scores[lax.rem(j, groups)] = grad
        back_q = dot(grad, keys_of(j // groups))
        dq[:, pl.ds(pl.multiple_of(j * head, head), head)] = turn(back_q, cosine[...], -sine[...]).astype(bf16)
        return carried

    for h in range(kv_heads):
        lax.fori_loop(h * groups, (h + 1) * groups, per_head, 0)
        these = slice(h * groups, (h + 1) * groups)
        grad_keys = dot_tn(
            d_scores[...].reshape(groups * rows, keys_count), queries[these].reshape(groups * rows, head)
        )
        grad_values = dot_tn(
            probs[these].reshape(groups * rows, keys_count), d_mixed[these].reshape(groups * rows, head)
        )
        kv_part[:, :, h * head : (h + 1) * head] = grad_keys.astype(bf16).reshape(size, rows, head)
        at = kv_width + h * head
        kv_part[:, :, at : at + head] = grad_values.astype(bf16).reshape(size, rows, head)
        if h == 0 and fused and line > 2:
            outs.step(line - 2)

    def give(i):
        there = lax.rem(c + size - i, size)
        return remote(kv_part.at[there], kv_other.at[i - 1], kv_send.at[i - 1], kv_recv.at[i - 1], there, e)

    for i in range(1, size):
        @pl.when(c - i >= 0)
        def _():
            give(i).start()

    def store(column, t):
        return pltpu.make_async_copy(
            stage.at[lax.rem(t, 2)], dense.at[:, :, pl.ds(pl.multiple_of(column + t * 256, 128), 256)], s_sem.at[lax.rem(t, 2)]
        )

    def gradients(left, right, column, count):
        def one(t, carried):
            @pl.when(t >= 2)
            def _():
                store(column, t - 2).wait()

            product = dot_tn(left[...], right[:, pl.ds(pl.multiple_of(t * 256, 256), 256)])
            stage[lax.rem(t, 2)] = product.astype(bf16).reshape(n, shard, 256)
            store(column, t).start()
            return carried

        lax.fori_loop(0, count, one, 0)
        for t in range(max(0, count - 2), count):
            store(column, t).wait()

    gradients(mixed, d_att, q_width + 2 * kv_width, width // 256)
    gradients(h1, dq, 0, q_width // 256)

    own = kv_part[c].astype(f32)
    dkv[...] = own
    for i in range(1, size):
        @pl.when(c + i < size)
        def _():
            give(i).wait_recv()
            dkv[...] += kv_other[i - 1].astype(f32)
    for j in range(kv_heads):
        at = slice(j * head, (j + 1) * head)
        dkv[:, at] = turn(dkv[:, at], cosine[...], -sine[...])
    dq[:, q_width:] = dkv[...].astype(bf16)
    dkv_low = dq.at[:, q_width:]
    gradients(h1, dkv_low, q_width, 2 * kv_width // 256)

    for d in range(line - 3, 0, -1):
        if fused:
            outs.step(d)

    loads[0].wait()

    def inputs(t, total):
        at = pl.ds(pl.multiple_of(t * 128, 128), 128)
        grad_h1 = dot_nt(dq[at, :], wqkv[...])
        normed, inverse = row_norm(tokens[at, :].astype(f32))
        total = total + jnp.sum(grad_h1 * normed, 0, keepdims=True)
        scaled = grad_h1 * gains[0:1, :]
        grad_tokens[at, :] = d_mid[at, :] + inverse * (
            scaled - normed * jnp.mean(scaled * normed, -1, keepdims=True)
        )
        return total

    gain_one = lax.fori_loop(0, rows // 128, inputs, jnp.zeros((1, width), f32))
    sub = lax.broadcasted_iota(jnp.int32, (128, width), 0)
    gain_rows = jnp.where(sub == experts, gain_one, jnp.where(sub == experts + 1, gain_two, 0.0))
    grad_small = (grad_small + gain_rows.T).astype(bf16).reshape(n, shard, 128)
    stage[0, :, :, 0:128] = grad_small
    small_store = pltpu.make_async_copy(
        stage.at[0, :, :, 0:128], dense.at[:, :, q_width + 2 * kv_width + width :], s_sem.at[0]
    )
    small_store.start()
    if fused:
        outs.step(0)

    def finish(t, carried):
        at = pl.ds(pl.multiple_of(t * 64, 64), 64)
        added = sum_out[0][p, at, :] if fused else out_part[at, :]
        output[at, :] = (mid[at, :] + added.astype(f32)).astype(bf16)
        return carried

    lax.fori_loop(0, rows // 64, finish, 0)
    small_store.wait()
    if fused:
        back.end()
        outs.end()
    for i in range(1, size):
        @pl.when(c - i >= 0)
        def _():
            give(i).wait_send()


def backward(experts, shard, back_part, out_part, tokens, mid, final, bias, small, gains, queries, keyval, mixed, lse,
             cosine, sine, qkv_full, out_full, collective_id):
    size, n = lax.axis_size("ctx"), lax.axis_size("exp")
    line = n // 2
    rows, width = tokens.shape
    heads, kv_heads, head = QUERY_HEADS, KEY_VALUE_HEADS, HEAD_WIDTH
    kv_both = 2 * kv_heads * head
    keys_count = size * rows
    f32, bf16 = jnp.float32, jnp.bfloat16
    dma = pltpu.SemaphoreType.DMA
    vmem = pl.BlockSpec(memory_space=pltpu.VMEM)
    shape = jax.ShapeDtypeStruct
    total = qkv_full.shape[1] + out_full.shape[1] + small.shape[1]
    fused = line <= 4
    summing = []
    if fused:
        summing = Summing.scratch(line, rows, back_part.shape[2]) + Summing.scratch(line, rows, width)
    else:
        back_part, out_part = scatter_rows(back_part, 5), scatter_rows(out_part, 6)
    return pl.pallas_call(
        functools.partial(backward_kernel, size, line, heads, kv_heads, experts, fused),
        out_shape=(
            shape((rows, width), bf16),
            shape((rows, width), f32),
            shape((n, shard, total), bf16),
        ),
        in_specs=[ANY if fused else vmem] * 2 + [vmem] * 12 + [ANY] * 2,
        out_specs=(vmem, vmem, ANY),
        scratch_shapes=summing
        + [
            pltpu.VMEM(qkv_full.shape, bf16),
            pltpu.VMEM(out_full.shape, bf16),
            pltpu.VMEM((heads, rows, keys_count), bf16),
            pltpu.VMEM((heads // kv_heads, rows, keys_count), bf16),
            pltpu.VMEM((heads, rows, head), bf16),
            pltpu.VMEM((rows, width), bf16),
            pltpu.VMEM((rows, width), f32),
            pltpu.VMEM((rows, width), bf16),
            pltpu.VMEM((rows, width), bf16),
            pltpu.VMEM((rows, heads * head + kv_both), bf16),
            pltpu.VMEM((rows, kv_both), f32),
            pltpu.VMEM((size, rows, kv_both), bf16),
            pltpu.VMEM((size - 1, rows, kv_both), bf16),
            pltpu.VMEM((2, n, shard, 256), bf16),
            dma((2,)),
            dma((size - 1,)),
            dma((size - 1,)),
            dma((2,)),
        ],
        compiler_params=pltpu.CompilerParams(
            collective_id=collective_id, has_side_effects=True, vmem_limit_bytes=62 << 20
        ),
        name="backward",
    )(back_part, out_part, tokens, mid, final, bias, small, gains, queries, keyval, mixed, lse, cosine, sine,
      qkv_full, out_full)


def rope_tables(first_row, row_count, head_size):
    half_size = head_size // 2
    frequency = ROPE_BASE ** (-jnp.arange(half_size, dtype=jnp.float32) * (2.0 / head_size))
    places = (first_row + jnp.arange(row_count, dtype=jnp.int32)).astype(jnp.float32)
    angles = places[:, None] * frequency[None, :]
    cosine = jnp.cos(angles)
    sine = jnp.sin(angles)
    return (jnp.concatenate([cosine, cosine], 1), jnp.concatenate([-sine, sine], 1))


def ein(spec, a, b):
    return jnp.einsum(spec, a, b, preferred_element_type=jnp.float32)


def shards(
    tokens,
    routes,
    gain_attn,
    w_query,
    key_value_weight,
    w_out,
    gain_ffn,
    w_router,
    w_gate,
    w_up,
    w_down,
    cotangent,
):
    f32 = jnp.float32
    bf16 = jnp.bfloat16
    rows, width = tokens.shape[1:]
    ctx_size, exp_size = lax.axis_size("ctx"), lax.axis_size("exp")
    ctx_index, exp_index = lax.axis_index("ctx"), lax.axis_index("exp")
    local_experts = w_gate.shape[0]
    experts = local_experts * exp_size
    top = routes.shape[2]
    capacity = 2 * rows * top // experts
    shard_rows = w_query.shape[0]
    heads, kv_heads, head = QUERY_HEADS, KEY_VALUE_HEADS, HEAD_WIDTH
    groups = heads // kv_heads
    q_width, kv_width = heads * head, kv_heads * head
    scaling = 1.0 / math.sqrt(head)
    first_row = ctx_index * rows

    named_own = jnp.any(routes[0][:, :, None] == jnp.arange(128, dtype=jnp.int32), axis=1)
    block = jnp.concatenate([cotangent[0], named_own.astype(bf16)], 1)
    small = jnp.concatenate(
        [
            w_router,
            gain_attn[:, None],
            gain_ffn[:, None],
            jnp.zeros((shard_rows, 128 - experts - 2), bf16),
        ],
        1,
    )
    qkv_full, out_full, small_full, rows_all = gather_weights(
        (jnp.concatenate([w_query, key_value_weight], 1), w_out, small), block, 1
    )
    gain_one = small_full[:, experts].astype(f32)
    gain_two = small_full[:, experts + 1].astype(f32)

    cosine, sine = rope_tables(first_row, rows, head)
    gains = jnp.stack([gain_one, gain_two])
    queries, keyval, mixed, lse, resid_mid, hidden_two = attend(
        tokens[0], gains, cosine, sine, qkv_full, out_full, 2
    )

    named = rows_all[:, :, width:]
    bias = jnp.where(named > 0, 0.0, NEG).astype(bf16)
    mine = exp_index * local_experts
    here = jnp.transpose(lax.dynamic_slice_in_dim(named, mine, local_experts, 2), (0, 2, 1))
    ahead = jnp.arange(rows)[:, None] < jnp.arange(rows)[None, :]
    slot = jnp.where(here > 0, ein("bjt,ts->bjs", here, ahead.astype(bf16)), -1.0)
    picks = (
        (slot[:, :, None, :] == jnp.arange(capacity, dtype=f32)[:, None])
        .astype(bf16)
        .reshape(exp_size, local_experts * capacity, rows)
    )
    hidden_all, out_part, back_part, grad_down, grad_gate, grad_up = expert_pass(
        hidden_two, rows_all, picks, bias, small_full, w_gate, w_up, w_down, 3
    )
    total_down, total_gate, total_up = lax.psum((grad_down, grad_gate, grad_up), "ctx")
    own_bias = lax.dynamic_index_in_dim(bias, exp_index, 0, keepdims=False)
    output, grad_input, dense_part = backward(
        experts, shard_rows, back_part, out_part, tokens[0], resid_mid, cotangent[0], own_bias, small_full, gains,
        queries, keyval, mixed, lse, cosine, sine, qkv_full, out_full, 4
    )
    dense = total_context(scatter_rows(dense_part, 7), 8).astype(f32)
    split = q_width + 2 * kv_width
    small_total = dense[:, split + width :]
    return (
        output[None],
        grad_input[None],
        small_total[:, experts],
        dense[:, :q_width],
        dense[:, q_width:split],
        dense[:, split : split + width],
        small_total[:, experts + 1],
        small_total[:, :experts],
        total_gate.astype(f32),
        total_up.astype(f32),
        total_down.astype(f32),
    )


def solution(mesh):
    rows, wide, deep = P("exp", "ctx", None), P("exp", None), P("exp", None, None)
    flat = P("exp")
    return jax.shard_map(
        shards,
        mesh=mesh,
        in_specs=(rows, rows, flat, wide, wide, wide, flat, wide, deep, deep, deep, rows),
        out_specs=(rows, rows, flat, wide, wide, wide, flat, wide, deep, deep, deep),
        check_vma=False,
    )
```

```python
import functools
import math

import jax
import jax.numpy as jnp
from jax import lax
from jax.experimental import pallas as pl
from jax.experimental.pallas import tpu as pltpu
from jax.sharding import PartitionSpec as P

MESH = pl.DeviceIdType.MESH
ANY = pl.BlockSpec(memory_space=pl.ANY)


def remote(src, dst, send, recv, ctx, exp):
    return pltpu.make_async_remote_copy(
        src_ref=src, dst_ref=dst, send_sem=send, recv_sem=recv, device_id=(ctx, exp), device_id_type=MESH
    )


def greet(pairs):
    barrier = pltpu.get_barrier_semaphore()
    count = 0
    for here, ctx, exp in pairs:
        if here is True:
            pl.semaphore_signal(barrier, inc=1, device_id=(ctx, exp), device_id_type=MESH)
            count = count + 1
        else:
            @pl.when(here)
            def _():
                pl.semaphore_signal(barrier, inc=1, device_id=(ctx, exp), device_id_type=MESH)
            count = count + here.astype(jnp.int32)
    pl.semaphore_wait(barrier, count)


QUERY_HEADS = 12
KEY_VALUE_HEADS = 2
HEAD_WIDTH = 128
EPS = 1e-06
NEG = -1e30
ROPE_BASE = 1000000.0


class Gathering:
    def __init__(self, line, own, out, sems, keep_own=True):
        self.line, self.own, self.out, self.keep_own = line, own, out, keep_own
        self.local_sem, self.z_send, self.z_recv, self.c_send, self.c_recv = sems
        self.c, self.e = lax.axis_index("ctx"), lax.axis_index("exp")
        self.p, self.k = self.e // 2, self.e % 2

    def along(self, q, src, to_right):
        there = self.e + 2 if to_right else self.e - 2
        way = 0 if to_right else 1
        return remote(src, self.out.at[2 * q + self.k], self.z_send.at[way, q], self.z_recv.at[q], self.c, there)

    def across(self, q, src):
        there = self.e + 1 - 2 * self.k
        return remote(src, self.out.at[2 * q + self.k], self.c_send.at[q], self.c_recv.at[q], self.c, there)

    def local(self):
        return pltpu.make_async_copy(self.own, self.out.at[self.e], self.local_sem)

    def ends(self, d):
        for to_right in (True, False):
            q = self.p - d if to_right else self.p + d
            here = (q >= 0) if to_right else (q < self.line)
            further = (self.p < self.line - 1) if to_right else (self.p > 0)
            yield to_right, q, here, further

    def begin(self):
        for to_right, q, _, further in self.ends(0):
            @pl.when(further)
            def _():
                self.along(q, self.own, to_right).start()

        self.across(self.p, self.own).start()
        if self.keep_own:
            self.local().start()

    def pump(self, d, onward=True):
        for to_right, q, here, further in self.ends(d):
            @pl.when(here)
            def _():
                block = self.out.at[2 * q + self.k]
                self.along(q, block, to_right).wait_recv()
                if onward:
                    @pl.when(further)
                    def _():
                        self.along(q, block, to_right).start()

                self.across(q, block).start()

    def forward(self, d):
        for to_right, q, here, further in self.ends(d):
            @pl.when(here & further)
            def _():
                self.along(q, self.out.at[2 * q + self.k], to_right).start()

    def finish(self, sent, crossed):
        for d in crossed:
            for to_right, q, here, _ in self.ends(d):
                if d > 0 or to_right:
                    @pl.when(here)
                    def _():
                        self.across(q, self.own).wait()
        for d in sent:
            for to_right, q, here, further in self.ends(d):
                @pl.when(here & further)
                def _():
                    self.along(q, self.own, to_right).wait_send()

    def end(self, hops=None):
        last = self.line if hops is None else min(self.line, hops + 1)
        if self.keep_own:
            self.local().wait()
        self.finish(range(self.line if hops is None else last - 1), range(last))

    @staticmethod
    def scratch(line):
        dma = pltpu.SemaphoreType.DMA
        return [dma, dma((2, line)), dma((line,)), dma((line,)), dma((line,))]


def gather_kernel(line, own, out, *sems):
    c, e = lax.axis_index("ctx"), lax.axis_index("exp")
    greet([(e >= 2, c, e - 2), (e < 2 * line - 2, c, e + 2), (True, c, e + 1 - 2 * (e % 2))])
    gathering = Gathering(line, own, out, sems)
    gathering.begin()
    for d in range(1, line):
        gathering.pump(d)
    gathering.end()


def gather_rows(own, collective_id):
    n = lax.axis_size("exp")
    return pl.pallas_call(
        functools.partial(gather_kernel, n // 2),
        out_shape=jax.ShapeDtypeStruct((n,) + own.shape, own.dtype),
        in_specs=[ANY],
        out_specs=ANY,
        scratch_shapes=Gathering.scratch(n // 2),
        compiler_params=pltpu.CompilerParams(collective_id=collective_id, has_side_effects=True),
        name="gather_rows",
    )(own)


def add_rows(dst, a, b, rows):
    step = math.gcd(rows, 64)

    def body(i, carried):
        at = pl.ds(pl.multiple_of(i * step, step), step)
        dst[at, :] = a[at, :] + b[at, :]
        return carried

    lax.fori_loop(0, rows // step, body, 0)


class Summing:
    def __init__(self, line, part, cross, moving, acc, tmp, sems):
        self.line, self.part, self.cross, self.moving = line, part, cross, moving
        self.acc, self.tmp = acc, tmp
        self.own_sem, self.tmp_sem, self.c_send, self.c_recv, self.z_send, self.z_recv = sems
        self.c, self.e = lax.axis_index("ctx"), lax.axis_index("exp")
        self.p, self.k = self.e // 2, self.e % 2
        self.rows, self.width = part.shape[1:]

    def across(self, q):
        there = self.e + 1 - 2 * self.k
        return remote(
            self.part.at[2 * q + 1 - self.k], self.cross.at[q], self.c_send.at[q], self.c_recv.at[q], self.c, there
        )

    def own(self, q):
        return pltpu.make_async_copy(self.part.at[2 * q + self.k], self.acc.at[q], self.own_sem.at[q])

    def load(self, src, side):
        into = self.tmp.at[side, pl.ds(0, self.rows), pl.ds(0, self.width)]
        return pltpu.make_async_copy(src, into, self.tmp_sem.at[side])

    def add(self, q, side):
        add_rows(self.acc.at[q], self.acc.at[q], self.tmp.at[side, pl.ds(0, self.rows), pl.ds(0, self.width)], self.rows)

    def along(self, q, to_right):
        there = self.e + 2 if to_right else self.e - 2
        place = q if to_right else jnp.where(q == self.p - 1, self.line, q)
        return remote(self.acc.at[q], self.moving.at[place], self.z_send.at[q], self.z_recv.at[place], self.c, there)

    def arrived(self, place):
        return remote(self.acc.at[0], self.moving.at[place], self.z_send.at[0], self.z_recv.at[place], self.c, self.e)

    def ends(self, d):
        for to_right in (True, False):
            if d > 0 or to_right:
                q = self.p + d if to_right else self.p - d
                here = (q < self.line) if to_right else (q >= 0)
                yield to_right, q, here, ((self.p > 0) if to_right else (self.p < self.line - 1))

    def begin(self):
        order = [(d, end) for d in range(self.line - 1, -1, -1) for end in self.ends(d)]
        for _, (_, q, here, _) in order:
            @pl.when(here)
            def _():
                self.across(q).start()
                self.own(q).start()
        for d, (to_right, q, here, behind) in order:
            side = 0 if to_right else 1

            @pl.when(here)
            def _():
                self.across(q).wait_recv()
                self.load(self.cross.at[q], side).start()
                self.own(q).wait()
                self.load(self.cross.at[q], side).wait()
                self.add(q, side)
                if d > 0:
                    @pl.when(jnp.logical_not(behind))
                    def _():
                        self.along(q, to_right).start()

    def step(self, d):
        if d > 0:
            for to_right, q, here, behind in self.ends(d):
                @pl.when(here & behind)
                def _():
                    self.arrived(q).wait_recv()
                    self.load(self.moving.at[q], 0 if to_right else 1).start()
            for to_right, q, here, behind in self.ends(d):
                @pl.when(here & behind)
                def _():
                    side = 0 if to_right else 1
                    self.load(self.moving.at[q], side).wait()
                    self.add(q, side)
                    self.along(q, to_right).start()
            return
        last = ((0, self.p, self.p > 0), (1, self.line, self.p < self.line - 1))
        for side, place, behind in last:
            @pl.when(behind)
            def _():
                self.arrived(place).wait_recv()
                self.load(self.moving.at[place], side).start()
        for side, place, behind in last:
            @pl.when(behind)
            def _():
                self.load(self.moving.at[place], side).wait()
                self.add(self.p, side)

    def result(self):
        return self.acc.at[self.p]

    def end(self):
        for d in range(self.line):
            for to_right, q, here, _ in self.ends(d):
                @pl.when(here)
                def _():
                    if d > 0:
                        self.along(q, to_right).wait_send()
                    self.across(q).wait_send()

    @staticmethod
    def scratch(line, rows, width):
        dma = pltpu.SemaphoreType.DMA
        return [
            pltpu.VMEM((line, rows, width), jnp.bfloat16),
            dma((line,)),
            dma((2,)),
            dma((line,)),
            dma((line,)),
            dma((line,)),
            dma((line + 1,)),
        ]

    @staticmethod
    def landing(line, rows, width):
        return [
            jax.ShapeDtypeStruct((line, rows, width), jnp.bfloat16),
            jax.ShapeDtypeStruct((line + 1, rows, width), jnp.bfloat16),
        ]


class Totals:
    ahead, lag, count, early = 6, 2, 12, 3

    def __init__(self, part, early_first, sends, recvs, total=None, first=None, second=None, buffers=None, sems=None):
        self.part, self.total, self.early_first, self.first, self.second = part, total, early_first, first, second
        self.sends, self.recvs = sends, recvs
        if buffers is not None:
            self.own, self.got, self.got_two = buffers
            self.load_sem, self.got_sem, self.store_sem = sems
            self.slots = self.own.shape[0]
        c, self.e = lax.axis_index("ctx"), lax.axis_index("exp")
        self.bits = (c % 2, c // 2)
        self.nbrs = (c + 1 - 2 * (c % 2), lax.rem(c + 2, 4))
        self.deep = part.shape[0] // self.count

    def axes(self, h):
        return (0, 1) if h == 0 else (1, 0)

    def rows(self, ref, t, h, kept_one, kept_two=None, mine_two=True):
        one, two = self.axes(h)
        quarter, eighth = self.deep // 4, self.deep // 8
        bit = self.bits[one] if kept_one else 1 - self.bits[one]
        start = t * self.deep + h * (self.deep // 2) + bit * quarter
        if kept_two is None:
            return ref.at[pl.ds(pl.multiple_of(start, 16), quarter), :]
        return ref.at[pl.ds(pl.multiple_of(start + self.bits[two] * eighth, 16), eighth), :]

    def piece(self, t, h, kept):
        eighth = self.deep // 8
        bit = self.bits[self.axes(h)[1]]
        start = (bit if kept else 1 - bit) * eighth
        return self.own.at[t % self.slots, h, pl.ds(pl.multiple_of(start, 16), eighth), :]

    def copy(self, stage, t, h):
        one, two = self.axes(h)
        if stage == 0:
            src, dst, there = self.rows(self.part, t, h, False), self.landed(t, h), one
        elif stage == 1:
            src, dst, there = self.piece(t, h, False), self.second.at[t, h], two
        elif stage == 2:
            src, dst, there = self.piece(t, h, True), self.rows(self.total, t, h, True, True), two
        else:
            src, dst, there = self.rows(self.total, t, h, True), self.rows(self.total, t, h, True), one
        return remote(src, dst, self.sends.at[stage, t, h], self.recvs.at[stage, t, h], self.nbrs[there], self.e)

    def landed(self, t, h):
        return self.early_first.at[t, h] if t < self.early else self.first.at[t - self.early, h]

    def start_early(self, t):
        for h in range(2):
            self.copy(0, t, h).start()

    def end_early(self):
        for t in range(self.early):
            for h in range(2):
                self.copy(0, t, h).wait()

    def load_own(self, t, h):
        return pltpu.make_async_copy(
            self.rows(self.part, t, h, True), self.own.at[t % self.slots, h], self.load_sem.at[t % 2, h]
        )

    def store(self, t, h):
        return pltpu.make_async_copy(
            self.piece(t, h, True), self.rows(self.total, t, h, True, True), self.store_sem.at[t % self.slots, h]
        )

    def begin(self):
        for t in range(self.early, min(self.early + self.ahead, self.count)):
            for h in range(2):
                self.copy(0, t, h).start()
        for h in range(2):
            self.load_own(0, h).start()

    @property
    def ticks(self):
        return self.count + 2 * self.lag

    def tick(self, t):
        count, lag = self.count, self.lag
        t_two, t_three = t - lag, t - 2 * lag
        loads = []
        if t < count:
            for h in range(2):
                if t >= self.early:
                    self.copy(0, t, h).wait_recv()
                came = pltpu.make_async_copy(self.landed(t, h), self.got.at[h], self.got_sem.at[0, h])
                came.start()
                loads.append(came)
            if t + self.early + self.ahead < count:
                for h in range(2):
                    self.copy(0, t + self.early + self.ahead, h).start()
        later = []
        if 0 <= t_two < count:
            for h in range(2):
                self.copy(1, t_two, h).wait_recv()
                came = pltpu.make_async_copy(self.second.at[t_two, h], self.got_two.at[h], self.got_sem.at[1, h])
                came.start()
                later.append(came)
        if t < count:
            for h in range(2):
                self.load_own(t, h).wait()
                loads[h].wait()
                mine = self.own.at[t % self.slots, h]
                add_rows(mine, mine, self.got.at[h], self.deep // 4)
                self.copy(1, t, h).start()
        if 0 <= t_two < count:
            for h in range(2):
                later[h].wait()
                mine = self.piece(t_two, h, True)
                add_rows(mine, mine, self.got_two.at[h], self.deep // 8)
                self.copy(2, t_two, h).start()
                self.store(t_two, h).start()
        if 0 <= t_three < count:
            for h in range(2):
                self.copy(2, t_three, h).wait_recv()
                self.store(t_three, h).wait()
                self.copy(3, t_three, h).start()
                self.copy(1, t_three, h).wait_send()
                self.copy(2, t_three, h).wait_send()
        if t + 1 < count:
            for h in range(2):
                self.load_own(t + 1, h).start()

    def end(self):
        for t in range(self.count):
            for h in range(2):
                if t >= self.early:
                    self.copy(0, t, h).wait_send()
                self.copy(3, t, h).wait()

    @staticmethod
    def early_scratch():
        dma = pltpu.SemaphoreType.DMA
        return [dma((1, Totals.early, 2)), dma((1, Totals.early, 2))]

    @staticmethod
    def early_landing(deep, width):
        return jax.ShapeDtypeStruct((Totals.early, 2, deep // 4, width), jnp.bfloat16)

    @staticmethod
    def scratch(deep, width):
        count = Totals.count
        dma = pltpu.SemaphoreType.DMA
        slots = 2 * Totals.lag + 1
        return [
            pltpu.VMEM((slots, 2, deep // 4, width), jnp.bfloat16),
            pltpu.VMEM((2, deep // 4, width), jnp.bfloat16),
            pltpu.VMEM((2, deep // 8, width), jnp.bfloat16),
            dma((4, count, 2)),
            dma((4, count, 2)),
            dma((2, 2)),
            dma((2, 2)),
            dma((slots, 2)),
        ]

    @staticmethod
    def landing(deep, width):
        return [
            jax.ShapeDtypeStruct((Totals.count - Totals.early, 2, deep // 4, width), jnp.bfloat16),
            jax.ShapeDtypeStruct((Totals.count, 2, deep // 8, width), jnp.bfloat16),
        ]


class Sharing:
    def __init__(self, size, part, total, summed, arrived, sems):
        self.size, self.part, self.total, self.summed, self.arrived_at = size, part, total, summed, arrived
        self.a_send, self.a_recv, self.b_send, self.b_recv, self.store_sem = sems
        self.c, self.e = lax.axis_index("ctx"), lax.axis_index("exp")
        self.piece = part.shape[0] // size

    def rows(self, ref, j):
        return ref.at[pl.ds(pl.multiple_of(j * self.piece, 16), self.piece), :]

    def there(self, i):
        return lax.rem(self.c + i + 1, self.size)

    def give(self, i):
        there = self.there(i)
        return remote(
            self.rows(self.part, there), self.arrived_at.at[i], self.a_send.at[i], self.a_recv.at[i], there, self.e
        )

    def hand(self, i):
        return remote(
            self.summed, self.rows(self.total, self.c), self.b_send.at[i], self.b_recv.at[i], self.there(i), self.e
        )

    def handed(self, i):
        source = lax.rem(self.c + self.size - 1 - i, self.size)
        return remote(
            self.summed, self.rows(self.total, source), self.b_send.at[i], self.b_recv.at[i], self.there(i), self.e
        )

    def store(self):
        return pltpu.make_async_copy(self.summed, self.rows(self.total, self.c), self.store_sem)

    def begin(self):
        for i in range(self.size - 1):
            self.give(i).start()

    def middle(self):
        for i in range(self.size - 1):
            self.give(i).wait_recv()
        for j in range(self.piece // 16):
            at = pl.ds(j * 16, 16)
            total = self.part[pl.ds(pl.multiple_of(self.c * self.piece + j * 16, 16), 16), :].astype(jnp.float32)
            for i in range(self.size - 1):
                total = total + self.arrived_at[i, at, :].astype(jnp.float32)
            self.summed[at, :] = total.astype(self.summed.dtype)
        for i in range(self.size - 1):
            self.hand(i).start()
        self.store().start()

    def end(self):
        self.store().wait()
        for i in range(self.size - 1):
            self.give(i).wait_send()
            self.hand(i).wait_send()
            self.handed(i).wait_recv()

    @staticmethod
    def scratch(size, rows, width):
        dma = pltpu.SemaphoreType.DMA
        return [
            pltpu.VMEM((rows // size, width), jnp.bfloat16),
            pltpu.VMEM((size - 1, rows // size, width), jnp.bfloat16),
            dma((size - 1,)),
            dma((size - 1,)),
            dma((size - 1,)),
            dma((size - 1,)),
            dma,
        ]


def weights_kernel(line, quarter, *refs):
    count = 3
    own, own_mask, own_block = refs[:count], refs[count], refs[count + 1]
    out, masks, blocks = refs[count + 2 : 2 * count + 2], refs[2 * count + 2], refs[2 * count + 3]
    held, refs = refs[2 * count + 4 : 3 * count + 4], refs[3 * count + 4 :]
    local_sem, own_send, own_recv, z_send, z_recv, xy_send, xy_recv, d_send, d_recv, c_send, c_recv = refs[:-10]
    c, e = lax.axis_index("ctx"), lax.axis_index("exp")
    p, k = e // 2, e % 2
    sibling = e + 1 - 2 * k
    rows = own[0].shape[0]
    nbr = (c + 1 - 2 * (c % 2), (c + 2) % 4)
    opposite = 3 - c
    greet(
        [
            (p > 0, c, e - 2),
            (p < line - 1, c, e + 2),
            (True, c, sibling),
            (True, nbr[0], e),
            (True, nbr[1], e),
        ]
    )

    def whole(a):
        return out[a].at[pl.ds(pl.multiple_of(e * rows, 16), rows), :]

    def piece(a, q, column):
        return out[a].at[pl.ds(pl.multiple_of((2 * q + k) * rows + column * quarter, 16), quarter), :]

    def own_piece(a):
        return own[a].at[pl.ds(pl.multiple_of(c * quarter, 16), quarter), :]

    def load(a):
        return pltpu.make_async_copy(own[a], held[a], local_sem.at[0, a])

    def local(a):
        return pltpu.make_async_copy(held[a], whole(a), local_sem.at[1, a])

    def own_across(a):
        return remote(own[a], whole(a), own_send.at[a], own_recv.at[a], c, sibling)

    def along(a, q, src, to_right):
        there = e + 2 if to_right else e - 2
        way = 0 if to_right else 1
        return remote(src, piece(a, q, c), z_send.at[way, q, a], z_recv.at[q, a], c, there)

    def beside(a, q, axis):
        return remote(piece(a, q, c), piece(a, q, c), xy_send.at[axis, q, a], xy_recv.at[axis, q, a], nbr[axis], e)

    def onward(a, q):
        came, goes = (0, 1) if a == 0 else (1, 0)
        block = piece(a, q, nbr[came])
        return remote(block, block, d_send.at[q, a], d_recv.at[q, a], nbr[goes], e)

    def across(a, q, j):
        column = (c, nbr[0], nbr[1], opposite)[j]
        block = piece(a, q, column)
        return remote(block, block, c_send.at[q, j, a], c_recv.at[q, j, a], c, sibling)

    arrays = range(count)
    marking = Gathering(line, own_mask, masks, refs[-10:-5])
    gathering = Gathering(line, own_block, blocks, refs[-5:], keep_own=False)
    marking.begin()
    for a in arrays:
        @pl.when(p < line - 1)
        def _():
            along(a, p, own_piece(a), True).start()

        @pl.when(p > 0)
        def _():
            along(a, p, own_piece(a), False).start()
    for a in arrays:
        own_across(a).start()
        load(a).start()
    for a in arrays:
        load(a).wait()
        local(a).start()

    def ends(d):
        for to_right in (True, False):
            q = p - d if to_right else p + d
            yield to_right, q, ((q >= 0) if to_right else (q < line))

    for d in range(1, line + 1):
        if d < line:
            for to_right, q, here in ends(d):
                further = (p < line - 1) if to_right else (p > 0)

                @pl.when(here)
                def _():
                    for a in arrays:
                        along(a, q, piece(a, q, c), to_right).wait_recv()

                        @pl.when(further)
                        def _():
                            along(a, q, piece(a, q, c), to_right).start()

                        beside(a, q, 0).start()
                        beside(a, q, 1).start()
                        across(a, q, 0).start()
        if d < line:
            marking.pump(d)
        if d == line - 1:
            gathering.begin()
        if d > 1:
            for to_right, q, here in ends(d - 1):
                @pl.when(here)
                def _():
                    for a in arrays:
                        came = 0 if a == 0 else 1
                        beside(a, q, came).wait_recv()
                        onward(a, q).start()
                        across(a, q, 1 + came).start()
                        beside(a, q, 1 - came).wait_recv()
                        across(a, q, 2 - came).start()
    for d in range(1, line):
        for to_right, q, here in ends(d):
            @pl.when(here)
            def _():
                for a in arrays:
                    onward(a, q).wait_recv()
                    across(a, q, 3).start()
    gathering.pump(1, onward=False)
    gathering.end(1)
    marking.end()
    for a in arrays:
        local(a).wait()
        own_across(a).wait()
    for d in range(0, line):
        for to_right, q, here in ends(d):
            further = (p < line - 1) if to_right else (p > 0)
            for a in arrays:
                @pl.when(here & further)
                def _():
                    along(a, q, piece(a, q, c), to_right).wait_send()
                if d > 0:
                    @pl.when(here)
                    def _():
                        beside(a, q, 0).wait_send()
                        beside(a, q, 1).wait_send()
                        onward(a, q).wait_send()
                        for j in range(4):
                            across(a, q, j).wait()


def planned(size, n, shard_rows):
    return size == 4 and 4 <= n <= 8 and (shard_rows // 4) % 16 == 0


def gather_weights(shards, mask, block, collective_id):
    n = lax.axis_size("exp")
    if not planned(lax.axis_size("ctx"), n, shards[0].shape[0]):
        whole = tuple(lax.all_gather(w, "exp", axis=0, tiled=True) for w in shards)
        return whole + (lax.all_gather(mask, "exp", axis=0), gather_rows(block, collective_id))
    line = n // 2
    count = len(shards)
    dma = pltpu.SemaphoreType.DMA
    return pl.pallas_call(
        functools.partial(weights_kernel, line, shards[0].shape[0] // 4),
        out_shape=tuple(jax.ShapeDtypeStruct((n * w.shape[0], w.shape[1]), w.dtype) for w in shards)
        + tuple(jax.ShapeDtypeStruct((n,) + w.shape, w.dtype) for w in (mask, block)),
        in_specs=[ANY] * (count + 2),
        out_specs=(ANY,) * (count + 2),
        scratch_shapes=[pltpu.VMEM(w.shape, w.dtype) for w in shards]
        + [
            dma((2, count)),
            dma((count,)),
            dma((count,)),
            dma((2, line, count)),
            dma((line, count)),
            dma((2, line, count)),
            dma((2, line, count)),
            dma((line, count)),
            dma((line, count)),
            dma((line, 4, count)),
            dma((line, 4, count)),
        ]
        + Gathering.scratch(line)
        + Gathering.scratch(line),
        compiler_params=pltpu.CompilerParams(collective_id=collective_id, has_side_effects=True),
        name="gather_weights",
    )(*shards, mask, block)


def dot(a, b):
    return lax.dot_general(a, b, (((1,), (0,)), ((), ())), preferred_element_type=jnp.float32)


def dot_nt(a, b):
    return lax.dot_general(a, b, (((1,), (1,)), ((), ())), preferred_element_type=jnp.float32)


def dot_tn(a, b):
    return lax.dot_general(a, b, (((0,), (0,)), ((), ())), preferred_element_type=jnp.float32)


def visit(p, line, i):
    both = jnp.minimum(p, line - 1 - p)
    d = jnp.where(i <= 2 * both, (i + 1) // 2, i - both)
    left = jnp.where(i <= 2 * both, i % 2 == 1, p > line - 1 - p)
    q = jnp.where(left, p - d, p + d)
    first = (i == 0) | (i > 2 * both) | (i % 2 == 1)
    return q, d, first


def expert_kernel(line, local, cap, hop, start, hidden, own_grads, grads_in, picks, bias, router, w_gate, w_up, w_down, *refs):
    hidden_all, out_part, back_part, grads, grads_all = refs[:5]
    if start:
        early_first, refs = refs[5], refs[:5] + refs[6:]
    wg, wu, wd, xs, ds, act, dg, du, es, h_buf, y_buf, out_stage, back_stage, in_stage, down_stage = refs[5:20]
    w_sem, own_sem, z_send, z_recv, c_send, c_recv, h_sem, y_sem, o_sem, b_sem, s_sem = refs[20:31]
    f32, bf16 = jnp.float32, jnp.bfloat16
    c, e = lax.axis_index("ctx"), lax.axis_index("exp")
    p, k = e // 2, e % 2
    sibling = e + 1 - 2 * k
    rows, width = hidden.shape
    hidden_units = wg.shape[2]
    slots = 2 * cap
    lanes = router.shape[1]

    loads = [
        pltpu.make_async_copy(src, dst, w_sem.at[i])
        for i, (src, dst) in enumerate(((w_gate, wg), (w_up, wu), (w_down, wd)))
    ]
    for copy in loads:
        copy.start()
    beside = [(True, c + 1 - 2 * (c % 2), e), (True, lax.rem(c + 2, 4), e)] if start else []
    greet([(p > 0, c, e - 2), (p < line - 1, c, e + 2), (True, c, sibling)] + beside)
    def along(q, src, to_right):
        there = e + 2 if to_right else e - 2
        return remote(src, hidden_all.at[2 * q + k], z_send.at[0 if to_right else 1, q], z_recv.at[q], c, there)

    def across(q, src):
        return remote(src, hidden_all.at[2 * q + k], c_send.at[q], c_recv.at[q], c, sibling)

    def load_hidden(q, slot):
        return pltpu.make_async_copy(hidden_all.at[pl.ds(2 * q, 2)], h_buf.at[slot], h_sem.at[slot])

    def load_grads(q, slot):
        return pltpu.make_async_copy(grads_all.at[pl.ds(2 * q, 2)], y_buf.at[slot], y_sem.at[slot])

    def load_own(buf, own, blocks, i):
        return [
            pltpu.make_async_copy(own, buf.at[0, k], own_sem.at[2 * i]),
            pltpu.make_async_copy(blocks.at[sibling], buf.at[0, 1 - k], own_sem.at[2 * i + 1]),
        ]

    def store_out(q, slot):
        return pltpu.make_async_copy(out_stage.at[slot], out_part.at[pl.ds(2 * q, 2)], o_sem.at[slot])

    def store_back(q, slot):
        return pltpu.make_async_copy(back_stage.at[slot], back_part.at[pl.ds(2 * q, 2)], b_sem.at[slot])

    @pl.when(p < line - 1)
    def _():
        along(p, hidden, True).start()

    @pl.when(p > 0)
    def _():
        along(p, hidden, False).start()

    across(p, hidden).start()
    if hop:
        hops = Gathering(line, grads_all.at[e], grads_all, refs[31:36])
        hops.forward(2)
    for copy in load_own(y_buf, own_grads, grads_all, 0):
        copy.start()

    def pump(d):
        for to_right in (True, False):
            q = p - d if to_right else p + d
            here = (q >= 0) if to_right else (q < line)
            further = (p < line - 1) if to_right else (p > 0)

            @pl.when(here)
            def _():
                block = hidden_all.at[2 * q + k]
                along(q, block, to_right).wait_recv()

                @pl.when(further)
                def _():
                    along(q, block, to_right).start()

                across(q, block).start()

    for copy in loads:
        copy.wait()

    def one_chip(i, carried):
        q, d, first = visit(p, line, i)
        slot = i % 2

        across(q, hidden).wait_recv()

        @pl.when(i == 0)
        def _():
            own = load_own(h_buf, hidden, hidden_all, 1)
            for copy in own:
                copy.start()
            for copy in own + load_own(y_buf, own_grads, grads_all, 0):
                copy.wait()

        @pl.when(i > 0)
        def _():
            load_hidden(q, slot).start()

        if hop:
            @pl.when(d == line - 1)
            def _():
                hops.pump(line - 1, onward=False)
                hops.finish([], [line - 1])
                load_grads(q, slot).start()

        after, d_after, _ = visit(p, line, i + 1)

        @pl.when((i < line - 1) & (d_after < (line - 1 if hop else line)))
        def _():
            load_grads(after, 1 - slot).start()

        @pl.when(i > 0)
        def _():
            load_hidden(q, slot).wait()
            load_grads(q, slot).wait()

        @pl.when(i >= 2)
        def _():
            store_out(visit(p, line, i - 2)[0], slot).wait()
            store_back(visit(p, line, i - 2)[0], slot).wait()

        gate_slots = []
        lane = lax.broadcasted_iota(jnp.int32, (local * cap, lanes), 1)
        expert_of_row = lax.broadcasted_iota(jnp.int32, (local * cap, lanes), 0) // cap
        for b in range(2):
            pick = picks[2 * q + b]
            block = h_buf[slot, b]
            picked = dot(pick, block).astype(bf16)
            for j in range(local):
                xs[j, q, b] = picked[j * cap : (j + 1) * cap]
            logits = dot(block, router[...]) + bias[2 * q + b].astype(f32)
            raised = jnp.exp(logits - jnp.max(logits, -1, keepdims=True))
            gates = raised / jnp.sum(raised, -1, keepdims=True)
            coarse = gates.astype(bf16)
            fine = (gates - coarse.astype(f32)).astype(bf16)
            at_slots = dot(pick, coarse) + dot(pick, fine)
            gate_slot = jnp.sum(jnp.where(lane == e * local + expert_of_row, at_slots, 0.0), -1, keepdims=True)
            gate_slots.append(gate_slot)
            grad_rows = dot(pick, y_buf[slot, b])
            grad_pairs = (gate_slot * grad_rows).astype(bf16)
            grad_rows = grad_rows.astype(bf16)
            for j in range(local):
                es[j, b] = grad_rows[j * cap : (j + 1) * cap]
                ds[j, q, b] = grad_pairs[j * cap : (j + 1) * cap]

        tile = 256
        for j in range(local):
            rows_j = xs[j, q].reshape(slots, width)
            grads_j = ds[j, q].reshape(slots, width)

            def units(t, carried):
                at = pl.ds(pl.multiple_of(t * tile, tile), tile)
                gate_pre = dot(rows_j, wg[j, :, at])
                up_pre = dot(rows_j, wu[j, :, at])
                grad_act = dot_nt(grads_j, wd[j, at, :])
                sigmoid = 1.0 / (1.0 + jnp.exp(-gate_pre))
                silu = gate_pre * sigmoid
                act[j, q, :, at] = (silu * up_pre).astype(bf16)
                dg[j, q, :, at] = (grad_act * up_pre * sigmoid * (1.0 + gate_pre * (1.0 - sigmoid))).astype(bf16)
                du[j, q, :, at] = (grad_act * silu).astype(bf16)
                return carried

            lax.fori_loop(0, hidden_units // tile, units, 0)

        wide = 512
        pick_pair = [picks[2 * q + b] for b in range(2)]

        def outputs(t, sums):
            at = pl.ds(pl.multiple_of(t * wide, wide), wide)
            gated, back, new_sums = [], [], []
            for j in range(local):
                y = dot(act[j, q], wd[j, :, at])
                back_j = dot_nt(dg[j, q], wg[j, at, :]) + dot_nt(du[j, q], wu[j, at, :])
                new = []
                for b in range(2):
                    half = slice(b * cap, (b + 1) * cap)
                    y_b = y[half]
                    new.append(sums[j][b] + jnp.sum(y_b * es[j, b, :, at].astype(f32), -1, keepdims=True))
                    gated.append((gate_slots[b][j * cap : (j + 1) * cap] * y_b).astype(bf16))
                    back.append(back_j[half].astype(bf16))
                new_sums.append(tuple(new))
            for b in range(2):
                mine = jnp.concatenate([gated[2 * j + b] for j in range(local)], 0)
                out_stage[slot, b, :, at] = dot_tn(pick_pair[b], mine).astype(bf16)
                mine = jnp.concatenate([back[2 * j + b] for j in range(local)], 0)
                back_stage[slot, b, :, at] = dot_tn(pick_pair[b], mine).astype(bf16)
            return tuple(new_sums)

        nothing = jnp.zeros((cap, 1), f32)
        sums = lax.fori_loop(
            0, width // wide, outputs, tuple((nothing, nothing) for _ in range(local))
        )
        for b in range(2):
            grad_gates = jnp.concatenate([sums[j][b] for j in range(local)], 0)
            coarse = grad_gates.astype(bf16).astype(f32)
            spot = e * local + expert_of_row
            spread = jnp.where(
                lane == spot, coarse, jnp.where(lane == spot + lanes // 2, grad_gates - coarse, 0.0)
            ).astype(bf16)
            back_stage[slot, b, :, width : width + lanes] = dot_tn(pick_pair[b], spread).astype(bf16)
        store_out(q, slot).start()
        store_back(q, slot).start()

        @pl.when(first & (d + 1 < line))
        def _():
            pump(d + 1)

        return carried

    lax.fori_loop(0, line, one_chip, 0)

    deep = line * slots
    tile = 256
    tiles = hidden_units // tile

    def products(left, right, stage, first_row, count):
        high = stage.shape[1]

        def stores(t):
            row = first_row + lax.div(t, tiles) * high
            return pltpu.make_async_copy(
                stage.at[lax.rem(t, 2)],
                grads.at[
                    pl.ds(pl.multiple_of(row, 16), high),
                    pl.ds(pl.multiple_of(lax.rem(t, tiles) * tile, tile), tile),
                ],
                s_sem.at[lax.rem(t, 2)],
            )

        def one_tile(t, carried):
            @pl.when(t >= 2)
            def _():
                stores(t - 2).wait()

            stage[lax.rem(t, 2)] = dot_tn(left(), right(pl.ds(pl.multiple_of(t * tile, tile), tile))).astype(bf16)
            stores(t).start()
            return carried

        lax.fori_loop(0, count, one_tile, 0)
        for t in range(max(0, count - 2), count):
            stores(jnp.int32(t)).wait()

    totals = Totals(grads, early_first, *refs[-2:]) if start else None
    sent = 0

    def send_ready(rows_done):
        nonlocal sent
        while start and sent < totals.early and (sent + 1) * totals.deep <= rows_done:
            totals.start_early(sent)
            sent += 1

    for i, source in enumerate((dg, du)):
        for j in range(local):
            products(
                lambda: xs[j].reshape(deep, width),
                lambda at: source[j, :, :, at].reshape(deep, tile),
                in_stage, (i * local + j) * width, tiles,
            )
            send_ready((i * local + j + 1) * width)
    for j in range(local):
        products(
            lambda: act[j].reshape(deep, hidden_units),
            lambda at: ds[j, :, :, :, at].reshape(deep, tile),
            down_stage, 2 * local * width + j * width, width // tile,
        )

    if start:
        totals.end_early()
    if hop:
        hops.finish([2], [])
    for i in range(max(0, line - 2), line):
        q = visit(p, line, jnp.int32(i))[0]
        store_out(q, i % 2).wait()
        store_back(q, i % 2).wait()
    for d in range(line):
        for to_right in (True, False):
            if d == 0 and not to_right:
                continue
            q = p - d if to_right else p + d
            here = (q >= 0) if to_right else (q < line)

            @pl.when(here)
            def _():
                across(q, hidden).wait_send()
    for d in range(line):
        for to_right in (True, False):
            q = p - d if to_right else p + d
            here = (q >= 0) if to_right else (q < line)
            further = (p < line - 1) if to_right else (p > 0)

            @pl.when(here & further)
            def _():
                along(q, hidden, to_right).wait_send()


def expert_pass(hop, start, hidden, own_grads, grads_all, picks, bias, router, w_gate, w_up, w_down, collective_id):
    n = lax.axis_size("exp")
    line = n // 2
    rows, width = hidden.shape
    local, _, units = w_gate.shape
    cap = picks.shape[1] // local
    bf16 = jnp.bfloat16
    lanes = router.shape[1]
    dma = pltpu.SemaphoreType.DMA
    vmem = pl.BlockSpec(memory_space=pltpu.VMEM)
    slots = n * cap
    return pl.pallas_call(
        functools.partial(expert_kernel, line, local, cap, hop, start),
        out_shape=(
            jax.ShapeDtypeStruct((n, rows, width), bf16),
            jax.ShapeDtypeStruct((n, rows, width), bf16),
            jax.ShapeDtypeStruct((n, rows, width + lanes), bf16),
            jax.ShapeDtypeStruct((3 * local * width, units), bf16),
            jax.ShapeDtypeStruct(grads_all.shape, bf16),
        )
        + ((Totals.early_landing(3 * local * width // Totals.count, units),) if start else ()),
        in_specs=[ANY, ANY, ANY, vmem, vmem, vmem, ANY, ANY, ANY],
        out_specs=(ANY,) * (6 if start else 5),
        input_output_aliases={2: 4},
        scratch_shapes=[
            pltpu.VMEM((local, width, units), bf16),
            pltpu.VMEM((local, width, units), bf16),
            pltpu.VMEM((local, units, width), bf16),
            pltpu.VMEM((local, line, 2, cap, width), bf16),
            pltpu.VMEM((local, line, 2, cap, width), bf16),
            pltpu.VMEM((local, line, 2 * cap, units), bf16),
            pltpu.VMEM((local, line, 2 * cap, units), bf16),
            pltpu.VMEM((local, line, 2 * cap, units), bf16),
            pltpu.VMEM((local, 2, cap, width), bf16),
            pltpu.VMEM((2, 2, rows, width), bf16),
            pltpu.VMEM((2, 2, rows, width), bf16),
            pltpu.VMEM((2, 2, rows, width), bf16),
            pltpu.VMEM((2, 2, rows, width + lanes), bf16),
            pltpu.VMEM((2, width, 256), bf16),
            pltpu.VMEM((2, units, 256), bf16),
            dma((3,)),
            dma((4,)),
            dma((2, line)),
            dma((line,)),
            dma((line,)),
            dma((line,)),
            dma((2,)),
            dma((2,)),
            dma((2,)),
            dma((2,)),
            dma((2,)),
        ]
        + (Gathering.scratch(line) if hop else [])
        + (Totals.early_scratch() if start else []),
        compiler_params=pltpu.CompilerParams(
            collective_id=collective_id, has_side_effects=True, vmem_limit_bytes=62 << 20
        ),
        name="expert_pass",
    )(hidden, own_grads, grads_all, picks, bias, router, w_gate, w_up, w_down)


def turn(block, cosine, signed_sine):
    return block * cosine + pltpu.roll(block, block.shape[1] // 2, 1) * signed_sine


def row_norm(block):
    inverse = lax.rsqrt(jnp.mean(block * block, -1, keepdims=True) + EPS)
    return block * inverse, inverse


def attend_kernel(size, line, hop, heads, kv_heads, tokens, gains, cosine, sine, qkv_hbm, out_hbm, rows_in, *refs):
    queries, keyval, mixed, lse, mid, hidden, rows_all = refs[:7]
    wqkv, wout, h1, w_sem, send, recv = refs[7:13]
    f32, bf16 = jnp.float32, jnp.bfloat16
    c, e = lax.axis_index("ctx"), lax.axis_index("exp")
    rows, width = tokens.shape
    head = HEAD_WIDTH
    groups = heads // kv_heads
    q_width, kv_width = heads * head, kv_heads * head
    loads = [
        pltpu.make_async_copy(qkv_hbm, wqkv, w_sem.at[0]),
        pltpu.make_async_copy(out_hbm, wout, w_sem.at[1]),
    ]
    for copy in loads:
        copy.start()
    others = [lax.rem(c + i, size) for i in range(1, size)]
    column = [(e >= 2, c, e - 2), (e < 2 * line - 2, c, e + 2), (True, c, e + 1 - 2 * (e % 2))]
    greet((column if hop else []) + [(True, there, e) for there in others])
    if hop:
        hops = Gathering(line, rows_all.at[e], rows_all, refs[13:])
        hops.forward(1)

    def step(t, carried):
        at = pl.ds(pl.multiple_of(t * 64, 64), 64)
        normed, _ = row_norm(tokens[at, :].astype(f32))
        h1[at, :] = (normed * gains[0:1, :]).astype(bf16)
        return carried

    lax.fori_loop(0, rows // 64, step, 0)
    loads[0].wait()
    kv = dot(h1[...], wqkv[:, q_width:])
    for j in range(kv_heads):
        at = slice(j * head, (j + 1) * head)
        keyval[c, :, at] = turn(kv[:, at], cosine[...], sine[...]).astype(bf16)
    keyval[c, :, kv_width:] = kv[:, kv_width:].astype(bf16)

    def give(i):
        return remote(keyval.at[c], keyval.at[c], send.at[i - 1], recv.at[i - 1], others[i - 1], e)

    for i in range(1, size):
        @pl.when(c + i < size)
        def _():
            give(i).start()

    for j in range(1, size):
        @pl.when(j > c)
        def _():
            keyval[j] = jnp.zeros((rows, 2 * kv_width), bf16)

    pair = 2 * head

    def project(t, carried):
        at = pl.ds(pl.multiple_of(t * pair, pair), pair)
        q = dot(h1[...], wqkv[:, at])
        for j in range(2):
            queries[2 * t + j] = turn(q[:, j * head : (j + 1) * head], cosine[...], sine[...]).astype(bf16)
        return carried

    lax.fori_loop(0, heads // 2, project, 0)
    for i in range(1, size):
        @pl.when(c - i >= 0)
        def _():
            give(i).wait_recv()

    keys_count = size * rows
    scaling = 1.0 / math.sqrt(head)
    lane = lax.broadcasted_iota(jnp.int32, (rows, 128), 1)

    def one_head(j):
        h = j // groups
        keys = keyval[:, :, pl.ds(pl.multiple_of(h * head, head), head)].reshape(keys_count, head)
        values = keyval[:, :, pl.ds(pl.multiple_of(kv_width + h * head, head), head)].reshape(keys_count, head)
        place = lax.broadcasted_iota(jnp.int32, (rows, keys_count), 1)
        row = c * rows + lax.broadcasted_iota(jnp.int32, (rows, keys_count), 0)
        scores = jnp.where(place <= row, dot_nt(queries[j], keys) * scaling, NEG)
        peak = jnp.max(scores, -1, keepdims=True)
        raised = jnp.exp(scores - peak)
        total = jnp.sum(raised, -1, keepdims=True)
        probs = (raised * (1.0 / total)).astype(bf16)
        return dot(probs, values), peak + jnp.log(total)

    def two_heads(t, stats):
        found = [one_head(2 * t + i) for i in range(2)]
        mixed[:, pl.ds(pl.multiple_of(t * pair, pair), pair)] = jnp.concatenate(
            [block for block, _ in found], 1
        ).astype(bf16)
        for i, (_, value) in enumerate(found):
            stats = jnp.where(lane == 2 * t + i, value, stats)
        return stats

    lse[...] = lax.fori_loop(0, heads // 2, two_heads, jnp.zeros((rows, 128), f32))
    if hop:
        hops.pump(2, onward=False)
    loads[1].wait()

    def outward(t, carried):
        at = pl.ds(pl.multiple_of(t * 256, 256), 256)
        mid[:, at] = tokens[:, at].astype(f32) + dot(mixed[...], wout[:, at])
        return carried

    lax.fori_loop(0, width // 256, outward, 0)

    def last(t, carried):
        at = pl.ds(pl.multiple_of(t * 64, 64), 64)
        normed, _ = row_norm(mid[at, :])
        hidden[at, :] = (normed * gains[1:2, :]).astype(bf16)
        return carried

    lax.fori_loop(0, rows // 64, last, 0)
    if hop:
        hops.finish([1], [2])
    for i in range(1, size):
        @pl.when(c + i < size)
        def _():
            give(i).wait_send()


def attend(hop, tokens, gains, cosine, sine, qkv_full, out_full, rows_all, collective_id):
    size, line = lax.axis_size("ctx"), lax.axis_size("exp") // 2
    rows, width = tokens.shape
    f32, bf16 = jnp.float32, jnp.bfloat16
    dma = pltpu.SemaphoreType.DMA
    vmem = pl.BlockSpec(memory_space=pltpu.VMEM)
    shape = jax.ShapeDtypeStruct
    return pl.pallas_call(
        functools.partial(attend_kernel, size, line, hop, QUERY_HEADS, KEY_VALUE_HEADS),
        out_shape=(
            shape((QUERY_HEADS, rows, HEAD_WIDTH), bf16),
            shape((size, rows, 2 * KEY_VALUE_HEADS * HEAD_WIDTH), bf16),
            shape((rows, QUERY_HEADS * HEAD_WIDTH), bf16),
            shape((rows, 128), f32),
            shape((rows, width), f32),
            shape((rows, width), bf16),
            shape(rows_all.shape, bf16),
        ),
        in_specs=[vmem] * 4 + [ANY] * 3,
        out_specs=(vmem,) * 6 + (ANY,),
        input_output_aliases={6: 6},
        scratch_shapes=[
            pltpu.VMEM(qkv_full.shape, bf16),
            pltpu.VMEM(out_full.shape, bf16),
            pltpu.VMEM((rows, width), bf16),
            dma((2,)),
            dma((size - 1,)),
            dma((size - 1,)),
        ]
        + (Gathering.scratch(line) if hop else []),
        compiler_params=pltpu.CompilerParams(
            collective_id=collective_id, has_side_effects=True, vmem_limit_bytes=48 << 20
        ),
        name="attend",
    )(tokens, gains, cosine, sine, qkv_full, out_full, rows_all)


def halves(values):
    coarse = values.astype(jnp.bfloat16)
    return coarse, (values - coarse.astype(jnp.float32)).astype(jnp.bfloat16)


def backward_kernel(size, line, heads, kv_heads, experts, fused, *refs):
    back_part, out_part, grads, early_first, tokens, mid, final, bias, small, gains = refs[:10]
    queries, keyval, mixed, lse, cosine, sine, qkv_hbm, out_hbm, output, grad_tokens, dense_out, dense_qkv = refs[10:22]
    refs = refs[22:]
    if fused:
        totals, total_out, total_qkv, land_one, land_two = refs[:5]
        landing, refs = refs[5:13], refs[13:]
        tmp = refs[0]
        sum_refs, refs = [refs[1 + 7 * i : 8 + 7 * i] for i in range(4)], refs[29:]
        total_scratch, refs = refs[:8], refs[8:]
        share_out, share_qkv, refs = refs[:7], refs[7:14], refs[14:]
    else:
        came, out_sum = back_part, out_part
    wqkv, wout, probs, d_scores, d_mixed, d_att, d_mid, h1, h2, dq, dkv, kv_part, kv_other, stage = refs[:14]
    w_sem, kv_send, kv_recv, s_sem = refs[14:]
    f32, bf16 = jnp.float32, jnp.bfloat16
    c, e = lax.axis_index("ctx"), lax.axis_index("exp")
    p, k = e // 2, e % 2
    rows, width = tokens.shape
    head = HEAD_WIDTH
    groups = heads // kv_heads
    q_width, kv_width = heads * head, kv_heads * head
    scaling = 1.0 / math.sqrt(head)
    keys_count = size * rows
    n = 2 * line
    shard = dense_out.shape[1]

    loads = [
        pltpu.make_async_copy(qkv_hbm, wqkv, w_sem.at[0]),
        pltpu.make_async_copy(out_hbm, wout, w_sem.at[1]),
    ]
    others = [lax.rem(c + i, size) for i in range(1, size)]
    column = [(p > 0, c, e - 2), (p < line - 1, c, e + 2), (True, c, e + 1 - 2 * k)]
    greet((column if fused else []) + [(True, there, e) for there in others])
    ticked = []

    def tick():
        if fused and len(ticked) < experts_total.ticks:
            experts_total.tick(len(ticked))
            ticked.append(1)

    if fused:
        experts_total = Totals(
            grads, early_first, *total_scratch[3:5], totals, land_one, land_two, total_scratch[:3], total_scratch[5:]
        )
        experts_total.begin()
        sums = [
            Summing(line, part, landing[2 * i], landing[2 * i + 1], sum_refs[i][0], tmp, sum_refs[i][1:])
            for i, part in enumerate((back_part, out_part, dense_out, dense_qkv))
        ]
        back, outs, dense_outs, dense_qkvs = sums
        came, out_sum = back.result(), outs.result()
        sharing_out = Sharing(size, dense_outs.result(), total_out, *share_out[:2], share_out[2:])
        sharing_qkv = Sharing(size, dense_qkvs.result(), total_qkv, *share_qkv[:2], share_qkv[2:])
        back.begin()
    for copy in loads:
        copy.start()

    lane = lax.broadcasted_iota(jnp.int32, (rows, 128), 1)

    def keys_of(h):
        return keyval[:, :, pl.ds(pl.multiple_of(h * head, head), head)].reshape(keys_count, head)

    def values_of(h):
        return keyval[:, :, pl.ds(pl.multiple_of(kv_width + h * head, head), head)].reshape(keys_count, head)

    def again(j, carried):
        place = lax.broadcasted_iota(jnp.int32, (rows, keys_count), 1)
        row = c * rows + lax.broadcasted_iota(jnp.int32, (rows, keys_count), 0)
        scores = dot_nt(queries[j], keys_of(j // groups)) * scaling
        level = jnp.sum(jnp.where(lane == j, lse[...], 0.0), -1, keepdims=True)
        probs[j] = jnp.exp(jnp.where(place <= row, scores - level, NEG)).astype(bf16)
        return carried

    def norms(t, carried):
        at = pl.ds(pl.multiple_of(t * 64, 64), 64)
        normed, _ = row_norm(mid[at, :])
        h2[at, :] = (normed * gains[1:2, :]).astype(bf16)
        normed, _ = row_norm(tokens[at, :].astype(f32))
        h1[at, :] = (normed * gains[0:1, :]).astype(bf16)
        return carried

    bounds = [heads * i // max(1, line - 1) for i in range(line)]
    for i, d in enumerate(range(line - 1, 0, -1)):
        if fused and i > 0:
            back.step(d)
        if i == 0:
            lax.fori_loop(0, rows // 64, norms, 0)
        lax.fori_loop(bounds[i], bounds[i + 1], again, 0)
        tick()
        if fused and d == 2:
            outs.begin()
    if fused:
        back.step(0)
        tick()

    logits = dot(h2[...], small[...]) + bias[...].astype(f32)
    raised = jnp.exp(logits - jnp.max(logits, -1, keepdims=True))
    gates = raised / jnp.sum(raised, -1, keepdims=True)
    extra = came[:, width:].astype(f32)
    grad_gates = extra + pltpu.roll(extra, extra.shape[1] // 2, 1)
    grad_logits = gates * (grad_gates - jnp.sum(gates * grad_gates, -1, keepdims=True))
    logits_hi, logits_lo = halves(grad_logits)
    grad_small = dot_tn(h2[...], logits_hi) + dot_tn(h2[...], logits_lo)

    def second_norm(t, total):
        at = pl.ds(pl.multiple_of(t * 32, 32), 32)
        normed, inverse = row_norm(mid[at, :])
        low, high = halves(grad_logits_ref[at, :])
        grad_h2 = came[at, :width].astype(f32) + dot_nt(low, small[...]) + dot_nt(high, small[...])
        total = total + jnp.sum(grad_h2 * normed, 0, keepdims=True)
        scaled = grad_h2 * gains[1:2, :]
        grad = final[at, :].astype(f32) + inverse * (scaled - normed * jnp.mean(scaled * normed, -1, keepdims=True))
        d_mid[at, :] = grad
        d_att[at, :] = grad.astype(bf16)
        return total

    grad_logits_ref = dkv.at[:, 0:128]
    dkv[:, 0:128] = grad_logits
    gain_two = lax.fori_loop(0, rows // 32, second_norm, jnp.zeros((1, width), f32))

    loads[1].wait()

    def mixing(t, carried):
        at = pl.ds(pl.multiple_of(t * 256, 256), 256)
        block = dot_nt(d_att[...], wout[at, :]).astype(bf16)
        for i in range(2):
            d_mixed[2 * t + i] = block[:, i * head : (i + 1) * head]
        return carried

    lax.fori_loop(0, q_width // 256, mixing, 0)
    if fused and line > 2:
        outs.step(line - 2)
    tick()

    def gradients(left, right, dense, column, count):
        def store(t):
            return pltpu.make_async_copy(
                stage.at[lax.rem(t, 2)],
                dense.at[:, :, pl.ds(pl.multiple_of(column + t * 256, 128), 256)],
                s_sem.at[lax.rem(t, 2)],
            )

        def one(t, carried):
            @pl.when(t >= 2)
            def _():
                store(t - 2).wait()

            product = dot_tn(left[...], right[:, pl.ds(pl.multiple_of(t * 256, 256), 256)])
            stage[lax.rem(t, 2)] = product.astype(bf16).reshape(n, shard, 256)
            store(t).start()
            return carried

        lax.fori_loop(0, count, one, 0)
        for t in range(max(0, count - 2), count):
            store(jnp.int32(t)).wait()

    gradients(mixed, d_att, dense_out, 0, width // 256)
    if fused:
        dense_outs.begin()
        tick()
        for d in range(line - 3, 0, -1):
            outs.step(d)

    def per_head(j, carried):
        grad_probs = dot_nt(d_mixed[j], values_of(j // groups))
        weights_now = probs[j].astype(f32)
        inner = jnp.sum(weights_now * grad_probs, -1, keepdims=True)
        grad = (weights_now * (grad_probs - inner) * scaling).astype(bf16)
        d_scores[lax.rem(j, groups)] = grad
        back_q = dot(grad, keys_of(j // groups))
        dq[:, pl.ds(pl.multiple_of(j * head, head), head)] = turn(back_q, cosine[...], -sine[...]).astype(bf16)
        return carried

    for h in range(kv_heads):
        lax.fori_loop(h * groups, (h + 1) * groups, per_head, 0)
        these = slice(h * groups, (h + 1) * groups)
        grad_keys = dot_tn(
            d_scores[...].reshape(groups * rows, keys_count), queries[these].reshape(groups * rows, head)
        )
        grad_values = dot_tn(
            probs[these].reshape(groups * rows, keys_count), d_mixed[these].reshape(groups * rows, head)
        )
        kv_part[:, :, h * head : (h + 1) * head] = grad_keys.astype(bf16).reshape(size, rows, head)
        at = kv_width + h * head
        kv_part[:, :, at : at + head] = grad_values.astype(bf16).reshape(size, rows, head)
        if h == 0 and fused:
            tick()
            outs.step(0)

    def give(i):
        there = lax.rem(c + size - i, size)
        return remote(kv_part.at[there], kv_other.at[i - 1], kv_send.at[i - 1], kv_recv.at[i - 1], there, e)

    for i in range(1, size):
        @pl.when(c - i >= 0)
        def _():
            give(i).start()

    tick()
    if fused and line > 2:
        dense_outs.step(line - 2)
    gradients(h1, dq, dense_qkv, 0, q_width // 256)
    tick()
    if fused:
        for d in range(line - 3, 0, -1):
            dense_outs.step(d)

    own = kv_part[c].astype(f32)
    dkv[...] = own
    for i in range(1, size):
        @pl.when(c + i < size)
        def _():
            give(i).wait_recv()
            dkv[...] += kv_other[i - 1].astype(f32)
    for j in range(kv_heads):
        at = slice(j * head, (j + 1) * head)
        dkv[:, at] = turn(dkv[:, at], cosine[...], -sine[...])
    dq[:, q_width:] = dkv[...].astype(bf16)
    dkv_low = dq.at[:, q_width:]
    gradients(h1, dkv_low, dense_qkv, q_width, 2 * kv_width // 256)
    loads[0].wait()

    def inputs(t, total):
        at = pl.ds(pl.multiple_of(t * 128, 128), 128)
        grad_h1 = dot_nt(dq[at, :], wqkv[...])
        normed, inverse = row_norm(tokens[at, :].astype(f32))
        total = total + jnp.sum(grad_h1 * normed, 0, keepdims=True)
        scaled = grad_h1 * gains[0:1, :]
        grad_tokens[at, :] = d_mid[at, :] + inverse * (
            scaled - normed * jnp.mean(scaled * normed, -1, keepdims=True)
        )
        return total

    gain_one = lax.fori_loop(0, rows // 128, inputs, jnp.zeros((1, width), f32))
    sub = lax.broadcasted_iota(jnp.int32, (128, width), 0)
    gain_rows = jnp.where(sub == experts, gain_one, jnp.where(sub == experts + 1, gain_two, 0.0))
    grad_small = (grad_small + gain_rows.T).astype(bf16).reshape(n, shard, 128)
    stage[0, :, :, 0:128] = grad_small
    small_store = pltpu.make_async_copy(
        stage.at[0, :, :, 0:128], dense_qkv.at[:, :, q_width + 2 * kv_width :], s_sem.at[0]
    )
    small_store.start()
    small_store.wait()
    tick()
    if fused:
        dense_qkvs.begin()

    def finish(t, carried):
        at = pl.ds(pl.multiple_of(t * 64, 64), 64)
        output[at, :] = (mid[at, :] + out_sum[at, :].astype(f32)).astype(bf16)
        return carried

    lax.fori_loop(0, rows // 64, finish, 0)
    if fused:
        tick()
        dense_outs.step(0)
        sharing_out.begin()
        for d in range(line - 2, -1, -1):
            tick()
            if d == 0:
                sharing_out.middle()
                tick()
            dense_qkvs.step(d)
        sharing_qkv.begin()
        tick()
        sharing_qkv.middle()
        while len(ticked) < experts_total.ticks:
            tick()
        for one in sums:
            one.end()
        sharing_out.end()
        sharing_qkv.end()
        experts_total.end()
    for i in range(1, size):
        @pl.when(c - i >= 0)
        def _():
            give(i).wait_send()


def backward(experts, shard, back_part, out_part, grads, early_first, tokens, mid, final, bias, small, gains, queries, keyval, mixed, lse,
             cosine, sine, qkv_full, out_full, collective_id):
    size, n = lax.axis_size("ctx"), lax.axis_size("exp")
    line = n // 2
    rows, width = tokens.shape
    heads, kv_heads, head = QUERY_HEADS, KEY_VALUE_HEADS, HEAD_WIDTH
    kv_both = 2 * kv_heads * head
    keys_count = size * rows
    f32, bf16 = jnp.float32, jnp.bfloat16
    dma = pltpu.SemaphoreType.DMA
    vmem = pl.BlockSpec(memory_space=pltpu.VMEM)
    shape = jax.ShapeDtypeStruct
    fused = planned(size, n, shard)
    out_width, qkv_width = width, qkv_full.shape[1] + small.shape[1]
    shapes = [
        shape((rows, width), bf16),
        shape((rows, width), f32),
        shape((n, shard, out_width), bf16),
        shape((n, shard, qkv_width), bf16),
    ]
    summing = []
    if fused:
        deep = grads.shape[0] // Totals.count
        shapes += [
            shape(grads.shape, bf16),
            shape((shard, out_width), bf16),
            shape((shard, qkv_width), bf16),
        ]
        shapes += Totals.landing(deep, grads.shape[1])
        for high, wide in ((rows, back_part.shape[2]), (rows, width), (shard, out_width), (shard, qkv_width)):
            shapes += Summing.landing(line, high, wide)
        widest = max(back_part.shape[2], width, out_width, qkv_width)
        summing = [
            pltpu.VMEM((2, rows, widest), bf16),
        ]
        for high, wide in ((rows, back_part.shape[2]), (rows, width), (shard, out_width), (shard, qkv_width)):
            summing += Summing.scratch(line, high, wide)
        summing += Totals.scratch(deep, grads.shape[1])
        summing += Sharing.scratch(size, shard, out_width) + Sharing.scratch(size, shard, qkv_width)
    else:
        back_part = lax.psum_scatter(back_part, "exp", scatter_dimension=0)
        out_part = lax.psum_scatter(out_part, "exp", scatter_dimension=0)
    found = pl.pallas_call(
        functools.partial(backward_kernel, size, line, heads, kv_heads, experts, fused),
        out_shape=tuple(shapes),
        in_specs=[ANY if fused else vmem] * 2 + [ANY] * 2 + [vmem] * 12 + [ANY] * 2,
        out_specs=(vmem, vmem) + (ANY,) * (len(shapes) - 2),
        scratch_shapes=summing
        + [
            pltpu.VMEM(qkv_full.shape, bf16),
            pltpu.VMEM(out_full.shape, bf16),
            pltpu.VMEM((heads, rows, keys_count), bf16),
            pltpu.VMEM((heads // kv_heads, rows, keys_count), bf16),
            pltpu.VMEM((heads, rows, head), bf16),
            pltpu.VMEM((rows, width), bf16),
            pltpu.VMEM((rows, width), f32),
            pltpu.VMEM((rows, width), bf16),
            pltpu.VMEM((rows, width), bf16),
            pltpu.VMEM((rows, heads * head + kv_both), bf16),
            pltpu.VMEM((rows, kv_both), f32),
            pltpu.VMEM((size, rows, kv_both), bf16),
            pltpu.VMEM((size - 1, rows, kv_both), bf16),
            pltpu.VMEM((2, n, shard, 256), bf16),
            dma((2,)),
            dma((size - 1,)),
            dma((size - 1,)),
            dma((2,)),
        ],
        compiler_params=pltpu.CompilerParams(
            collective_id=collective_id, has_side_effects=True, vmem_limit_bytes=62 << 20
        ),
        name="backward",
    )(back_part, out_part, grads, early_first, tokens, mid, final, bias, small, gains, queries, keyval, mixed, lse, cosine, sine,
      qkv_full, out_full)
    if fused:
        return found[:2] + found[4:7]
    dense_out, dense_qkv = (lax.psum_scatter(part, "exp", scatter_dimension=0) for part in found[2:4])
    return found[:2] + (lax.psum(grads, "ctx"), lax.psum(dense_out, "ctx"), lax.psum(dense_qkv, "ctx"))


def rope_tables(first_row, row_count, head_size):
    half_size = head_size // 2
    frequency = ROPE_BASE ** (-jnp.arange(half_size, dtype=jnp.float32) * (2.0 / head_size))
    places = (first_row + jnp.arange(row_count, dtype=jnp.int32)).astype(jnp.float32)
    angles = places[:, None] * frequency[None, :]
    cosine = jnp.cos(angles)
    sine = jnp.sin(angles)
    return (jnp.concatenate([cosine, cosine], 1), jnp.concatenate([-sine, sine], 1))


def ein(spec, a, b):
    return jnp.einsum(spec, a, b, preferred_element_type=jnp.float32)


def shards(
    tokens,
    routes,
    gain_attn,
    w_query,
    key_value_weight,
    w_out,
    gain_ffn,
    w_router,
    w_gate,
    w_up,
    w_down,
    cotangent,
):
    f32 = jnp.float32
    bf16 = jnp.bfloat16
    rows, width = tokens.shape[1:]
    ctx_size, exp_size = lax.axis_size("ctx"), lax.axis_size("exp")
    ctx_index, exp_index = lax.axis_index("ctx"), lax.axis_index("exp")
    local_experts = w_gate.shape[0]
    experts = local_experts * exp_size
    top = routes.shape[2]
    capacity = 2 * rows * top // experts
    shard_rows = w_query.shape[0]
    heads, kv_heads, head = QUERY_HEADS, KEY_VALUE_HEADS, HEAD_WIDTH
    groups = heads // kv_heads
    q_width, kv_width = heads * head, kv_heads * head
    scaling = 1.0 / math.sqrt(head)
    first_row = ctx_index * rows

    named_own = jnp.any(routes[0][:, :, None] == jnp.arange(128, dtype=jnp.int32), axis=1)
    small = jnp.concatenate(
        [
            w_router,
            gain_attn[:, None],
            gain_ffn[:, None],
            jnp.zeros((shard_rows, 128 - experts - 2), bf16),
        ],
        1,
    )
    qkv_full, out_full, small_full, named, rows_all = gather_weights(
        (jnp.concatenate([w_query, key_value_weight], 1), w_out, small), named_own.astype(bf16), cotangent[0], 1
    )
    gain_one = small_full[:, experts].astype(f32)
    gain_two = small_full[:, experts + 1].astype(f32)

    cosine, sine = rope_tables(first_row, rows, head)
    gains = jnp.stack([gain_one, gain_two])
    hops = planned(ctx_size, exp_size, shard_rows)
    queries, keyval, mixed, lse, resid_mid, hidden_two, rows_all = attend(
        hops, tokens[0], gains, cosine, sine, qkv_full, out_full, rows_all, 2
    )

    bias = jnp.where(named > 0, 0.0, NEG).astype(bf16)
    mine = exp_index * local_experts
    here = jnp.transpose(lax.dynamic_slice_in_dim(named, mine, local_experts, 2), (0, 2, 1))
    ahead = jnp.arange(rows)[:, None] < jnp.arange(rows)[None, :]
    slot = jnp.where(here > 0, ein("bjt,ts->bjs", here, ahead.astype(bf16)), -1.0)
    picks = (
        (slot[:, :, None, :] == jnp.arange(capacity, dtype=f32)[:, None])
        .astype(bf16)
        .reshape(exp_size, local_experts * capacity, rows)
    )
    _, out_part, back_part, grads, *early_first = expert_pass(
        hops and exp_size > 6, hops, hidden_two, cotangent[0], rows_all, picks, bias, small_full, w_gate, w_up, w_down, 3
    )
    own_bias = lax.dynamic_index_in_dim(bias, exp_index, 0, keepdims=False)
    output, grad_input, grads, dense_out, dense_qkv = backward(
        experts, shard_rows, back_part, out_part, grads, early_first[-1], tokens[0], resid_mid, cotangent[0], own_bias, small_full, gains,
        queries, keyval, mixed, lse, cosine, sine, qkv_full, out_full, 4
    )
    small_total = dense_qkv[:, q_width + 2 * kv_width :].astype(f32)
    half = local_experts * width
    units = w_gate.shape[2]
    grad_down = grads[2 * half :].astype(f32).reshape(local_experts, width // units, units, units)
    return (
        output[None],
        grad_input[None],
        small_total[:, experts],
        dense_qkv[:, :q_width].astype(f32),
        dense_qkv[:, q_width : q_width + 2 * kv_width].astype(f32),
        dense_out.astype(f32),
        small_total[:, experts + 1],
        small_total[:, :experts],
        grads[:half].astype(f32).reshape(w_gate.shape),
        grads[half : 2 * half].astype(f32).reshape(w_gate.shape),
        jnp.transpose(grad_down, (0, 2, 1, 3)).reshape(w_down.shape),
    )


def solution(mesh):
    rows, wide, deep = P("exp", "ctx", None), P("exp", None), P("exp", None, None)
    flat = P("exp")
    return jax.shard_map(
        shards,
        mesh=mesh,
        in_specs=(rows, rows, flat, wide, wide, wide, flat, wide, deep, deep, deep, rows),
        out_specs=(rows, rows, flat, wide, wide, wide, flat, wide, deep, deep, deep),
        check_vma=False,
    )
```

```python
import functools
import math

import jax
import jax.numpy as jnp
from jax import lax
from jax.experimental import pallas as pl
from jax.experimental.pallas import tpu as pltpu
from jax.sharding import PartitionSpec as P

MESH = pl.DeviceIdType.MESH
ANY = pl.BlockSpec(memory_space=pl.ANY)


def remote(src, dst, send, recv, ctx, exp):
    return pltpu.make_async_remote_copy(
        src_ref=src, dst_ref=dst, send_sem=send, recv_sem=recv, device_id=(ctx, exp), device_id_type=MESH
    )


def greet(pairs):
    barrier = pltpu.get_barrier_semaphore()
    count = 0
    for here, ctx, exp in pairs:
        if here is True:
            pl.semaphore_signal(barrier, inc=1, device_id=(ctx, exp), device_id_type=MESH)
            count = count + 1
        else:
            @pl.when(here)
            def _():
                pl.semaphore_signal(barrier, inc=1, device_id=(ctx, exp), device_id_type=MESH)
            count = count + here.astype(jnp.int32)
    pl.semaphore_wait(barrier, count)


QUERY_HEADS = 12
KEY_VALUE_HEADS = 2
HEAD_WIDTH = 128
EPS = 1e-06
NEG = -1e30
ROPE_BASE = 1000000.0


class Gathering:
    def __init__(self, line, own, out, sems, keep_own=True, window=None):
        self.line, self.keep_own = line, keep_own
        self.window = pl.ds(*window) if window is not None else pl.ds(0, out.shape[1])
        self.own, self.whole = own.at[self.window], out
        self.local_sem, self.z_send, self.z_recv, self.c_send, self.c_recv = sems
        self.c, self.e = lax.axis_index("ctx"), lax.axis_index("exp")
        self.p, self.k = self.e // 2, self.e % 2

    def block(self, q):
        return self.whole.at[2 * q + self.k, self.window]

    def along(self, q, src, to_right):
        there = self.e + 2 if to_right else self.e - 2
        way = 0 if to_right else 1
        return remote(src, self.block(q), self.z_send.at[way, q], self.z_recv.at[q], self.c, there)

    def across(self, q, src):
        there = self.e + 1 - 2 * self.k
        return remote(src, self.block(q), self.c_send.at[q], self.c_recv.at[q], self.c, there)

    def local(self):
        return pltpu.make_async_copy(self.own, self.whole.at[self.e, self.window], self.local_sem)

    def ends(self, d):
        for to_right in (True, False):
            q = self.p - d if to_right else self.p + d
            here = (q >= 0) if to_right else (q < self.line)
            further = (self.p < self.line - 1) if to_right else (self.p > 0)
            yield to_right, q, here, further

    def begin(self):
        for to_right, q, _, further in self.ends(0):
            @pl.when(further)
            def _():
                self.along(q, self.own, to_right).start()

        self.across(self.p, self.own).start()
        if self.keep_own:
            self.local().start()

    def pump(self, d, onward=True):
        for to_right, q, here, further in self.ends(d):
            @pl.when(here)
            def _():
                block = self.block(q)
                self.along(q, block, to_right).wait_recv()
                if onward:
                    @pl.when(further)
                    def _():
                        self.along(q, block, to_right).start()

                self.across(q, block).start()

    def forward(self, d):
        for to_right, q, here, further in self.ends(d):
            @pl.when(here & further)
            def _():
                self.along(q, self.block(q), to_right).start()

    def finish(self, sent, crossed):
        for d in crossed:
            for to_right, q, here, _ in self.ends(d):
                if d > 0 or to_right:
                    @pl.when(here)
                    def _():
                        self.across(q, self.own).wait()
        for d in sent:
            for to_right, q, here, further in self.ends(d):
                @pl.when(here & further)
                def _():
                    self.along(q, self.own, to_right).wait_send()

    def end(self, hops=None):
        last = self.line if hops is None else min(self.line, hops + 1)
        if self.keep_own:
            self.local().wait()
        self.finish(range(self.line if hops is None else last - 1), range(last))

    @staticmethod
    def scratch(line):
        dma = pltpu.SemaphoreType.DMA
        return [dma, dma((2, line)), dma((line,)), dma((line,)), dma((line,))]


def gather_kernel(line, own, out, *sems):
    c, e = lax.axis_index("ctx"), lax.axis_index("exp")
    greet([(e >= 2, c, e - 2), (e < 2 * line - 2, c, e + 2), (True, c, e + 1 - 2 * (e % 2))])
    gathering = Gathering(line, own, out, sems)
    gathering.begin()
    for d in range(1, line):
        gathering.pump(d)
    gathering.end()


def gather_rows(own, collective_id):
    n = lax.axis_size("exp")
    return pl.pallas_call(
        functools.partial(gather_kernel, n // 2),
        out_shape=jax.ShapeDtypeStruct((n,) + own.shape, own.dtype),
        in_specs=[ANY],
        out_specs=ANY,
        scratch_shapes=Gathering.scratch(n // 2),
        compiler_params=pltpu.CompilerParams(collective_id=collective_id, has_side_effects=True),
        name="gather_rows",
    )(own)


def add_rows(dst, a, b, rows):
    step = math.gcd(rows, 64)

    def body(i, carried):
        at = pl.ds(pl.multiple_of(i * step, step), step)
        dst[at, :] = a[at, :] + b[at, :]
        return carried

    lax.fori_loop(0, rows // step, body, 0)


class Summing:
    def __init__(self, line, part, cross, moving, acc, tmp, sems):
        self.line, self.part, self.cross, self.moving = line, part, cross, moving
        self.acc, self.tmp = acc, tmp
        self.own_sem, self.tmp_sem, self.c_send, self.c_recv, self.z_send, self.z_recv = sems
        self.c, self.e = lax.axis_index("ctx"), lax.axis_index("exp")
        self.p, self.k = self.e // 2, self.e % 2
        self.rows, self.width = part.shape[1:]

    def across(self, q):
        there = self.e + 1 - 2 * self.k
        return remote(
            self.part.at[2 * q + 1 - self.k], self.cross.at[q], self.c_send.at[q], self.c_recv.at[q], self.c, there
        )

    def own(self, q):
        return pltpu.make_async_copy(self.part.at[2 * q + self.k], self.acc.at[q], self.own_sem.at[q])

    def load(self, src, side):
        into = self.tmp.at[side, pl.ds(0, self.rows), pl.ds(0, self.width)]
        return pltpu.make_async_copy(src, into, self.tmp_sem.at[side])

    def add(self, q, side):
        add_rows(self.acc.at[q], self.acc.at[q], self.tmp.at[side, pl.ds(0, self.rows), pl.ds(0, self.width)], self.rows)

    def along(self, q, to_right):
        there = self.e + 2 if to_right else self.e - 2
        place = q if to_right else jnp.where(q == self.p - 1, self.line, q)
        return remote(self.acc.at[q], self.moving.at[place], self.z_send.at[q], self.z_recv.at[place], self.c, there)

    def arrived(self, place):
        return remote(self.acc.at[0], self.moving.at[place], self.z_send.at[0], self.z_recv.at[place], self.c, self.e)

    def ends(self, d):
        for to_right in (True, False):
            if d > 0 or to_right:
                q = self.p + d if to_right else self.p - d
                here = (q < self.line) if to_right else (q >= 0)
                yield to_right, q, here, ((self.p > 0) if to_right else (self.p < self.line - 1))

    def begin(self):
        order = [(d, end) for d in range(self.line - 1, -1, -1) for end in self.ends(d)]
        for _, (_, q, here, _) in order:
            @pl.when(here)
            def _():
                self.across(q).start()
                self.own(q).start()
        for d, (to_right, q, here, behind) in order:
            side = 0 if to_right else 1

            @pl.when(here)
            def _():
                self.across(q).wait_recv()
                self.load(self.cross.at[q], side).start()
                self.own(q).wait()
                self.load(self.cross.at[q], side).wait()
                self.add(q, side)
                if d > 0:
                    @pl.when(jnp.logical_not(behind))
                    def _():
                        self.along(q, to_right).start()

    def step(self, d):
        if d > 0:
            for to_right, q, here, behind in self.ends(d):
                @pl.when(here & behind)
                def _():
                    self.arrived(q).wait_recv()
                    self.load(self.moving.at[q], 0 if to_right else 1).start()
            for to_right, q, here, behind in self.ends(d):
                @pl.when(here & behind)
                def _():
                    side = 0 if to_right else 1
                    self.load(self.moving.at[q], side).wait()
                    self.add(q, side)
                    self.along(q, to_right).start()
            return
        last = ((0, self.p, self.p > 0), (1, self.line, self.p < self.line - 1))
        for side, place, behind in last:
            @pl.when(behind)
            def _():
                self.arrived(place).wait_recv()
                self.load(self.moving.at[place], side).start()
        for side, place, behind in last:
            @pl.when(behind)
            def _():
                self.load(self.moving.at[place], side).wait()
                self.add(self.p, side)

    def result(self):
        return self.acc.at[self.p]

    def end(self):
        for d in range(self.line):
            for to_right, q, here, _ in self.ends(d):
                @pl.when(here)
                def _():
                    if d > 0:
                        self.along(q, to_right).wait_send()
                    self.across(q).wait_send()

    @staticmethod
    def scratch(line, rows, width):
        dma = pltpu.SemaphoreType.DMA
        return [
            pltpu.VMEM((line, rows, width), jnp.bfloat16),
            dma((line,)),
            dma((2,)),
            dma((line,)),
            dma((line,)),
            dma((line,)),
            dma((line + 1,)),
        ]

    @staticmethod
    def landing(line, rows, width):
        return [
            jax.ShapeDtypeStruct((line, rows, width), jnp.bfloat16),
            jax.ShapeDtypeStruct((line + 1, rows, width), jnp.bfloat16),
        ]


class Totals:
    ahead, lag, count, early = 4, 1, 12, 4

    def __init__(self, part, early_first, sends, recvs, total=None, first=None, second=None, buffers=None, sems=None):
        self.part, self.total, self.early_first, self.first, self.second = part, total, early_first, first, second
        self.sends, self.recvs = sends, recvs
        if buffers is not None:
            self.own, self.got, self.got_two = buffers
            self.load_sem, self.got_sem, self.store_sem = sems
            self.slots = self.own.shape[0]
        c, self.e = lax.axis_index("ctx"), lax.axis_index("exp")
        self.bits = (c % 2, c // 2)
        self.nbrs = (c + 1 - 2 * (c % 2), lax.rem(c + 2, 4))
        self.deep = part.shape[0] // self.count

    def axes(self, h):
        return (0, 1) if h == 0 else (1, 0)

    def rows(self, ref, t, h, kept_one, kept_two=None, mine_two=True):
        one, two = self.axes(h)
        quarter, eighth = self.deep // 4, self.deep // 8
        bit = self.bits[one] if kept_one else 1 - self.bits[one]
        start = t * self.deep + h * (self.deep // 2) + bit * quarter
        if kept_two is None:
            return ref.at[pl.ds(pl.multiple_of(start, 16), quarter), :]
        return ref.at[pl.ds(pl.multiple_of(start + self.bits[two] * eighth, 16), eighth), :]

    def piece(self, t, h, kept):
        eighth = self.deep // 8
        bit = self.bits[self.axes(h)[1]]
        start = (bit if kept else 1 - bit) * eighth
        return self.own.at[t % self.slots, h, pl.ds(pl.multiple_of(start, 16), eighth), :]

    def copy(self, stage, t, h):
        one, two = self.axes(h)
        if stage == 0:
            src, dst, there = self.rows(self.part, t, h, False), self.landed(t, h), one
        elif stage == 1:
            src, dst, there = self.piece(t, h, False), self.second.at[t, h], two
        elif stage == 2:
            src, dst, there = self.piece(t, h, True), self.rows(self.total, t, h, True, True), two
        else:
            src, dst, there = self.rows(self.total, t, h, True), self.rows(self.total, t, h, True), one
        return remote(src, dst, self.sends.at[stage, t, h], self.recvs.at[stage, t, h], self.nbrs[there], self.e)

    def landed(self, t, h):
        return self.early_first.at[t, h] if t < self.early else self.first.at[t - self.early, h]

    def start_early(self, t):
        for h in range(2):
            self.copy(0, t, h).start()

    def end_early(self):
        for t in range(self.early):
            for h in range(2):
                self.copy(0, t, h).wait()

    def load_own(self, t, h):
        return pltpu.make_async_copy(
            self.rows(self.part, t, h, True), self.own.at[t % self.slots, h], self.load_sem.at[t % 2, h]
        )

    def store(self, t, h):
        return pltpu.make_async_copy(
            self.piece(t, h, True), self.rows(self.total, t, h, True, True), self.store_sem.at[t % self.slots, h]
        )

    def begin(self):
        for t in range(self.early, min(self.early + self.ahead, self.count)):
            for h in range(2):
                self.copy(0, t, h).start()
        for h in range(2):
            self.load_own(0, h).start()

    @property
    def ticks(self):
        return self.count + 2 * self.lag

    def tick(self, t):
        count, lag = self.count, self.lag
        t_two, t_three = t - lag, t - 2 * lag
        loads = []
        if t < count:
            for h in range(2):
                if t >= self.early:
                    self.copy(0, t, h).wait_recv()
                came = pltpu.make_async_copy(self.landed(t, h), self.got.at[h], self.got_sem.at[0, h])
                came.start()
                loads.append(came)
            if t + self.early + self.ahead < count:
                for h in range(2):
                    self.copy(0, t + self.early + self.ahead, h).start()
        later = []
        if 0 <= t_two < count:
            for h in range(2):
                self.copy(1, t_two, h).wait_recv()
                came = pltpu.make_async_copy(self.second.at[t_two, h], self.got_two.at[h], self.got_sem.at[1, h])
                came.start()
                later.append(came)
        if t < count:
            for h in range(2):
                self.load_own(t, h).wait()
                loads[h].wait()
                mine = self.own.at[t % self.slots, h]
                add_rows(mine, mine, self.got.at[h], self.deep // 4)
                self.copy(1, t, h).start()
        if 0 <= t_two < count:
            for h in range(2):
                later[h].wait()
                mine = self.piece(t_two, h, True)
                add_rows(mine, mine, self.got_two.at[h], self.deep // 8)
                self.copy(2, t_two, h).start()
                self.store(t_two, h).start()
        if 0 <= t_three < count:
            for h in range(2):
                self.copy(2, t_three, h).wait_recv()
                self.store(t_three, h).wait()
                self.copy(3, t_three, h).start()
                self.copy(1, t_three, h).wait_send()
                self.copy(2, t_three, h).wait_send()
        if t + 1 < count:
            for h in range(2):
                self.load_own(t + 1, h).start()

    def end(self):
        for t in range(self.count):
            for h in range(2):
                if t >= self.early:
                    self.copy(0, t, h).wait_send()
                self.copy(3, t, h).wait()

    @staticmethod
    def early_scratch():
        dma = pltpu.SemaphoreType.DMA
        return [dma((1, Totals.early, 2)), dma((1, Totals.early, 2))]

    @staticmethod
    def early_landing(deep, width):
        return jax.ShapeDtypeStruct((Totals.early, 2, deep // 4, width), jnp.bfloat16)

    @staticmethod
    def scratch(deep, width):
        count = Totals.count
        dma = pltpu.SemaphoreType.DMA
        slots = 2 * Totals.lag + 1
        return [
            pltpu.VMEM((slots, 2, deep // 4, width), jnp.bfloat16),
            pltpu.VMEM((2, deep // 4, width), jnp.bfloat16),
            pltpu.VMEM((2, deep // 8, width), jnp.bfloat16),
            dma((4, count, 2)),
            dma((4, count, 2)),
            dma((2, 2)),
            dma((2, 2)),
            dma((slots, 2)),
        ]

    @staticmethod
    def landing(deep, width):
        return [
            jax.ShapeDtypeStruct((Totals.count - Totals.early, 2, deep // 4, width), jnp.bfloat16),
            jax.ShapeDtypeStruct((Totals.count, 2, deep // 8, width), jnp.bfloat16),
        ]


class Sharing:
    def __init__(self, size, part, total, summed, arrived, sems):
        self.size, self.part, self.total, self.summed, self.arrived_at = size, part, total, summed, arrived
        self.a_send, self.a_recv, self.b_send, self.b_recv, self.store_sem = sems
        self.c, self.e = lax.axis_index("ctx"), lax.axis_index("exp")
        self.piece = part.shape[0] // size

    def rows(self, ref, j):
        return ref.at[pl.ds(pl.multiple_of(j * self.piece, 16), self.piece), :]

    def there(self, i):
        return lax.rem(self.c + i + 1, self.size)

    def give(self, i):
        there = self.there(i)
        return remote(
            self.rows(self.part, there), self.arrived_at.at[i], self.a_send.at[i], self.a_recv.at[i], there, self.e
        )

    def hand(self, i):
        return remote(
            self.summed, self.rows(self.total, self.c), self.b_send.at[i], self.b_recv.at[i], self.there(i), self.e
        )

    def handed(self, i):
        source = lax.rem(self.c + self.size - 1 - i, self.size)
        return remote(
            self.summed, self.rows(self.total, source), self.b_send.at[i], self.b_recv.at[i], self.there(i), self.e
        )

    def store(self):
        return pltpu.make_async_copy(self.summed, self.rows(self.total, self.c), self.store_sem)

    def begin(self):
        for i in range(self.size - 1):
            self.give(i).start()

    def middle(self):
        for i in range(self.size - 1):
            self.give(i).wait_recv()
        for j in range(self.piece // 16):
            at = pl.ds(j * 16, 16)
            total = self.part[pl.ds(pl.multiple_of(self.c * self.piece + j * 16, 16), 16), :].astype(jnp.float32)
            for i in range(self.size - 1):
                total = total + self.arrived_at[i, at, :].astype(jnp.float32)
            self.summed[at, :] = total.astype(self.summed.dtype)
        for i in range(self.size - 1):
            self.hand(i).start()
        self.store().start()

    def end(self):
        self.store().wait()
        for i in range(self.size - 1):
            self.give(i).wait_send()
            self.hand(i).wait_send()
            self.handed(i).wait_recv()

    @staticmethod
    def scratch(size, rows, width):
        dma = pltpu.SemaphoreType.DMA
        return [
            pltpu.VMEM((rows // size, width), jnp.bfloat16),
            pltpu.VMEM((size - 1, rows // size, width), jnp.bfloat16),
            dma((size - 1,)),
            dma((size - 1,)),
            dma((size - 1,)),
            dma((size - 1,)),
            dma,
        ]


def weights_kernel(line, quarter, *refs):
    count = 3
    own, own_mask, own_block = refs[:count], refs[count], refs[count + 1]
    out, masks, blocks = refs[count + 2 : 2 * count + 2], refs[2 * count + 2], refs[2 * count + 3]
    held, refs = refs[2 * count + 4 : 3 * count + 4], refs[3 * count + 4 :]
    local_sem, own_send, own_recv, z_send, z_recv, xy_send, xy_recv, d_send, d_recv, c_send, c_recv = refs[:-10]
    c, e = lax.axis_index("ctx"), lax.axis_index("exp")
    p, k = e // 2, e % 2
    sibling = e + 1 - 2 * k
    rows = own[0].shape[0]
    nbr = (c + 1 - 2 * (c % 2), (c + 2) % 4)
    opposite = 3 - c
    greet(
        [
            (p > 0, c, e - 2),
            (p < line - 1, c, e + 2),
            (True, c, sibling),
            (True, nbr[0], e),
            (True, nbr[1], e),
        ]
    )

    def whole(a):
        return out[a].at[pl.ds(pl.multiple_of(e * rows, 16), rows), :]

    def piece(a, q, column):
        return out[a].at[pl.ds(pl.multiple_of((2 * q + k) * rows + column * quarter, 16), quarter), :]

    def own_piece(a):
        return own[a].at[pl.ds(pl.multiple_of(c * quarter, 16), quarter), :]

    def load(a):
        return pltpu.make_async_copy(own[a], held[a], local_sem.at[0, a])

    def local(a):
        return pltpu.make_async_copy(held[a], whole(a), local_sem.at[1, a])

    def own_across(a):
        return remote(own[a], whole(a), own_send.at[a], own_recv.at[a], c, sibling)

    def along(a, q, src, to_right):
        there = e + 2 if to_right else e - 2
        way = 0 if to_right else 1
        return remote(src, piece(a, q, c), z_send.at[way, q, a], z_recv.at[q, a], c, there)

    def beside(a, q, axis):
        return remote(piece(a, q, c), piece(a, q, c), xy_send.at[axis, q, a], xy_recv.at[axis, q, a], nbr[axis], e)

    def onward(a, q):
        came, goes = (0, 1) if a == 0 else (1, 0)
        block = piece(a, q, nbr[came])
        return remote(block, block, d_send.at[q, a], d_recv.at[q, a], nbr[goes], e)

    def across(a, q, j):
        column = (c, nbr[0], nbr[1], opposite)[j]
        block = piece(a, q, column)
        return remote(block, block, c_send.at[q, j, a], c_recv.at[q, j, a], c, sibling)

    arrays = range(count)
    marking = Gathering(line, own_mask, masks, refs[-10:-5])
    gathering = Gathering(line, own_block, blocks, refs[-5:], keep_own=False)
    marking.begin()
    for a in arrays:
        @pl.when(p < line - 1)
        def _():
            along(a, p, own_piece(a), True).start()

        @pl.when(p > 0)
        def _():
            along(a, p, own_piece(a), False).start()
    for a in arrays:
        own_across(a).start()
        load(a).start()
    for a in arrays:
        load(a).wait()
        local(a).start()

    def ends(d):
        for to_right in (True, False):
            q = p - d if to_right else p + d
            yield to_right, q, ((q >= 0) if to_right else (q < line))

    for d in range(1, line + 1):
        if d < line:
            for to_right, q, here in ends(d):
                further = (p < line - 1) if to_right else (p > 0)

                @pl.when(here)
                def _():
                    for a in arrays:
                        along(a, q, piece(a, q, c), to_right).wait_recv()

                        @pl.when(further)
                        def _():
                            along(a, q, piece(a, q, c), to_right).start()

                        beside(a, q, 0).start()
                        beside(a, q, 1).start()
                        across(a, q, 0).start()
        if d < line:
            marking.pump(d)
        if d == line - 1:
            gathering.begin()
        if d > 1:
            for to_right, q, here in ends(d - 1):
                @pl.when(here)
                def _():
                    for a in arrays:
                        came = 0 if a == 0 else 1
                        beside(a, q, came).wait_recv()
                        onward(a, q).start()
                        across(a, q, 1 + came).start()
                        beside(a, q, 1 - came).wait_recv()
                        across(a, q, 2 - came).start()
    for d in range(1, line):
        for to_right, q, here in ends(d):
            @pl.when(here)
            def _():
                for a in arrays:
                    onward(a, q).wait_recv()
                    across(a, q, 3).start()
    gathering.pump(1, onward=False)
    gathering.end(1)
    marking.end()
    for a in arrays:
        local(a).wait()
        own_across(a).wait()
    for d in range(0, line):
        for to_right, q, here in ends(d):
            further = (p < line - 1) if to_right else (p > 0)
            for a in arrays:
                @pl.when(here & further)
                def _():
                    along(a, q, piece(a, q, c), to_right).wait_send()
                if d > 0:
                    @pl.when(here)
                    def _():
                        beside(a, q, 0).wait_send()
                        beside(a, q, 1).wait_send()
                        onward(a, q).wait_send()
                        for j in range(4):
                            across(a, q, j).wait()


def planned(size, n, shard_rows):
    return size == 4 and n in (4, 6, 8) and (shard_rows // 4) % 16 == 0


def gather_weights(shards, mask, block, collective_id):
    n = lax.axis_size("exp")
    if not planned(lax.axis_size("ctx"), n, shards[0].shape[0]):
        whole = tuple(lax.all_gather(w, "exp", axis=0, tiled=True) for w in shards)
        return whole + (lax.all_gather(mask, "exp", axis=0), gather_rows(block, collective_id))
    line = n // 2
    count = len(shards)
    dma = pltpu.SemaphoreType.DMA
    return pl.pallas_call(
        functools.partial(weights_kernel, line, shards[0].shape[0] // 4),
        out_shape=tuple(jax.ShapeDtypeStruct((n * w.shape[0], w.shape[1]), w.dtype) for w in shards)
        + tuple(jax.ShapeDtypeStruct((n,) + w.shape, w.dtype) for w in (mask, block)),
        in_specs=[ANY] * (count + 2),
        out_specs=(ANY,) * (count + 2),
        scratch_shapes=[pltpu.VMEM(w.shape, w.dtype) for w in shards]
        + [
            dma((2, count)),
            dma((count,)),
            dma((count,)),
            dma((2, line, count)),
            dma((line, count)),
            dma((2, line, count)),
            dma((2, line, count)),
            dma((line, count)),
            dma((line, count)),
            dma((line, 4, count)),
            dma((line, 4, count)),
        ]
        + Gathering.scratch(line)
        + Gathering.scratch(line),
        compiler_params=pltpu.CompilerParams(
            collective_id=collective_id, has_side_effects=True, vmem_limit_bytes=62 << 20
        ),
        name="gather_weights",
    )(*shards, mask, block)


def dot(a, b):
    return lax.dot_general(a, b, (((1,), (0,)), ((), ())), preferred_element_type=jnp.float32)


def dot_nt(a, b):
    return lax.dot_general(a, b, (((1,), (1,)), ((), ())), preferred_element_type=jnp.float32)


def dot_tn(a, b):
    return lax.dot_general(a, b, (((0,), (0,)), ((), ())), preferred_element_type=jnp.float32)


def visit(p, line, i):
    both = jnp.minimum(p, line - 1 - p)
    d = jnp.where(i <= 2 * both, (i + 1) // 2, i - both)
    left = jnp.where(i <= 2 * both, i % 2 == 1, p > line - 1 - p)
    q = jnp.where(left, p - d, p + d)
    first = (i == 0) | (i > 2 * both) | (i % 2 == 1)
    return q, d, first


def expert_kernel(line, local, cap, hop, start, hidden, own_grads, grads_in, named, router, w_gate, w_up, w_down, *refs):
    hidden_all, out_part, back_part, grads, grads_all = refs[:5]
    if start:
        early_first, refs = refs[5], refs[:5] + refs[6:]
    wg, wu, wd, xs, ds, act, dg, du, es, h_buf, y_buf, out_stage, back_stage, in_stage, down_stage = refs[5:20]
    picks, xs_turned, act_turned, gate_kept, refs = *refs[20:24], refs[:20] + refs[24:]
    w_sem, own_sem, z_send, z_recv, c_send, c_recv, h_sem, y_sem, o_sem, b_sem, s_sem = refs[20:31]
    f32, bf16 = jnp.float32, jnp.bfloat16
    c, e = lax.axis_index("ctx"), lax.axis_index("exp")
    p, k = e // 2, e % 2
    sibling = e + 1 - 2 * k
    rows, width = hidden.shape
    hidden_units = wg.shape[2]
    slots = 2 * cap
    lanes = router.shape[1]

    loads = [
        pltpu.make_async_copy(src, dst, w_sem.at[i])
        for i, (src, dst) in enumerate(((w_gate, wg), (w_up, wu), (w_down, wd)))
    ]
    for copy in loads:
        copy.start()
    beside = [(True, c + 1 - 2 * (c % 2), e), (True, lax.rem(c + 2, 4), e)] if start else []
    greet([(p > 0, c, e - 2), (p < line - 1, c, e + 2), (True, c, sibling)] + beside)
    def along(q, src, to_right):
        there = e + 2 if to_right else e - 2
        return remote(src, hidden_all.at[2 * q + k], z_send.at[0 if to_right else 1, q], z_recv.at[q], c, there)

    def across(q, src):
        return remote(src, hidden_all.at[2 * q + k], c_send.at[q], c_recv.at[q], c, sibling)

    def load_hidden(q, slot):
        return pltpu.make_async_copy(hidden_all.at[pl.ds(2 * q, 2)], h_buf.at[slot], h_sem.at[slot])

    def load_grads(q, slot):
        return pltpu.make_async_copy(grads_all.at[pl.ds(2 * q, 2)], y_buf.at[slot], y_sem.at[slot])

    def load_own(buf, own, blocks, i):
        return [
            pltpu.make_async_copy(own, buf.at[0, k], own_sem.at[2 * i]),
            pltpu.make_async_copy(blocks.at[sibling], buf.at[0, 1 - k], own_sem.at[2 * i + 1]),
        ]

    def store_out(q, slot):
        return pltpu.make_async_copy(out_stage.at[slot], out_part.at[pl.ds(2 * q, 2)], o_sem.at[slot])

    def store_back(q, slot):
        return pltpu.make_async_copy(back_stage.at[slot], back_part.at[pl.ds(2 * q, 2)], b_sem.at[slot])

    @pl.when(p < line - 1)
    def _():
        along(p, hidden, True).start()

    @pl.when(p > 0)
    def _():
        along(p, hidden, False).start()

    across(p, hidden).start()
    if hop:
        hops = Gathering(line, grads_all.at[e], grads_all, refs[31:36], window=(rows // 2, rows // 2))
        hops.forward(2)
    for copy in load_own(y_buf, own_grads, grads_all, 0):
        copy.start()

    def pump(d):
        for to_right in (True, False):
            q = p - d if to_right else p + d
            here = (q >= 0) if to_right else (q < line)
            further = (p < line - 1) if to_right else (p > 0)

            @pl.when(here)
            def _():
                block = hidden_all.at[2 * q + k]
                along(q, block, to_right).wait_recv()

                @pl.when(further)
                def _():
                    along(q, block, to_right).start()

                across(q, block).start()

    for copy in loads:
        copy.wait()

    lane = lax.broadcasted_iota(jnp.int32, (local * cap, lanes), 1)
    expert_of_row = lax.broadcasted_iota(jnp.int32, (local * cap, lanes), 0) // cap

    def units_of(j, q):
        tile = 256
        rows_j = xs[j].reshape(slots, width)
        xs_turned[j, :, pl.ds(pl.multiple_of(q * slots, slots), slots)] = rows_j.T
        grads_j = ds[j, q].reshape(slots, width)

        def units(t, carried):
            at = pl.ds(pl.multiple_of(t * tile, tile), tile)
            gate_pre = dot(rows_j, wg[j, :, at])
            up_pre = dot(rows_j, wu[j, :, at])
            grad_act = dot_nt(grads_j, wd[j, at, :])
            sigmoid = 1.0 / (1.0 + jnp.exp(-gate_pre))
            silu = gate_pre * sigmoid
            hidden_low = (silu * up_pre).astype(bf16)
            act[j, :, at] = hidden_low
            act_turned[j, at, pl.ds(pl.multiple_of(q * slots, slots), slots)] = hidden_low.T
            dg[j, q, :, at] = (grad_act * up_pre * sigmoid * (1.0 + gate_pre * (1.0 - sigmoid))).astype(bf16)
            du[j, q, :, at] = (grad_act * silu).astype(bf16)
            return carried

        lax.fori_loop(0, hidden_units // tile, units, 0)

    def give_back(q, slot):
        wide = 512
        pick_pair = [picks[b] for b in range(2)]

        def outputs(t, sums):
            at = pl.ds(pl.multiple_of(t * wide, wide), wide)
            gated, back, new_sums = [], [], []
            for j in range(local):
                y = dot(act[j], wd[j, :, at])
                back_j = dot_nt(dg[j, q], wg[j, at, :]) + dot_nt(du[j, q], wu[j, at, :])
                new = []
                for b in range(2):
                    half = slice(b * cap, (b + 1) * cap)
                    y_b = y[half]
                    new.append(sums[j][b] + jnp.sum(y_b * es[j, b, :, at].astype(f32), -1, keepdims=True))
                    gated.append((gate_kept[b, j * cap : (j + 1) * cap, 0:1] * y_b).astype(bf16))
                    back.append(back_j[half].astype(bf16))
                new_sums.append(tuple(new))
            for b in range(2):
                mine = jnp.concatenate([gated[2 * j + b] for j in range(local)], 0)
                out_stage[slot, b, :, at] = dot_tn(pick_pair[b], mine).astype(bf16)
                mine = jnp.concatenate([back[2 * j + b] for j in range(local)], 0)
                back_stage[slot, b, :, at] = dot_tn(pick_pair[b], mine).astype(bf16)
            return tuple(new_sums)

        nothing = jnp.zeros((cap, 1), f32)
        sums = lax.fori_loop(
            0, width // wide, outputs, tuple((nothing, nothing) for _ in range(local))
        )
        for b in range(2):
            grad_gates = jnp.concatenate([sums[j][b] for j in range(local)], 0)
            coarse = grad_gates.astype(bf16).astype(f32)
            spot = e * local + expert_of_row
            spread = jnp.where(
                lane == spot, coarse, jnp.where(lane == spot + lanes // 2, grad_gates - coarse, 0.0)
            ).astype(bf16)
            back_stage[slot, b, :, width : width + lanes] = dot_tn(pick_pair[b], spread).astype(bf16)
        store_out(q, slot).start()
        store_back(q, slot).start()

    def one_chip(i, carried):
        q, d, first = visit(p, line, i)
        slot = i % 2

        across(q, hidden).wait_recv()

        @pl.when(i == 0)
        def _():
            own = load_own(h_buf, hidden, hidden_all, 1)
            for copy in own:
                copy.start()
            for copy in own + load_own(y_buf, own_grads, grads_all, 0):
                copy.wait()

        @pl.when(i > 0)
        def _():
            load_hidden(q, slot).start()

        if hop:
            @pl.when(d == line - 1)
            def _():
                hops.pump(line - 1, onward=False)
                hops.finish([], [line - 1])
                load_grads(q, slot).start()

        after, d_after, _ = visit(p, line, i + 1)

        @pl.when((i < line - 1) & (d_after < (line - 1 if hop else line)))
        def _():
            load_grads(after, 1 - slot).start()

        @pl.when(i > 0)
        def _():
            load_hidden(q, slot).wait()
            load_grads(q, slot).wait()

        @pl.when(i >= 2)
        def _():
            store_out(visit(p, line, i - 2)[0], slot).wait()
            store_back(visit(p, line, i - 2)[0], slot).wait()

        place = lax.broadcasted_iota(jnp.int32, (cap, rows), 0).astype(f32)
        sub = lax.broadcasted_iota(jnp.int32, (lanes, rows), 0)
        upper = lax.broadcasted_iota(jnp.int32, (rows, 2 * rows), 0)
        column = lax.broadcasted_iota(jnp.int32, (rows, 2 * rows), 1)
        ahead = jnp.where((upper < column) & (column < rows) | (upper + rows == column), 1.0, 0.0).astype(bf16)
        for b in range(2):
            marks = named[2 * q + b]
            counted = dot_tn(marks, ahead)
            slots_of = jnp.where(counted[:, rows:] > 0.5, counted[:, :rows], -1.0)
            for j in range(local):
                row = jnp.sum(jnp.where(sub == e * local + j, slots_of, 0.0), 0, keepdims=True)
                picks[b, j * cap : (j + 1) * cap] = jnp.where(place == row, 1.0, 0.0).astype(bf16)
            pick = picks[b]
            block = h_buf[slot, b]
            picked = dot(pick, block).astype(bf16)
            for j in range(local):
                xs[j, b] = picked[j * cap : (j + 1) * cap]
            logits = jnp.where(marks.astype(f32) > 0.5, dot(block, router[...]), NEG)
            raised = jnp.exp(logits - jnp.max(logits, -1, keepdims=True))
            gates = raised / jnp.sum(raised, -1, keepdims=True)
            coarse = gates.astype(bf16)
            fine = (gates - coarse.astype(f32)).astype(bf16)
            at_slots = dot(pick, coarse) + dot(pick, fine)
            gate_slot = jnp.sum(jnp.where(lane == e * local + expert_of_row, at_slots, 0.0), -1, keepdims=True)
            gate_kept[b] = jnp.broadcast_to(gate_slot, gate_kept.shape[1:])
            grad_rows = dot(pick, y_buf[slot, b])
            grad_pairs = (gate_slot * grad_rows).astype(bf16)
            grad_rows = grad_rows.astype(bf16)
            for j in range(local):
                es[j, b] = grad_rows[j * cap : (j + 1) * cap]
                ds[j, q, b] = grad_pairs[j * cap : (j + 1) * cap]

        units_of(0, q)

        @pl.when(i < line - 1)
        def _():
            for j in range(1, local):
                units_of(j, q)
            give_back(q, slot)

        @pl.when(first & (d + 1 < line))
        def _():
            pump(d + 1)

        return carried

    lax.fori_loop(0, line, one_chip, 0)

    deep = line * slots
    tile = 256
    tiles = hidden_units // tile

    def products(left, right, stage, first_row, count):
        high = stage.shape[1]

        def stores(t):
            row = first_row + lax.div(t, tiles) * high
            return pltpu.make_async_copy(
                stage.at[lax.rem(t, 2)],
                grads.at[
                    pl.ds(pl.multiple_of(row, 16), high),
                    pl.ds(pl.multiple_of(lax.rem(t, tiles) * tile, tile), tile),
                ],
                s_sem.at[lax.rem(t, 2)],
            )

        def one_tile(t, carried):
            @pl.when(t >= 2)
            def _():
                stores(t - 2).wait()

            stage[lax.rem(t, 2)] = dot(left[...], right(pl.ds(pl.multiple_of(t * tile, tile), tile))).astype(bf16)
            stores(t).start()
            return carried

        lax.fori_loop(0, count, one_tile, 0)
        for t in range(max(0, count - 2), count):
            stores(jnp.int32(t)).wait()

    totals = Totals(grads, early_first, *refs[-2:]) if start else None
    sent = 0

    def send_ready(rows_done):
        nonlocal sent
        while start and sent < totals.early and (sent + 1) * totals.deep <= rows_done:
            totals.start_early(sent)
            sent += 1

    last_chip = visit(p, line, jnp.int32(line - 1))[0]
    for i, source in enumerate((dg, du)):
        for j in range(local):
            if i == 0 and j > 0:
                units_of(j, last_chip)
            products(
                xs_turned.at[j],
                lambda at: source[j, :, :, at].reshape(deep, tile),
                in_stage, (i * local + j) * width, tiles,
            )
            send_ready((i * local + j + 1) * width)
    for j in range(local):
        products(
            act_turned.at[j],
            lambda at: ds[j, :, :, :, at].reshape(deep, tile),
            down_stage, 2 * local * width + j * width, width // tile,
        )

    give_back(last_chip, (line - 1) % 2)

    if start:
        totals.end_early()
    if hop:
        hops.finish([2], [])
    for i in range(max(0, line - 2), line):
        q = visit(p, line, jnp.int32(i))[0]
        store_out(q, i % 2).wait()
        store_back(q, i % 2).wait()
    for d in range(line):
        for to_right in (True, False):
            if d == 0 and not to_right:
                continue
            q = p - d if to_right else p + d
            here = (q >= 0) if to_right else (q < line)

            @pl.when(here)
            def _():
                across(q, hidden).wait_send()
    for d in range(line):
        for to_right in (True, False):
            q = p - d if to_right else p + d
            here = (q >= 0) if to_right else (q < line)
            further = (p < line - 1) if to_right else (p > 0)

            @pl.when(here & further)
            def _():
                along(q, hidden, to_right).wait_send()


def expert_pass(hop, start, cap, hidden, own_grads, grads_all, named, router, w_gate, w_up, w_down, collective_id):
    n = lax.axis_size("exp")
    line = n // 2
    rows, width = hidden.shape
    local, _, units = w_gate.shape
    bf16 = jnp.bfloat16
    lanes = router.shape[1]
    dma = pltpu.SemaphoreType.DMA
    vmem = pl.BlockSpec(memory_space=pltpu.VMEM)
    slots = n * cap
    return pl.pallas_call(
        functools.partial(expert_kernel, line, local, cap, hop, start),
        out_shape=(
            jax.ShapeDtypeStruct((n, rows, width), bf16),
            jax.ShapeDtypeStruct((n, rows, width), bf16),
            jax.ShapeDtypeStruct((n, rows, width + lanes), bf16),
            jax.ShapeDtypeStruct((3 * local * width, units), bf16),
            jax.ShapeDtypeStruct(grads_all.shape, bf16),
        )
        + ((Totals.early_landing(3 * local * width // Totals.count, units),) if start else ()),
        in_specs=[ANY, ANY, ANY, vmem, vmem, ANY, ANY, ANY],
        out_specs=(ANY,) * (6 if start else 5),
        input_output_aliases={2: 4},
        scratch_shapes=[
            pltpu.VMEM((local, width, units), bf16),
            pltpu.VMEM((local, width, units), bf16),
            pltpu.VMEM((local, units, width), bf16),
            pltpu.VMEM((local, 2, cap, width), bf16),
            pltpu.VMEM((local, line, 2, cap, width), bf16),
            pltpu.VMEM((local, 2 * cap, units), bf16),
            pltpu.VMEM((local, line, 2 * cap, units), bf16),
            pltpu.VMEM((local, line, 2 * cap, units), bf16),
            pltpu.VMEM((local, 2, cap, width), bf16),
            pltpu.VMEM((2, 2, rows, width), bf16),
            pltpu.VMEM((2, 2, rows, width), bf16),
            pltpu.VMEM((2, 2, rows, width), bf16),
            pltpu.VMEM((2, 2, rows, width + lanes), bf16),
            pltpu.VMEM((2, width, 256), bf16),
            pltpu.VMEM((2, units, 256), bf16),
            pltpu.VMEM((2, local * cap, rows), bf16),
            pltpu.VMEM((local, width, n * cap), bf16),
            pltpu.VMEM((local, units, n * cap), bf16),
            pltpu.VMEM((2, local * cap, 128), jnp.float32),
            dma((3,)),
            dma((4,)),
            dma((2, line)),
            dma((line,)),
            dma((line,)),
            dma((line,)),
            dma((2,)),
            dma((2,)),
            dma((2,)),
            dma((2,)),
            dma((2,)),
        ]
        + (Gathering.scratch(line) if hop else [])
        + (Totals.early_scratch() if start else []),
        compiler_params=pltpu.CompilerParams(
            collective_id=collective_id, has_side_effects=True, vmem_limit_bytes=62 << 20
        ),
        name="expert_pass",
    )(hidden, own_grads, grads_all, named, router, w_gate, w_up, w_down)


def turn(block, cosine, signed_sine):
    return block * cosine + pltpu.roll(block, block.shape[1] // 2, 1) * signed_sine


def row_norm(block):
    inverse = lax.rsqrt(jnp.mean(block * block, -1, keepdims=True) + EPS)
    return block * inverse, inverse


def attend_kernel(size, line, hop, experts, heads, kv_heads, tokens, small, cosine, sine, qkv_hbm, out_hbm, rows_in, *refs):
    targets, rows_all = refs[:7], refs[7]
    held, refs = refs[8:15], refs[15:]
    queries, keyval, mixed, lse, mid, hidden, gains = held
    wqkv, wout, h1, w_sem, send, recv, o_sem = refs[:7]
    f32, bf16 = jnp.float32, jnp.bfloat16
    c, e = lax.axis_index("ctx"), lax.axis_index("exp")
    rows, width = tokens.shape
    head = HEAD_WIDTH
    groups = heads // kv_heads
    q_width, kv_width = heads * head, kv_heads * head
    loads = [
        pltpu.make_async_copy(qkv_hbm, wqkv, w_sem.at[0]),
        pltpu.make_async_copy(out_hbm, wout, w_sem.at[1]),
    ]
    for copy in loads:
        copy.start()
    others = [lax.rem(c + i, size) for i in range(1, size)]
    column = [(e >= 2, c, e - 2), (e < 2 * line - 2, c, e + 2), (True, c, e + 1 - 2 * (e % 2))]
    greet((column if hop else []) + [(True, there, e) for there in others])
    if hop:
        half = rows // 2
        early, late = (
            Gathering(line, rows_all.at[e], rows_all, refs[7 + 5 * i : 12 + 5 * i], window=(i * half, half)) for i in range(2)
        )
        early.forward(1)
        late.forward(1)

    def leave(i):
        return pltpu.make_async_copy(held[i], targets[i], o_sem.at[i])

    turned = small[...].astype(f32).T
    gains[...] = turned[experts : experts + 8]
    leave(6).start()

    def step(t, carried):
        at = pl.ds(pl.multiple_of(t * 64, 64), 64)
        normed, _ = row_norm(tokens[at, :].astype(f32))
        h1[at, :] = (normed * gains[0:1, :]).astype(bf16)
        return carried

    lax.fori_loop(0, rows // 64, step, 0)
    loads[0].wait()
    kv = dot(h1[...], wqkv[:, q_width:])
    for j in range(kv_heads):
        at = slice(j * head, (j + 1) * head)
        keyval[c, :, at] = turn(kv[:, at], cosine[...], sine[...]).astype(bf16)
    keyval[c, :, kv_width:] = kv[:, kv_width:].astype(bf16)

    def give(i):
        return remote(keyval.at[c], keyval.at[c], send.at[i - 1], recv.at[i - 1], others[i - 1], e)

    for i in range(1, size):
        @pl.when(c + i < size)
        def _():
            give(i).start()

    for j in range(1, size):
        @pl.when(j > c)
        def _():
            keyval[j] = jnp.zeros((rows, 2 * kv_width), bf16)

    pair = 2 * head

    def project(t, carried):
        at = pl.ds(pl.multiple_of(t * pair, pair), pair)
        q = dot(h1[...], wqkv[:, at])
        for j in range(2):
            queries[2 * t + j] = turn(q[:, j * head : (j + 1) * head], cosine[...], sine[...]).astype(bf16)
        return carried

    lax.fori_loop(0, heads // 2, project, 0)
    leave(0).start()
    if hop:
        early.pump(2)
    for i in range(1, size):
        @pl.when(c - i >= 0)
        def _():
            give(i).wait_recv()
    leave(1).start()

    keys_count = size * rows
    scaling = 1.0 / math.sqrt(head)
    lane = lax.broadcasted_iota(jnp.int32, (rows, 128), 1)

    def one_head(j):
        h = j // groups
        keys = keyval[:, :, pl.ds(pl.multiple_of(h * head, head), head)].reshape(keys_count, head)
        values = keyval[:, :, pl.ds(pl.multiple_of(kv_width + h * head, head), head)].reshape(keys_count, head)
        place = lax.broadcasted_iota(jnp.int32, (rows, keys_count), 1)
        row = c * rows + lax.broadcasted_iota(jnp.int32, (rows, keys_count), 0)
        scores = jnp.where(place <= row, dot_nt(queries[j], keys) * scaling, NEG)
        peak = jnp.max(scores, -1, keepdims=True)
        raised = jnp.exp(scores - peak)
        total = jnp.sum(raised, -1, keepdims=True)
        probs = (raised * (1.0 / total)).astype(bf16)
        return dot(probs, values), peak + jnp.log(total)

    def two_heads(t, stats):
        found = [one_head(2 * t + i) for i in range(2)]
        mixed[:, pl.ds(pl.multiple_of(t * pair, pair), pair)] = jnp.concatenate(
            [block for block, _ in found], 1
        ).astype(bf16)
        for i, (_, value) in enumerate(found):
            stats = jnp.where(lane == 2 * t + i, value, stats)
        return stats

    lse[...] = lax.fori_loop(0, heads // 2, two_heads, jnp.zeros((rows, 128), f32))
    leave(2).start()
    leave(3).start()
    if hop:
        late.pump(2, onward=False)
    loads[1].wait()

    def outward(t, carried):
        at = pl.ds(pl.multiple_of(t * 256, 256), 256)
        mid[:, at] = tokens[:, at].astype(f32) + dot(mixed[...], wout[:, at])
        return carried

    lax.fori_loop(0, width // 256, outward, 0)
    leave(4).start()

    def last(t, carried):
        at = pl.ds(pl.multiple_of(t * 64, 64), 64)
        normed, _ = row_norm(mid[at, :])
        hidden[at, :] = (normed * gains[1:2, :]).astype(bf16)
        return carried

    lax.fori_loop(0, rows // 64, last, 0)
    leave(5).start()
    if hop:
        early.pump(3, onward=False)
        early.finish([1, 2], [2, 3])
        late.finish([1], [2])
    for i in range(7):
        leave(i).wait()
    for i in range(1, size):
        @pl.when(c + i < size)
        def _():
            give(i).wait_send()


def attend(hop, experts, tokens, small, cosine, sine, qkv_full, out_full, rows_all, collective_id):
    size, line = lax.axis_size("ctx"), lax.axis_size("exp") // 2
    rows, width = tokens.shape
    f32, bf16 = jnp.float32, jnp.bfloat16
    dma = pltpu.SemaphoreType.DMA
    vmem = pl.BlockSpec(memory_space=pltpu.VMEM)
    shape = jax.ShapeDtypeStruct
    made = (
        shape((QUERY_HEADS, rows, HEAD_WIDTH), bf16),
        shape((size, rows, 2 * KEY_VALUE_HEADS * HEAD_WIDTH), bf16),
        shape((rows, QUERY_HEADS * HEAD_WIDTH), bf16),
        shape((rows, 128), f32),
        shape((rows, width), f32),
        shape((rows, width), bf16),
        shape((8, width), f32),
    )
    return pl.pallas_call(
        functools.partial(attend_kernel, size, line, hop, experts, QUERY_HEADS, KEY_VALUE_HEADS),
        out_shape=made + (shape(rows_all.shape, bf16),),
        in_specs=[vmem] * 4 + [ANY] * 3,
        out_specs=(ANY,) * 8,
        input_output_aliases={6: 7},
        scratch_shapes=[pltpu.VMEM(one.shape, one.dtype) for one in made]
        + [
            pltpu.VMEM(qkv_full.shape, bf16),
            pltpu.VMEM(out_full.shape, bf16),
            pltpu.VMEM((rows, width), bf16),
            dma((2,)),
            dma((size - 1,)),
            dma((size - 1,)),
            dma((7,)),
        ]
        + (Gathering.scratch(line) * 2 if hop else []),
        compiler_params=pltpu.CompilerParams(
            collective_id=collective_id, has_side_effects=True, vmem_limit_bytes=62 << 20
        ),
        name="attend",
    )(tokens, small, cosine, sine, qkv_full, out_full, rows_all)


def halves(values):
    coarse = values.astype(jnp.bfloat16)
    return coarse, (values - coarse.astype(jnp.float32)).astype(jnp.bfloat16)


def backward_kernel(size, line, heads, kv_heads, experts, fused, *refs):
    back_part, out_part, grads, early_first, tokens, mid, final, marks, small, gains = refs[:10]
    queries, keyval, mixed, lse, cosine, sine, qkv_hbm, out_hbm, output, grad_tokens, dense_out, dense_qkv = refs[10:22]
    refs = refs[22:]
    if fused:
        totals, total_out, total_qkv, land_one, land_two = refs[:5]
        landing, refs = refs[5:13], refs[13:]
        tmp = refs[0]
        sum_refs, refs = [refs[1 + 7 * i : 8 + 7 * i] for i in range(4)], refs[29:]
        total_scratch, refs = refs[:8], refs[8:]
        share_out, share_qkv, refs = refs[:7], refs[7:14], refs[14:]
    else:
        came, out_sum = back_part, out_part
    wqkv, wout, probs, d_scores, d_mixed, d_att, d_mid, h1, h2, dq, dkv, kv_part, kv_other, stage = refs[:14]
    w_sem, kv_send, kv_recv, s_sem = refs[14:]
    f32, bf16 = jnp.float32, jnp.bfloat16
    c, e = lax.axis_index("ctx"), lax.axis_index("exp")
    p, k = e // 2, e % 2
    rows, width = tokens.shape
    head = HEAD_WIDTH
    groups = heads // kv_heads
    q_width, kv_width = heads * head, kv_heads * head
    scaling = 1.0 / math.sqrt(head)
    keys_count = size * rows
    n = 2 * line
    shard = dense_out.shape[1]

    loads = [
        pltpu.make_async_copy(qkv_hbm, wqkv, w_sem.at[0]),
        pltpu.make_async_copy(out_hbm, wout, w_sem.at[1]),
    ]
    others = [lax.rem(c + i, size) for i in range(1, size)]
    column = [(p > 0, c, e - 2), (p < line - 1, c, e + 2), (True, c, e + 1 - 2 * k)]
    greet((column if fused else []) + [(True, there, e) for there in others])
    ticked = []

    def tick():
        if fused and len(ticked) < experts_total.ticks:
            experts_total.tick(len(ticked))
            ticked.append(1)

    if fused:
        experts_total = Totals(
            grads, early_first, *total_scratch[3:5], totals, land_one, land_two, total_scratch[:3], total_scratch[5:]
        )
        experts_total.begin()
        sums = [
            Summing(line, part, landing[2 * i], landing[2 * i + 1], sum_refs[i][0], tmp, sum_refs[i][1:])
            for i, part in enumerate((back_part, out_part, dense_out, dense_qkv))
        ]
        back, outs, dense_outs, dense_qkvs = sums
        came, out_sum = back.result(), outs.result()
        sharing_out = Sharing(size, dense_outs.result(), total_out, *share_out[:2], share_out[2:])
        sharing_qkv = Sharing(size, dense_qkvs.result(), total_qkv, *share_qkv[:2], share_qkv[2:])
        back.begin()
    for copy in loads:
        copy.start()

    lane = lax.broadcasted_iota(jnp.int32, (rows, 128), 1)

    def keys_of(h):
        return keyval[:, :, pl.ds(pl.multiple_of(h * head, head), head)].reshape(keys_count, head)

    def values_of(h):
        return keyval[:, :, pl.ds(pl.multiple_of(kv_width + h * head, head), head)].reshape(keys_count, head)

    def again(j, carried):
        place = lax.broadcasted_iota(jnp.int32, (rows, keys_count), 1)
        row = c * rows + lax.broadcasted_iota(jnp.int32, (rows, keys_count), 0)
        scores = dot_nt(queries[j], keys_of(j // groups)) * scaling
        level = jnp.sum(jnp.where(lane == j, lse[...], 0.0), -1, keepdims=True)
        probs[j] = jnp.exp(jnp.where(place <= row, scores - level, NEG)).astype(bf16)
        return carried

    def norms(t, carried):
        at = pl.ds(pl.multiple_of(t * 64, 64), 64)
        normed, _ = row_norm(mid[at, :])
        h2[at, :] = (normed * gains[1:2, :]).astype(bf16)
        normed, _ = row_norm(tokens[at, :].astype(f32))
        h1[at, :] = (normed * gains[0:1, :]).astype(bf16)
        return carried

    bounds = [heads * i // max(1, line - 1) for i in range(line)]
    for i, d in enumerate(range(line - 1, 0, -1)):
        if fused and i > 0:
            back.step(d)
        if i == 0:
            lax.fori_loop(0, rows // 64, norms, 0)
        lax.fori_loop(bounds[i], bounds[i + 1], again, 0)
        tick()
        if fused and d == 2:
            outs.begin()
    if fused:
        back.step(0)
        tick()

    logits = jnp.where(marks[...].astype(f32) > 0.5, dot(h2[...], small[...]), NEG)
    raised = jnp.exp(logits - jnp.max(logits, -1, keepdims=True))
    gates = raised / jnp.sum(raised, -1, keepdims=True)
    extra = came[:, width:].astype(f32)
    grad_gates = extra + pltpu.roll(extra, extra.shape[1] // 2, 1)
    grad_logits = gates * (grad_gates - jnp.sum(gates * grad_gates, -1, keepdims=True))
    logits_hi, logits_lo = halves(grad_logits)
    grad_small = dot_tn(h2[...], logits_hi) + dot_tn(h2[...], logits_lo)

    def second_norm(t, total):
        at = pl.ds(pl.multiple_of(t * 32, 32), 32)
        normed, inverse = row_norm(mid[at, :])
        low, high = halves(grad_logits_ref[at, :])
        grad_h2 = came[at, :width].astype(f32) + dot_nt(low, small[...]) + dot_nt(high, small[...])
        total = total + jnp.sum(grad_h2 * normed, 0, keepdims=True)
        scaled = grad_h2 * gains[1:2, :]
        grad = final[at, :].astype(f32) + inverse * (scaled - normed * jnp.mean(scaled * normed, -1, keepdims=True))
        d_mid[at, :] = grad
        d_att[at, :] = grad.astype(bf16)
        return total

    grad_logits_ref = dkv.at[:, 0:128]
    dkv[:, 0:128] = grad_logits
    gain_two = lax.fori_loop(0, rows // 32, second_norm, jnp.zeros((1, width), f32))

    loads[1].wait()

    def mixing(t, carried):
        at = pl.ds(pl.multiple_of(t * 256, 256), 256)
        block = dot_nt(d_att[...], wout[at, :]).astype(bf16)
        for i in range(2):
            d_mixed[2 * t + i] = block[:, i * head : (i + 1) * head]
        return carried

    lax.fori_loop(0, q_width // 256, mixing, 0)
    if fused and line > 2:
        outs.step(line - 2)
    tick()

    def gradients(left, right, dense, column, count):
        def store(t):
            return pltpu.make_async_copy(
                stage.at[lax.rem(t, 2)],
                dense.at[:, :, pl.ds(pl.multiple_of(column + t * 256, 128), 256)],
                s_sem.at[lax.rem(t, 2)],
            )

        def one(t, carried):
            @pl.when(t >= 2)
            def _():
                store(t - 2).wait()

            product = dot_tn(left[...], right[:, pl.ds(pl.multiple_of(t * 256, 256), 256)])
            stage[lax.rem(t, 2)] = product.astype(bf16).reshape(n, shard, 256)
            store(t).start()
            return carried

        lax.fori_loop(0, count, one, 0)
        for t in range(max(0, count - 2), count):
            store(jnp.int32(t)).wait()

    gradients(mixed, d_att, dense_out, 0, width // 256)
    if fused:
        dense_outs.begin()
        tick()
        for d in range(line - 3, 0, -1):
            outs.step(d)

    def per_head(j, carried):
        grad_probs = dot_nt(d_mixed[j], values_of(j // groups))
        weights_now = probs[j].astype(f32)
        inner = jnp.sum(weights_now * grad_probs, -1, keepdims=True)
        grad = (weights_now * (grad_probs - inner) * scaling).astype(bf16)
        d_scores[lax.rem(j, groups)] = grad
        back_q = dot(grad, keys_of(j // groups))
        dq[:, pl.ds(pl.multiple_of(j * head, head), head)] = turn(back_q, cosine[...], -sine[...]).astype(bf16)
        return carried

    for h in range(kv_heads):
        lax.fori_loop(h * groups, (h + 1) * groups, per_head, 0)
        these = slice(h * groups, (h + 1) * groups)
        grad_keys = dot_tn(
            d_scores[...].reshape(groups * rows, keys_count), queries[these].reshape(groups * rows, head)
        )
        grad_values = dot_tn(
            probs[these].reshape(groups * rows, keys_count), d_mixed[these].reshape(groups * rows, head)
        )
        kv_part[:, :, h * head : (h + 1) * head] = grad_keys.astype(bf16).reshape(size, rows, head)
        at = kv_width + h * head
        kv_part[:, :, at : at + head] = grad_values.astype(bf16).reshape(size, rows, head)
        if h == 0 and fused:
            tick()
            outs.step(0)

    def give(i):
        there = lax.rem(c + size - i, size)
        return remote(kv_part.at[there], kv_other.at[i - 1], kv_send.at[i - 1], kv_recv.at[i - 1], there, e)

    for i in range(1, size):
        @pl.when(c - i >= 0)
        def _():
            give(i).start()

    tick()
    if fused and line > 2:
        dense_outs.step(line - 2)
    gradients(h1, dq, dense_qkv, 0, q_width // 256)
    tick()
    if fused:
        for d in range(line - 3, 0, -1):
            dense_outs.step(d)

    own = kv_part[c].astype(f32)
    dkv[...] = own
    for i in range(1, size):
        @pl.when(c + i < size)
        def _():
            give(i).wait_recv()
            dkv[...] += kv_other[i - 1].astype(f32)
    for j in range(kv_heads):
        at = slice(j * head, (j + 1) * head)
        dkv[:, at] = turn(dkv[:, at], cosine[...], -sine[...])
    dq[:, q_width:] = dkv[...].astype(bf16)
    dkv_low = dq.at[:, q_width:]
    gradients(h1, dkv_low, dense_qkv, q_width, 2 * kv_width // 256)
    loads[0].wait()

    def inputs(t, total):
        at = pl.ds(pl.multiple_of(t * 128, 128), 128)
        grad_h1 = dot_nt(dq[at, :], wqkv[...])
        normed, inverse = row_norm(tokens[at, :].astype(f32))
        total = total + jnp.sum(grad_h1 * normed, 0, keepdims=True)
        scaled = grad_h1 * gains[0:1, :]
        grad_tokens[at, :] = d_mid[at, :] + inverse * (
            scaled - normed * jnp.mean(scaled * normed, -1, keepdims=True)
        )
        return total

    gain_one = lax.fori_loop(0, rows // 128, inputs, jnp.zeros((1, width), f32))
    sub = lax.broadcasted_iota(jnp.int32, (128, width), 0)
    gain_rows = jnp.where(sub == experts, gain_one, jnp.where(sub == experts + 1, gain_two, 0.0))
    grad_small = (grad_small + gain_rows.T).astype(bf16).reshape(n, shard, 128)
    stage[0, :, :, 0:128] = grad_small
    small_store = pltpu.make_async_copy(
        stage.at[0, :, :, 0:128], dense_qkv.at[:, :, q_width + 2 * kv_width :], s_sem.at[0]
    )
    small_store.start()
    small_store.wait()
    tick()
    if fused:
        dense_qkvs.begin()

    def finish(t, carried):
        at = pl.ds(pl.multiple_of(t * 64, 64), 64)
        output[at, :] = (mid[at, :] + out_sum[at, :].astype(f32)).astype(bf16)
        return carried

    lax.fori_loop(0, rows // 64, finish, 0)
    if fused:
        tick()
        dense_outs.step(0)
        sharing_out.begin()
        for d in range(line - 2, -1, -1):
            tick()
            if d == 0:
                sharing_out.middle()
                tick()
            dense_qkvs.step(d)
        sharing_qkv.begin()
        tick()
        sharing_qkv.middle()
        while len(ticked) < experts_total.ticks:
            tick()
        for one in sums:
            one.end()
        sharing_out.end()
        sharing_qkv.end()
        experts_total.end()
    for i in range(1, size):
        @pl.when(c - i >= 0)
        def _():
            give(i).wait_send()


def backward(experts, shard, back_part, out_part, grads, early_first, tokens, mid, final, marks, small, gains, queries, keyval, mixed, lse,
             cosine, sine, qkv_full, out_full, collective_id):
    size, n = lax.axis_size("ctx"), lax.axis_size("exp")
    line = n // 2
    rows, width = tokens.shape
    heads, kv_heads, head = QUERY_HEADS, KEY_VALUE_HEADS, HEAD_WIDTH
    kv_both = 2 * kv_heads * head
    keys_count = size * rows
    f32, bf16 = jnp.float32, jnp.bfloat16
    dma = pltpu.SemaphoreType.DMA
    vmem = pl.BlockSpec(memory_space=pltpu.VMEM)
    shape = jax.ShapeDtypeStruct
    fused = planned(size, n, shard)
    out_width, qkv_width = width, qkv_full.shape[1] + small.shape[1]
    shapes = [
        shape((rows, width), bf16),
        shape((rows, width), f32),
        shape((n, shard, out_width), bf16),
        shape((n, shard, qkv_width), bf16),
    ]
    summing = []
    if fused:
        deep = grads.shape[0] // Totals.count
        shapes += [
            shape(grads.shape, bf16),
            shape((shard, out_width), bf16),
            shape((shard, qkv_width), bf16),
        ]
        shapes += Totals.landing(deep, grads.shape[1])
        for high, wide in ((rows, back_part.shape[2]), (rows, width), (shard, out_width), (shard, qkv_width)):
            shapes += Summing.landing(line, high, wide)
        widest = max(back_part.shape[2], width, out_width, qkv_width)
        summing = [
            pltpu.VMEM((2, rows, widest), bf16),
        ]
        for high, wide in ((rows, back_part.shape[2]), (rows, width), (shard, out_width), (shard, qkv_width)):
            summing += Summing.scratch(line, high, wide)
        summing += Totals.scratch(deep, grads.shape[1])
        summing += Sharing.scratch(size, shard, out_width) + Sharing.scratch(size, shard, qkv_width)
    else:
        back_part = lax.psum_scatter(back_part, "exp", scatter_dimension=0)
        out_part = lax.psum_scatter(out_part, "exp", scatter_dimension=0)
    found = pl.pallas_call(
        functools.partial(backward_kernel, size, line, heads, kv_heads, experts, fused),
        out_shape=tuple(shapes),
        in_specs=[ANY if fused else vmem] * 2 + [ANY] * 2 + [vmem] * 12 + [ANY] * 2,
        out_specs=(vmem, vmem) + (ANY,) * (len(shapes) - 2),
        scratch_shapes=summing
        + [
            pltpu.VMEM(qkv_full.shape, bf16),
            pltpu.VMEM(out_full.shape, bf16),
            pltpu.VMEM((heads, rows, keys_count), bf16),
            pltpu.VMEM((heads // kv_heads, rows, keys_count), bf16),
            pltpu.VMEM((heads, rows, head), bf16),
            pltpu.VMEM((rows, width), bf16),
            pltpu.VMEM((rows, width), f32),
            pltpu.VMEM((rows, width), bf16),
            pltpu.VMEM((rows, width), bf16),
            pltpu.VMEM((rows, heads * head + kv_both), bf16),
            pltpu.VMEM((rows, kv_both), f32),
            pltpu.VMEM((size, rows, kv_both), bf16),
            pltpu.VMEM((size - 1, rows, kv_both), bf16),
            pltpu.VMEM((2, n, shard, 256), bf16),
            dma((2,)),
            dma((size - 1,)),
            dma((size - 1,)),
            dma((2,)),
        ],
        compiler_params=pltpu.CompilerParams(
            collective_id=collective_id, has_side_effects=True, vmem_limit_bytes=62 << 20
        ),
        name="backward",
    )(back_part, out_part, grads, early_first, tokens, mid, final, marks, small, gains, queries, keyval, mixed, lse, cosine, sine,
      qkv_full, out_full)
    if fused:
        return found[:2] + found[4:7]
    dense_out, dense_qkv = (lax.psum_scatter(part, "exp", scatter_dimension=0) for part in found[2:4])
    return found[:2] + (lax.psum(grads, "ctx"), lax.psum(dense_out, "ctx"), lax.psum(dense_qkv, "ctx"))


def widen_kernel(total, dense_out, dense_qkv, gate, up, down, w_out, w_query, w_keyval, held, held_out, held_qkv, *refs):
    wide, wide_out, wide_query, wide_keyval, in_sem, out_sem, dense_in, dense_done = refs
    f32 = jnp.float32
    high = held.shape[1]
    blocks, slots = held.shape[0], wide.shape[0]
    per, tall = blocks // 3, gate.shape[1] // high

    def load(i):
        return pltpu.make_async_copy(total.at[pl.ds(i * high, high)], held.at[i], in_sem.at[i])

    def store(i):
        n, at = i // per, i % per
        if n < 2:
            target = (gate, up)[n].at[at // tall, pl.ds(at % tall * high, high)]
        else:
            target = down.at[at // tall, :, pl.ds(at % tall * high, high)]
        return pltpu.make_async_copy(wide.at[i % slots], target, out_sem.at[i % slots])

    small_in = [
        pltpu.make_async_copy(src, dst, dense_in.at[i])
        for i, (src, dst) in enumerate(((dense_out, held_out), (dense_qkv, held_qkv)))
    ]
    small_done = [
        pltpu.make_async_copy(src, dst, dense_done.at[i])
        for i, (src, dst) in enumerate(((wide_out, w_out), (wide_query, w_query), (wide_keyval, w_keyval)))
    ]
    load(0).start()
    for copy in small_in:
        copy.start()
    for i in range(1, blocks):
        load(i).start()
    for i in range(blocks):
        load(i).wait()
        if i >= slots:
            store(i - slots).wait()
        wide[i % slots] = held[i].astype(f32)
        store(i).start()
        if i == 0:
            for copy in small_in:
                copy.wait()
            split = w_query.shape[1]
            wide_out[...] = held_out[...].astype(f32)
            wide_query[...] = held_qkv[:, :split].astype(f32)
            wide_keyval[...] = held_qkv[:, split : split + w_keyval.shape[1]].astype(f32)
            for copy in small_done:
                copy.start()
    for i in range(max(0, blocks - slots), blocks):
        store(i).wait()
    for copy in small_done:
        copy.wait()


def widen(total, dense_out, dense_qkv, local, width, units, q_width, kv_both):
    f32 = jnp.float32
    blocks, slots = total.shape[0] // units, 4
    shard = dense_out.shape[0]
    shape = jax.ShapeDtypeStruct
    dma = pltpu.SemaphoreType.DMA
    dense = [(shard, width), (shard, q_width), (shard, kv_both)]
    return pl.pallas_call(
        widen_kernel,
        out_shape=(
            shape((local, width, units), f32),
            shape((local, width, units), f32),
            shape((local, units, width), f32),
            *(shape(one, f32) for one in dense),
        ),
        in_specs=[ANY] * 3,
        out_specs=(ANY,) * 6,
        scratch_shapes=[
            pltpu.VMEM((blocks, units, units), total.dtype),
            pltpu.VMEM(dense_out.shape, dense_out.dtype),
            pltpu.VMEM(dense_qkv.shape, dense_qkv.dtype),
            pltpu.VMEM((slots, units, units), f32),
            *(pltpu.VMEM(one, f32) for one in dense),
            dma((blocks,)),
            dma((slots,)),
            dma((2,)),
            dma((3,)),
        ],
        compiler_params=pltpu.CompilerParams(vmem_limit_bytes=56 << 20),
        name="widen",
    )(total, dense_out, dense_qkv)


def rope_tables(first_row, row_count, head_size):
    half_size = head_size // 2
    frequency = ROPE_BASE ** (-jnp.arange(half_size, dtype=jnp.float32) * (2.0 / head_size))
    places = (first_row + jnp.arange(row_count, dtype=jnp.int32)).astype(jnp.float32)
    angles = places[:, None] * frequency[None, :]
    cosine = jnp.cos(angles)
    sine = jnp.sin(angles)
    return (jnp.concatenate([cosine, cosine], 1), jnp.concatenate([-sine, sine], 1))


def ein(spec, a, b):
    return jnp.einsum(spec, a, b, preferred_element_type=jnp.float32)


def shards(
    tokens,
    routes,
    gain_attn,
    w_query,
    key_value_weight,
    w_out,
    gain_ffn,
    w_router,
    w_gate,
    w_up,
    w_down,
    cotangent,
):
    f32 = jnp.float32
    bf16 = jnp.bfloat16
    rows, width = tokens.shape[1:]
    ctx_size, exp_size = lax.axis_size("ctx"), lax.axis_size("exp")
    ctx_index, exp_index = lax.axis_index("ctx"), lax.axis_index("exp")
    local_experts = w_gate.shape[0]
    experts = local_experts * exp_size
    top = routes.shape[2]
    capacity = 2 * rows * top // experts
    shard_rows = w_query.shape[0]
    heads, kv_heads, head = QUERY_HEADS, KEY_VALUE_HEADS, HEAD_WIDTH
    groups = heads // kv_heads
    q_width, kv_width = heads * head, kv_heads * head
    scaling = 1.0 / math.sqrt(head)
    first_row = ctx_index * rows

    named_own = jnp.any(routes[0][:, :, None] == jnp.arange(128, dtype=jnp.int32), axis=1).astype(bf16)
    small = jnp.concatenate(
        [
            w_router,
            gain_attn[:, None],
            gain_ffn[:, None],
            jnp.zeros((shard_rows, 128 - experts - 2), bf16),
        ],
        1,
    )
    qkv_full, out_full, small_full, named, rows_all = gather_weights(
        (jnp.concatenate([w_query, key_value_weight], 1), w_out, small), named_own, cotangent[0], 1
    )

    cosine, sine = rope_tables(first_row, rows, head)
    hops = planned(ctx_size, exp_size, shard_rows)
    queries, keyval, mixed, lse, resid_mid, hidden_two, gains, rows_all = attend(
        hops, experts, tokens[0], small_full, cosine, sine, qkv_full, out_full, rows_all, 2
    )

    _, out_part, back_part, grads, *early_first = expert_pass(
        hops and exp_size > 6, hops, capacity, hidden_two, cotangent[0], rows_all, named, small_full, w_gate, w_up, w_down, 3
    )
    output, grad_input, grads, dense_out, dense_qkv = backward(
        experts, shard_rows, back_part, out_part, grads, early_first[-1], tokens[0], resid_mid, cotangent[0], named_own, small_full, gains,
        queries, keyval, mixed, lse, cosine, sine, qkv_full, out_full, 4
    )
    small_total = dense_qkv[:, q_width + 2 * kv_width :].astype(f32)
    grad_gate, grad_up, grad_down, grad_out, grad_query, grad_keyval = widen(
        grads, dense_out, dense_qkv, local_experts, width, w_gate.shape[2], q_width, 2 * kv_width
    )
    return (
        output[None],
        grad_input[None],
        small_total[:, experts],
        grad_query,
        grad_keyval,
        grad_out,
        small_total[:, experts + 1],
        small_total[:, :experts],
        grad_gate,
        grad_up,
        grad_down,
    )


def solution(mesh):
    rows, wide, deep = P("exp", "ctx", None), P("exp", None), P("exp", None, None)
    flat = P("exp")
    return jax.shard_map(
        shards,
        mesh=mesh,
        in_specs=(rows, rows, flat, wide, wide, wide, flat, wide, deep, deep, deep, rows),
        out_specs=(rows, rows, flat, wide, wide, wide, flat, wide, deep, deep, deep),
        check_vma=False,
    )
```

```python
import functools
import math

import jax
import jax.numpy as jnp
from jax import lax
from jax.experimental import pallas as pl
from jax.experimental.pallas import tpu as pltpu
from jax.sharding import PartitionSpec as P

MESH = pl.DeviceIdType.MESH
ANY = pl.BlockSpec(memory_space=pl.ANY)


def remote(src, dst, send, recv, ctx, exp):
    return pltpu.make_async_remote_copy(
        src_ref=src, dst_ref=dst, send_sem=send, recv_sem=recv, device_id=(ctx, exp), device_id_type=MESH
    )


def greet(pairs):
    barrier = pltpu.get_barrier_semaphore()
    count = 0
    for here, ctx, exp in pairs:
        if here is True:
            pl.semaphore_signal(barrier, inc=1, device_id=(ctx, exp), device_id_type=MESH)
            count = count + 1
        else:
            @pl.when(here)
            def _():
                pl.semaphore_signal(barrier, inc=1, device_id=(ctx, exp), device_id_type=MESH)
            count = count + here.astype(jnp.int32)
    pl.semaphore_wait(barrier, count)


QUERY_HEADS = 12
KEY_VALUE_HEADS = 2
HEAD_WIDTH = 128
EPS = 1e-06
NEG = -1e30
ROPE_BASE = 1000000.0


class Gathering:
    def __init__(self, line, own, out, sems, keep_own=True, window=None):
        self.line, self.keep_own = line, keep_own
        self.window = pl.ds(*window) if window is not None else pl.ds(0, out.shape[1])
        self.own, self.whole = own.at[self.window], out
        self.local_sem, self.z_send, self.z_recv, self.c_send, self.c_recv = sems
        self.c, self.e = lax.axis_index("ctx"), lax.axis_index("exp")
        self.p, self.k = self.e // 2, self.e % 2

    def block(self, q):
        return self.whole.at[2 * q + self.k, self.window]

    def along(self, q, src, to_right):
        there = self.e + 2 if to_right else self.e - 2
        way = 0 if to_right else 1
        return remote(src, self.block(q), self.z_send.at[way, q], self.z_recv.at[q], self.c, there)

    def across(self, q, src):
        there = self.e + 1 - 2 * self.k
        return remote(src, self.block(q), self.c_send.at[q], self.c_recv.at[q], self.c, there)

    def local(self):
        return pltpu.make_async_copy(self.own, self.whole.at[self.e, self.window], self.local_sem)

    def ends(self, d):
        for to_right in (True, False):
            q = self.p - d if to_right else self.p + d
            here = (q >= 0) if to_right else (q < self.line)
            further = (self.p < self.line - 1) if to_right else (self.p > 0)
            yield to_right, q, here, further

    def begin(self):
        for to_right, q, _, further in self.ends(0):
            @pl.when(further)
            def _():
                self.along(q, self.own, to_right).start()

        self.across(self.p, self.own).start()
        if self.keep_own:
            self.local().start()

    def pump(self, d, onward=True):
        for to_right, q, here, further in self.ends(d):
            @pl.when(here)
            def _():
                block = self.block(q)
                self.along(q, block, to_right).wait_recv()
                if onward:
                    @pl.when(further)
                    def _():
                        self.along(q, block, to_right).start()

                self.across(q, block).start()

    def forward(self, d):
        for to_right, q, here, further in self.ends(d):
            @pl.when(here & further)
            def _():
                self.along(q, self.block(q), to_right).start()

    def finish(self, sent, crossed):
        for d in crossed:
            for to_right, q, here, _ in self.ends(d):
                if d > 0 or to_right:
                    @pl.when(here)
                    def _():
                        self.across(q, self.own).wait()
        for d in sent:
            for to_right, q, here, further in self.ends(d):
                @pl.when(here & further)
                def _():
                    self.along(q, self.own, to_right).wait_send()

    def end(self, hops=None):
        last = self.line if hops is None else min(self.line, hops + 1)
        if self.keep_own:
            self.local().wait()
        self.finish(range(self.line if hops is None else last - 1), range(last))

    @staticmethod
    def scratch(line):
        dma = pltpu.SemaphoreType.DMA
        return [dma, dma((2, line)), dma((line,)), dma((line,)), dma((line,))]


def gather_kernel(line, own, out, *sems):
    c, e = lax.axis_index("ctx"), lax.axis_index("exp")
    greet([(e >= 2, c, e - 2), (e < 2 * line - 2, c, e + 2), (True, c, e + 1 - 2 * (e % 2))])
    gathering = Gathering(line, own, out, sems)
    gathering.begin()
    for d in range(1, line):
        gathering.pump(d)
    gathering.end()


def gather_rows(own, collective_id):
    n = lax.axis_size("exp")
    return pl.pallas_call(
        functools.partial(gather_kernel, n // 2),
        out_shape=jax.ShapeDtypeStruct((n,) + own.shape, own.dtype),
        in_specs=[ANY],
        out_specs=ANY,
        scratch_shapes=Gathering.scratch(n // 2),
        compiler_params=pltpu.CompilerParams(collective_id=collective_id, has_side_effects=True),
        name="gather_rows",
    )(own)


def add_rows(dst, a, b, rows):
    step = math.gcd(rows, 64)

    def body(i, carried):
        at = pl.ds(pl.multiple_of(i * step, step), step)
        dst[at, :] = a[at, :] + b[at, :]
        return carried

    lax.fori_loop(0, rows // step, body, 0)


class Summing:
    def __init__(self, line, part, cross, moving, acc, tmp, sems, early=None):
        self.line, self.part, self.cross, self.moving, self.early = line, part, cross, moving, early
        self.acc, self.tmp = acc, tmp
        self.own_sem, self.tmp_sem, self.c_send, self.c_recv, self.z_send, self.z_recv = sems
        self.c, self.e = lax.axis_index("ctx"), lax.axis_index("exp")
        self.p, self.k = self.e // 2, self.e % 2
        self.rows, self.width = part.shape[1:]

    def across(self, q):
        there = self.e + 1 - 2 * self.k
        return remote(
            self.part.at[2 * q + 1 - self.k], self.cross.at[q], self.c_send.at[q], self.c_recv.at[q], self.c, there
        )

    def own(self, q):
        return pltpu.make_async_copy(self.part.at[2 * q + self.k], self.acc.at[q], self.own_sem.at[q])

    def load(self, src, side):
        into = self.tmp.at[side, pl.ds(0, self.rows), pl.ds(0, self.width)]
        return pltpu.make_async_copy(src, into, self.tmp_sem.at[side])

    def add(self, q, side):
        add_rows(self.acc.at[q], self.acc.at[q], self.tmp.at[side, pl.ds(0, self.rows), pl.ds(0, self.width)], self.rows)

    def along(self, q, to_right):
        there = self.e + 2 if to_right else self.e - 2
        place = q if to_right else jnp.where(q == self.p - 1, self.line, q)
        return remote(self.acc.at[q], self.moving.at[place], self.z_send.at[q], self.z_recv.at[place], self.c, there)

    def arrived(self, place):
        return remote(self.acc.at[0], self.moving.at[place], self.z_send.at[0], self.z_recv.at[place], self.c, self.e)

    def ends(self, d):
        for to_right in (True, False):
            if d > 0 or to_right:
                q = self.p + d if to_right else self.p - d
                here = (q < self.line) if to_right else (q >= 0)
                behind = (self.p > 0) if to_right else (self.p < self.line - 1)
                if d == 1 and self.early is not None:
                    here = here & behind
                yield to_right, q, here, behind

    def begin(self):
        order = [(d, end) for d in range(self.line - 1, -1, -1) for end in self.ends(d)]
        for _, (_, q, here, _) in order:
            @pl.when(here)
            def _():
                self.across(q).start()
                self.own(q).start()
        for d, (to_right, q, here, behind) in order:
            side = 0 if to_right else 1

            @pl.when(here)
            def _():
                self.across(q).wait_recv()
                self.load(self.cross.at[q], side).start()
                self.own(q).wait()
                self.load(self.cross.at[q], side).wait()
                self.add(q, side)
                if d > 0:
                    @pl.when(jnp.logical_not(behind))
                    def _():
                        self.along(q, to_right).start()

    def step(self, d):
        if d > 0:
            for to_right, q, here, behind in self.ends(d):
                @pl.when(here & behind)
                def _():
                    self.arrived(q).wait_recv()
                    self.load(self.moving.at[q], 0 if to_right else 1).start()
            for to_right, q, here, behind in self.ends(d):
                @pl.when(here & behind)
                def _():
                    side = 0 if to_right else 1
                    self.load(self.moving.at[q], side).wait()
                    self.add(q, side)
                    self.along(q, to_right).start()
            return
        last = ((0, self.p, self.p > 0), (1, self.line, self.p < self.line - 1))
        for side, place, behind in last:
            if self.early is not None:
                from_end = (self.p == 1) if side == 0 else (self.p == self.line - 2)

                @pl.when(from_end)
                def _():
                    self.load(self.early, side).start()

                arrives = behind & jnp.logical_not(from_end)
            else:
                arrives = behind

            @pl.when(arrives)
            def _():
                self.arrived(place).wait_recv()
                self.load(self.moving.at[place], side).start()
        for side, place, behind in last:
            @pl.when(behind)
            def _():
                self.load(self.moving.at[place], side).wait()
                self.add(self.p, side)

    def result(self):
        return self.acc.at[self.p]

    def end(self):
        for d in range(self.line):
            for to_right, q, here, _ in self.ends(d):
                @pl.when(here)
                def _():
                    if d > 0:
                        self.along(q, to_right).wait_send()
                    self.across(q).wait_send()

    @staticmethod
    def scratch(line, rows, width):
        dma = pltpu.SemaphoreType.DMA
        return [
            pltpu.VMEM((line, rows, width), jnp.bfloat16),
            dma((line,)),
            dma((2,)),
            dma((line,)),
            dma((line,)),
            dma((line,)),
            dma((line + 1,)),
        ]

    @staticmethod
    def landing(line, rows, width):
        return [
            jax.ShapeDtypeStruct((line, rows, width), jnp.bfloat16),
            jax.ShapeDtypeStruct((line + 1, rows, width), jnp.bfloat16),
        ]


class Totals:
    ahead, lag, count, early = 4, 1, 12, 4

    def __init__(self, part, early_first, sends, recvs, total=None, first=None, second=None, buffers=None, sems=None):
        self.part, self.total, self.early_first, self.first, self.second = part, total, early_first, first, second
        self.sends, self.recvs = sends, recvs
        if buffers is not None:
            self.own, self.got, self.got_two = buffers
            self.load_sem, self.got_sem, self.store_sem = sems
            self.slots = self.own.shape[0]
        c, self.e = lax.axis_index("ctx"), lax.axis_index("exp")
        self.bits = (c % 2, c // 2)
        self.nbrs = (c + 1 - 2 * (c % 2), lax.rem(c + 2, 4))
        self.deep = part.shape[0] // self.count

    def axes(self, h):
        return (0, 1) if h == 0 else (1, 0)

    def rows(self, ref, t, h, kept_one, kept_two=None, mine_two=True):
        one, two = self.axes(h)
        quarter, eighth = self.deep // 4, self.deep // 8
        bit = self.bits[one] if kept_one else 1 - self.bits[one]
        start = t * self.deep + h * (self.deep // 2) + bit * quarter
        if kept_two is None:
            return ref.at[pl.ds(pl.multiple_of(start, 16), quarter), :]
        return ref.at[pl.ds(pl.multiple_of(start + self.bits[two] * eighth, 16), eighth), :]

    def piece(self, t, h, kept):
        eighth = self.deep // 8
        bit = self.bits[self.axes(h)[1]]
        start = (bit if kept else 1 - bit) * eighth
        return self.own.at[t % self.slots, h, pl.ds(pl.multiple_of(start, 16), eighth), :]

    def copy(self, stage, t, h):
        one, two = self.axes(h)
        if stage == 0:
            src, dst, there = self.rows(self.part, t, h, False), self.landed(t, h), one
        elif stage == 1:
            src, dst, there = self.piece(t, h, False), self.second.at[t, h], two
        elif stage == 2:
            src, dst, there = self.piece(t, h, True), self.rows(self.total, t, h, True, True), two
        else:
            src, dst, there = self.rows(self.total, t, h, True), self.rows(self.total, t, h, True), one
        return remote(src, dst, self.sends.at[stage, t, h], self.recvs.at[stage, t, h], self.nbrs[there], self.e)

    def landed(self, t, h):
        return self.early_first.at[t, h] if t < self.early else self.first.at[t - self.early, h]

    def start_early(self, t):
        for h in range(2):
            self.copy(0, t, h).start()

    def end_early(self):
        for t in range(self.early):
            for h in range(2):
                self.copy(0, t, h).wait()

    def load_own(self, t, h):
        return pltpu.make_async_copy(
            self.rows(self.part, t, h, True), self.own.at[t % self.slots, h], self.load_sem.at[t % 2, h]
        )

    def store(self, t, h):
        return pltpu.make_async_copy(
            self.piece(t, h, True), self.rows(self.total, t, h, True, True), self.store_sem.at[t % self.slots, h]
        )

    def begin(self):
        for t in range(self.early, min(self.early + self.ahead, self.count)):
            for h in range(2):
                self.copy(0, t, h).start()
        for h in range(2):
            self.load_own(0, h).start()

    @property
    def ticks(self):
        return self.count + 2 * self.lag

    def tick(self, t):
        count, lag = self.count, self.lag
        t_two, t_three = t - lag, t - 2 * lag
        loads = []
        if t < count:
            for h in range(2):
                if t >= self.early:
                    self.copy(0, t, h).wait_recv()
                came = pltpu.make_async_copy(self.landed(t, h), self.got.at[h], self.got_sem.at[0, h])
                came.start()
                loads.append(came)
            if t + self.early + self.ahead < count:
                for h in range(2):
                    self.copy(0, t + self.early + self.ahead, h).start()
        later = []
        if 0 <= t_two < count:
            for h in range(2):
                self.copy(1, t_two, h).wait_recv()
                came = pltpu.make_async_copy(self.second.at[t_two, h], self.got_two.at[h], self.got_sem.at[1, h])
                came.start()
                later.append(came)
        if t < count:
            for h in range(2):
                self.load_own(t, h).wait()
                loads[h].wait()
                mine = self.own.at[t % self.slots, h]
                add_rows(mine, mine, self.got.at[h], self.deep // 4)
                self.copy(1, t, h).start()
        if 0 <= t_two < count:
            for h in range(2):
                later[h].wait()
                mine = self.piece(t_two, h, True)
                add_rows(mine, mine, self.got_two.at[h], self.deep // 8)
                self.copy(2, t_two, h).start()
                self.store(t_two, h).start()
        if 0 <= t_three < count:
            for h in range(2):
                self.copy(2, t_three, h).wait_recv()
                self.store(t_three, h).wait()
                self.copy(3, t_three, h).start()
                self.copy(1, t_three, h).wait_send()
                self.copy(2, t_three, h).wait_send()
        if t + 1 < count:
            for h in range(2):
                self.load_own(t + 1, h).start()

    def end(self):
        for t in range(self.count):
            for h in range(2):
                if t >= self.early:
                    self.copy(0, t, h).wait_send()
                self.copy(3, t, h).wait()

    @staticmethod
    def early_scratch():
        dma = pltpu.SemaphoreType.DMA
        return [dma((1, Totals.early, 2)), dma((1, Totals.early, 2))]

    @staticmethod
    def early_landing(deep, width):
        return jax.ShapeDtypeStruct((Totals.early, 2, deep // 4, width), jnp.bfloat16)

    @staticmethod
    def scratch(deep, width):
        count = Totals.count
        dma = pltpu.SemaphoreType.DMA
        slots = 2 * Totals.lag + 1
        return [
            pltpu.VMEM((slots, 2, deep // 4, width), jnp.bfloat16),
            pltpu.VMEM((2, deep // 4, width), jnp.bfloat16),
            pltpu.VMEM((2, deep // 8, width), jnp.bfloat16),
            dma((4, count, 2)),
            dma((4, count, 2)),
            dma((2, 2)),
            dma((2, 2)),
            dma((slots, 2)),
        ]

    @staticmethod
    def landing(deep, width):
        return [
            jax.ShapeDtypeStruct((Totals.count - Totals.early, 2, deep // 4, width), jnp.bfloat16),
            jax.ShapeDtypeStruct((Totals.count, 2, deep // 8, width), jnp.bfloat16),
        ]


class Sharing:
    def __init__(self, part, total, landed, sems):
        self.part, self.total = part, total
        self.one, self.two = landed[:2], landed[2:]
        self.sends, self.recvs, self.store_sem = sems
        c, self.e = lax.axis_index("ctx"), lax.axis_index("exp")
        self.bits = (c % 2, c // 2)
        self.nbrs = (c + 1 - 2 * (c % 2), lax.rem(c + 2, 4))
        self.rows, self.width = part.shape

    @staticmethod
    def columns(width):
        first = width // 256 * 128
        return ((0, first), (first, width - first))

    def window(self, ref, h, kept_one, kept_two=None):
        one, two = (0, 1) if h == 0 else (1, 0)
        half, quarter = self.rows // 2, self.rows // 4
        start = (self.bits[one] if kept_one else 1 - self.bits[one]) * half
        count = half
        if kept_two is not None:
            start = start + (self.bits[two] if kept_two else 1 - self.bits[two]) * quarter
            count = quarter
        return ref.at[pl.ds(pl.multiple_of(start, 16), count), pl.ds(*self.columns(self.width)[h])]

    def copy(self, stage, h):
        one, two = (0, 1) if h == 0 else (1, 0)
        if stage == 0:
            src, dst, there = self.window(self.part, h, False), self.one[h], one
        elif stage == 1:
            src, dst, there = self.window(self.part, h, True, False), self.two[h], two
        elif stage == 2:
            src, dst, there = self.window(self.part, h, True, True), self.window(self.total, h, True, True), two
        else:
            src, dst, there = self.window(self.total, h, True), self.window(self.total, h, True), one
        return remote(src, dst, self.sends.at[stage, h], self.recvs.at[stage, h], self.nbrs[there], self.e)

    def store(self, h):
        return pltpu.make_async_copy(
            self.window(self.part, h, True, True), self.window(self.total, h, True, True), self.store_sem.at[h]
        )

    def begin(self):
        for h in range(2):
            self.copy(0, h).start()

    def second(self):
        for h in range(2):
            self.copy(0, h).wait_recv()
            kept = self.window(self.part, h, True)
            add_rows(kept, kept, self.one[h], self.rows // 2)
            self.copy(1, h).start()

    def third(self):
        for h in range(2):
            self.copy(1, h).wait_recv()
            kept = self.window(self.part, h, True, True)
            add_rows(kept, kept, self.two[h], self.rows // 4)
            self.copy(2, h).start()
            self.store(h).start()

    def fourth(self):
        for h in range(2):
            self.store(h).wait()
            self.copy(2, h).wait_recv()
            self.copy(3, h).start()

    def end(self):
        for h in range(2):
            for stage in range(3):
                self.copy(stage, h).wait_send()
            self.copy(3, h).wait()

    @staticmethod
    def scratch(rows, width):
        dma = pltpu.SemaphoreType.DMA
        wide = [count for _, count in Sharing.columns(width)]
        return [
            *(pltpu.VMEM((rows // 2, one), jnp.bfloat16) for one in wide),
            *(pltpu.VMEM((rows // 4, one), jnp.bfloat16) for one in wide),
            dma((4, 2)),
            dma((4, 2)),
            dma((2,)),
        ]


def weights_kernel(line, quarter, *refs):
    count = 3
    own, own_mask, own_block = refs[:count], refs[count], refs[count + 1]
    out, masks, blocks = refs[count + 2 : 2 * count + 2], refs[2 * count + 2], refs[2 * count + 3]
    held, refs = refs[2 * count + 4 : 3 * count + 4], refs[3 * count + 4 :]
    local_sem, own_send, own_recv, z_send, z_recv, xy_send, xy_recv, d_send, d_recv, c_send, c_recv = refs[:-10]
    c, e = lax.axis_index("ctx"), lax.axis_index("exp")
    p, k = e // 2, e % 2
    sibling = e + 1 - 2 * k
    rows = own[0].shape[0]
    nbr = (c + 1 - 2 * (c % 2), (c + 2) % 4)
    opposite = 3 - c
    greet(
        [
            (p > 0, c, e - 2),
            (p < line - 1, c, e + 2),
            (True, c, sibling),
            (True, nbr[0], e),
            (True, nbr[1], e),
        ]
    )

    def whole(a):
        return out[a].at[pl.ds(pl.multiple_of(e * rows, 16), rows), :]

    def piece(a, q, column):
        return out[a].at[pl.ds(pl.multiple_of((2 * q + k) * rows + column * quarter, 16), quarter), :]

    def own_piece(a):
        return own[a].at[pl.ds(pl.multiple_of(c * quarter, 16), quarter), :]

    def load(a):
        return pltpu.make_async_copy(own[a], held[a], local_sem.at[0, a])

    def local(a):
        return pltpu.make_async_copy(held[a], whole(a), local_sem.at[1, a])

    def own_across(a):
        return remote(own[a], whole(a), own_send.at[a], own_recv.at[a], c, sibling)

    def along(a, q, src, to_right):
        there = e + 2 if to_right else e - 2
        way = 0 if to_right else 1
        return remote(src, piece(a, q, c), z_send.at[way, q, a], z_recv.at[q, a], c, there)

    def beside(a, q, axis):
        return remote(piece(a, q, c), piece(a, q, c), xy_send.at[axis, q, a], xy_recv.at[axis, q, a], nbr[axis], e)

    def onward(a, q):
        came, goes = (0, 1) if a == 0 else (1, 0)
        block = piece(a, q, nbr[came])
        return remote(block, block, d_send.at[q, a], d_recv.at[q, a], nbr[goes], e)

    def across(a, q, j):
        column = (c, nbr[0], nbr[1], opposite)[j]
        block = piece(a, q, column)
        return remote(block, block, c_send.at[q, j, a], c_recv.at[q, j, a], c, sibling)

    arrays = range(count)
    marking = Gathering(line, own_mask, masks, refs[-10:-5])
    gathering = Gathering(line, own_block, blocks, refs[-5:], keep_own=False)
    marking.begin()
    for a in arrays:
        @pl.when(p < line - 1)
        def _():
            along(a, p, own_piece(a), True).start()

        @pl.when(p > 0)
        def _():
            along(a, p, own_piece(a), False).start()
    for a in arrays:
        own_across(a).start()
        load(a).start()
    for a in arrays:
        load(a).wait()
        local(a).start()

    def ends(d):
        for to_right in (True, False):
            q = p - d if to_right else p + d
            yield to_right, q, ((q >= 0) if to_right else (q < line))

    for d in range(1, line + 1):
        if d < line:
            for to_right, q, here in ends(d):
                further = (p < line - 1) if to_right else (p > 0)

                @pl.when(here)
                def _():
                    for a in arrays:
                        along(a, q, piece(a, q, c), to_right).wait_recv()

                        @pl.when(further)
                        def _():
                            along(a, q, piece(a, q, c), to_right).start()

                        beside(a, q, 0).start()
                        beside(a, q, 1).start()
                        across(a, q, 0).start()
        if d < line:
            marking.pump(d)
        if d == line - 1:
            gathering.begin()
        if d > 1:
            for to_right, q, here in ends(d - 1):
                @pl.when(here)
                def _():
                    for a in arrays:
                        came = 0 if a == 0 else 1
                        beside(a, q, came).wait_recv()
                        onward(a, q).start()
                        across(a, q, 1 + came).start()
                        beside(a, q, 1 - came).wait_recv()
                        across(a, q, 2 - came).start()
    for d in range(1, line):
        for to_right, q, here in ends(d):
            @pl.when(here)
            def _():
                for a in arrays:
                    onward(a, q).wait_recv()
                    across(a, q, 3).start()
    gathering.pump(1, onward=False)
    gathering.end(1)
    marking.end()
    for a in arrays:
        local(a).wait()
        own_across(a).wait()
    for d in range(0, line):
        for to_right, q, here in ends(d):
            further = (p < line - 1) if to_right else (p > 0)
            for a in arrays:
                @pl.when(here & further)
                def _():
                    along(a, q, piece(a, q, c), to_right).wait_send()
                if d > 0:
                    @pl.when(here)
                    def _():
                        beside(a, q, 0).wait_send()
                        beside(a, q, 1).wait_send()
                        onward(a, q).wait_send()
                        for j in range(4):
                            across(a, q, j).wait()


def planned(size, n, shard_rows):
    return size == 4 and n == 8 and (shard_rows // 4) % 16 == 0


def gather_weights(shards, mask, block, collective_id):
    n = lax.axis_size("exp")
    if not planned(lax.axis_size("ctx"), n, shards[0].shape[0]):
        whole = tuple(lax.all_gather(w, "exp", axis=0, tiled=True) for w in shards)
        return whole + (lax.all_gather(mask, "exp", axis=0), gather_rows(block, collective_id))
    line = n // 2
    count = len(shards)
    dma = pltpu.SemaphoreType.DMA
    return pl.pallas_call(
        functools.partial(weights_kernel, line, shards[0].shape[0] // 4),
        out_shape=tuple(jax.ShapeDtypeStruct((n * w.shape[0], w.shape[1]), w.dtype) for w in shards)
        + tuple(jax.ShapeDtypeStruct((n,) + w.shape, w.dtype) for w in (mask, block)),
        in_specs=[ANY] * (count + 2),
        out_specs=(ANY,) * (count + 2),
        scratch_shapes=[pltpu.VMEM(w.shape, w.dtype) for w in shards]
        + [
            dma((2, count)),
            dma((count,)),
            dma((count,)),
            dma((2, line, count)),
            dma((line, count)),
            dma((2, line, count)),
            dma((2, line, count)),
            dma((line, count)),
            dma((line, count)),
            dma((line, 4, count)),
            dma((line, 4, count)),
        ]
        + Gathering.scratch(line)
        + Gathering.scratch(line),
        compiler_params=pltpu.CompilerParams(
            collective_id=collective_id, has_side_effects=True, vmem_limit_bytes=62 << 20
        ),
        name="gather_weights",
    )(*shards, mask, block)


def dot(a, b):
    return lax.dot_general(a, b, (((1,), (0,)), ((), ())), preferred_element_type=jnp.float32)


def dot_nt(a, b):
    return lax.dot_general(a, b, (((1,), (1,)), ((), ())), preferred_element_type=jnp.float32)


def dot_tn(a, b):
    return lax.dot_general(a, b, (((0,), (0,)), ((), ())), preferred_element_type=jnp.float32)


def visit(p, line, i):
    both = jnp.minimum(p, line - 1 - p)
    d = jnp.where(i <= 2 * both, (i + 1) // 2, i - both)
    left = jnp.where(i <= 2 * both, i % 2 == 1, p > line - 1 - p)
    q = jnp.where(left, p - d, p + d)
    first = (i == 0) | (i > 2 * both) | (i % 2 == 1)
    return q, d, first


def expert_kernel(line, local, cap, hop, start, hidden, own_grads, grads_in, named, router, w_gate, w_up, w_down, *refs):
    hidden_all, out_part, back_part, grads, grads_all = refs[:5]
    if start:
        early_first, early_sums, refs = refs[5], refs[6:8], refs[:5] + refs[8:]
    wg, wu, wd, xs, ds, act, dg, du, es, h_buf, y_buf, out_stage, back_stage, in_stage, down_stage = refs[5:20]
    picks, xs_turned, act_turned, gate_kept, refs = *refs[20:24], refs[:20] + refs[24:]
    if start:
        crossed, refs = refs[20:22], refs[:20] + refs[22:]
        hop_sem, refs = refs[-1], refs[:-1]
    w_sem, own_sem, z_send, z_recv, c_send, c_recv, h_sem, y_sem, o_sem, b_sem, s_sem = refs[20:31]
    f32, bf16 = jnp.float32, jnp.bfloat16
    c, e = lax.axis_index("ctx"), lax.axis_index("exp")
    p, k = e // 2, e % 2
    sibling = e + 1 - 2 * k
    rows, width = hidden.shape
    hidden_units = wg.shape[2]
    slots = 2 * cap
    lanes = router.shape[1]

    loads = [
        pltpu.make_async_copy(src, dst, w_sem.at[i])
        for i, (src, dst) in enumerate(((w_gate, wg), (w_up, wu), (w_down, wd)))
    ]
    for copy in loads:
        copy.start()
    beside = [(True, c + 1 - 2 * (c % 2), e), (True, lax.rem(c + 2, 4), e)] if start else []
    greet([(p > 0, c, e - 2), (p < line - 1, c, e + 2), (True, c, sibling)] + beside)
    def along(q, src, to_right):
        there = e + 2 if to_right else e - 2
        return remote(src, hidden_all.at[2 * q + k], z_send.at[0 if to_right else 1, q], z_recv.at[q], c, there)

    def across(q, src):
        return remote(src, hidden_all.at[2 * q + k], c_send.at[q], c_recv.at[q], c, sibling)

    def load_hidden(q, slot):
        return pltpu.make_async_copy(hidden_all.at[pl.ds(2 * q, 2)], h_buf.at[slot], h_sem.at[slot])

    def load_grads(q, slot):
        return pltpu.make_async_copy(grads_all.at[pl.ds(2 * q, 2)], y_buf.at[slot], y_sem.at[slot])

    def load_own(buf, own, blocks, i):
        return [
            pltpu.make_async_copy(own, buf.at[0, k], own_sem.at[2 * i]),
            pltpu.make_async_copy(blocks.at[sibling], buf.at[0, 1 - k], own_sem.at[2 * i + 1]),
        ]

    def store_out(q, slot):
        return pltpu.make_async_copy(out_stage.at[slot], out_part.at[pl.ds(2 * q, 2)], o_sem.at[slot])

    def store_back(q, slot):
        return pltpu.make_async_copy(back_stage.at[slot], back_part.at[pl.ds(2 * q, 2)], b_sem.at[slot])

    @pl.when(p < line - 1)
    def _():
        along(p, hidden, True).start()

    @pl.when(p > 0)
    def _():
        along(p, hidden, False).start()

    across(p, hidden).start()
    if hop:
        hops = Gathering(line, grads_all.at[e], grads_all, refs[31:36], window=(rows // 2, rows // 2))
        hops.forward(2)
    for copy in load_own(y_buf, own_grads, grads_all, 0):
        copy.start()

    def pump(d):
        for to_right in (True, False):
            q = p - d if to_right else p + d
            here = (q >= 0) if to_right else (q < line)
            further = (p < line - 1) if to_right else (p > 0)

            @pl.when(here)
            def _():
                block = hidden_all.at[2 * q + k]
                along(q, block, to_right).wait_recv()

                @pl.when(further)
                def _():
                    along(q, block, to_right).start()

                across(q, block).start()

    for copy in loads:
        copy.wait()

    lane = lax.broadcasted_iota(jnp.int32, (local * cap, lanes), 1)
    expert_of_row = lax.broadcasted_iota(jnp.int32, (local * cap, lanes), 0) // cap

    def units_of(j, q):
        tile = 256
        rows_j = xs[j].reshape(slots, width)
        xs_turned[j, :, pl.ds(pl.multiple_of(q * slots, slots), slots)] = rows_j.T
        grads_j = ds[j, q].reshape(slots, width)

        def units(t, carried):
            at = pl.ds(pl.multiple_of(t * tile, tile), tile)
            gate_pre = dot(rows_j, wg[j, :, at])
            up_pre = dot(rows_j, wu[j, :, at])
            grad_act = dot_nt(grads_j, wd[j, at, :])
            sigmoid = 1.0 / (1.0 + jnp.exp(-gate_pre))
            silu = gate_pre * sigmoid
            hidden_low = (silu * up_pre).astype(bf16)
            act[j, :, at] = hidden_low
            act_turned[j, at, pl.ds(pl.multiple_of(q * slots, slots), slots)] = hidden_low.T
            dg[j, q, :, at] = (grad_act * up_pre * sigmoid * (1.0 + gate_pre * (1.0 - sigmoid))).astype(bf16)
            du[j, q, :, at] = (grad_act * silu).astype(bf16)
            return carried

        lax.fori_loop(0, hidden_units // tile, units, 0)

    def give_back(q, slot):
        wide = 512
        pick_pair = [picks[b] for b in range(2)]

        def outputs(t, sums):
            at = pl.ds(pl.multiple_of(t * wide, wide), wide)
            gated, back, new_sums = [], [], []
            for j in range(local):
                y = dot(act[j], wd[j, :, at])
                back_j = dot_nt(dg[j, q], wg[j, at, :]) + dot_nt(du[j, q], wu[j, at, :])
                new = []
                for b in range(2):
                    half = slice(b * cap, (b + 1) * cap)
                    y_b = y[half]
                    new.append(sums[j][b] + jnp.sum(y_b * es[j, b, :, at].astype(f32), -1, keepdims=True))
                    gated.append((gate_kept[b, j * cap : (j + 1) * cap, 0:1] * y_b).astype(bf16))
                    back.append(back_j[half].astype(bf16))
                new_sums.append(tuple(new))
            for b in range(2):
                mine = jnp.concatenate([gated[2 * j + b] for j in range(local)], 0)
                out_stage[slot, b, :, at] = dot_tn(pick_pair[b], mine).astype(bf16)
                mine = jnp.concatenate([back[2 * j + b] for j in range(local)], 0)
                back_stage[slot, b, :, at] = dot_tn(pick_pair[b], mine).astype(bf16)
            return tuple(new_sums)

        nothing = jnp.zeros((cap, 1), f32)
        sums = lax.fori_loop(
            0, width // wide, outputs, tuple((nothing, nothing) for _ in range(local))
        )
        for b in range(2):
            grad_gates = jnp.concatenate([sums[j][b] for j in range(local)], 0)
            coarse = grad_gates.astype(bf16).astype(f32)
            spot = e * local + expert_of_row
            spread = jnp.where(
                lane == spot, coarse, jnp.where(lane == spot + lanes // 2, grad_gates - coarse, 0.0)
            ).astype(bf16)
            back_stage[slot, b, :, width : width + lanes] = dot_tn(pick_pair[b], spread).astype(bf16)
        store_out(q, slot).start()
        store_back(q, slot).start()

    at_end = (p == 0) | (p == line - 1)

    def cross_over(n):
        stage = (back_stage, out_stage)[n]
        return remote(stage.at[1, 1 - k], crossed[n], hop_sem.at[n, 0], hop_sem.at[n, 1], c, sibling)

    def send_ahead(n):
        there = jnp.where(p == 0, e + 2, e - 2)
        return remote(crossed[n], early_sums[n], hop_sem.at[n, 2], hop_sem.at[n, 3], c, there)

    def one_chip(i, carried):
        q, d, first = visit(p, line, i)
        slot = i % 2

        across(q, hidden).wait_recv()

        @pl.when(i == 0)
        def _():
            own = load_own(h_buf, hidden, hidden_all, 1)
            for copy in own:
                copy.start()
            for copy in own + load_own(y_buf, own_grads, grads_all, 0):
                copy.wait()

        @pl.when(i > 0)
        def _():
            load_hidden(q, slot).start()

        if hop:
            @pl.when(d == line - 1)
            def _():
                hops.pump(line - 1, onward=False)
                hops.finish([], [line - 1])
                load_grads(q, slot).start()

        after, d_after, _ = visit(p, line, i + 1)

        @pl.when((i < line - 1) & (d_after < (line - 1 if hop else line)))
        def _():
            load_grads(after, 1 - slot).start()

        @pl.when(i > 0)
        def _():
            load_hidden(q, slot).wait()
            load_grads(q, slot).wait()

        @pl.when(i >= 2)
        def _():
            store_out(visit(p, line, i - 2)[0], slot).wait()
            store_back(visit(p, line, i - 2)[0], slot).wait()

        place = lax.broadcasted_iota(jnp.int32, (cap, rows), 0).astype(f32)
        sub = lax.broadcasted_iota(jnp.int32, (lanes, rows), 0)
        upper = lax.broadcasted_iota(jnp.int32, (rows, 2 * rows), 0)
        column = lax.broadcasted_iota(jnp.int32, (rows, 2 * rows), 1)
        ahead = jnp.where((upper < column) & (column < rows) | (upper + rows == column), 1.0, 0.0).astype(bf16)
        for b in range(2):
            marks = named[2 * q + b]
            counted = dot_tn(marks, ahead)
            slots_of = jnp.where(counted[:, rows:] > 0.5, counted[:, :rows], -1.0)
            for j in range(local):
                row = jnp.sum(jnp.where(sub == e * local + j, slots_of, 0.0), 0, keepdims=True)
                picks[b, j * cap : (j + 1) * cap] = jnp.where(place == row, 1.0, 0.0).astype(bf16)
            pick = picks[b]
            block = h_buf[slot, b]
            picked = dot(pick, block).astype(bf16)
            for j in range(local):
                xs[j, b] = picked[j * cap : (j + 1) * cap]
            logits = jnp.where(marks.astype(f32) > 0.5, dot(block, router[...]), NEG)
            raised = jnp.exp(logits - jnp.max(logits, -1, keepdims=True))
            gates = raised / jnp.sum(raised, -1, keepdims=True)
            coarse = gates.astype(bf16)
            fine = (gates - coarse.astype(f32)).astype(bf16)
            at_slots = dot(pick, coarse) + dot(pick, fine)
            gate_slot = jnp.sum(jnp.where(lane == e * local + expert_of_row, at_slots, 0.0), -1, keepdims=True)
            gate_kept[b] = jnp.broadcast_to(gate_slot, gate_kept.shape[1:])
            grad_rows = dot(pick, y_buf[slot, b])
            grad_pairs = (gate_slot * grad_rows).astype(bf16)
            grad_rows = grad_rows.astype(bf16)
            for j in range(local):
                es[j, b] = grad_rows[j * cap : (j + 1) * cap]
                ds[j, q, b] = grad_pairs[j * cap : (j + 1) * cap]

        units_of(0, q)

        @pl.when(i < line - 1)
        def _():
            for j in range(1, local):
                units_of(j, q)
            give_back(q, slot)

        @pl.when(first & (d + 1 < line))
        def _():
            pump(d + 1)

        if start:
            @pl.when(at_end & (i == 1))
            def _():
                for n in range(2):
                    cross_over(n).start()

            @pl.when(at_end & (i == 2))
            def _():
                for n, stage in enumerate((back_stage, out_stage)):
                    cross_over(n).wait()
                    add_rows(crossed[n], crossed[n], stage.at[1, k], rows)
                    send_ahead(n).start()

        return carried

    lax.fori_loop(0, line, one_chip, 0)

    deep = line * slots
    tile = 256
    tiles = hidden_units // tile

    def products(left, right, stage, first_row, count):
        high = stage.shape[1]

        def stores(t):
            row = first_row + lax.div(t, tiles) * high
            return pltpu.make_async_copy(
                stage.at[lax.rem(t, 2)],
                grads.at[
                    pl.ds(pl.multiple_of(row, 16), high),
                    pl.ds(pl.multiple_of(lax.rem(t, tiles) * tile, tile), tile),
                ],
                s_sem.at[lax.rem(t, 2)],
            )

        def one_tile(t, carried):
            @pl.when(t >= 2)
            def _():
                stores(t - 2).wait()

            stage[lax.rem(t, 2)] = dot(left[...], right(pl.ds(pl.multiple_of(t * tile, tile), tile))).astype(bf16)
            stores(t).start()
            return carried

        lax.fori_loop(0, count, one_tile, 0)
        for t in range(max(0, count - 2), count):
            stores(jnp.int32(t)).wait()

    totals = Totals(grads, early_first, *refs[-2:]) if start else None
    sent = 0

    def send_ready(rows_done):
        nonlocal sent
        while start and sent < totals.early and (sent + 1) * totals.deep <= rows_done:
            totals.start_early(sent)
            sent += 1

    last_chip = visit(p, line, jnp.int32(line - 1))[0]
    for i, source in enumerate((dg, du)):
        for j in range(local):
            if i == 0 and j > 0:
                units_of(j, last_chip)
            products(
                xs_turned.at[j],
                lambda at: source[j, :, :, at].reshape(deep, tile),
                in_stage, (i * local + j) * width, tiles,
            )
            send_ready((i * local + j + 1) * width)
    for j in range(local):
        products(
            act_turned.at[j],
            lambda at: ds[j, :, :, :, at].reshape(deep, tile),
            down_stage, 2 * local * width + j * width, width // tile,
        )

    give_back(last_chip, (line - 1) % 2)

    if start:
        totals.end_early()

        @pl.when(at_end)
        def _():
            for n in range(2):
                send_ahead(n).wait_send()

        @pl.when((p == 1) | (p == line - 2))
        def _():
            for n in range(2):
                send_ahead(n).wait_recv()

    if hop:
        hops.finish([2], [])
    for i in range(max(0, line - 2), line):
        q = visit(p, line, jnp.int32(i))[0]
        store_out(q, i % 2).wait()
        store_back(q, i % 2).wait()
    for d in range(line):
        for to_right in (True, False):
            if d == 0 and not to_right:
                continue
            q = p - d if to_right else p + d
            here = (q >= 0) if to_right else (q < line)

            @pl.when(here)
            def _():
                across(q, hidden).wait_send()
    for d in range(line):
        for to_right in (True, False):
            q = p - d if to_right else p + d
            here = (q >= 0) if to_right else (q < line)
            further = (p < line - 1) if to_right else (p > 0)

            @pl.when(here & further)
            def _():
                along(q, hidden, to_right).wait_send()


def expert_pass(hop, start, cap, hidden, own_grads, grads_all, named, router, w_gate, w_up, w_down, collective_id):
    n = lax.axis_size("exp")
    line = n // 2
    rows, width = hidden.shape
    local, _, units = w_gate.shape
    bf16 = jnp.bfloat16
    lanes = router.shape[1]
    dma = pltpu.SemaphoreType.DMA
    vmem = pl.BlockSpec(memory_space=pltpu.VMEM)
    early = (
        Totals.early_landing(3 * local * width // Totals.count, units),
        jax.ShapeDtypeStruct((rows, width + lanes), bf16),
        jax.ShapeDtypeStruct((rows, width), bf16),
    )
    return pl.pallas_call(
        functools.partial(expert_kernel, line, local, cap, hop, start),
        out_shape=(
            jax.ShapeDtypeStruct((n, rows, width), bf16),
            jax.ShapeDtypeStruct((n, rows, width), bf16),
            jax.ShapeDtypeStruct((n, rows, width + lanes), bf16),
            jax.ShapeDtypeStruct((3 * local * width, units), bf16),
            jax.ShapeDtypeStruct(grads_all.shape, bf16),
        )
        + (early if start else ()),
        in_specs=[ANY, ANY, ANY, vmem, vmem, ANY, ANY, ANY],
        out_specs=(ANY,) * (8 if start else 5),
        input_output_aliases={2: 4},
        scratch_shapes=[
            pltpu.VMEM((local, width, units), bf16),
            pltpu.VMEM((local, width, units), bf16),
            pltpu.VMEM((local, units, width), bf16),
            pltpu.VMEM((local, 2, cap, width), bf16),
            pltpu.VMEM((local, line, 2, cap, width), bf16),
            pltpu.VMEM((local, 2 * cap, units), bf16),
            pltpu.VMEM((local, line, 2 * cap, units), bf16),
            pltpu.VMEM((local, line, 2 * cap, units), bf16),
            pltpu.VMEM((local, 2, cap, width), bf16),
            pltpu.VMEM((2, 2, rows, width), bf16),
            pltpu.VMEM((2, 2, rows, width), bf16),
            pltpu.VMEM((2, 2, rows, width), bf16),
            pltpu.VMEM((2, 2, rows, width + lanes), bf16),
            pltpu.VMEM((2, width, 256), bf16),
            pltpu.VMEM((2, units, 256), bf16),
            pltpu.VMEM((2, local * cap, rows), bf16),
            pltpu.VMEM((local, width, n * cap), bf16),
            pltpu.VMEM((local, units, n * cap), bf16),
            pltpu.VMEM((2, local * cap, 128), jnp.float32),
        ]
        + ([pltpu.VMEM(one.shape, bf16) for one in early[1:]] if start else [])
        + [
            dma((3,)),
            dma((4,)),
            dma((2, line)),
            dma((line,)),
            dma((line,)),
            dma((line,)),
            dma((2,)),
            dma((2,)),
            dma((2,)),
            dma((2,)),
            dma((2,)),
        ]
        + (Gathering.scratch(line) if hop else [])
        + (Totals.early_scratch() + [dma((2, 4))] if start else []),
        compiler_params=pltpu.CompilerParams(
            collective_id=collective_id, has_side_effects=True, vmem_limit_bytes=62 << 20
        ),
        name="expert_pass",
    )(hidden, own_grads, grads_all, named, router, w_gate, w_up, w_down)


def turn(block, cosine, signed_sine):
    return block * cosine + pltpu.roll(block, block.shape[1] // 2, 1) * signed_sine


def row_norm(block):
    inverse = lax.rsqrt(jnp.mean(block * block, -1, keepdims=True) + EPS)
    return block * inverse, inverse


def attend_kernel(size, line, hop, experts, heads, kv_heads, tokens, small, cosine, sine, qkv_hbm, out_hbm, rows_in, *refs):
    targets, rows_all = refs[:7], refs[7]
    held, refs = refs[8:15], refs[15:]
    queries, keyval, mixed, lse, mid, hidden, gains = held
    wqkv, wout, h1, w_sem, send, recv, o_sem = refs[:7]
    f32, bf16 = jnp.float32, jnp.bfloat16
    c, e = lax.axis_index("ctx"), lax.axis_index("exp")
    rows, width = tokens.shape
    head = HEAD_WIDTH
    groups = heads // kv_heads
    q_width, kv_width = heads * head, kv_heads * head
    loads = [
        pltpu.make_async_copy(qkv_hbm, wqkv, w_sem.at[0]),
        pltpu.make_async_copy(out_hbm, wout, w_sem.at[1]),
    ]
    for copy in loads:
        copy.start()
    others = [lax.rem(c + i, size) for i in range(1, size)]
    column = [(e >= 2, c, e - 2), (e < 2 * line - 2, c, e + 2), (True, c, e + 1 - 2 * (e % 2))]
    greet((column if hop else []) + [(True, there, e) for there in others])
    if hop:
        half = rows // 2
        early, late = (
            Gathering(line, rows_all.at[e], rows_all, refs[7 + 5 * i : 12 + 5 * i], window=(i * half, half)) for i in range(2)
        )
        early.forward(1)
        late.forward(1)

    def leave(i):
        return pltpu.make_async_copy(held[i], targets[i], o_sem.at[i])

    turned = small[...].astype(f32).T
    gains[...] = turned[experts : experts + 8]
    leave(6).start()

    def step(t, carried):
        at = pl.ds(pl.multiple_of(t * 64, 64), 64)
        normed, _ = row_norm(tokens[at, :].astype(f32))
        h1[at, :] = (normed * gains[0:1, :]).astype(bf16)
        return carried

    lax.fori_loop(0, rows // 64, step, 0)
    loads[0].wait()
    kv = dot(h1[...], wqkv[:, q_width:])
    for j in range(kv_heads):
        at = slice(j * head, (j + 1) * head)
        keyval[c, :, at] = turn(kv[:, at], cosine[...], sine[...]).astype(bf16)
    keyval[c, :, kv_width:] = kv[:, kv_width:].astype(bf16)

    def give(i):
        return remote(keyval.at[c], keyval.at[c], send.at[i - 1], recv.at[i - 1], others[i - 1], e)

    for i in range(1, size):
        @pl.when(c + i < size)
        def _():
            give(i).start()

    for j in range(1, size):
        @pl.when(j > c)
        def _():
            keyval[j] = jnp.zeros((rows, 2 * kv_width), bf16)

    pair = 2 * head

    def project(t, carried):
        at = pl.ds(pl.multiple_of(t * pair, pair), pair)
        q = dot(h1[...], wqkv[:, at])
        for j in range(2):
            queries[2 * t + j] = turn(q[:, j * head : (j + 1) * head], cosine[...], sine[...]).astype(bf16)
        return carried

    lax.fori_loop(0, heads // 2, project, 0)
    leave(0).start()
    if hop:
        early.pump(2)
    for i in range(1, size):
        @pl.when(c - i >= 0)
        def _():
            give(i).wait_recv()
    leave(1).start()

    keys_count = size * rows
    scaling = 1.0 / math.sqrt(head)
    lane = lax.broadcasted_iota(jnp.int32, (rows, 128), 1)

    def one_head(j):
        h = j // groups
        keys = keyval[:, :, pl.ds(pl.multiple_of(h * head, head), head)].reshape(keys_count, head)
        values = keyval[:, :, pl.ds(pl.multiple_of(kv_width + h * head, head), head)].reshape(keys_count, head)
        place = lax.broadcasted_iota(jnp.int32, (rows, keys_count), 1)
        row = c * rows + lax.broadcasted_iota(jnp.int32, (rows, keys_count), 0)
        scores = jnp.where(place <= row, dot_nt(queries[j], keys) * scaling, NEG)
        peak = jnp.max(scores, -1, keepdims=True)
        raised = jnp.exp(scores - peak)
        total = jnp.sum(raised, -1, keepdims=True)
        probs = (raised * (1.0 / total)).astype(bf16)
        return dot(probs, values), peak + jnp.log(total)

    def two_heads(t, stats):
        found = [one_head(2 * t + i) for i in range(2)]
        mixed[:, pl.ds(pl.multiple_of(t * pair, pair), pair)] = jnp.concatenate(
            [block for block, _ in found], 1
        ).astype(bf16)
        for i, (_, value) in enumerate(found):
            stats = jnp.where(lane == 2 * t + i, value, stats)
        return stats

    lse[...] = lax.fori_loop(0, heads // 2, two_heads, jnp.zeros((rows, 128), f32))
    leave(2).start()
    leave(3).start()
    if hop:
        late.pump(2, onward=False)
    loads[1].wait()

    def outward(t, carried):
        at = pl.ds(pl.multiple_of(t * 256, 256), 256)
        mid[:, at] = tokens[:, at].astype(f32) + dot(mixed[...], wout[:, at])
        return carried

    lax.fori_loop(0, width // 256, outward, 0)
    leave(4).start()

    def last(t, carried):
        at = pl.ds(pl.multiple_of(t * 64, 64), 64)
        normed, _ = row_norm(mid[at, :])
        hidden[at, :] = (normed * gains[1:2, :]).astype(bf16)
        return carried

    lax.fori_loop(0, rows // 64, last, 0)
    leave(5).start()
    if hop:
        early.pump(3, onward=False)
        early.finish([1, 2], [2, 3])
        late.finish([1], [2])
    for i in range(7):
        leave(i).wait()
    for i in range(1, size):
        @pl.when(c + i < size)
        def _():
            give(i).wait_send()


def attend(hop, experts, tokens, small, cosine, sine, qkv_full, out_full, rows_all, collective_id):
    size, line = lax.axis_size("ctx"), lax.axis_size("exp") // 2
    rows, width = tokens.shape
    f32, bf16 = jnp.float32, jnp.bfloat16
    dma = pltpu.SemaphoreType.DMA
    vmem = pl.BlockSpec(memory_space=pltpu.VMEM)
    shape = jax.ShapeDtypeStruct
    made = (
        shape((QUERY_HEADS, rows, HEAD_WIDTH), bf16),
        shape((size, rows, 2 * KEY_VALUE_HEADS * HEAD_WIDTH), bf16),
        shape((rows, QUERY_HEADS * HEAD_WIDTH), bf16),
        shape((rows, 128), f32),
        shape((rows, width), f32),
        shape((rows, width), bf16),
        shape((8, width), f32),
    )
    return pl.pallas_call(
        functools.partial(attend_kernel, size, line, hop, experts, QUERY_HEADS, KEY_VALUE_HEADS),
        out_shape=made + (shape(rows_all.shape, bf16),),
        in_specs=[vmem] * 4 + [ANY] * 3,
        out_specs=(ANY,) * 8,
        input_output_aliases={6: 7},
        scratch_shapes=[pltpu.VMEM(one.shape, one.dtype) for one in made]
        + [
            pltpu.VMEM(qkv_full.shape, bf16),
            pltpu.VMEM(out_full.shape, bf16),
            pltpu.VMEM((rows, width), bf16),
            dma((2,)),
            dma((size - 1,)),
            dma((size - 1,)),
            dma((7,)),
        ]
        + (Gathering.scratch(line) * 2 if hop else []),
        compiler_params=pltpu.CompilerParams(
            collective_id=collective_id, has_side_effects=True, vmem_limit_bytes=62 << 20
        ),
        name="attend",
    )(tokens, small, cosine, sine, qkv_full, out_full, rows_all)


def halves(values):
    coarse = values.astype(jnp.bfloat16)
    return coarse, (values - coarse.astype(jnp.float32)).astype(jnp.bfloat16)


def backward_kernel(size, line, heads, kv_heads, experts, fused, *refs):
    back_part, out_part, grads, early_first, early_back, early_out, tokens, mid, final, marks, small, gains = refs[:12]
    queries, keyval, mixed, lse, cosine, sine, qkv_hbm, out_hbm, output, grad_tokens = refs[12:22]
    (dense_out, dense_q, dense_kv), refs = refs[22:25], refs[25:]
    if fused:
        totals, total_out, total_q, total_kv, land_one, land_two = refs[:6]
        landing, refs = refs[6:16], refs[16:]
        tmp = refs[0]
        sum_refs, refs = [refs[1 + 7 * i : 8 + 7 * i] for i in range(5)], refs[36:]
        total_scratch, refs = refs[:8], refs[8:]
        share_out, share_q, share_kv, refs = refs[:7], refs[7:14], refs[14:21], refs[21:]
    else:
        came, out_sum = back_part, out_part
    wqkv, wout, probs, d_scores, d_mixed, d_att, d_mid, h1, h2, dq, dkv, kv_part, kv_other, stage = refs[:14]
    w_sem, kv_send, kv_recv, s_sem = refs[14:]
    f32, bf16 = jnp.float32, jnp.bfloat16
    c, e = lax.axis_index("ctx"), lax.axis_index("exp")
    p, k = e // 2, e % 2
    rows, width = tokens.shape
    head = HEAD_WIDTH
    groups = heads // kv_heads
    q_width, kv_width = heads * head, kv_heads * head
    scaling = 1.0 / math.sqrt(head)
    keys_count = size * rows
    n = 2 * line
    shard = dense_out.shape[1]

    loads = [
        pltpu.make_async_copy(qkv_hbm, wqkv, w_sem.at[0]),
        pltpu.make_async_copy(out_hbm, wout, w_sem.at[1]),
    ]
    others = [lax.rem(c + i, size) for i in range(1, size)]
    column = [(p > 0, c, e - 2), (p < line - 1, c, e + 2), (True, c, e + 1 - 2 * k)]
    greet((column if fused else []) + [(True, there, e) for there in others])
    ticked = []

    def tick():
        if fused and len(ticked) < experts_total.ticks:
            experts_total.tick(len(ticked))
            ticked.append(1)

    if fused:
        experts_total = Totals(
            grads, early_first, *total_scratch[3:5], totals, land_one, land_two, total_scratch[:3], total_scratch[5:]
        )
        experts_total.begin()
        sums = [
            Summing(
                line, part, landing[2 * i], landing[2 * i + 1], sum_refs[i][0], tmp, sum_refs[i][1:],
                (early_back, early_out, None, None, None)[i],
            )
            for i, part in enumerate((back_part, out_part, dense_out, dense_q, dense_kv))
        ]
        back, outs, dense_outs, dense_qs, dense_kvs = sums
        came, out_sum = back.result(), outs.result()
        sharing_out = Sharing(dense_outs.result(), total_out, share_out[:4], share_out[4:])
        sharing_q = Sharing(dense_qs.result(), total_q, share_q[:4], share_q[4:])
        sharing_kv = Sharing(dense_kvs.result(), total_kv, share_kv[:4], share_kv[4:])
        back.begin()
    for copy in loads:
        copy.start()

    lane = lax.broadcasted_iota(jnp.int32, (rows, 128), 1)

    def keys_of(h):
        return keyval[:, :, pl.ds(pl.multiple_of(h * head, head), head)].reshape(keys_count, head)

    def values_of(h):
        return keyval[:, :, pl.ds(pl.multiple_of(kv_width + h * head, head), head)].reshape(keys_count, head)

    def again(j, carried):
        place = lax.broadcasted_iota(jnp.int32, (rows, keys_count), 1)
        row = c * rows + lax.broadcasted_iota(jnp.int32, (rows, keys_count), 0)
        scores = dot_nt(queries[j], keys_of(j // groups)) * scaling
        level = jnp.sum(jnp.where(lane == j, lse[...], 0.0), -1, keepdims=True)
        probs[j] = jnp.exp(jnp.where(place <= row, scores - level, NEG)).astype(bf16)
        return carried

    def norms(t, carried):
        at = pl.ds(pl.multiple_of(t * 64, 64), 64)
        normed, _ = row_norm(mid[at, :])
        h2[at, :] = (normed * gains[1:2, :]).astype(bf16)
        normed, _ = row_norm(tokens[at, :].astype(f32))
        h1[at, :] = (normed * gains[0:1, :]).astype(bf16)
        return carried

    bounds = [heads * i // max(1, line - 1) for i in range(line)]
    for i, d in enumerate(range(line - 1, 0, -1)):
        if fused and i > 0:
            back.step(d)
        if i == 0:
            lax.fori_loop(0, rows // 64, norms, 0)
        lax.fori_loop(bounds[i], bounds[i + 1], again, 0)
        tick()
        if fused and d == 2:
            outs.begin()
    if fused:
        back.step(0)
        tick()

    logits = jnp.where(marks[...].astype(f32) > 0.5, dot(h2[...], small[...]), NEG)
    raised = jnp.exp(logits - jnp.max(logits, -1, keepdims=True))
    gates = raised / jnp.sum(raised, -1, keepdims=True)
    extra = came[:, width:].astype(f32)
    grad_gates = extra + pltpu.roll(extra, extra.shape[1] // 2, 1)
    grad_logits = gates * (grad_gates - jnp.sum(gates * grad_gates, -1, keepdims=True))
    logits_hi, logits_lo = halves(grad_logits)
    grad_small = dot_tn(h2[...], logits_hi) + dot_tn(h2[...], logits_lo)

    def second_norm(t, total):
        at = pl.ds(pl.multiple_of(t * 32, 32), 32)
        normed, inverse = row_norm(mid[at, :])
        low, high = halves(grad_logits_ref[at, :])
        grad_h2 = came[at, :width].astype(f32) + dot_nt(low, small[...]) + dot_nt(high, small[...])
        total = total + jnp.sum(grad_h2 * normed, 0, keepdims=True)
        scaled = grad_h2 * gains[1:2, :]
        grad = final[at, :].astype(f32) + inverse * (scaled - normed * jnp.mean(scaled * normed, -1, keepdims=True))
        d_mid[at, :] = grad
        d_att[at, :] = grad.astype(bf16)
        return total

    grad_logits_ref = dkv.at[:, 0:128]
    dkv[:, 0:128] = grad_logits
    gain_two = lax.fori_loop(0, rows // 32, second_norm, jnp.zeros((1, width), f32))

    loads[1].wait()

    def mixing(t, carried):
        at = pl.ds(pl.multiple_of(t * 256, 256), 256)
        block = dot_nt(d_att[...], wout[at, :]).astype(bf16)
        for i in range(2):
            d_mixed[2 * t + i] = block[:, i * head : (i + 1) * head]
        return carried

    lax.fori_loop(0, q_width // 256, mixing, 0)
    if fused and line > 2:
        outs.step(line - 2)
    tick()

    def gradients(left, right, dense, column, count):
        def store(t):
            return pltpu.make_async_copy(
                stage.at[lax.rem(t, 2)],
                dense.at[:, :, pl.ds(pl.multiple_of(column + t * 256, 128), 256)],
                s_sem.at[lax.rem(t, 2)],
            )

        def one(t, carried):
            @pl.when(t >= 2)
            def _():
                store(t - 2).wait()

            product = dot_tn(left[...], right[:, pl.ds(pl.multiple_of(t * 256, 256), 256)])
            stage[lax.rem(t, 2)] = product.astype(bf16).reshape(n, shard, 256)
            store(t).start()
            return carried

        lax.fori_loop(0, count, one, 0)
        for t in range(max(0, count - 2), count):
            store(jnp.int32(t)).wait()

    gradients(mixed, d_att, dense_out, 0, width // 256)
    if fused:
        dense_outs.begin()
        tick()
        for d in range(line - 3, 0, -1):
            outs.step(d)

    def per_head(j, carried):
        grad_probs = dot_nt(d_mixed[j], values_of(j // groups))
        weights_now = probs[j].astype(f32)
        inner = jnp.sum(weights_now * grad_probs, -1, keepdims=True)
        grad = (weights_now * (grad_probs - inner) * scaling).astype(bf16)
        d_scores[lax.rem(j, groups)] = grad
        back_q = dot(grad, keys_of(j // groups))
        dq[:, pl.ds(pl.multiple_of(j * head, head), head)] = turn(back_q, cosine[...], -sine[...]).astype(bf16)
        return carried

    for h in range(kv_heads):
        lax.fori_loop(h * groups, (h + 1) * groups, per_head, 0)
        these = slice(h * groups, (h + 1) * groups)
        grad_keys = dot_tn(
            d_scores[...].reshape(groups * rows, keys_count), queries[these].reshape(groups * rows, head)
        )
        grad_values = dot_tn(
            probs[these].reshape(groups * rows, keys_count), d_mixed[these].reshape(groups * rows, head)
        )
        kv_part[:, :, h * head : (h + 1) * head] = grad_keys.astype(bf16).reshape(size, rows, head)
        at = kv_width + h * head
        kv_part[:, :, at : at + head] = grad_values.astype(bf16).reshape(size, rows, head)
        if h == 0 and fused:
            tick()
            outs.step(0)

    def give(i):
        there = lax.rem(c + size - i, size)
        return remote(kv_part.at[there], kv_other.at[i - 1], kv_send.at[i - 1], kv_recv.at[i - 1], there, e)

    for i in range(1, size):
        @pl.when(c - i >= 0)
        def _():
            give(i).start()

    tick()
    if fused and line > 2:
        dense_outs.step(line - 2)
    gradients(h1, dq, dense_q, 0, q_width // 256)
    if fused:
        dense_qs.begin()
    tick()

    own = kv_part[c].astype(f32)
    dkv[...] = own
    for i in range(1, size):
        @pl.when(c + i < size)
        def _():
            give(i).wait_recv()
            dkv[...] += kv_other[i - 1].astype(f32)
    for j in range(kv_heads):
        at = slice(j * head, (j + 1) * head)
        dkv[:, at] = turn(dkv[:, at], cosine[...], -sine[...])
    dq[:, q_width:] = dkv[...].astype(bf16)
    dkv_low = dq.at[:, q_width:]
    gradients(h1, dkv_low, dense_kv, 0, 2 * kv_width // 256)
    if fused:
        for d in range(line - 3, 0, -1):
            dense_outs.step(d)
    loads[0].wait()

    def inputs(t, total):
        at = pl.ds(pl.multiple_of(t * 128, 128), 128)
        grad_h1 = dot_nt(dq[at, :], wqkv[...])
        normed, inverse = row_norm(tokens[at, :].astype(f32))
        total = total + jnp.sum(grad_h1 * normed, 0, keepdims=True)
        scaled = grad_h1 * gains[0:1, :]
        grad_tokens[at, :] = d_mid[at, :] + inverse * (
            scaled - normed * jnp.mean(scaled * normed, -1, keepdims=True)
        )
        return total

    gain_one = lax.fori_loop(0, rows // 128, inputs, jnp.zeros((1, width), f32))
    sub = lax.broadcasted_iota(jnp.int32, (128, width), 0)
    gain_rows = jnp.where(sub == experts, gain_one, jnp.where(sub == experts + 1, gain_two, 0.0))
    grad_small = (grad_small + gain_rows.T).astype(bf16).reshape(n, shard, 128)
    stage[0, :, :, 0:128] = grad_small
    small_store = pltpu.make_async_copy(
        stage.at[0, :, :, 0:128], dense_kv.at[:, :, 2 * kv_width :], s_sem.at[0]
    )
    small_store.start()
    small_store.wait()
    tick()
    if fused:
        dense_kvs.begin()

    def finish(t, carried):
        at = pl.ds(pl.multiple_of(t * 64, 64), 64)
        output[at, :] = (mid[at, :] + out_sum[at, :].astype(f32)).astype(bf16)
        return carried

    lax.fori_loop(0, rows // 64, finish, 0)
    if fused:
        dense_outs.step(0)
        sharing_out.begin()
        tick()
        for d in range(line - 2, -1, -1):
            dense_qs.step(d)
            if d == 0:
                sharing_q.begin()
            tick()
            if d == line - 2:
                sharing_out.second()
            dense_kvs.step(d)
            if d == line - 3:
                sharing_out.third()
        sharing_kv.begin()
        sharing_q.second()
        sharing_out.fourth()
        tick()
        sharing_kv.second()
        sharing_q.third()
        while len(ticked) < experts_total.ticks:
            tick()
        sharing_kv.third()
        sharing_q.fourth()
        sharing_kv.fourth()
        for one in sums:
            one.end()
        sharing_out.end()
        sharing_q.end()
        sharing_kv.end()
        experts_total.end()
    for i in range(1, size):
        @pl.when(c - i >= 0)
        def _():
            give(i).wait_send()


def backward(experts, shard, back_part, out_part, grads, early, tokens, mid, final, marks, small, gains, queries, keyval, mixed, lse,
             cosine, sine, qkv_full, out_full, collective_id):
    size, n = lax.axis_size("ctx"), lax.axis_size("exp")
    line = n // 2
    rows, width = tokens.shape
    heads, kv_heads, head = QUERY_HEADS, KEY_VALUE_HEADS, HEAD_WIDTH
    kv_both = 2 * kv_heads * head
    keys_count = size * rows
    f32, bf16 = jnp.float32, jnp.bfloat16
    dma = pltpu.SemaphoreType.DMA
    vmem = pl.BlockSpec(memory_space=pltpu.VMEM)
    shape = jax.ShapeDtypeStruct
    fused = planned(size, n, shard)
    dense_widths = (width, heads * head, kv_both + small.shape[1])
    shapes = [
        shape((rows, width), bf16),
        shape((rows, width), f32),
        *(shape((n, shard, wide), bf16) for wide in dense_widths),
    ]
    summing = []
    if fused:
        deep = grads.shape[0] // Totals.count
        shapes += [
            shape(grads.shape, bf16),
            *(shape((shard, wide), bf16) for wide in dense_widths),
        ]
        shapes += Totals.landing(deep, grads.shape[1])
        summed = [(rows, back_part.shape[2]), (rows, width)] + [(shard, wide) for wide in dense_widths]
        for high, wide in summed:
            shapes += Summing.landing(line, high, wide)
        widest = max(wide for _, wide in summed)
        summing = [
            pltpu.VMEM((2, rows, widest), bf16),
        ]
        for high, wide in summed:
            summing += Summing.scratch(line, high, wide)
        summing += Totals.scratch(deep, grads.shape[1])
        for wide in dense_widths:
            summing += Sharing.scratch(shard, wide)
    else:
        back_part = lax.psum_scatter(back_part, "exp", scatter_dimension=0)
        out_part = lax.psum_scatter(out_part, "exp", scatter_dimension=0)
    found = pl.pallas_call(
        functools.partial(backward_kernel, size, line, heads, kv_heads, experts, fused),
        out_shape=tuple(shapes),
        in_specs=[ANY if fused else vmem] * 2 + [ANY] * 4 + [vmem] * 12 + [ANY] * 2,
        out_specs=(vmem, vmem) + (ANY,) * (len(shapes) - 2),
        scratch_shapes=summing
        + [
            pltpu.VMEM(qkv_full.shape, bf16),
            pltpu.VMEM(out_full.shape, bf16),
            pltpu.VMEM((heads, rows, keys_count), bf16),
            pltpu.VMEM((heads // kv_heads, rows, keys_count), bf16),
            pltpu.VMEM((heads, rows, head), bf16),
            pltpu.VMEM((rows, width), bf16),
            pltpu.VMEM((rows, width), f32),
            pltpu.VMEM((rows, width), bf16),
            pltpu.VMEM((rows, width), bf16),
            pltpu.VMEM((rows, heads * head + kv_both), bf16),
            pltpu.VMEM((rows, kv_both), f32),
            pltpu.VMEM((size, rows, kv_both), bf16),
            pltpu.VMEM((size - 1, rows, kv_both), bf16),
            pltpu.VMEM((2, n, shard, 256), bf16),
            dma((2,)),
            dma((size - 1,)),
            dma((size - 1,)),
            dma((2,)),
        ],
        compiler_params=pltpu.CompilerParams(
            collective_id=collective_id, has_side_effects=True, vmem_limit_bytes=62 << 20
        ),
        name="backward",
    )(back_part, out_part, grads, *early, tokens, mid, final, marks, small, gains, queries, keyval, mixed, lse, cosine, sine,
      qkv_full, out_full)
    if fused:
        return found[:2] + found[5:9]
    dense = tuple(lax.psum_scatter(part, "exp", scatter_dimension=0) for part in found[2:5])
    return found[:2] + (lax.psum(grads, "ctx"),) + tuple(lax.psum(part, "ctx") for part in dense)


def widen_kernel(total, *refs):
    dense, (gate, up, down), dense_to, held, refs = refs[:3], refs[3:6], refs[6:9], refs[9], refs[10:]
    held_dense, wide, wide_dense, (in_sem, out_sem, dense_in, dense_done) = refs[:3], refs[3], refs[4:7], refs[7:]
    f32 = jnp.float32
    high = held.shape[1]
    blocks, slots = held.shape[0], wide.shape[0]
    per, tall = blocks // 3, gate.shape[1] // high

    def load(i):
        return pltpu.make_async_copy(total.at[pl.ds(i * high, high)], held.at[i], in_sem.at[i])

    def store(i):
        n, at = i // per, i % per
        if n < 2:
            target = (gate, up)[n].at[at // tall, pl.ds(at % tall * high, high)]
        else:
            target = down.at[at // tall, :, pl.ds(at % tall * high, high)]
        return pltpu.make_async_copy(wide.at[i % slots], target, out_sem.at[i % slots])

    small_in = [
        pltpu.make_async_copy(src, dst, dense_in.at[i])
        for i, (src, dst) in enumerate(zip(dense, held_dense))
    ]
    small_done = [
        pltpu.make_async_copy(src, dst, dense_done.at[i])
        for i, (src, dst) in enumerate(zip(wide_dense, dense_to))
    ]
    load(0).start()
    for copy in small_in:
        copy.start()
    for i in range(1, blocks):
        load(i).start()
    for i in range(blocks):
        load(i).wait()
        if i >= slots:
            store(i - slots).wait()
        wide[i % slots] = held[i].astype(f32)
        store(i).start()
        if i == 0:
            for copy in small_in:
                copy.wait()
            for src, dst in zip(held_dense, wide_dense):
                dst[...] = src[:, : dst.shape[1]].astype(f32)
            for copy in small_done:
                copy.start()
    for i in range(max(0, blocks - slots), blocks):
        store(i).wait()
    for copy in small_done:
        copy.wait()


def widen(total, parts, local, width, units, kv_both):
    f32 = jnp.float32
    blocks, slots = total.shape[0] // units, 4
    shape = jax.ShapeDtypeStruct
    dma = pltpu.SemaphoreType.DMA
    dense = [parts[0].shape, parts[1].shape, (parts[2].shape[0], kv_both)]
    return pl.pallas_call(
        widen_kernel,
        out_shape=(
            shape((local, width, units), f32),
            shape((local, width, units), f32),
            shape((local, units, width), f32),
            *(shape(one, f32) for one in dense),
        ),
        in_specs=[ANY] * 4,
        out_specs=(ANY,) * 6,
        scratch_shapes=[
            pltpu.VMEM((blocks, units, units), total.dtype),
            *(pltpu.VMEM(one.shape, one.dtype) for one in parts),
            pltpu.VMEM((slots, units, units), f32),
            *(pltpu.VMEM(one, f32) for one in dense),
            dma((blocks,)),
            dma((slots,)),
            dma((3,)),
            dma((3,)),
        ],
        compiler_params=pltpu.CompilerParams(vmem_limit_bytes=56 << 20),
        name="widen",
    )(total, *parts)


def rope_tables(first_row, row_count, head_size):
    half_size = head_size // 2
    frequency = ROPE_BASE ** (-jnp.arange(half_size, dtype=jnp.float32) * (2.0 / head_size))
    places = (first_row + jnp.arange(row_count, dtype=jnp.int32)).astype(jnp.float32)
    angles = places[:, None] * frequency[None, :]
    cosine = jnp.cos(angles)
    sine = jnp.sin(angles)
    return (jnp.concatenate([cosine, cosine], 1), jnp.concatenate([-sine, sine], 1))


def ein(spec, a, b):
    return jnp.einsum(spec, a, b, preferred_element_type=jnp.float32)


def shards(
    tokens,
    routes,
    gain_attn,
    w_query,
    key_value_weight,
    w_out,
    gain_ffn,
    w_router,
    w_gate,
    w_up,
    w_down,
    cotangent,
):
    f32 = jnp.float32
    bf16 = jnp.bfloat16
    rows, width = tokens.shape[1:]
    ctx_size, exp_size = lax.axis_size("ctx"), lax.axis_size("exp")
    ctx_index, exp_index = lax.axis_index("ctx"), lax.axis_index("exp")
    local_experts = w_gate.shape[0]
    experts = local_experts * exp_size
    top = routes.shape[2]
    capacity = 2 * rows * top // experts
    shard_rows = w_query.shape[0]
    heads, kv_heads, head = QUERY_HEADS, KEY_VALUE_HEADS, HEAD_WIDTH
    groups = heads // kv_heads
    q_width, kv_width = heads * head, kv_heads * head
    scaling = 1.0 / math.sqrt(head)
    first_row = ctx_index * rows

    named_own = jnp.any(routes[0][:, :, None] == jnp.arange(128, dtype=jnp.int32), axis=1).astype(bf16)
    small = jnp.concatenate(
        [
            w_router,
            gain_attn[:, None],
            gain_ffn[:, None],
            jnp.zeros((shard_rows, 128 - experts - 2), bf16),
        ],
        1,
    )
    qkv_full, out_full, small_full, named, rows_all = gather_weights(
        (jnp.concatenate([w_query, key_value_weight], 1), w_out, small), named_own, cotangent[0], 1
    )

    cosine, sine = rope_tables(first_row, rows, head)
    hops = planned(ctx_size, exp_size, shard_rows)
    queries, keyval, mixed, lse, resid_mid, hidden_two, gains, rows_all = attend(
        hops, experts, tokens[0], small_full, cosine, sine, qkv_full, out_full, rows_all, 2
    )

    _, out_part, back_part, grads, _, *early = expert_pass(
        hops and exp_size > 6, hops, capacity, hidden_two, cotangent[0], rows_all, named, small_full, w_gate, w_up, w_down, 3
    )
    output, grad_input, grads, *dense = backward(
        experts, shard_rows, back_part, out_part, grads, early or [grads] * 3, tokens[0], resid_mid, cotangent[0], named_own, small_full, gains,
        queries, keyval, mixed, lse, cosine, sine, qkv_full, out_full, 4
    )
    small_total = dense[2][:, 2 * kv_width :].astype(f32)
    grad_gate, grad_up, grad_down, grad_out, grad_query, grad_keyval = widen(
        grads, dense, local_experts, width, w_gate.shape[2], 2 * kv_width
    )
    return (
        output[None],
        grad_input[None],
        small_total[:, experts],
        grad_query,
        grad_keyval,
        grad_out,
        small_total[:, experts + 1],
        small_total[:, :experts],
        grad_gate,
        grad_up,
        grad_down,
    )


def solution(mesh):
    rows, wide, deep = P("exp", "ctx", None), P("exp", None), P("exp", None, None)
    flat = P("exp")
    return jax.shard_map(
        shards,
        mesh=mesh,
        in_specs=(rows, rows, flat, wide, wide, wide, flat, wide, deep, deep, deep, rows),
        out_specs=(rows, rows, flat, wide, wide, wide, flat, wide, deep, deep, deep),
        check_vma=False,
    )
```

```python
import functools
import math

import jax
import jax.numpy as jnp
from jax import lax
from jax.experimental import pallas as pl
from jax.experimental.pallas import tpu as pltpu
from jax.sharding import PartitionSpec as P

MESH = pl.DeviceIdType.MESH
ANY = pl.BlockSpec(memory_space=pl.ANY)


def remote(src, dst, send, recv, ctx, exp):
    return pltpu.make_async_remote_copy(
        src_ref=src, dst_ref=dst, send_sem=send, recv_sem=recv, device_id=(ctx, exp), device_id_type=MESH
    )


def greet(pairs):
    barrier = pltpu.get_barrier_semaphore()
    count = 0
    for here, ctx, exp in pairs:
        if here is True:
            pl.semaphore_signal(barrier, inc=1, device_id=(ctx, exp), device_id_type=MESH)
            count = count + 1
        else:
            @pl.when(here)
            def _():
                pl.semaphore_signal(barrier, inc=1, device_id=(ctx, exp), device_id_type=MESH)
            count = count + here.astype(jnp.int32)
    pl.semaphore_wait(barrier, count)


QUERY_HEADS = 12
KEY_VALUE_HEADS = 2
HEAD_WIDTH = 128
EPS = 1e-06
NEG = -1e30
ROPE_BASE = 1000000.0


class Gathering:
    def __init__(self, line, own, out, sems, keep_own=True, window=None):
        self.line, self.keep_own = line, keep_own
        self.window = pl.ds(*window) if window is not None else pl.ds(0, out.shape[1])
        self.own, self.whole = own.at[self.window], out
        self.local_sem, self.z_send, self.z_recv, self.c_send, self.c_recv = sems
        self.c, self.e = lax.axis_index("ctx"), lax.axis_index("exp")
        self.p, self.k = self.e // 2, self.e % 2

    def block(self, q):
        return self.whole.at[2 * q + self.k, self.window]

    def along(self, q, src, to_right):
        there = self.e + 2 if to_right else self.e - 2
        way = 0 if to_right else 1
        return remote(src, self.block(q), self.z_send.at[way, q], self.z_recv.at[q], self.c, there)

    def across(self, q, src):
        there = self.e + 1 - 2 * self.k
        return remote(src, self.block(q), self.c_send.at[q], self.c_recv.at[q], self.c, there)

    def local(self):
        return pltpu.make_async_copy(self.own, self.whole.at[self.e, self.window], self.local_sem)

    def ends(self, d):
        for to_right in (True, False):
            q = self.p - d if to_right else self.p + d
            here = (q >= 0) if to_right else (q < self.line)
            further = (self.p < self.line - 1) if to_right else (self.p > 0)
            yield to_right, q, here, further

    def begin(self):
        for to_right, q, _, further in self.ends(0):
            @pl.when(further)
            def _():
                self.along(q, self.own, to_right).start()

        self.across(self.p, self.own).start()
        if self.keep_own:
            self.local().start()

    def pump(self, d, onward=True):
        for to_right, q, here, further in self.ends(d):
            @pl.when(here)
            def _():
                block = self.block(q)
                self.along(q, block, to_right).wait_recv()
                if onward:
                    @pl.when(further)
                    def _():
                        self.along(q, block, to_right).start()

                self.across(q, block).start()

    def forward(self, d):
        for to_right, q, here, further in self.ends(d):
            @pl.when(here & further)
            def _():
                self.along(q, self.block(q), to_right).start()

    def finish(self, sent, crossed):
        for d in crossed:
            for to_right, q, here, _ in self.ends(d):
                if d > 0 or to_right:
                    @pl.when(here)
                    def _():
                        self.across(q, self.own).wait()
        for d in sent:
            for to_right, q, here, further in self.ends(d):
                @pl.when(here & further)
                def _():
                    self.along(q, self.own, to_right).wait_send()

    def end(self, hops=None):
        last = self.line if hops is None else min(self.line, hops + 1)
        if self.keep_own:
            self.local().wait()
        self.finish(range(self.line if hops is None else last - 1), range(last))

    @staticmethod
    def scratch(line):
        dma = pltpu.SemaphoreType.DMA
        return [dma, dma((2, line)), dma((line,)), dma((line,)), dma((line,))]


def gather_kernel(line, own, out, *sems):
    c, e = lax.axis_index("ctx"), lax.axis_index("exp")
    greet([(e >= 2, c, e - 2), (e < 2 * line - 2, c, e + 2), (True, c, e + 1 - 2 * (e % 2))])
    gathering = Gathering(line, own, out, sems)
    gathering.begin()
    for d in range(1, line):
        gathering.pump(d)
    gathering.end()


def gather_rows(own, collective_id):
    n = lax.axis_size("exp")
    return pl.pallas_call(
        functools.partial(gather_kernel, n // 2),
        out_shape=jax.ShapeDtypeStruct((n,) + own.shape, own.dtype),
        in_specs=[ANY],
        out_specs=ANY,
        scratch_shapes=Gathering.scratch(n // 2),
        compiler_params=pltpu.CompilerParams(collective_id=collective_id, has_side_effects=True),
        name="gather_rows",
    )(own)


def add_rows(dst, a, b, rows):
    step = math.gcd(rows, 64)

    def body(i, carried):
        at = pl.ds(pl.multiple_of(i * step, step), step)
        dst[at, :] = a[at, :] + b[at, :]
        return carried

    lax.fori_loop(0, rows // step, body, 0)


class Summing:
    def __init__(self, line, part, cross, moving, acc, tmp, sems, early=None):
        self.line, self.part, self.cross, self.moving, self.early = line, part, cross, moving, early
        self.acc, self.tmp = acc, tmp
        self.own_sem, self.tmp_sem, self.c_send, self.c_recv, self.z_send, self.z_recv = sems
        self.c, self.e = lax.axis_index("ctx"), lax.axis_index("exp")
        self.p, self.k = self.e // 2, self.e % 2
        self.rows, self.width = part.shape[1:]

    def across(self, q):
        there = self.e + 1 - 2 * self.k
        return remote(
            self.part.at[2 * q + 1 - self.k], self.cross.at[q], self.c_send.at[q], self.c_recv.at[q], self.c, there
        )

    def own(self, q):
        return pltpu.make_async_copy(self.part.at[2 * q + self.k], self.acc.at[q], self.own_sem.at[q])

    def load(self, src, side):
        into = self.tmp.at[side, pl.ds(0, self.rows), pl.ds(0, self.width)]
        return pltpu.make_async_copy(src, into, self.tmp_sem.at[side])

    def add(self, q, side):
        add_rows(self.acc.at[q], self.acc.at[q], self.tmp.at[side, pl.ds(0, self.rows), pl.ds(0, self.width)], self.rows)

    def along(self, q, to_right):
        there = self.e + 2 if to_right else self.e - 2
        place = q if to_right else jnp.where(q == self.p - 1, self.line, q)
        return remote(self.acc.at[q], self.moving.at[place], self.z_send.at[q], self.z_recv.at[place], self.c, there)

    def arrived(self, place):
        return remote(self.acc.at[0], self.moving.at[place], self.z_send.at[0], self.z_recv.at[place], self.c, self.e)

    def ends(self, d):
        for to_right in (True, False):
            if d > 0 or to_right:
                q = self.p + d if to_right else self.p - d
                here = (q < self.line) if to_right else (q >= 0)
                behind = (self.p > 0) if to_right else (self.p < self.line - 1)
                if d == 1 and self.early is not None:
                    here = here & behind
                yield to_right, q, here, behind

    def begin(self):
        order = [(d, end) for d in range(self.line - 1, -1, -1) for end in self.ends(d)]
        for _, (_, q, here, _) in order:
            @pl.when(here)
            def _():
                self.across(q).start()
                self.own(q).start()
        for d, (to_right, q, here, behind) in order:
            side = 0 if to_right else 1

            @pl.when(here)
            def _():
                self.across(q).wait_recv()
                self.load(self.cross.at[q], side).start()
                self.own(q).wait()
                self.load(self.cross.at[q], side).wait()
                self.add(q, side)
                if d > 0:
                    @pl.when(jnp.logical_not(behind))
                    def _():
                        self.along(q, to_right).start()

    def step(self, d):
        if d > 0:
            for to_right, q, here, behind in self.ends(d):
                @pl.when(here & behind)
                def _():
                    self.arrived(q).wait_recv()
                    self.load(self.moving.at[q], 0 if to_right else 1).start()
            for to_right, q, here, behind in self.ends(d):
                @pl.when(here & behind)
                def _():
                    side = 0 if to_right else 1
                    self.load(self.moving.at[q], side).wait()
                    self.add(q, side)
                    self.along(q, to_right).start()
            return
        last = ((0, self.p, self.p > 0), (1, self.line, self.p < self.line - 1))
        for side, place, behind in last:
            if self.early is not None:
                from_end = (self.p == 1) if side == 0 else (self.p == self.line - 2)

                @pl.when(from_end)
                def _():
                    self.load(self.early, side).start()

                arrives = behind & jnp.logical_not(from_end)
            else:
                arrives = behind

            @pl.when(arrives)
            def _():
                self.arrived(place).wait_recv()
                self.load(self.moving.at[place], side).start()
        for side, place, behind in last:
            @pl.when(behind)
            def _():
                self.load(self.moving.at[place], side).wait()
                self.add(self.p, side)

    def result(self):
        return self.acc.at[self.p]

    def end(self):
        for d in range(self.line):
            for to_right, q, here, _ in self.ends(d):
                @pl.when(here)
                def _():
                    if d > 0:
                        self.along(q, to_right).wait_send()
                    self.across(q).wait_send()

    @staticmethod
    def scratch(line, rows, width):
        dma = pltpu.SemaphoreType.DMA
        return [
            pltpu.VMEM((line, rows, width), jnp.bfloat16),
            dma((line,)),
            dma((2,)),
            dma((line,)),
            dma((line,)),
            dma((line,)),
            dma((line + 1,)),
        ]

    @staticmethod
    def landing(line, rows, width):
        return [
            jax.ShapeDtypeStruct((line, rows, width), jnp.bfloat16),
            jax.ShapeDtypeStruct((line + 1, rows, width), jnp.bfloat16),
        ]


class Totals:
    ahead, lag, count, early = 4, 1, 12, 4

    def __init__(self, part, early_first, sends, recvs, total=None, first=None, second=None, buffers=None, sems=None):
        self.part, self.total, self.early_first, self.first, self.second = part, total, early_first, first, second
        self.sends, self.recvs = sends, recvs
        if buffers is not None:
            self.own, self.got, self.got_two = buffers
            self.load_sem, self.got_sem, self.store_sem = sems
            self.slots = self.own.shape[0]
        c, self.e = lax.axis_index("ctx"), lax.axis_index("exp")
        self.bits = (c % 2, c // 2)
        self.nbrs = (c + 1 - 2 * (c % 2), lax.rem(c + 2, 4))
        self.deep = part.shape[0] // self.count

    def axes(self, h):
        return (0, 1) if h == 0 else (1, 0)

    def rows(self, ref, t, h, kept_one, kept_two=None, mine_two=True):
        one, two = self.axes(h)
        quarter, eighth = self.deep // 4, self.deep // 8
        bit = self.bits[one] if kept_one else 1 - self.bits[one]
        start = t * self.deep + h * (self.deep // 2) + bit * quarter
        if kept_two is None:
            return ref.at[pl.ds(pl.multiple_of(start, 16), quarter), :]
        return ref.at[pl.ds(pl.multiple_of(start + self.bits[two] * eighth, 16), eighth), :]

    def piece(self, t, h, kept):
        eighth = self.deep // 8
        bit = self.bits[self.axes(h)[1]]
        start = (bit if kept else 1 - bit) * eighth
        return self.own.at[t % self.slots, h, pl.ds(pl.multiple_of(start, 16), eighth), :]

    def copy(self, stage, t, h):
        one, two = self.axes(h)
        if stage == 0:
            src, dst, there = self.rows(self.part, t, h, False), self.landed(t, h), one
        elif stage == 1:
            src, dst, there = self.piece(t, h, False), self.second.at[t, h], two
        elif stage == 2:
            src, dst, there = self.piece(t, h, True), self.rows(self.total, t, h, True, True), two
        else:
            src, dst, there = self.rows(self.total, t, h, True), self.rows(self.total, t, h, True), one
        return remote(src, dst, self.sends.at[stage, t, h], self.recvs.at[stage, t, h], self.nbrs[there], self.e)

    def landed(self, t, h):
        return self.early_first.at[t, h] if t < self.early else self.first.at[t - self.early, h]

    def start_early(self, t):
        for h in range(2):
            self.copy(0, t, h).start()

    def end_early(self):
        for t in range(self.early):
            for h in range(2):
                self.copy(0, t, h).wait()

    def load_own(self, t, h):
        return pltpu.make_async_copy(
            self.rows(self.part, t, h, True), self.own.at[t % self.slots, h], self.load_sem.at[t % 2, h]
        )

    def store(self, t, h):
        return pltpu.make_async_copy(
            self.piece(t, h, True), self.rows(self.total, t, h, True, True), self.store_sem.at[t % self.slots, h]
        )

    def begin(self):
        for t in range(self.early, min(self.early + self.ahead, self.count)):
            for h in range(2):
                self.copy(0, t, h).start()
        for h in range(2):
            self.load_own(0, h).start()

    @property
    def ticks(self):
        return self.count + 2 * self.lag

    def tick(self, t):
        count, lag = self.count, self.lag
        t_two, t_three = t - lag, t - 2 * lag
        loads = []
        if t < count:
            for h in range(2):
                if t >= self.early:
                    self.copy(0, t, h).wait_recv()
                came = pltpu.make_async_copy(self.landed(t, h), self.got.at[h], self.got_sem.at[0, h])
                came.start()
                loads.append(came)
            if t + self.early + self.ahead < count:
                for h in range(2):
                    self.copy(0, t + self.early + self.ahead, h).start()
        later = []
        if 0 <= t_two < count:
            for h in range(2):
                self.copy(1, t_two, h).wait_recv()
                came = pltpu.make_async_copy(self.second.at[t_two, h], self.got_two.at[h], self.got_sem.at[1, h])
                came.start()
                later.append(came)
        if t < count:
            for h in range(2):
                self.load_own(t, h).wait()
                loads[h].wait()
                mine = self.own.at[t % self.slots, h]
                add_rows(mine, mine, self.got.at[h], self.deep // 4)
                self.copy(1, t, h).start()
        if 0 <= t_two < count:
            for h in range(2):
                later[h].wait()
                mine = self.piece(t_two, h, True)
                add_rows(mine, mine, self.got_two.at[h], self.deep // 8)
                self.copy(2, t_two, h).start()
                self.store(t_two, h).start()
        if 0 <= t_three < count:
            for h in range(2):
                self.copy(2, t_three, h).wait_recv()
                self.store(t_three, h).wait()
                self.copy(3, t_three, h).start()
                self.copy(1, t_three, h).wait_send()
                self.copy(2, t_three, h).wait_send()
        if t + 1 < count:
            for h in range(2):
                self.load_own(t + 1, h).start()

    def end(self):
        for t in range(self.count):
            for h in range(2):
                if t >= self.early:
                    self.copy(0, t, h).wait_send()
                self.copy(3, t, h).wait()

    @staticmethod
    def early_scratch():
        dma = pltpu.SemaphoreType.DMA
        return [dma((1, Totals.early, 2)), dma((1, Totals.early, 2))]

    @staticmethod
    def early_landing(deep, width):
        return jax.ShapeDtypeStruct((Totals.early, 2, deep // 4, width), jnp.bfloat16)

    @staticmethod
    def scratch(deep, width):
        count = Totals.count
        dma = pltpu.SemaphoreType.DMA
        slots = 2 * Totals.lag + 1
        return [
            pltpu.VMEM((slots, 2, deep // 4, width), jnp.bfloat16),
            pltpu.VMEM((2, deep // 4, width), jnp.bfloat16),
            pltpu.VMEM((2, deep // 8, width), jnp.bfloat16),
            dma((4, count, 2)),
            dma((4, count, 2)),
            dma((2, 2)),
            dma((2, 2)),
            dma((slots, 2)),
        ]

    @staticmethod
    def landing(deep, width):
        return [
            jax.ShapeDtypeStruct((Totals.count - Totals.early, 2, deep // 4, width), jnp.bfloat16),
            jax.ShapeDtypeStruct((Totals.count, 2, deep // 8, width), jnp.bfloat16),
        ]


class Sharing:
    def __init__(self, part, total, landed, sems):
        self.part, self.total = part, total
        self.one, self.two = landed[:2], landed[2:]
        self.sends, self.recvs, self.store_sem = sems
        c, self.e = lax.axis_index("ctx"), lax.axis_index("exp")
        self.bits = (c % 2, c // 2)
        self.nbrs = (c + 1 - 2 * (c % 2), lax.rem(c + 2, 4))
        self.rows, self.width = part.shape

    @staticmethod
    def columns(width):
        first = width // 256 * 128
        return ((0, first), (first, width - first))

    def window(self, ref, h, kept_one, kept_two=None):
        one, two = (0, 1) if h == 0 else (1, 0)
        half, quarter = self.rows // 2, self.rows // 4
        start = (self.bits[one] if kept_one else 1 - self.bits[one]) * half
        count = half
        if kept_two is not None:
            start = start + (self.bits[two] if kept_two else 1 - self.bits[two]) * quarter
            count = quarter
        return ref.at[pl.ds(pl.multiple_of(start, 16), count), pl.ds(*self.columns(self.width)[h])]

    def copy(self, stage, h):
        one, two = (0, 1) if h == 0 else (1, 0)
        if stage == 0:
            src, dst, there = self.window(self.part, h, False), self.one[h], one
        elif stage == 1:
            src, dst, there = self.window(self.part, h, True, False), self.two[h], two
        elif stage == 2:
            src, dst, there = self.window(self.part, h, True, True), self.window(self.total, h, True, True), two
        else:
            src, dst, there = self.window(self.total, h, True), self.window(self.total, h, True), one
        return remote(src, dst, self.sends.at[stage, h], self.recvs.at[stage, h], self.nbrs[there], self.e)

    def store(self, h):
        return pltpu.make_async_copy(
            self.window(self.part, h, True, True), self.window(self.total, h, True, True), self.store_sem.at[h]
        )

    def begin(self):
        for h in range(2):
            self.copy(0, h).start()

    def second(self):
        for h in range(2):
            self.copy(0, h).wait_recv()
            kept = self.window(self.part, h, True)
            add_rows(kept, kept, self.one[h], self.rows // 2)
            self.copy(1, h).start()

    def third(self):
        for h in range(2):
            self.copy(1, h).wait_recv()
            kept = self.window(self.part, h, True, True)
            add_rows(kept, kept, self.two[h], self.rows // 4)
            self.copy(2, h).start()
            self.store(h).start()

    def fourth(self):
        for h in range(2):
            self.store(h).wait()
            self.copy(2, h).wait_recv()
            self.copy(3, h).start()

    def end(self):
        for h in range(2):
            for stage in range(3):
                self.copy(stage, h).wait_send()
            self.copy(3, h).wait()

    @staticmethod
    def scratch(rows, width):
        dma = pltpu.SemaphoreType.DMA
        wide = [count for _, count in Sharing.columns(width)]
        return [
            *(pltpu.VMEM((rows // 2, one), jnp.bfloat16) for one in wide),
            *(pltpu.VMEM((rows // 4, one), jnp.bfloat16) for one in wide),
            dma((4, 2)),
            dma((4, 2)),
            dma((2,)),
        ]


def weights_kernel(line, quarter, *refs):
    count = 3
    own, own_mask, own_block = refs[: count + 1], refs[count + 1], refs[count + 2]
    refs = refs[1:]
    out, masks, blocks = refs[count + 2 : 2 * count + 2], refs[2 * count + 2], refs[2 * count + 3]
    held, refs = refs[2 * count + 4 : 3 * count + 4], refs[3 * count + 4 :]
    local_sem, own_send, own_recv, z_send, z_recv, xy_send, xy_recv, d_send, d_recv, c_send, c_recv = refs[:-10]
    c, e = lax.axis_index("ctx"), lax.axis_index("exp")
    p, k = e // 2, e % 2
    sibling = e + 1 - 2 * k
    rows, split = own[0].shape
    places = (held[0].at[:, 0:split], held[0].at[:, split:], *held[1:])
    loads = [pltpu.make_async_copy(src, dst, local_sem.at[0, i]) for i, (src, dst) in enumerate(zip(own, places))]
    for copy in loads:
        copy.start()
    nbr = (c + 1 - 2 * (c % 2), (c + 2) % 4)
    opposite = 3 - c
    greet(
        [
            (p > 0, c, e - 2),
            (p < line - 1, c, e + 2),
            (True, c, sibling),
            (True, nbr[0], e),
            (True, nbr[1], e),
        ]
    )

    def whole(a):
        return out[a].at[pl.ds(pl.multiple_of(e * rows, 16), rows), :]

    def piece(a, q, column):
        return out[a].at[pl.ds(pl.multiple_of((2 * q + k) * rows + column * quarter, 16), quarter), :]

    def own_piece(a):
        return held[a].at[pl.ds(pl.multiple_of(c * quarter, 16), quarter), :]

    def local(a):
        return pltpu.make_async_copy(held[a], whole(a), local_sem.at[1, a])

    def own_across(a):
        return remote(held[a], whole(a), own_send.at[a], own_recv.at[a], c, sibling)

    def along(a, q, src, to_right):
        there = e + 2 if to_right else e - 2
        way = 0 if to_right else 1
        return remote(src, piece(a, q, c), z_send.at[way, q, a], z_recv.at[q, a], c, there)

    def beside(a, q, axis):
        return remote(piece(a, q, c), piece(a, q, c), xy_send.at[axis, q, a], xy_recv.at[axis, q, a], nbr[axis], e)

    def onward(a, q):
        came, goes = (0, 1) if a == 0 else (1, 0)
        block = piece(a, q, nbr[came])
        return remote(block, block, d_send.at[q, a], d_recv.at[q, a], nbr[goes], e)

    def across(a, q, j):
        column = (c, nbr[0], nbr[1], opposite)[j]
        block = piece(a, q, column)
        return remote(block, block, c_send.at[q, j, a], c_recv.at[q, j, a], c, sibling)

    for copy in loads:
        copy.wait()
    arrays = range(count)
    marking = Gathering(line, own_mask, masks, refs[-10:-5])
    gathering = Gathering(line, own_block, blocks, refs[-5:], keep_own=False)
    marking.begin()
    for a in arrays:
        @pl.when(p < line - 1)
        def _():
            along(a, p, own_piece(a), True).start()

        @pl.when(p > 0)
        def _():
            along(a, p, own_piece(a), False).start()
    for a in arrays:
        own_across(a).start()
        local(a).start()

    def ends(d):
        for to_right in (True, False):
            q = p - d if to_right else p + d
            yield to_right, q, ((q >= 0) if to_right else (q < line))

    for d in range(1, line + 1):
        if d < line:
            for to_right, q, here in ends(d):
                further = (p < line - 1) if to_right else (p > 0)

                @pl.when(here)
                def _():
                    for a in arrays:
                        along(a, q, piece(a, q, c), to_right).wait_recv()

                        @pl.when(further)
                        def _():
                            along(a, q, piece(a, q, c), to_right).start()

                        beside(a, q, 0).start()
                        beside(a, q, 1).start()
                        across(a, q, 0).start()
        if d < line:
            marking.pump(d)
        if d == line - 1:
            gathering.begin()
        if d > 1:
            for to_right, q, here in ends(d - 1):
                @pl.when(here)
                def _():
                    for a in arrays:
                        came = 0 if a == 0 else 1
                        beside(a, q, came).wait_recv()
                        onward(a, q).start()
                        across(a, q, 1 + came).start()
                        beside(a, q, 1 - came).wait_recv()
                        across(a, q, 2 - came).start()
    for d in range(1, line):
        for to_right, q, here in ends(d):
            @pl.when(here)
            def _():
                for a in arrays:
                    onward(a, q).wait_recv()
                    across(a, q, 3).start()
    gathering.pump(1, onward=False)
    gathering.end(1)
    marking.end()
    for a in arrays:
        local(a).wait()
        own_across(a).wait()
    for d in range(0, line):
        for to_right, q, here in ends(d):
            further = (p < line - 1) if to_right else (p > 0)
            for a in arrays:
                @pl.when(here & further)
                def _():
                    along(a, q, piece(a, q, c), to_right).wait_send()
                if d > 0:
                    @pl.when(here)
                    def _():
                        beside(a, q, 0).wait_send()
                        beside(a, q, 1).wait_send()
                        onward(a, q).wait_send()
                        for j in range(4):
                            across(a, q, j).wait()


def planned(size, n, shard_rows):
    return size == 4 and n == 8 and (shard_rows // 4) % 16 == 0


def gather_weights(shards, mask, block, collective_id):
    n = lax.axis_size("exp")
    rows, high = shards[0].shape[0], n * shards[0].shape[0]
    if not planned(lax.axis_size("ctx"), n, rows):
        shards = (jnp.concatenate(shards[:2], 1), *shards[2:])
        whole = tuple(lax.all_gather(w, "exp", axis=0, tiled=True) for w in shards)
        return whole + (lax.all_gather(mask, "exp", axis=0), gather_rows(block, collective_id))
    line = n // 2
    count = len(shards) - 1
    widths = (shards[0].shape[1] + shards[1].shape[1], *(w.shape[1] for w in shards[2:]))
    dtype = mask.dtype
    dma = pltpu.SemaphoreType.DMA
    return pl.pallas_call(
        functools.partial(weights_kernel, line, rows // 4),
        out_shape=tuple(jax.ShapeDtypeStruct((high, wide), dtype) for wide in widths)
        + tuple(jax.ShapeDtypeStruct((n,) + w.shape, w.dtype) for w in (mask, block)),
        in_specs=[ANY] * (count + 3),
        out_specs=(ANY,) * (count + 2),
        scratch_shapes=[pltpu.VMEM((rows, wide), dtype) for wide in widths]
        + [
            dma((2, count + 1)),
            dma((count,)),
            dma((count,)),
            dma((2, line, count)),
            dma((line, count)),
            dma((2, line, count)),
            dma((2, line, count)),
            dma((line, count)),
            dma((line, count)),
            dma((line, 4, count)),
            dma((line, 4, count)),
        ]
        + Gathering.scratch(line)
        + Gathering.scratch(line),
        compiler_params=pltpu.CompilerParams(
            collective_id=collective_id, has_side_effects=True, vmem_limit_bytes=62 << 20
        ),
        name="gather_weights",
    )(*shards, mask, block)


def dot(a, b):
    return lax.dot_general(a, b, (((1,), (0,)), ((), ())), preferred_element_type=jnp.float32)


def dot_nt(a, b):
    return lax.dot_general(a, b, (((1,), (1,)), ((), ())), preferred_element_type=jnp.float32)


def dot_tn(a, b):
    return lax.dot_general(a, b, (((0,), (0,)), ((), ())), preferred_element_type=jnp.float32)


def visit(p, line, i):
    both = jnp.minimum(p, line - 1 - p)
    d = jnp.where(i <= 2 * both, (i + 1) // 2, i - both)
    left = jnp.where(i <= 2 * both, i % 2 == 1, p > line - 1 - p)
    q = jnp.where(left, p - d, p + d)
    first = (i == 0) | (i > 2 * both) | (i % 2 == 1)
    return q, d, first


def expert_kernel(line, local, cap, hop, start, hidden, own_grads, grads_in, named, router, w_gate, w_up, w_down, *refs):
    hidden_all, out_part, back_part, grads, grads_all = refs[:5]
    if start:
        early_first, early_sums, refs = refs[5], refs[6:8], refs[:5] + refs[8:]
    wg, wu, wd, xs, ds, act, dg, du, es, h_buf, y_buf, out_stage, back_stage, in_stage, down_stage = refs[5:20]
    picks, xs_turned, act_turned, gate_kept, refs = *refs[20:24], refs[:20] + refs[24:]
    if start:
        crossed, refs = refs[20:22], refs[:20] + refs[22:]
        hop_sem, refs = refs[-1], refs[:-1]
    w_sem, own_sem, z_send, z_recv, c_send, c_recv, h_sem, y_sem, o_sem, b_sem, s_sem = refs[20:31]
    f32, bf16 = jnp.float32, jnp.bfloat16
    c, e = lax.axis_index("ctx"), lax.axis_index("exp")
    p, k = e // 2, e % 2
    sibling = e + 1 - 2 * k
    rows, width = hidden.shape
    hidden_units = wg.shape[2]
    slots = 2 * cap
    lanes = router.shape[1]

    loads = [
        pltpu.make_async_copy(src, dst, w_sem.at[i])
        for i, (src, dst) in enumerate(((w_gate, wg), (w_up, wu), (w_down, wd)))
    ]
    for copy in loads:
        copy.start()
    beside = [(True, c + 1 - 2 * (c % 2), e), (True, lax.rem(c + 2, 4), e)] if start else []
    greet([(p > 0, c, e - 2), (p < line - 1, c, e + 2), (True, c, sibling)] + beside)
    def along(q, src, to_right):
        there = e + 2 if to_right else e - 2
        return remote(src, hidden_all.at[2 * q + k], z_send.at[0 if to_right else 1, q], z_recv.at[q], c, there)

    def across(q, src):
        return remote(src, hidden_all.at[2 * q + k], c_send.at[q], c_recv.at[q], c, sibling)

    def load_hidden(q, slot):
        return pltpu.make_async_copy(hidden_all.at[pl.ds(2 * q, 2)], h_buf.at[slot], h_sem.at[slot])

    def load_grads(q, slot):
        return pltpu.make_async_copy(grads_all.at[pl.ds(2 * q, 2)], y_buf.at[slot], y_sem.at[slot])

    def load_own(buf, own, blocks, i):
        return [
            pltpu.make_async_copy(own, buf.at[0, k], own_sem.at[2 * i]),
            pltpu.make_async_copy(blocks.at[sibling], buf.at[0, 1 - k], own_sem.at[2 * i + 1]),
        ]

    def store_out(q, slot):
        return pltpu.make_async_copy(out_stage.at[slot], out_part.at[pl.ds(2 * q, 2)], o_sem.at[slot])

    def store_back(q, slot):
        return pltpu.make_async_copy(back_stage.at[slot], back_part.at[pl.ds(2 * q, 2)], b_sem.at[slot])

    @pl.when(p < line - 1)
    def _():
        along(p, hidden, True).start()

    @pl.when(p > 0)
    def _():
        along(p, hidden, False).start()

    across(p, hidden).start()
    if hop:
        hops = Gathering(line, grads_all.at[e], grads_all, refs[31:36], window=(rows // 2, rows // 2))
        hops.forward(2)
    for copy in load_own(y_buf, own_grads, grads_all, 0):
        copy.start()

    def pump(d):
        for to_right in (True, False):
            q = p - d if to_right else p + d
            here = (q >= 0) if to_right else (q < line)
            further = (p < line - 1) if to_right else (p > 0)

            @pl.when(here)
            def _():
                block = hidden_all.at[2 * q + k]
                along(q, block, to_right).wait_recv()

                @pl.when(further)
                def _():
                    along(q, block, to_right).start()

                across(q, block).start()

    for copy in loads:
        copy.wait()

    lane = lax.broadcasted_iota(jnp.int32, (local * cap, lanes), 1)
    expert_of_row = lax.broadcasted_iota(jnp.int32, (local * cap, lanes), 0) // cap

    def units_of(j, q):
        tile = 256
        rows_j = xs[j].reshape(slots, width)
        xs_turned[j, :, pl.ds(pl.multiple_of(q * slots, slots), slots)] = rows_j.T
        grads_j = ds[j, q].reshape(slots, width)

        def units(t, carried):
            at = pl.ds(pl.multiple_of(t * tile, tile), tile)
            gate_pre = dot(rows_j, wg[j, :, at])
            up_pre = dot(rows_j, wu[j, :, at])
            grad_act = dot_nt(grads_j, wd[j, at, :])
            sigmoid = 1.0 / (1.0 + jnp.exp(-gate_pre))
            silu = gate_pre * sigmoid
            hidden_low = (silu * up_pre).astype(bf16)
            act[j, :, at] = hidden_low
            act_turned[j, at, pl.ds(pl.multiple_of(q * slots, slots), slots)] = hidden_low.T
            dg[j, q, :, at] = (grad_act * up_pre * sigmoid * (1.0 + gate_pre * (1.0 - sigmoid))).astype(bf16)
            du[j, q, :, at] = (grad_act * silu).astype(bf16)
            return carried

        lax.fori_loop(0, hidden_units // tile, units, 0)

    def give_back(q, slot):
        wide = 512
        pick_pair = [picks[b] for b in range(2)]

        def outputs(t, sums):
            at = pl.ds(pl.multiple_of(t * wide, wide), wide)
            gated, back, new_sums = [], [], []
            for j in range(local):
                y = dot(act[j], wd[j, :, at])
                back_j = dot_nt(dg[j, q], wg[j, at, :]) + dot_nt(du[j, q], wu[j, at, :])
                new = []
                for b in range(2):
                    half = slice(b * cap, (b + 1) * cap)
                    y_b = y[half]
                    new.append(sums[j][b] + jnp.sum(y_b * es[j, b, :, at].astype(f32), -1, keepdims=True))
                    gated.append((gate_kept[b, j * cap : (j + 1) * cap, 0:1] * y_b).astype(bf16))
                    back.append(back_j[half].astype(bf16))
                new_sums.append(tuple(new))
            for b in range(2):
                mine = jnp.concatenate([gated[2 * j + b] for j in range(local)], 0)
                out_stage[slot, b, :, at] = dot_tn(pick_pair[b], mine).astype(bf16)
                mine = jnp.concatenate([back[2 * j + b] for j in range(local)], 0)
                back_stage[slot, b, :, at] = dot_tn(pick_pair[b], mine).astype(bf16)
            return tuple(new_sums)

        nothing = jnp.zeros((cap, 1), f32)
        sums = lax.fori_loop(
            0, width // wide, outputs, tuple((nothing, nothing) for _ in range(local))
        )
        for b in range(2):
            grad_gates = jnp.concatenate([sums[j][b] for j in range(local)], 0)
            coarse = grad_gates.astype(bf16).astype(f32)
            spot = e * local + expert_of_row
            spread = jnp.where(
                lane == spot, coarse, jnp.where(lane == spot + lanes // 2, grad_gates - coarse, 0.0)
            ).astype(bf16)
            back_stage[slot, b, :, width : width + lanes] = dot_tn(pick_pair[b], spread).astype(bf16)
        store_out(q, slot).start()
        store_back(q, slot).start()

    at_end = (p == 0) | (p == line - 1)

    def cross_over(n):
        stage = (back_stage, out_stage)[n]
        return remote(stage.at[1, 1 - k], crossed[n], hop_sem.at[n, 0], hop_sem.at[n, 1], c, sibling)

    def send_ahead(n):
        there = jnp.where(p == 0, e + 2, e - 2)
        return remote(crossed[n], early_sums[n], hop_sem.at[n, 2], hop_sem.at[n, 3], c, there)

    def one_chip(i, carried):
        q, d, first = visit(p, line, i)
        slot = i % 2

        across(q, hidden).wait_recv()

        @pl.when(i == 0)
        def _():
            own = load_own(h_buf, hidden, hidden_all, 1)
            for copy in own:
                copy.start()
            for copy in own + load_own(y_buf, own_grads, grads_all, 0):
                copy.wait()

        @pl.when(i > 0)
        def _():
            load_hidden(q, slot).start()

        if hop:
            @pl.when(d == line - 1)
            def _():
                hops.pump(line - 1, onward=False)
                hops.finish([], [line - 1])
                load_grads(q, slot).start()

        after, d_after, _ = visit(p, line, i + 1)

        @pl.when((i < line - 1) & (d_after < (line - 1 if hop else line)))
        def _():
            load_grads(after, 1 - slot).start()

        @pl.when(i > 0)
        def _():
            load_hidden(q, slot).wait()
            load_grads(q, slot).wait()

        @pl.when(i >= 2)
        def _():
            store_out(visit(p, line, i - 2)[0], slot).wait()
            store_back(visit(p, line, i - 2)[0], slot).wait()

        place = lax.broadcasted_iota(jnp.int32, (cap, rows), 0).astype(f32)
        sub = lax.broadcasted_iota(jnp.int32, (lanes, rows), 0)
        upper = lax.broadcasted_iota(jnp.int32, (rows, 2 * rows), 0)
        column = lax.broadcasted_iota(jnp.int32, (rows, 2 * rows), 1)
        ahead = jnp.where((upper < column) & (column < rows) | (upper + rows == column), 1.0, 0.0).astype(bf16)
        for b in range(2):
            marks = named[2 * q + b]
            counted = dot_tn(marks, ahead)
            slots_of = jnp.where(counted[:, rows:] > 0.5, counted[:, :rows], -1.0)
            for j in range(local):
                row = jnp.sum(jnp.where(sub == e * local + j, slots_of, 0.0), 0, keepdims=True)
                picks[b, j * cap : (j + 1) * cap] = jnp.where(place == row, 1.0, 0.0).astype(bf16)
            pick = picks[b]
            block = h_buf[slot, b]
            picked = dot(pick, block).astype(bf16)
            for j in range(local):
                xs[j, b] = picked[j * cap : (j + 1) * cap]
            logits = jnp.where(marks.astype(f32) > 0.5, dot(block, router[...]), NEG)
            raised = jnp.exp(logits - jnp.max(logits, -1, keepdims=True))
            gates = raised / jnp.sum(raised, -1, keepdims=True)
            coarse = gates.astype(bf16)
            fine = (gates - coarse.astype(f32)).astype(bf16)
            at_slots = dot(pick, coarse) + dot(pick, fine)
            gate_slot = jnp.sum(jnp.where(lane == e * local + expert_of_row, at_slots, 0.0), -1, keepdims=True)
            gate_kept[b] = jnp.broadcast_to(gate_slot, gate_kept.shape[1:])
            grad_rows = dot(pick, y_buf[slot, b])
            grad_pairs = (gate_slot * grad_rows).astype(bf16)
            grad_rows = grad_rows.astype(bf16)
            for j in range(local):
                es[j, b] = grad_rows[j * cap : (j + 1) * cap]
                ds[j, q, b] = grad_pairs[j * cap : (j + 1) * cap]

        units_of(0, q)

        @pl.when(i < line - 1)
        def _():
            for j in range(1, local):
                units_of(j, q)
            give_back(q, slot)

        @pl.when(first & (d + 1 < line))
        def _():
            pump(d + 1)

        if start:
            @pl.when(at_end & (i == 1))
            def _():
                for n in range(2):
                    cross_over(n).start()

            @pl.when(at_end & (i == 2))
            def _():
                for n, stage in enumerate((back_stage, out_stage)):
                    cross_over(n).wait()
                    add_rows(crossed[n], crossed[n], stage.at[1, k], rows)
                    send_ahead(n).start()

        return carried

    lax.fori_loop(0, line, one_chip, 0)

    deep = line * slots
    tile = 256
    tiles = hidden_units // tile

    def products(left, right, stage, first_row, count):
        high = stage.shape[1]

        def stores(t):
            row = first_row + lax.div(t, tiles) * high
            return pltpu.make_async_copy(
                stage.at[lax.rem(t, 2)],
                grads.at[
                    pl.ds(pl.multiple_of(row, 16), high),
                    pl.ds(pl.multiple_of(lax.rem(t, tiles) * tile, tile), tile),
                ],
                s_sem.at[lax.rem(t, 2)],
            )

        def one_tile(t, carried):
            @pl.when(t >= 2)
            def _():
                stores(t - 2).wait()

            stage[lax.rem(t, 2)] = dot(left[...], right(pl.ds(pl.multiple_of(t * tile, tile), tile))).astype(bf16)
            stores(t).start()
            return carried

        lax.fori_loop(0, count, one_tile, 0)
        for t in range(max(0, count - 2), count):
            stores(jnp.int32(t)).wait()

    totals = Totals(grads, early_first, *refs[-2:]) if start else None
    sent = 0

    def send_ready(rows_done):
        nonlocal sent
        while start and sent < totals.early and (sent + 1) * totals.deep <= rows_done:
            totals.start_early(sent)
            sent += 1

    last_chip = visit(p, line, jnp.int32(line - 1))[0]
    for i, source in enumerate((dg, du)):
        for j in range(local):
            if i == 0 and j > 0:
                units_of(j, last_chip)
            products(
                xs_turned.at[j],
                lambda at: source[j, :, :, at].reshape(deep, tile),
                in_stage, (i * local + j) * width, tiles,
            )
            send_ready((i * local + j + 1) * width)
    for j in range(local):
        products(
            act_turned.at[j],
            lambda at: ds[j, :, :, :, at].reshape(deep, tile),
            down_stage, 2 * local * width + j * width, width // tile,
        )

    give_back(last_chip, (line - 1) % 2)

    if start:
        totals.end_early()

        @pl.when(at_end)
        def _():
            for n in range(2):
                send_ahead(n).wait_send()

        @pl.when((p == 1) | (p == line - 2))
        def _():
            for n in range(2):
                send_ahead(n).wait_recv()

    if hop:
        hops.finish([2], [])
    for i in range(max(0, line - 2), line):
        q = visit(p, line, jnp.int32(i))[0]
        store_out(q, i % 2).wait()
        store_back(q, i % 2).wait()
    for d in range(line):
        for to_right in (True, False):
            if d == 0 and not to_right:
                continue
            q = p - d if to_right else p + d
            here = (q >= 0) if to_right else (q < line)

            @pl.when(here)
            def _():
                across(q, hidden).wait_send()
    for d in range(line):
        for to_right in (True, False):
            q = p - d if to_right else p + d
            here = (q >= 0) if to_right else (q < line)
            further = (p < line - 1) if to_right else (p > 0)

            @pl.when(here & further)
            def _():
                along(q, hidden, to_right).wait_send()


def expert_pass(hop, start, cap, hidden, own_grads, grads_all, named, router, w_gate, w_up, w_down, collective_id):
    n = lax.axis_size("exp")
    line = n // 2
    rows, width = hidden.shape
    local, _, units = w_gate.shape
    bf16 = jnp.bfloat16
    lanes = router.shape[1]
    dma = pltpu.SemaphoreType.DMA
    vmem = pl.BlockSpec(memory_space=pltpu.VMEM)
    early = (
        Totals.early_landing(3 * local * width // Totals.count, units),
        jax.ShapeDtypeStruct((rows, width + lanes), bf16),
        jax.ShapeDtypeStruct((rows, width), bf16),
    )
    return pl.pallas_call(
        functools.partial(expert_kernel, line, local, cap, hop, start),
        out_shape=(
            jax.ShapeDtypeStruct((n, rows, width), bf16),
            jax.ShapeDtypeStruct((n, rows, width), bf16),
            jax.ShapeDtypeStruct((n, rows, width + lanes), bf16),
            jax.ShapeDtypeStruct((3 * local * width, units), bf16),
            jax.ShapeDtypeStruct(grads_all.shape, bf16),
        )
        + (early if start else ()),
        in_specs=[ANY, ANY, ANY, vmem, vmem, ANY, ANY, ANY],
        out_specs=(ANY,) * (8 if start else 5),
        input_output_aliases={2: 4},
        scratch_shapes=[
            pltpu.VMEM((local, width, units), bf16),
            pltpu.VMEM((local, width, units), bf16),
            pltpu.VMEM((local, units, width), bf16),
            pltpu.VMEM((local, 2, cap, width), bf16),
            pltpu.VMEM((local, line, 2, cap, width), bf16),
            pltpu.VMEM((local, 2 * cap, units), bf16),
            pltpu.VMEM((local, line, 2 * cap, units), bf16),
            pltpu.VMEM((local, line, 2 * cap, units), bf16),
            pltpu.VMEM((local, 2, cap, width), bf16),
            pltpu.VMEM((2, 2, rows, width), bf16),
            pltpu.VMEM((2, 2, rows, width), bf16),
            pltpu.VMEM((2, 2, rows, width), bf16),
            pltpu.VMEM((2, 2, rows, width + lanes), bf16),
            pltpu.VMEM((2, width, 256), bf16),
            pltpu.VMEM((2, units, 256), bf16),
            pltpu.VMEM((2, local * cap, rows), bf16),
            pltpu.VMEM((local, width, n * cap), bf16),
            pltpu.VMEM((local, units, n * cap), bf16),
            pltpu.VMEM((2, local * cap, 128), jnp.float32),
        ]
        + ([pltpu.VMEM(one.shape, bf16) for one in early[1:]] if start else [])
        + [
            dma((3,)),
            dma((4,)),
            dma((2, line)),
            dma((line,)),
            dma((line,)),
            dma((line,)),
            dma((2,)),
            dma((2,)),
            dma((2,)),
            dma((2,)),
            dma((2,)),
        ]
        + (Gathering.scratch(line) if hop else [])
        + (Totals.early_scratch() + [dma((2, 4))] if start else []),
        compiler_params=pltpu.CompilerParams(
            collective_id=collective_id, has_side_effects=True, vmem_limit_bytes=62 << 20
        ),
        name="expert_pass",
    )(hidden, own_grads, grads_all, named, router, w_gate, w_up, w_down)


def turn(block, cosine, signed_sine):
    return block * cosine + pltpu.roll(block, block.shape[1] // 2, 1) * signed_sine


def row_norm(block):
    inverse = lax.rsqrt(jnp.mean(block * block, -1, keepdims=True) + EPS)
    return block * inverse, inverse


def attend_kernel(size, line, hop, experts, heads, kv_heads, tokens, small, cosine, sine, qkv_hbm, out_hbm, rows_in, *refs):
    targets, rows_all = refs[:7], refs[7]
    held, refs = refs[8:15], refs[15:]
    queries, keyval, mixed, lse, mid, hidden, gains = held
    wqkv, wout, h1, w_sem, send, recv, o_sem = refs[:7]
    f32, bf16 = jnp.float32, jnp.bfloat16
    c, e = lax.axis_index("ctx"), lax.axis_index("exp")
    rows, width = tokens.shape
    head = HEAD_WIDTH
    groups = heads // kv_heads
    q_width, kv_width = heads * head, kv_heads * head
    loads = [
        pltpu.make_async_copy(qkv_hbm, wqkv, w_sem.at[0]),
        pltpu.make_async_copy(out_hbm, wout, w_sem.at[1]),
    ]
    for copy in loads:
        copy.start()
    others = [lax.rem(c + i, size) for i in range(1, size)]
    column = [(e >= 2, c, e - 2), (e < 2 * line - 2, c, e + 2), (True, c, e + 1 - 2 * (e % 2))]
    greet((column if hop else []) + [(True, there, e) for there in others])
    if hop:
        half = rows // 2
        early, late = (
            Gathering(line, rows_all.at[e], rows_all, refs[7 + 5 * i : 12 + 5 * i], window=(i * half, half)) for i in range(2)
        )
        early.forward(1)
        late.forward(1)

    def leave(i):
        return pltpu.make_async_copy(held[i], targets[i], o_sem.at[i])

    turned = small[...].astype(f32).T
    gains[...] = turned[experts : experts + 8]
    leave(6).start()

    def step(t, carried):
        at = pl.ds(pl.multiple_of(t * 64, 64), 64)
        normed, _ = row_norm(tokens[at, :].astype(f32))
        h1[at, :] = (normed * gains[0:1, :]).astype(bf16)
        return carried

    lax.fori_loop(0, rows // 64, step, 0)
    loads[0].wait()
    kv = dot(h1[...], wqkv[:, q_width:])
    for j in range(kv_heads):
        at = slice(j * head, (j + 1) * head)
        keyval[c, :, at] = turn(kv[:, at], cosine[...], sine[...]).astype(bf16)
    keyval[c, :, kv_width:] = kv[:, kv_width:].astype(bf16)

    def give(i):
        return remote(keyval.at[c], keyval.at[c], send.at[i - 1], recv.at[i - 1], others[i - 1], e)

    for i in range(1, size):
        @pl.when(c + i < size)
        def _():
            give(i).start()

    for j in range(1, size):
        @pl.when(j > c)
        def _():
            keyval[j] = jnp.zeros((rows, 2 * kv_width), bf16)

    pair = 2 * head

    def project(t, carried):
        at = pl.ds(pl.multiple_of(t * pair, pair), pair)
        q = dot(h1[...], wqkv[:, at])
        for j in range(2):
            queries[2 * t + j] = turn(q[:, j * head : (j + 1) * head], cosine[...], sine[...]).astype(bf16)
        return carried

    lax.fori_loop(0, heads // 2, project, 0)
    leave(0).start()
    if hop:
        early.pump(2)
    for i in range(1, size):
        @pl.when(c - i >= 0)
        def _():
            give(i).wait_recv()
    leave(1).start()

    keys_count = size * rows
    scaling = 1.0 / math.sqrt(head)
    lane = lax.broadcasted_iota(jnp.int32, (rows, 128), 1)

    def one_head(j):
        h = j // groups
        keys = keyval[:, :, pl.ds(pl.multiple_of(h * head, head), head)].reshape(keys_count, head)
        values = keyval[:, :, pl.ds(pl.multiple_of(kv_width + h * head, head), head)].reshape(keys_count, head)
        place = lax.broadcasted_iota(jnp.int32, (rows, keys_count), 1)
        row = c * rows + lax.broadcasted_iota(jnp.int32, (rows, keys_count), 0)
        scores = jnp.where(place <= row, dot_nt(queries[j], keys) * scaling, NEG)
        peak = jnp.max(scores, -1, keepdims=True)
        raised = jnp.exp(scores - peak)
        total = jnp.sum(raised, -1, keepdims=True)
        probs = (raised * (1.0 / total)).astype(bf16)
        return dot(probs, values), peak + jnp.log(total)

    def two_heads(t, stats):
        found = [one_head(2 * t + i) for i in range(2)]
        mixed[:, pl.ds(pl.multiple_of(t * pair, pair), pair)] = jnp.concatenate(
            [block for block, _ in found], 1
        ).astype(bf16)
        for i, (_, value) in enumerate(found):
            stats = jnp.where(lane == 2 * t + i, value, stats)
        return stats

    lse[...] = lax.fori_loop(0, heads // 2, two_heads, jnp.zeros((rows, 128), f32))
    leave(2).start()
    leave(3).start()
    if hop:
        late.pump(2, onward=False)
    loads[1].wait()

    def outward(t, carried):
        at = pl.ds(pl.multiple_of(t * 256, 256), 256)
        mid[:, at] = tokens[:, at].astype(f32) + dot(mixed[...], wout[:, at])
        return carried

    lax.fori_loop(0, width // 256, outward, 0)
    leave(4).start()

    def last(t, carried):
        at = pl.ds(pl.multiple_of(t * 64, 64), 64)
        normed, _ = row_norm(mid[at, :])
        hidden[at, :] = (normed * gains[1:2, :]).astype(bf16)
        return carried

    lax.fori_loop(0, rows // 64, last, 0)
    leave(5).start()
    if hop:
        early.pump(3, onward=False)
        early.finish([1, 2], [2, 3])
        late.finish([1], [2])
    for i in range(7):
        leave(i).wait()
    for i in range(1, size):
        @pl.when(c + i < size)
        def _():
            give(i).wait_send()


def attend(hop, experts, tokens, small, cosine, sine, qkv_full, out_full, rows_all, collective_id):
    size, line = lax.axis_size("ctx"), lax.axis_size("exp") // 2
    rows, width = tokens.shape
    f32, bf16 = jnp.float32, jnp.bfloat16
    dma = pltpu.SemaphoreType.DMA
    vmem = pl.BlockSpec(memory_space=pltpu.VMEM)
    shape = jax.ShapeDtypeStruct
    made = (
        shape((QUERY_HEADS, rows, HEAD_WIDTH), bf16),
        shape((size, rows, 2 * KEY_VALUE_HEADS * HEAD_WIDTH), bf16),
        shape((rows, QUERY_HEADS * HEAD_WIDTH), bf16),
        shape((rows, 128), f32),
        shape((rows, width), f32),
        shape((rows, width), bf16),
        shape((8, width), f32),
    )
    return pl.pallas_call(
        functools.partial(attend_kernel, size, line, hop, experts, QUERY_HEADS, KEY_VALUE_HEADS),
        out_shape=made + (shape(rows_all.shape, bf16),),
        in_specs=[vmem] * 4 + [ANY] * 3,
        out_specs=(ANY,) * 8,
        input_output_aliases={6: 7},
        scratch_shapes=[pltpu.VMEM(one.shape, one.dtype) for one in made]
        + [
            pltpu.VMEM(qkv_full.shape, bf16),
            pltpu.VMEM(out_full.shape, bf16),
            pltpu.VMEM((rows, width), bf16),
            dma((2,)),
            dma((size - 1,)),
            dma((size - 1,)),
            dma((7,)),
        ]
        + (Gathering.scratch(line) * 2 if hop else []),
        compiler_params=pltpu.CompilerParams(
            collective_id=collective_id, has_side_effects=True, vmem_limit_bytes=62 << 20
        ),
        name="attend",
    )(tokens, small, cosine, sine, qkv_full, out_full, rows_all)


def halves(values):
    coarse = values.astype(jnp.bfloat16)
    return coarse, (values - coarse.astype(jnp.float32)).astype(jnp.bfloat16)


def backward_kernel(size, line, heads, kv_heads, experts, fused, *refs):
    back_part, out_part, grads, early_first, early_back, early_out, tokens, mid, final, marks, small, gains = refs[:12]
    queries, keyval, mixed, lse, cosine, sine, qkv_hbm, out_hbm, output, grad_tokens = refs[12:22]
    (dense_out, dense_q, dense_kv), refs = refs[22:25], refs[25:]
    if fused:
        totals, total_out, total_q, total_kv, land_one, land_two = refs[:6]
        landing, refs = refs[6:16], refs[16:]
        tmp = refs[0]
        sum_refs, refs = [refs[1 + 7 * i : 8 + 7 * i] for i in range(5)], refs[36:]
        total_scratch, refs = refs[:8], refs[8:]
        share_out, share_q, share_kv, refs = refs[:7], refs[7:14], refs[14:21], refs[21:]
    else:
        came, out_sum = back_part, out_part
    wqkv, wout, probs, d_scores, d_mixed, d_att, d_mid, h1, h2, dq, dkv, kv_part, kv_other, stage = refs[:14]
    w_sem, kv_send, kv_recv, s_sem = refs[14:]
    f32, bf16 = jnp.float32, jnp.bfloat16
    c, e = lax.axis_index("ctx"), lax.axis_index("exp")
    p, k = e // 2, e % 2
    rows, width = tokens.shape
    head = HEAD_WIDTH
    groups = heads // kv_heads
    q_width, kv_width = heads * head, kv_heads * head
    scaling = 1.0 / math.sqrt(head)
    keys_count = size * rows
    n = 2 * line
    shard = dense_out.shape[1]

    loads = [
        pltpu.make_async_copy(qkv_hbm, wqkv, w_sem.at[0]),
        pltpu.make_async_copy(out_hbm, wout, w_sem.at[1]),
    ]
    others = [lax.rem(c + i, size) for i in range(1, size)]
    column = [(p > 0, c, e - 2), (p < line - 1, c, e + 2), (True, c, e + 1 - 2 * k)]
    greet((column if fused else []) + [(True, there, e) for there in others])
    ticked = []

    def tick():
        if fused and len(ticked) < experts_total.ticks:
            experts_total.tick(len(ticked))
            ticked.append(1)

    if fused:
        experts_total = Totals(
            grads, early_first, *total_scratch[3:5], totals, land_one, land_two, total_scratch[:3], total_scratch[5:]
        )
        experts_total.begin()
        sums = [
            Summing(
                line, part, landing[2 * i], landing[2 * i + 1], sum_refs[i][0], tmp, sum_refs[i][1:],
                (early_back, early_out, None, None, None)[i],
            )
            for i, part in enumerate((back_part, out_part, dense_out, dense_q, dense_kv))
        ]
        back, outs, dense_outs, dense_qs, dense_kvs = sums
        came, out_sum = back.result(), outs.result()
        sharing_out = Sharing(dense_outs.result(), total_out, share_out[:4], share_out[4:])
        sharing_q = Sharing(dense_qs.result(), total_q, share_q[:4], share_q[4:])
        sharing_kv = Sharing(dense_kvs.result(), total_kv, share_kv[:4], share_kv[4:])
        back.begin()
    for copy in loads:
        copy.start()

    lane = lax.broadcasted_iota(jnp.int32, (rows, 128), 1)

    def keys_of(h):
        return keyval[:, :, pl.ds(pl.multiple_of(h * head, head), head)].reshape(keys_count, head)

    def values_of(h):
        return keyval[:, :, pl.ds(pl.multiple_of(kv_width + h * head, head), head)].reshape(keys_count, head)

    def again(j, carried):
        place = lax.broadcasted_iota(jnp.int32, (rows, keys_count), 1)
        row = c * rows + lax.broadcasted_iota(jnp.int32, (rows, keys_count), 0)
        scores = dot_nt(queries[j], keys_of(j // groups)) * scaling
        level = jnp.sum(jnp.where(lane == j, lse[...], 0.0), -1, keepdims=True)
        probs[j] = jnp.exp(jnp.where(place <= row, scores - level, NEG)).astype(bf16)
        return carried

    def norms(t, carried):
        at = pl.ds(pl.multiple_of(t * 64, 64), 64)
        normed, _ = row_norm(mid[at, :])
        h2[at, :] = (normed * gains[1:2, :]).astype(bf16)
        normed, _ = row_norm(tokens[at, :].astype(f32))
        h1[at, :] = (normed * gains[0:1, :]).astype(bf16)
        return carried

    bounds = [heads * i // max(1, line - 1) for i in range(line)]
    for i, d in enumerate(range(line - 1, 0, -1)):
        if fused and i > 0:
            back.step(d)
        if i == 0:
            lax.fori_loop(0, rows // 64, norms, 0)
        lax.fori_loop(bounds[i], bounds[i + 1], again, 0)
        tick()
        if fused and d == 2:
            outs.begin()
            tick()
    if fused:
        back.step(0)
        tick()

    logits = jnp.where(marks[...].astype(f32) > 0.5, dot(h2[...], small[...]), NEG)
    raised = jnp.exp(logits - jnp.max(logits, -1, keepdims=True))
    gates = raised / jnp.sum(raised, -1, keepdims=True)
    extra = came[:, width:].astype(f32)
    grad_gates = extra + pltpu.roll(extra, extra.shape[1] // 2, 1)
    grad_logits = gates * (grad_gates - jnp.sum(gates * grad_gates, -1, keepdims=True))
    logits_hi, logits_lo = halves(grad_logits)
    grad_small = dot_tn(h2[...], logits_hi) + dot_tn(h2[...], logits_lo)

    def second_norm(t, total):
        at = pl.ds(pl.multiple_of(t * 32, 32), 32)
        normed, inverse = row_norm(mid[at, :])
        low, high = halves(grad_logits_ref[at, :])
        grad_h2 = came[at, :width].astype(f32) + dot_nt(low, small[...]) + dot_nt(high, small[...])
        total = total + jnp.sum(grad_h2 * normed, 0, keepdims=True)
        scaled = grad_h2 * gains[1:2, :]
        grad = final[at, :].astype(f32) + inverse * (scaled - normed * jnp.mean(scaled * normed, -1, keepdims=True))
        d_mid[at, :] = grad
        d_att[at, :] = grad.astype(bf16)
        return total

    grad_logits_ref = dkv.at[:, 0:128]
    dkv[:, 0:128] = grad_logits
    gain_two = lax.fori_loop(0, rows // 32, second_norm, jnp.zeros((1, width), f32))

    loads[1].wait()

    def mixing(t, carried):
        at = pl.ds(pl.multiple_of(t * 256, 256), 256)
        block = dot_nt(d_att[...], wout[at, :]).astype(bf16)
        for i in range(2):
            d_mixed[2 * t + i] = block[:, i * head : (i + 1) * head]
        return carried

    lax.fori_loop(0, q_width // 256, mixing, 0)
    if fused and line > 2:
        outs.step(line - 2)
    tick()

    def gradients(left, right, dense, column, count):
        def store(t):
            return pltpu.make_async_copy(
                stage.at[lax.rem(t, 2)],
                dense.at[:, :, pl.ds(pl.multiple_of(column + t * 256, 128), 256)],
                s_sem.at[lax.rem(t, 2)],
            )

        def one(t, carried):
            @pl.when(t >= 2)
            def _():
                store(t - 2).wait()

            product = dot_tn(left[...], right[:, pl.ds(pl.multiple_of(t * 256, 256), 256)])
            stage[lax.rem(t, 2)] = product.astype(bf16).reshape(n, shard, 256)
            store(t).start()
            return carried

        lax.fori_loop(0, count, one, 0)
        for t in range(max(0, count - 2), count):
            store(jnp.int32(t)).wait()

    gradients(mixed, d_att, dense_out, 0, width // 256)
    if fused:
        dense_outs.begin()
        tick()
        for d in range(line - 3, 0, -1):
            outs.step(d)

    def per_head(j, carried):
        grad_probs = dot_nt(d_mixed[j], values_of(j // groups))
        weights_now = probs[j].astype(f32)
        inner = jnp.sum(weights_now * grad_probs, -1, keepdims=True)
        grad = (weights_now * (grad_probs - inner) * scaling).astype(bf16)
        d_scores[lax.rem(j, groups)] = grad
        back_q = dot(grad, keys_of(j // groups))
        dq[:, pl.ds(pl.multiple_of(j * head, head), head)] = turn(back_q, cosine[...], -sine[...]).astype(bf16)
        return carried

    for h in range(kv_heads):
        lax.fori_loop(h * groups, (h + 1) * groups, per_head, 0)
        these = slice(h * groups, (h + 1) * groups)
        grad_keys = dot_tn(
            d_scores[...].reshape(groups * rows, keys_count), queries[these].reshape(groups * rows, head)
        )
        grad_values = dot_tn(
            probs[these].reshape(groups * rows, keys_count), d_mixed[these].reshape(groups * rows, head)
        )
        kv_part[:, :, h * head : (h + 1) * head] = grad_keys.astype(bf16).reshape(size, rows, head)
        at = kv_width + h * head
        kv_part[:, :, at : at + head] = grad_values.astype(bf16).reshape(size, rows, head)
        if h == 0 and fused:
            tick()
            outs.step(0)

    def give(i):
        there = lax.rem(c + size - i, size)
        return remote(kv_part.at[there], kv_other.at[i - 1], kv_send.at[i - 1], kv_recv.at[i - 1], there, e)

    for i in range(1, size):
        @pl.when(c - i >= 0)
        def _():
            give(i).start()

    tick()
    if fused and line > 2:
        dense_outs.step(line - 2)
    gradients(h1, dq, dense_q, 0, q_width // 256)
    if fused:
        dense_qs.begin()
    tick()

    own = kv_part[c].astype(f32)
    dkv[...] = own
    for i in range(1, size):
        @pl.when(c + i < size)
        def _():
            give(i).wait_recv()
            dkv[...] += kv_other[i - 1].astype(f32)
    for j in range(kv_heads):
        at = slice(j * head, (j + 1) * head)
        dkv[:, at] = turn(dkv[:, at], cosine[...], -sine[...])
    dq[:, q_width:] = dkv[...].astype(bf16)
    dkv_low = dq.at[:, q_width:]
    gradients(h1, dkv_low, dense_kv, 0, 2 * kv_width // 256)
    if fused:
        for d in range(line - 3, 0, -1):
            dense_outs.step(d)
    loads[0].wait()

    def inputs(t, total):
        at = pl.ds(pl.multiple_of(t * 128, 128), 128)
        grad_h1 = dot_nt(dq[at, :], wqkv[...])
        normed, inverse = row_norm(tokens[at, :].astype(f32))
        total = total + jnp.sum(grad_h1 * normed, 0, keepdims=True)
        scaled = grad_h1 * gains[0:1, :]
        grad_tokens[at, :] = d_mid[at, :] + inverse * (
            scaled - normed * jnp.mean(scaled * normed, -1, keepdims=True)
        )
        return total

    gain_one = lax.fori_loop(0, rows // 128, inputs, jnp.zeros((1, width), f32))
    sub = lax.broadcasted_iota(jnp.int32, (128, width), 0)
    gain_rows = jnp.where(sub == experts, gain_one, jnp.where(sub == experts + 1, gain_two, 0.0))
    grad_small = (grad_small + gain_rows.T).astype(bf16).reshape(n, shard, 128)
    stage[0, :, :, 0:128] = grad_small
    small_store = pltpu.make_async_copy(
        stage.at[0, :, :, 0:128], dense_kv.at[:, :, 2 * kv_width :], s_sem.at[0]
    )
    small_store.start()
    small_store.wait()
    tick()
    if fused:
        dense_kvs.begin()

    def finish(t, carried):
        at = pl.ds(pl.multiple_of(t * 64, 64), 64)
        output[at, :] = (mid[at, :] + out_sum[at, :].astype(f32)).astype(bf16)
        return carried

    lax.fori_loop(0, rows // 64, finish, 0)
    if fused:
        dense_outs.step(0)
        sharing_out.begin()
        tick()
        for d in range(line - 2, -1, -1):
            dense_qs.step(d)
            if d == 0:
                sharing_q.begin()
            tick()
            if d == line - 2:
                sharing_out.second()
            dense_kvs.step(d)
            if d == line - 3:
                sharing_out.third()
        sharing_kv.begin()
        sharing_q.second()
        sharing_out.fourth()
        tick()
        sharing_kv.second()
        sharing_q.third()
        while len(ticked) < experts_total.ticks:
            tick()
        sharing_kv.third()
        sharing_q.fourth()
        sharing_kv.fourth()
        for one in sums:
            one.end()
        sharing_out.end()
        sharing_q.end()
        sharing_kv.end()
        experts_total.end()
    for i in range(1, size):
        @pl.when(c - i >= 0)
        def _():
            give(i).wait_send()


def backward(experts, shard, back_part, out_part, grads, early, tokens, mid, final, marks, small, gains, queries, keyval, mixed, lse,
             cosine, sine, qkv_full, out_full, collective_id):
    size, n = lax.axis_size("ctx"), lax.axis_size("exp")
    line = n // 2
    rows, width = tokens.shape
    heads, kv_heads, head = QUERY_HEADS, KEY_VALUE_HEADS, HEAD_WIDTH
    kv_both = 2 * kv_heads * head
    keys_count = size * rows
    f32, bf16 = jnp.float32, jnp.bfloat16
    dma = pltpu.SemaphoreType.DMA
    vmem = pl.BlockSpec(memory_space=pltpu.VMEM)
    shape = jax.ShapeDtypeStruct
    fused = planned(size, n, shard)
    dense_widths = (width, heads * head, kv_both + small.shape[1])
    shapes = [
        shape((rows, width), bf16),
        shape((rows, width), f32),
        *(shape((n, shard, wide), bf16) for wide in dense_widths),
    ]
    summing = []
    if fused:
        deep = grads.shape[0] // Totals.count
        shapes += [
            shape(grads.shape, bf16),
            *(shape((shard, wide), bf16) for wide in dense_widths),
        ]
        shapes += Totals.landing(deep, grads.shape[1])
        summed = [(rows, back_part.shape[2]), (rows, width)] + [(shard, wide) for wide in dense_widths]
        for high, wide in summed:
            shapes += Summing.landing(line, high, wide)
        widest = max(wide for _, wide in summed)
        summing = [
            pltpu.VMEM((2, rows, widest), bf16),
        ]
        for high, wide in summed:
            summing += Summing.scratch(line, high, wide)
        summing += Totals.scratch(deep, grads.shape[1])
        for wide in dense_widths:
            summing += Sharing.scratch(shard, wide)
    else:
        back_part = lax.psum_scatter(back_part, "exp", scatter_dimension=0)
        out_part = lax.psum_scatter(out_part, "exp", scatter_dimension=0)
    found = pl.pallas_call(
        functools.partial(backward_kernel, size, line, heads, kv_heads, experts, fused),
        out_shape=tuple(shapes),
        in_specs=[ANY if fused else vmem] * 2 + [ANY] * 4 + [vmem] * 12 + [ANY] * 2,
        out_specs=(vmem, vmem) + (ANY,) * (len(shapes) - 2),
        scratch_shapes=summing
        + [
            pltpu.VMEM(qkv_full.shape, bf16),
            pltpu.VMEM(out_full.shape, bf16),
            pltpu.VMEM((heads, rows, keys_count), bf16),
            pltpu.VMEM((heads // kv_heads, rows, keys_count), bf16),
            pltpu.VMEM((heads, rows, head), bf16),
            pltpu.VMEM((rows, width), bf16),
            pltpu.VMEM((rows, width), f32),
            pltpu.VMEM((rows, width), bf16),
            pltpu.VMEM((rows, width), bf16),
            pltpu.VMEM((rows, heads * head + kv_both), bf16),
            pltpu.VMEM((rows, kv_both), f32),
            pltpu.VMEM((size, rows, kv_both), bf16),
            pltpu.VMEM((size - 1, rows, kv_both), bf16),
            pltpu.VMEM((2, n, shard, 256), bf16),
            dma((2,)),
            dma((size - 1,)),
            dma((size - 1,)),
            dma((2,)),
        ],
        compiler_params=pltpu.CompilerParams(
            collective_id=collective_id, has_side_effects=True, vmem_limit_bytes=62 << 20
        ),
        name="backward",
    )(back_part, out_part, grads, *early, tokens, mid, final, marks, small, gains, queries, keyval, mixed, lse, cosine, sine,
      qkv_full, out_full)
    if fused:
        return found[:2] + found[5:9]
    dense = tuple(lax.psum_scatter(part, "exp", scatter_dimension=0) for part in found[2:5])
    return found[:2] + (lax.psum(grads, "ctx"),) + tuple(lax.psum(part, "ctx") for part in dense)


def widen_kernel(total, *refs):
    dense, (gate, up, down), dense_to, held, refs = refs[:3], refs[3:6], refs[6:9], refs[9], refs[10:]
    held_dense, wide, wide_dense, (in_sem, out_sem, dense_in, dense_done) = refs[:3], refs[3], refs[4:7], refs[7:]
    f32 = jnp.float32
    high = held.shape[1]
    blocks, slots = held.shape[0], wide.shape[0]
    per, tall = blocks // 3, gate.shape[1] // high

    def load(i):
        return pltpu.make_async_copy(total.at[pl.ds(i * high, high)], held.at[i], in_sem.at[i])

    def store(i):
        n, at = i // per, i % per
        if n < 2:
            target = (gate, up)[n].at[at // tall, pl.ds(at % tall * high, high)]
        else:
            target = down.at[at // tall, :, pl.ds(at % tall * high, high)]
        return pltpu.make_async_copy(wide.at[i % slots], target, out_sem.at[i % slots])

    small_in = [
        pltpu.make_async_copy(src, dst, dense_in.at[i])
        for i, (src, dst) in enumerate(zip(dense, held_dense))
    ]
    small_done = [
        pltpu.make_async_copy(src, dst, dense_done.at[i])
        for i, (src, dst) in enumerate(zip(wide_dense, dense_to))
    ]
    load(0).start()
    for copy in small_in:
        copy.start()
    for i in range(1, blocks):
        load(i).start()
    for i in range(blocks):
        load(i).wait()
        if i >= slots:
            store(i - slots).wait()
        wide[i % slots] = held[i].astype(f32)
        store(i).start()
        if i == 0:
            for copy in small_in:
                copy.wait()
            for src, dst in zip(held_dense, wide_dense):
                dst[...] = src[:, : dst.shape[1]].astype(f32)
            for copy in small_done:
                copy.start()
    for i in range(max(0, blocks - slots), blocks):
        store(i).wait()
    for copy in small_done:
        copy.wait()


def widen(total, parts, local, width, units, kv_both):
    f32 = jnp.float32
    blocks, slots = total.shape[0] // units, 4
    shape = jax.ShapeDtypeStruct
    dma = pltpu.SemaphoreType.DMA
    dense = [parts[0].shape, parts[1].shape, (parts[2].shape[0], kv_both)]
    return pl.pallas_call(
        widen_kernel,
        out_shape=(
            shape((local, width, units), f32),
            shape((local, width, units), f32),
            shape((local, units, width), f32),
            *(shape(one, f32) for one in dense),
        ),
        in_specs=[ANY] * 4,
        out_specs=(ANY,) * 6,
        scratch_shapes=[
            pltpu.VMEM((blocks, units, units), total.dtype),
            *(pltpu.VMEM(one.shape, one.dtype) for one in parts),
            pltpu.VMEM((slots, units, units), f32),
            *(pltpu.VMEM(one, f32) for one in dense),
            dma((blocks,)),
            dma((slots,)),
            dma((3,)),
            dma((3,)),
        ],
        compiler_params=pltpu.CompilerParams(vmem_limit_bytes=56 << 20),
        name="widen",
    )(total, *parts)


def rope_tables(first_row, row_count, head_size):
    half_size = head_size // 2
    frequency = ROPE_BASE ** (-jnp.arange(half_size, dtype=jnp.float32) * (2.0 / head_size))
    places = (first_row + jnp.arange(row_count, dtype=jnp.int32)).astype(jnp.float32)
    angles = places[:, None] * frequency[None, :]
    cosine = jnp.cos(angles)
    sine = jnp.sin(angles)
    return (jnp.concatenate([cosine, cosine], 1), jnp.concatenate([-sine, sine], 1))


def ein(spec, a, b):
    return jnp.einsum(spec, a, b, preferred_element_type=jnp.float32)


def shards(
    tokens,
    routes,
    gain_attn,
    w_query,
    key_value_weight,
    w_out,
    gain_ffn,
    w_router,
    w_gate,
    w_up,
    w_down,
    cotangent,
):
    f32 = jnp.float32
    bf16 = jnp.bfloat16
    rows, width = tokens.shape[1:]
    ctx_size, exp_size = lax.axis_size("ctx"), lax.axis_size("exp")
    ctx_index, exp_index = lax.axis_index("ctx"), lax.axis_index("exp")
    local_experts = w_gate.shape[0]
    experts = local_experts * exp_size
    top = routes.shape[2]
    capacity = 2 * rows * top // experts
    shard_rows = w_query.shape[0]
    heads, kv_heads, head = QUERY_HEADS, KEY_VALUE_HEADS, HEAD_WIDTH
    groups = heads // kv_heads
    q_width, kv_width = heads * head, kv_heads * head
    scaling = 1.0 / math.sqrt(head)
    first_row = ctx_index * rows

    named_own = jnp.max((routes[0][:, :, None] == jnp.arange(128, dtype=jnp.int32)).astype(bf16), axis=1)
    small = jnp.concatenate(
        [
            w_router,
            gain_attn[:, None],
            gain_ffn[:, None],
            jnp.zeros((shard_rows, 128 - experts - 2), bf16),
        ],
        1,
    )
    qkv_full, out_full, small_full, named, rows_all = gather_weights(
        (w_query, key_value_weight, w_out, small), named_own, cotangent[0], 1
    )

    cosine, sine = rope_tables(first_row, rows, head)
    hops = planned(ctx_size, exp_size, shard_rows)
    queries, keyval, mixed, lse, resid_mid, hidden_two, gains, rows_all = attend(
        hops, experts, tokens[0], small_full, cosine, sine, qkv_full, out_full, rows_all, 2
    )

    _, out_part, back_part, grads, _, *early = expert_pass(
        hops and exp_size > 6, hops, capacity, hidden_two, cotangent[0], rows_all, named, small_full, w_gate, w_up, w_down, 3
    )
    output, grad_input, grads, *dense = backward(
        experts, shard_rows, back_part, out_part, grads, early or [grads] * 3, tokens[0], resid_mid, cotangent[0], named_own, small_full, gains,
        queries, keyval, mixed, lse, cosine, sine, qkv_full, out_full, 4
    )
    small_total = dense[2][:, 2 * kv_width :].astype(f32)
    grad_gate, grad_up, grad_down, grad_out, grad_query, grad_keyval = widen(
        grads, dense, local_experts, width, w_gate.shape[2], 2 * kv_width
    )
    return (
        output[None],
        grad_input[None],
        small_total[:, experts],
        grad_query,
        grad_keyval,
        grad_out,
        small_total[:, experts + 1],
        small_total[:, :experts],
        grad_gate,
        grad_up,
        grad_down,
    )


def solution(mesh):
    rows, wide, deep = P("exp", "ctx", None), P("exp", None), P("exp", None, None)
    flat = P("exp")
    return jax.shard_map(
        shards,
        mesh=mesh,
        in_specs=(rows, rows, flat, wide, wide, wide, flat, wide, deep, deep, deep, rows),
        out_specs=(rows, rows, flat, wide, wide, wide, flat, wide, deep, deep, deep),
        check_vma=False,
    )
```

```python
import functools
import math

import jax
import jax.numpy as jnp
from jax import lax
from jax.experimental import pallas as pl
from jax.experimental.pallas import tpu as pltpu
from jax.sharding import PartitionSpec as P

MESH = pl.DeviceIdType.MESH
ANY = pl.BlockSpec(memory_space=pl.ANY)


def remote(src, dst, send, recv, ctx, exp):
    return pltpu.make_async_remote_copy(
        src_ref=src, dst_ref=dst, send_sem=send, recv_sem=recv, device_id=(ctx, exp), device_id_type=MESH
    )


def greet(pairs):
    barrier = pltpu.get_barrier_semaphore()
    count = 0
    for here, ctx, exp in pairs:
        if here is True:
            pl.semaphore_signal(barrier, inc=1, device_id=(ctx, exp), device_id_type=MESH)
            count = count + 1
        else:
            @pl.when(here)
            def _():
                pl.semaphore_signal(barrier, inc=1, device_id=(ctx, exp), device_id_type=MESH)
            count = count + here.astype(jnp.int32)
    pl.semaphore_wait(barrier, count)


QUERY_HEADS = 12
KEY_VALUE_HEADS = 2
HEAD_WIDTH = 128
EPS = 1e-06
NEG = -1e30
ROPE_BASE = 1000000.0


class Gathering:
    def __init__(self, line, own, out, sems, keep_own=True, window=None):
        self.line, self.keep_own = line, keep_own
        self.window = pl.ds(*window) if window is not None else pl.ds(0, out.shape[1])
        self.own, self.whole = own.at[self.window], out
        self.local_sem, self.z_send, self.z_recv, self.c_send, self.c_recv = sems
        self.c, self.e = lax.axis_index("ctx"), lax.axis_index("exp")
        self.p, self.k = self.e // 2, self.e % 2

    def block(self, q):
        return self.whole.at[2 * q + self.k, self.window]

    def along(self, q, src, to_right):
        there = self.e + 2 if to_right else self.e - 2
        way = 0 if to_right else 1
        return remote(src, self.block(q), self.z_send.at[way, q], self.z_recv.at[q], self.c, there)

    def across(self, q, src):
        there = self.e + 1 - 2 * self.k
        return remote(src, self.block(q), self.c_send.at[q], self.c_recv.at[q], self.c, there)

    def local(self):
        return pltpu.make_async_copy(self.own, self.whole.at[self.e, self.window], self.local_sem)

    def ends(self, d):
        for to_right in (True, False):
            q = self.p - d if to_right else self.p + d
            here = (q >= 0) if to_right else (q < self.line)
            further = (self.p < self.line - 1) if to_right else (self.p > 0)
            yield to_right, q, here, further

    def begin(self):
        for to_right, q, _, further in self.ends(0):
            @pl.when(further)
            def _():
                self.along(q, self.own, to_right).start()

        self.across(self.p, self.own).start()
        if self.keep_own:
            self.local().start()

    def pump(self, d, onward=True):
        for to_right, q, here, further in self.ends(d):
            @pl.when(here)
            def _():
                block = self.block(q)
                self.along(q, block, to_right).wait_recv()
                if onward:
                    @pl.when(further)
                    def _():
                        self.along(q, block, to_right).start()

                self.across(q, block).start()

    def forward(self, d):
        for to_right, q, here, further in self.ends(d):
            @pl.when(here & further)
            def _():
                self.along(q, self.block(q), to_right).start()

    def finish(self, sent, crossed):
        for d in crossed:
            for to_right, q, here, _ in self.ends(d):
                if d > 0 or to_right:
                    @pl.when(here)
                    def _():
                        self.across(q, self.own).wait()
        for d in sent:
            for to_right, q, here, further in self.ends(d):
                @pl.when(here & further)
                def _():
                    self.along(q, self.own, to_right).wait_send()

    def end(self, hops=None):
        last = self.line if hops is None else min(self.line, hops + 1)
        if self.keep_own:
            self.local().wait()
        self.finish(range(self.line if hops is None else last - 1), range(last))

    @staticmethod
    def scratch(line):
        dma = pltpu.SemaphoreType.DMA
        return [dma, dma((2, line)), dma((line,)), dma((line,)), dma((line,))]


def gather_kernel(line, own, out, *sems):
    c, e = lax.axis_index("ctx"), lax.axis_index("exp")
    greet([(e >= 2, c, e - 2), (e < 2 * line - 2, c, e + 2), (True, c, e + 1 - 2 * (e % 2))])
    gathering = Gathering(line, own, out, sems)
    gathering.begin()
    for d in range(1, line):
        gathering.pump(d)
    gathering.end()


def gather_rows(own, collective_id):
    n = lax.axis_size("exp")
    return pl.pallas_call(
        functools.partial(gather_kernel, n // 2),
        out_shape=jax.ShapeDtypeStruct((n,) + own.shape, own.dtype),
        in_specs=[ANY],
        out_specs=ANY,
        scratch_shapes=Gathering.scratch(n // 2),
        compiler_params=pltpu.CompilerParams(collective_id=collective_id, has_side_effects=True),
        name="gather_rows",
    )(own)


def add_rows(dst, a, b, rows):
    step = math.gcd(rows, 64)

    def body(i, carried):
        at = pl.ds(pl.multiple_of(i * step, step), step)
        dst[at, :] = a[at, :] + b[at, :]
        return carried

    lax.fori_loop(0, rows // step, body, 0)


class Summing:
    def __init__(self, line, part, cross, moving, acc, tmp, sems, early=None):
        self.line, self.part, self.cross, self.moving, self.early = line, part, cross, moving, early
        self.acc, self.tmp = acc, tmp
        self.own_sem, self.tmp_sem, self.c_send, self.c_recv, self.z_send, self.z_recv = sems
        self.c, self.e = lax.axis_index("ctx"), lax.axis_index("exp")
        self.p, self.k = self.e // 2, self.e % 2
        self.rows, self.width = part.shape[1:]

    def across(self, q):
        there = self.e + 1 - 2 * self.k
        return remote(
            self.part.at[2 * q + 1 - self.k], self.cross.at[q], self.c_send.at[q], self.c_recv.at[q], self.c, there
        )

    def own(self, q):
        return pltpu.make_async_copy(self.part.at[2 * q + self.k], self.acc.at[q], self.own_sem.at[q])

    def load(self, src, side):
        into = self.tmp.at[side, pl.ds(0, self.rows), pl.ds(0, self.width)]
        return pltpu.make_async_copy(src, into, self.tmp_sem.at[side])

    def add(self, q, side):
        add_rows(self.acc.at[q], self.acc.at[q], self.tmp.at[side, pl.ds(0, self.rows), pl.ds(0, self.width)], self.rows)

    def along(self, q, to_right):
        there = self.e + 2 if to_right else self.e - 2
        place = q if to_right else jnp.where(q == self.p - 1, self.line, q)
        return remote(self.acc.at[q], self.moving.at[place], self.z_send.at[q], self.z_recv.at[place], self.c, there)

    def arrived(self, place):
        return remote(self.acc.at[0], self.moving.at[place], self.z_send.at[0], self.z_recv.at[place], self.c, self.e)

    def ends(self, d):
        for to_right in (True, False):
            if d > 0 or to_right:
                q = self.p + d if to_right else self.p - d
                here = (q < self.line) if to_right else (q >= 0)
                behind = (self.p > 0) if to_right else (self.p < self.line - 1)
                if d == 1 and self.early is not None:
                    here = here & behind
                yield to_right, q, here, behind

    def begin(self):
        order = [(d, end) for d in range(self.line - 1, -1, -1) for end in self.ends(d)]
        for _, (_, q, here, _) in order:
            @pl.when(here)
            def _():
                self.across(q).start()
                self.own(q).start()
        for d, (to_right, q, here, behind) in order:
            side = 0 if to_right else 1

            @pl.when(here)
            def _():
                self.across(q).wait_recv()
                self.load(self.cross.at[q], side).start()
                self.own(q).wait()
                self.load(self.cross.at[q], side).wait()
                self.add(q, side)
                if d > 0:
                    @pl.when(jnp.logical_not(behind))
                    def _():
                        self.along(q, to_right).start()

    def step(self, d):
        if d > 0:
            for to_right, q, here, behind in self.ends(d):
                @pl.when(here & behind)
                def _():
                    self.arrived(q).wait_recv()
                    self.load(self.moving.at[q], 0 if to_right else 1).start()
            for to_right, q, here, behind in self.ends(d):
                @pl.when(here & behind)
                def _():
                    side = 0 if to_right else 1
                    self.load(self.moving.at[q], side).wait()
                    self.add(q, side)
                    self.along(q, to_right).start()
            return
        last = ((0, self.p, self.p > 0), (1, self.line, self.p < self.line - 1))
        for side, place, behind in last:
            if self.early is not None:
                from_end = (self.p == 1) if side == 0 else (self.p == self.line - 2)

                @pl.when(from_end)
                def _():
                    self.load(self.early, side).start()

                arrives = behind & jnp.logical_not(from_end)
            else:
                arrives = behind

            @pl.when(arrives)
            def _():
                self.arrived(place).wait_recv()
                self.load(self.moving.at[place], side).start()
        for side, place, behind in last:
            @pl.when(behind)
            def _():
                self.load(self.moving.at[place], side).wait()
                self.add(self.p, side)

    def result(self):
        return self.acc.at[self.p]

    def end(self):
        for d in range(self.line):
            for to_right, q, here, _ in self.ends(d):
                @pl.when(here)
                def _():
                    if d > 0:
                        self.along(q, to_right).wait_send()
                    self.across(q).wait_send()

    @staticmethod
    def scratch(line, rows, width):
        dma = pltpu.SemaphoreType.DMA
        return [
            pltpu.VMEM((line, rows, width), jnp.bfloat16),
            dma((line,)),
            dma((2,)),
            dma((line,)),
            dma((line,)),
            dma((line,)),
            dma((line + 1,)),
        ]

    @staticmethod
    def landing(line, rows, width):
        return [
            jax.ShapeDtypeStruct((line, rows, width), jnp.bfloat16),
            jax.ShapeDtypeStruct((line + 1, rows, width), jnp.bfloat16),
        ]


class Totals:
    ahead, lag, count, early = 4, 1, 12, 4

    def __init__(self, part, early_first, sends, recvs, total=None, first=None, second=None, buffers=None, sems=None):
        self.part, self.total, self.early_first, self.first, self.second = part, total, early_first, first, second
        self.sends, self.recvs = sends, recvs
        if buffers is not None:
            self.own, self.got, self.got_two = buffers
            self.load_sem, self.got_sem, self.store_sem = sems
            self.slots = self.own.shape[0]
        c, self.e = lax.axis_index("ctx"), lax.axis_index("exp")
        self.bits = (c % 2, c // 2)
        self.nbrs = (c + 1 - 2 * (c % 2), lax.rem(c + 2, 4))
        self.deep = part.shape[0] // self.count

    def axes(self, h):
        return (0, 1) if h == 0 else (1, 0)

    def rows(self, ref, t, h, kept_one, kept_two=None, mine_two=True):
        one, two = self.axes(h)
        quarter, eighth = self.deep // 4, self.deep // 8
        bit = self.bits[one] if kept_one else 1 - self.bits[one]
        start = t * self.deep + h * (self.deep // 2) + bit * quarter
        if kept_two is None:
            return ref.at[pl.ds(pl.multiple_of(start, 16), quarter), :]
        return ref.at[pl.ds(pl.multiple_of(start + self.bits[two] * eighth, 16), eighth), :]

    def piece(self, t, h, kept):
        eighth = self.deep // 8
        bit = self.bits[self.axes(h)[1]]
        start = (bit if kept else 1 - bit) * eighth
        return self.own.at[t % self.slots, h, pl.ds(pl.multiple_of(start, 16), eighth), :]

    def copy(self, stage, t, h):
        one, two = self.axes(h)
        if stage == 0:
            src, dst, there = self.rows(self.part, t, h, False), self.landed(t, h), one
        elif stage == 1:
            src, dst, there = self.piece(t, h, False), self.second.at[t, h], two
        elif stage == 2:
            src, dst, there = self.piece(t, h, True), self.rows(self.total, t, h, True, True), two
        else:
            src, dst, there = self.rows(self.total, t, h, True), self.rows(self.total, t, h, True), one
        return remote(src, dst, self.sends.at[stage, t, h], self.recvs.at[stage, t, h], self.nbrs[there], self.e)

    def landed(self, t, h):
        return self.early_first.at[t, h] if t < self.early else self.first.at[t - self.early, h]

    def start_early(self, t):
        for h in range(2):
            self.copy(0, t, h).start()

    def end_early(self):
        for t in range(self.early):
            for h in range(2):
                self.copy(0, t, h).wait()

    def load_own(self, t, h):
        return pltpu.make_async_copy(
            self.rows(self.part, t, h, True), self.own.at[t % self.slots, h], self.load_sem.at[t % 2, h]
        )

    def store(self, t, h):
        return pltpu.make_async_copy(
            self.piece(t, h, True), self.rows(self.total, t, h, True, True), self.store_sem.at[t % self.slots, h]
        )

    def begin(self):
        for t in range(self.early, min(self.early + self.ahead, self.count)):
            for h in range(2):
                self.copy(0, t, h).start()
        for h in range(2):
            self.load_own(0, h).start()

    @property
    def ticks(self):
        return self.count + 2 * self.lag

    def tick(self, t):
        count, lag = self.count, self.lag
        t_two, t_three = t - lag, t - 2 * lag
        loads = []
        if t < count:
            for h in range(2):
                if t >= self.early:
                    self.copy(0, t, h).wait_recv()
                came = pltpu.make_async_copy(self.landed(t, h), self.got.at[h], self.got_sem.at[0, h])
                came.start()
                loads.append(came)
            if t + self.early + self.ahead < count:
                for h in range(2):
                    self.copy(0, t + self.early + self.ahead, h).start()
        later = []
        if 0 <= t_two < count:
            for h in range(2):
                self.copy(1, t_two, h).wait_recv()
                came = pltpu.make_async_copy(self.second.at[t_two, h], self.got_two.at[h], self.got_sem.at[1, h])
                came.start()
                later.append(came)
        if t < count:
            for h in range(2):
                self.load_own(t, h).wait()
                loads[h].wait()
                mine = self.own.at[t % self.slots, h]
                add_rows(mine, mine, self.got.at[h], self.deep // 4)
                self.copy(1, t, h).start()
        if 0 <= t_two < count:
            for h in range(2):
                later[h].wait()
                mine = self.piece(t_two, h, True)
                add_rows(mine, mine, self.got_two.at[h], self.deep // 8)
                self.copy(2, t_two, h).start()
                self.store(t_two, h).start()
        if 0 <= t_three < count:
            for h in range(2):
                self.copy(2, t_three, h).wait_recv()
                self.store(t_three, h).wait()
                self.copy(3, t_three, h).start()
                self.copy(1, t_three, h).wait_send()
                self.copy(2, t_three, h).wait_send()
        if t + 1 < count:
            for h in range(2):
                self.load_own(t + 1, h).start()

    def end(self):
        for t in range(self.count):
            for h in range(2):
                if t >= self.early:
                    self.copy(0, t, h).wait_send()
                self.copy(3, t, h).wait()

    @staticmethod
    def early_scratch():
        dma = pltpu.SemaphoreType.DMA
        return [dma((1, Totals.early, 2)), dma((1, Totals.early, 2))]

    @staticmethod
    def early_landing(deep, width):
        return jax.ShapeDtypeStruct((Totals.early, 2, deep // 4, width), jnp.bfloat16)

    @staticmethod
    def scratch(deep, width):
        count = Totals.count
        dma = pltpu.SemaphoreType.DMA
        slots = 2 * Totals.lag + 1
        return [
            pltpu.VMEM((slots, 2, deep // 4, width), jnp.bfloat16),
            pltpu.VMEM((2, deep // 4, width), jnp.bfloat16),
            pltpu.VMEM((2, deep // 8, width), jnp.bfloat16),
            dma((4, count, 2)),
            dma((4, count, 2)),
            dma((2, 2)),
            dma((2, 2)),
            dma((slots, 2)),
        ]

    @staticmethod
    def landing(deep, width):
        return [
            jax.ShapeDtypeStruct((Totals.count - Totals.early, 2, deep // 4, width), jnp.bfloat16),
            jax.ShapeDtypeStruct((Totals.count, 2, deep // 8, width), jnp.bfloat16),
        ]


class Sharing:
    def __init__(self, part, total, landed, sems):
        self.part, self.total = part, total
        self.one, self.two = landed[:2], landed[2:]
        self.sends, self.recvs, self.store_sem = sems
        c, self.e = lax.axis_index("ctx"), lax.axis_index("exp")
        self.bits = (c % 2, c // 2)
        self.nbrs = (c + 1 - 2 * (c % 2), lax.rem(c + 2, 4))
        self.rows, self.width = part.shape

    @staticmethod
    def columns(width):
        first = width // 256 * 128
        return ((0, first), (first, width - first))

    def window(self, ref, h, kept_one, kept_two=None):
        one, two = (0, 1) if h == 0 else (1, 0)
        half, quarter = self.rows // 2, self.rows // 4
        start = (self.bits[one] if kept_one else 1 - self.bits[one]) * half
        count = half
        if kept_two is not None:
            start = start + (self.bits[two] if kept_two else 1 - self.bits[two]) * quarter
            count = quarter
        return ref.at[pl.ds(pl.multiple_of(start, 16), count), pl.ds(*self.columns(self.width)[h])]

    def copy(self, stage, h):
        one, two = (0, 1) if h == 0 else (1, 0)
        if stage == 0:
            src, dst, there = self.window(self.part, h, False), self.one[h], one
        elif stage == 1:
            src, dst, there = self.window(self.part, h, True, False), self.two[h], two
        elif stage == 2:
            src, dst, there = self.window(self.part, h, True, True), self.window(self.total, h, True, True), two
        else:
            src, dst, there = self.window(self.total, h, True), self.window(self.total, h, True), one
        return remote(src, dst, self.sends.at[stage, h], self.recvs.at[stage, h], self.nbrs[there], self.e)

    def store(self, h):
        return pltpu.make_async_copy(
            self.window(self.part, h, True, True), self.window(self.total, h, True, True), self.store_sem.at[h]
        )

    def begin(self):
        for h in range(2):
            self.copy(0, h).start()

    def second(self):
        for h in range(2):
            self.copy(0, h).wait_recv()
            kept = self.window(self.part, h, True)
            add_rows(kept, kept, self.one[h], self.rows // 2)
            self.copy(1, h).start()

    def third(self):
        for h in range(2):
            self.copy(1, h).wait_recv()
            kept = self.window(self.part, h, True, True)
            add_rows(kept, kept, self.two[h], self.rows // 4)
            self.copy(2, h).start()
            self.store(h).start()

    def fourth(self):
        for h in range(2):
            self.store(h).wait()
            self.copy(2, h).wait_recv()
            self.copy(3, h).start()

    def end(self):
        for h in range(2):
            for stage in range(3):
                self.copy(stage, h).wait_send()
            self.copy(3, h).wait()

    @staticmethod
    def scratch(rows, width):
        dma = pltpu.SemaphoreType.DMA
        wide = [count for _, count in Sharing.columns(width)]
        return [
            *(pltpu.VMEM((rows // 2, one), jnp.bfloat16) for one in wide),
            *(pltpu.VMEM((rows // 4, one), jnp.bfloat16) for one in wide),
            dma((4, 2)),
            dma((4, 2)),
            dma((2,)),
        ]


def weights_kernel(line, quarter, *refs):
    count = 3
    own, own_mask, own_block = refs[: count + 1], refs[count + 1], refs[count + 2]
    refs = refs[1:]
    out, masks, blocks = refs[count + 2 : 2 * count + 2], refs[2 * count + 2], refs[2 * count + 3]
    held, refs = refs[2 * count + 4 : 3 * count + 4], refs[3 * count + 4 :]
    local_sem, own_send, own_recv, z_send, z_recv, xy_send, xy_recv, d_send, d_recv, c_send, c_recv = refs[:-10]
    c, e = lax.axis_index("ctx"), lax.axis_index("exp")
    p, k = e // 2, e % 2
    sibling = e + 1 - 2 * k
    rows, split = own[0].shape
    places = (held[0].at[:, 0:split], held[0].at[:, split:], *held[1:])
    loads = [pltpu.make_async_copy(src, dst, local_sem.at[0, i]) for i, (src, dst) in enumerate(zip(own, places))]
    for copy in loads:
        copy.start()
    nbr = (c + 1 - 2 * (c % 2), (c + 2) % 4)
    opposite = 3 - c
    greet(
        [
            (p > 0, c, e - 2),
            (p < line - 1, c, e + 2),
            (True, c, sibling),
            (True, nbr[0], e),
            (True, nbr[1], e),
        ]
    )

    def whole(a):
        return out[a].at[pl.ds(pl.multiple_of(e * rows, 16), rows), :]

    def piece(a, q, column):
        return out[a].at[pl.ds(pl.multiple_of((2 * q + k) * rows + column * quarter, 16), quarter), :]

    def own_piece(a):
        return held[a].at[pl.ds(pl.multiple_of(c * quarter, 16), quarter), :]

    def local(a):
        return pltpu.make_async_copy(held[a], whole(a), local_sem.at[1, a])

    def own_across(a):
        return remote(held[a], whole(a), own_send.at[a], own_recv.at[a], c, sibling)

    def along(a, q, src, to_right):
        there = e + 2 if to_right else e - 2
        way = 0 if to_right else 1
        return remote(src, piece(a, q, c), z_send.at[way, q, a], z_recv.at[q, a], c, there)

    def beside(a, q, axis):
        return remote(piece(a, q, c), piece(a, q, c), xy_send.at[axis, q, a], xy_recv.at[axis, q, a], nbr[axis], e)

    def onward(a, q):
        came, goes = (0, 1) if a == 0 else (1, 0)
        block = piece(a, q, nbr[came])
        return remote(block, block, d_send.at[q, a], d_recv.at[q, a], nbr[goes], e)

    def across(a, q, j):
        column = (c, nbr[0], nbr[1], opposite)[j]
        block = piece(a, q, column)
        return remote(block, block, c_send.at[q, j, a], c_recv.at[q, j, a], c, sibling)

    for copy in loads:
        copy.wait()
    arrays = range(count)
    marking = Gathering(line, own_mask, masks, refs[-10:-5])
    gathering = Gathering(line, own_block, blocks, refs[-5:], keep_own=False)
    marking.begin()
    for a in arrays:
        @pl.when(p < line - 1)
        def _():
            along(a, p, own_piece(a), True).start()

        @pl.when(p > 0)
        def _():
            along(a, p, own_piece(a), False).start()
    for a in arrays:
        own_across(a).start()
        local(a).start()

    def ends(d):
        for to_right in (True, False):
            q = p - d if to_right else p + d
            yield to_right, q, ((q >= 0) if to_right else (q < line))

    for d in range(1, line + 1):
        if d < line:
            for to_right, q, here in ends(d):
                further = (p < line - 1) if to_right else (p > 0)

                @pl.when(here)
                def _():
                    for a in arrays:
                        along(a, q, piece(a, q, c), to_right).wait_recv()

                        @pl.when(further)
                        def _():
                            along(a, q, piece(a, q, c), to_right).start()

                        beside(a, q, 0).start()
                        beside(a, q, 1).start()
                        across(a, q, 0).start()
        if d < line:
            marking.pump(d)
        if d == line - 1:
            gathering.begin()
        if d > 1:
            for to_right, q, here in ends(d - 1):
                @pl.when(here)
                def _():
                    for a in arrays:
                        came = 0 if a == 0 else 1
                        beside(a, q, came).wait_recv()
                        onward(a, q).start()
                        across(a, q, 1 + came).start()
                        beside(a, q, 1 - came).wait_recv()
                        across(a, q, 2 - came).start()
    for d in range(1, line):
        for to_right, q, here in ends(d):
            @pl.when(here)
            def _():
                for a in arrays:
                    onward(a, q).wait_recv()
                    across(a, q, 3).start()
    gathering.pump(1, onward=False)
    gathering.end(1)
    marking.end()
    for a in arrays:
        local(a).wait()
        own_across(a).wait()
    for d in range(0, line):
        for to_right, q, here in ends(d):
            further = (p < line - 1) if to_right else (p > 0)
            for a in arrays:
                @pl.when(here & further)
                def _():
                    along(a, q, piece(a, q, c), to_right).wait_send()
                if d > 0:
                    @pl.when(here)
                    def _():
                        beside(a, q, 0).wait_send()
                        beside(a, q, 1).wait_send()
                        onward(a, q).wait_send()
                        for j in range(4):
                            across(a, q, j).wait()


def planned(size, n, shard_rows):
    return size == 4 and n == 8 and (shard_rows // 4) % 16 == 0


def gather_weights(shards, mask, block, collective_id):
    n = lax.axis_size("exp")
    rows, high = shards[0].shape[0], n * shards[0].shape[0]
    if not planned(lax.axis_size("ctx"), n, rows):
        shards = (jnp.concatenate(shards[:2], 1), *shards[2:])
        whole = tuple(lax.all_gather(w, "exp", axis=0, tiled=True) for w in shards)
        return whole + (lax.all_gather(mask, "exp", axis=0), gather_rows(block, collective_id))
    line = n // 2
    count = len(shards) - 1
    widths = (shards[0].shape[1] + shards[1].shape[1], *(w.shape[1] for w in shards[2:]))
    dtype = mask.dtype
    dma = pltpu.SemaphoreType.DMA
    return pl.pallas_call(
        functools.partial(weights_kernel, line, rows // 4),
        out_shape=tuple(jax.ShapeDtypeStruct((high, wide), dtype) for wide in widths)
        + tuple(jax.ShapeDtypeStruct((n,) + w.shape, w.dtype) for w in (mask, block)),
        in_specs=[ANY] * (count + 3),
        out_specs=(ANY,) * (count + 2),
        scratch_shapes=[pltpu.VMEM((rows, wide), dtype) for wide in widths]
        + [
            dma((2, count + 1)),
            dma((count,)),
            dma((count,)),
            dma((2, line, count)),
            dma((line, count)),
            dma((2, line, count)),
            dma((2, line, count)),
            dma((line, count)),
            dma((line, count)),
            dma((line, 4, count)),
            dma((line, 4, count)),
        ]
        + Gathering.scratch(line)
        + Gathering.scratch(line),
        compiler_params=pltpu.CompilerParams(
            collective_id=collective_id, has_side_effects=True, vmem_limit_bytes=62 << 20
        ),
        name="gather_weights",
    )(*shards, mask, block)


def dot(a, b):
    return lax.dot_general(a, b, (((1,), (0,)), ((), ())), preferred_element_type=jnp.float32)


def dot_nt(a, b):
    return lax.dot_general(a, b, (((1,), (1,)), ((), ())), preferred_element_type=jnp.float32)


def dot_tn(a, b):
    return lax.dot_general(a, b, (((0,), (0,)), ((), ())), preferred_element_type=jnp.float32)


def visit(p, line, i):
    both = jnp.minimum(p, line - 1 - p)
    d = jnp.where(i <= 2 * both, (i + 1) // 2, i - both)
    left = jnp.where(i <= 2 * both, i % 2 == 1, p > line - 1 - p)
    q = jnp.where(left, p - d, p + d)
    first = (i == 0) | (i > 2 * both) | (i % 2 == 1)
    return q, d, first


def expert_kernel(line, local, cap, hop, start, hidden, own_grads, grads_in, named, router, w_gate, w_up, w_down, *refs):
    hidden_all, out_part, back_part, grads, grads_all = refs[:5]
    if start:
        early_first, early_sums, refs = refs[5], refs[6:8], refs[:5] + refs[8:]
    wg, wu, wd, xs, ds, act, dg, du, es, h_buf, y_buf, out_stage, back_stage, in_stage, down_stage = refs[5:20]
    picks, xs_turned, act_turned, gate_kept, refs = *refs[20:24], refs[:20] + refs[24:]
    if start:
        crossed, refs = refs[20:22], refs[:20] + refs[22:]
        hop_sem, refs = refs[-1], refs[:-1]
    w_sem, own_sem, z_send, z_recv, c_send, c_recv, h_sem, y_sem, o_sem, b_sem, s_sem = refs[20:31]
    f32, bf16 = jnp.float32, jnp.bfloat16
    c, e = lax.axis_index("ctx"), lax.axis_index("exp")
    p, k = e // 2, e % 2
    sibling = e + 1 - 2 * k
    rows, width = hidden.shape
    hidden_units = wg.shape[2]
    slots = 2 * cap
    lanes = router.shape[1]

    loads = [
        pltpu.make_async_copy(src, dst, w_sem.at[i])
        for i, (src, dst) in enumerate(((w_gate, wg), (w_up, wu), (w_down, wd)))
    ]
    for copy in loads:
        copy.start()
    beside = [(True, c + 1 - 2 * (c % 2), e), (True, lax.rem(c + 2, 4), e)] if start else []
    greet([(p > 0, c, e - 2), (p < line - 1, c, e + 2), (True, c, sibling)] + beside)
    def along(q, src, to_right):
        there = e + 2 if to_right else e - 2
        return remote(src, hidden_all.at[2 * q + k], z_send.at[0 if to_right else 1, q], z_recv.at[q], c, there)

    def across(q, src):
        return remote(src, hidden_all.at[2 * q + k], c_send.at[q], c_recv.at[q], c, sibling)

    def load_hidden(q, slot):
        return pltpu.make_async_copy(hidden_all.at[pl.ds(2 * q, 2)], h_buf.at[slot], h_sem.at[slot])

    def load_grads(q, slot):
        return pltpu.make_async_copy(grads_all.at[pl.ds(2 * q, 2)], y_buf.at[slot], y_sem.at[slot])

    def load_own(buf, own, blocks, i):
        return [
            pltpu.make_async_copy(own, buf.at[0, k], own_sem.at[2 * i]),
            pltpu.make_async_copy(blocks.at[sibling], buf.at[0, 1 - k], own_sem.at[2 * i + 1]),
        ]

    def store_out(q, slot):
        return pltpu.make_async_copy(out_stage.at[slot], out_part.at[pl.ds(2 * q, 2)], o_sem.at[slot])

    def store_back(q, slot):
        return pltpu.make_async_copy(back_stage.at[slot], back_part.at[pl.ds(2 * q, 2)], b_sem.at[slot])

    @pl.when(p < line - 1)
    def _():
        along(p, hidden, True).start()

    @pl.when(p > 0)
    def _():
        along(p, hidden, False).start()

    across(p, hidden).start()
    if hop:
        hops = Gathering(line, grads_all.at[e], grads_all, refs[31:36], window=(rows // 2, rows // 2))
        hops.forward(2)
    for copy in load_own(y_buf, own_grads, grads_all, 0):
        copy.start()

    def pump(d):
        for to_right in (True, False):
            q = p - d if to_right else p + d
            here = (q >= 0) if to_right else (q < line)
            further = (p < line - 1) if to_right else (p > 0)

            @pl.when(here)
            def _():
                block = hidden_all.at[2 * q + k]
                along(q, block, to_right).wait_recv()

                @pl.when(further)
                def _():
                    along(q, block, to_right).start()

                across(q, block).start()

    for copy in loads:
        copy.wait()

    lane = lax.broadcasted_iota(jnp.int32, (local * cap, lanes), 1)
    expert_of_row = lax.broadcasted_iota(jnp.int32, (local * cap, lanes), 0) // cap

    def units_of(j, q):
        tile = 256
        rows_j = xs[j].reshape(slots, width)
        xs_turned[j, :, pl.ds(pl.multiple_of(q * slots, slots), slots)] = rows_j.T
        grads_j = ds[j, q].reshape(slots, width)

        def units(t, carried):
            at = pl.ds(pl.multiple_of(t * tile, tile), tile)
            gate_pre = dot(rows_j, wg[j, :, at])
            up_pre = dot(rows_j, wu[j, :, at])
            grad_act = dot_nt(grads_j, wd[j, at, :])
            sigmoid = 1.0 / (1.0 + jnp.exp(-gate_pre))
            silu = gate_pre * sigmoid
            hidden_low = (silu * up_pre).astype(bf16)
            act[j, :, at] = hidden_low
            act_turned[j, at, pl.ds(pl.multiple_of(q * slots, slots), slots)] = hidden_low.T
            dg[j, q, :, at] = (grad_act * up_pre * sigmoid * (1.0 + gate_pre * (1.0 - sigmoid))).astype(bf16)
            du[j, q, :, at] = (grad_act * silu).astype(bf16)
            return carried

        lax.fori_loop(0, hidden_units // tile, units, 0)

    def give_back(q, slot):
        wide = 512
        pick_pair = [picks[b] for b in range(2)]

        def outputs(t, sums):
            at = pl.ds(pl.multiple_of(t * wide, wide), wide)
            gated, back, new_sums = [], [], []
            for j in range(local):
                y = dot(act[j], wd[j, :, at])
                back_j = dot_nt(dg[j, q], wg[j, at, :]) + dot_nt(du[j, q], wu[j, at, :])
                new = []
                for b in range(2):
                    half = slice(b * cap, (b + 1) * cap)
                    y_b = y[half]
                    new.append(sums[j][b] + jnp.sum(y_b * es[j, b, :, at].astype(f32), -1, keepdims=True))
                    gated.append((gate_kept[b, j * cap : (j + 1) * cap, 0:1] * y_b).astype(bf16))
                    back.append(back_j[half].astype(bf16))
                new_sums.append(tuple(new))
            for b in range(2):
                mine = jnp.concatenate([gated[2 * j + b] for j in range(local)], 0)
                out_stage[slot, b, :, at] = dot_tn(pick_pair[b], mine).astype(bf16)
                mine = jnp.concatenate([back[2 * j + b] for j in range(local)], 0)
                back_stage[slot, b, :, at] = dot_tn(pick_pair[b], mine).astype(bf16)
            return tuple(new_sums)

        nothing = jnp.zeros((cap, 1), f32)
        sums = lax.fori_loop(
            0, width // wide, outputs, tuple((nothing, nothing) for _ in range(local))
        )
        for b in range(2):
            grad_gates = jnp.concatenate([sums[j][b] for j in range(local)], 0)
            coarse = grad_gates.astype(bf16).astype(f32)
            spot = e * local + expert_of_row
            spread = jnp.where(
                lane == spot, coarse, jnp.where(lane == spot + lanes // 2, grad_gates - coarse, 0.0)
            ).astype(bf16)
            back_stage[slot, b, :, width : width + lanes] = dot_tn(pick_pair[b], spread).astype(bf16)
        store_out(q, slot).start()
        store_back(q, slot).start()

    at_end = (p == 0) | (p == line - 1)

    def cross_over(n):
        stage = (back_stage, out_stage)[n]
        return remote(stage.at[1, 1 - k], crossed[n], hop_sem.at[n, 0], hop_sem.at[n, 1], c, sibling)

    def send_ahead(n):
        there = jnp.where(p == 0, e + 2, e - 2)
        return remote(crossed[n], early_sums[n], hop_sem.at[n, 2], hop_sem.at[n, 3], c, there)

    def one_chip(i, carried):
        q, d, first = visit(p, line, i)
        slot = i % 2

        across(q, hidden).wait_recv()

        @pl.when(i == 0)
        def _():
            own = load_own(h_buf, hidden, hidden_all, 1)
            for copy in own:
                copy.start()
            for copy in own + load_own(y_buf, own_grads, grads_all, 0):
                copy.wait()

        @pl.when(i > 0)
        def _():
            load_hidden(q, slot).start()

        if hop:
            @pl.when(d == line - 1)
            def _():
                hops.pump(line - 1, onward=False)
                hops.finish([], [line - 1])
                load_grads(q, slot).start()

        after, d_after, _ = visit(p, line, i + 1)

        @pl.when((i < line - 1) & (d_after < (line - 1 if hop else line)))
        def _():
            load_grads(after, 1 - slot).start()

        @pl.when(i > 0)
        def _():
            load_hidden(q, slot).wait()
            load_grads(q, slot).wait()

        @pl.when(i >= 2)
        def _():
            store_out(visit(p, line, i - 2)[0], slot).wait()
            store_back(visit(p, line, i - 2)[0], slot).wait()

        place = lax.broadcasted_iota(jnp.int32, (cap, rows), 0).astype(f32)
        sub = lax.broadcasted_iota(jnp.int32, (lanes, rows), 0)
        upper = lax.broadcasted_iota(jnp.int32, (rows, 2 * rows), 0)
        column = lax.broadcasted_iota(jnp.int32, (rows, 2 * rows), 1)
        ahead = jnp.where((upper < column) & (column < rows) | (upper + rows == column), 1.0, 0.0).astype(bf16)
        for b in range(2):
            marks = named[2 * q + b]
            counted = dot_tn(marks, ahead)
            slots_of = jnp.where(counted[:, rows:] > 0.5, counted[:, :rows], -1.0)
            for j in range(local):
                row = jnp.sum(jnp.where(sub == e * local + j, slots_of, 0.0), 0, keepdims=True)
                picks[b, j * cap : (j + 1) * cap] = jnp.where(place == row, 1.0, 0.0).astype(bf16)
            pick = picks[b]
            block = h_buf[slot, b]
            picked = dot(pick, block).astype(bf16)
            for j in range(local):
                xs[j, b] = picked[j * cap : (j + 1) * cap]
            logits = jnp.where(marks.astype(f32) > 0.5, dot(block, router[...]), NEG)
            raised = jnp.exp(logits - jnp.max(logits, -1, keepdims=True))
            gates = raised / jnp.sum(raised, -1, keepdims=True)
            coarse = gates.astype(bf16)
            fine = (gates - coarse.astype(f32)).astype(bf16)
            at_slots = dot(pick, coarse) + dot(pick, fine)
            gate_slot = jnp.sum(jnp.where(lane == e * local + expert_of_row, at_slots, 0.0), -1, keepdims=True)
            gate_kept[b] = jnp.broadcast_to(gate_slot, gate_kept.shape[1:])
            grad_rows = dot(pick, y_buf[slot, b])
            grad_pairs = (gate_slot * grad_rows).astype(bf16)
            grad_rows = grad_rows.astype(bf16)
            for j in range(local):
                es[j, b] = grad_rows[j * cap : (j + 1) * cap]
                ds[j, q, b] = grad_pairs[j * cap : (j + 1) * cap]

        units_of(0, q)

        @pl.when(i < line - 1)
        def _():
            for j in range(1, local):
                units_of(j, q)
            give_back(q, slot)

        @pl.when(first & (d + 1 < line))
        def _():
            pump(d + 1)

        if start:
            @pl.when(at_end & (i == 1))
            def _():
                for n in range(2):
                    cross_over(n).start()

            @pl.when(at_end & (i == 2))
            def _():
                for n, stage in enumerate((back_stage, out_stage)):
                    cross_over(n).wait()
                    add_rows(crossed[n], crossed[n], stage.at[1, k], rows)
                    send_ahead(n).start()

        return carried

    lax.fori_loop(0, line, one_chip, 0)

    deep = line * slots
    tile = 256
    tiles = hidden_units // tile

    def products(left, right, stage, first_row, count):
        high = stage.shape[1]

        def stores(t):
            row = first_row + lax.div(t, tiles) * high
            return pltpu.make_async_copy(
                stage.at[lax.rem(t, 2)],
                grads.at[
                    pl.ds(pl.multiple_of(row, 16), high),
                    pl.ds(pl.multiple_of(lax.rem(t, tiles) * tile, tile), tile),
                ],
                s_sem.at[lax.rem(t, 2)],
            )

        def one_tile(t, carried):
            @pl.when(t >= 2)
            def _():
                stores(t - 2).wait()

            stage[lax.rem(t, 2)] = dot(left[...], right(pl.ds(pl.multiple_of(t * tile, tile), tile))).astype(bf16)
            stores(t).start()
            return carried

        lax.fori_loop(0, count, one_tile, 0)
        for t in range(max(0, count - 2), count):
            stores(jnp.int32(t)).wait()

    totals = Totals(grads, early_first, *refs[-2:]) if start else None
    sent = 0

    def send_ready(rows_done):
        nonlocal sent
        while start and sent < totals.early and (sent + 1) * totals.deep <= rows_done:
            totals.start_early(sent)
            sent += 1

    last_chip = visit(p, line, jnp.int32(line - 1))[0]
    for i, source in enumerate((dg, du)):
        for j in range(local):
            if i == 0 and j > 0:
                units_of(j, last_chip)
            products(
                xs_turned.at[j],
                lambda at: source[j, :, :, at].reshape(deep, tile),
                in_stage, (i * local + j) * width, tiles,
            )
            send_ready((i * local + j + 1) * width)
    for j in range(local):
        products(
            act_turned.at[j],
            lambda at: ds[j, :, :, :, at].reshape(deep, tile),
            down_stage, 2 * local * width + j * width, width // tile,
        )

    give_back(last_chip, (line - 1) % 2)

    if start:
        totals.end_early()

        @pl.when(at_end)
        def _():
            for n in range(2):
                send_ahead(n).wait_send()

        @pl.when((p == 1) | (p == line - 2))
        def _():
            for n in range(2):
                send_ahead(n).wait_recv()

    if hop:
        hops.finish([2], [])
    for i in range(max(0, line - 2), line):
        q = visit(p, line, jnp.int32(i))[0]
        store_out(q, i % 2).wait()
        store_back(q, i % 2).wait()
    for d in range(line):
        for to_right in (True, False):
            if d == 0 and not to_right:
                continue
            q = p - d if to_right else p + d
            here = (q >= 0) if to_right else (q < line)

            @pl.when(here)
            def _():
                across(q, hidden).wait_send()
    for d in range(line):
        for to_right in (True, False):
            q = p - d if to_right else p + d
            here = (q >= 0) if to_right else (q < line)
            further = (p < line - 1) if to_right else (p > 0)

            @pl.when(here & further)
            def _():
                along(q, hidden, to_right).wait_send()


def expert_pass(hop, start, cap, hidden, own_grads, grads_all, named, router, w_gate, w_up, w_down, collective_id):
    n = lax.axis_size("exp")
    line = n // 2
    rows, width = hidden.shape
    local, _, units = w_gate.shape
    bf16 = jnp.bfloat16
    lanes = router.shape[1]
    dma = pltpu.SemaphoreType.DMA
    vmem = pl.BlockSpec(memory_space=pltpu.VMEM)
    early = (
        Totals.early_landing(3 * local * width // Totals.count, units),
        jax.ShapeDtypeStruct((rows, width + lanes), bf16),
        jax.ShapeDtypeStruct((rows, width), bf16),
    )
    return pl.pallas_call(
        functools.partial(expert_kernel, line, local, cap, hop, start),
        out_shape=(
            jax.ShapeDtypeStruct((n, rows, width), bf16),
            jax.ShapeDtypeStruct((n, rows, width), bf16),
            jax.ShapeDtypeStruct((n, rows, width + lanes), bf16),
            jax.ShapeDtypeStruct((3 * local * width, units), bf16),
            jax.ShapeDtypeStruct(grads_all.shape, bf16),
        )
        + (early if start else ()),
        in_specs=[ANY, ANY, ANY, vmem, vmem, ANY, ANY, ANY],
        out_specs=(ANY,) * (8 if start else 5),
        input_output_aliases={2: 4},
        scratch_shapes=[
            pltpu.VMEM((local, width, units), bf16),
            pltpu.VMEM((local, width, units), bf16),
            pltpu.VMEM((local, units, width), bf16),
            pltpu.VMEM((local, 2, cap, width), bf16),
            pltpu.VMEM((local, line, 2, cap, width), bf16),
            pltpu.VMEM((local, 2 * cap, units), bf16),
            pltpu.VMEM((local, line, 2 * cap, units), bf16),
            pltpu.VMEM((local, line, 2 * cap, units), bf16),
            pltpu.VMEM((local, 2, cap, width), bf16),
            pltpu.VMEM((2, 2, rows, width), bf16),
            pltpu.VMEM((2, 2, rows, width), bf16),
            pltpu.VMEM((2, 2, rows, width), bf16),
            pltpu.VMEM((2, 2, rows, width + lanes), bf16),
            pltpu.VMEM((2, width, 256), bf16),
            pltpu.VMEM((2, units, 256), bf16),
            pltpu.VMEM((2, local * cap, rows), bf16),
            pltpu.VMEM((local, width, n * cap), bf16),
            pltpu.VMEM((local, units, n * cap), bf16),
            pltpu.VMEM((2, local * cap, 128), jnp.float32),
        ]
        + ([pltpu.VMEM(one.shape, bf16) for one in early[1:]] if start else [])
        + [
            dma((3,)),
            dma((4,)),
            dma((2, line)),
            dma((line,)),
            dma((line,)),
            dma((line,)),
            dma((2,)),
            dma((2,)),
            dma((2,)),
            dma((2,)),
            dma((2,)),
        ]
        + (Gathering.scratch(line) if hop else [])
        + (Totals.early_scratch() + [dma((2, 4))] if start else []),
        compiler_params=pltpu.CompilerParams(
            collective_id=collective_id, has_side_effects=True, vmem_limit_bytes=62 << 20
        ),
        name="expert_pass",
    )(hidden, own_grads, grads_all, named, router, w_gate, w_up, w_down)


def turn(block, cosine, signed_sine):
    return block * cosine + pltpu.roll(block, block.shape[1] // 2, 1) * signed_sine


def row_norm(block):
    inverse = lax.rsqrt(jnp.mean(block * block, -1, keepdims=True) + EPS)
    return block * inverse, inverse


def attend_kernel(size, line, hop, experts, heads, kv_heads, tokens, small, cosine, sine, qkv_hbm, out_hbm, rows_in, *refs):
    targets, rows_all = refs[:7], refs[7]
    held, refs = refs[8:15], refs[15:]
    queries, keyval, mixed, lse, mid, hidden, gains = held
    wqkv, wout, h1, w_sem, send, recv, o_sem = refs[:7]
    f32, bf16 = jnp.float32, jnp.bfloat16
    c, e = lax.axis_index("ctx"), lax.axis_index("exp")
    rows, width = tokens.shape
    head = HEAD_WIDTH
    groups = heads // kv_heads
    q_width, kv_width = heads * head, kv_heads * head
    loads = [
        pltpu.make_async_copy(qkv_hbm, wqkv, w_sem.at[0]),
        pltpu.make_async_copy(out_hbm, wout, w_sem.at[1]),
    ]
    for copy in loads:
        copy.start()
    others = [lax.rem(c + i, size) for i in range(1, size)]
    column = [(e >= 2, c, e - 2), (e < 2 * line - 2, c, e + 2), (True, c, e + 1 - 2 * (e % 2))]
    greet((column if hop else []) + [(True, there, e) for there in others])
    if hop:
        half = rows // 2
        early, late = (
            Gathering(line, rows_all.at[e], rows_all, refs[7 + 5 * i : 12 + 5 * i], window=(i * half, half)) for i in range(2)
        )
        early.forward(1)
        late.forward(1)

    def leave(i):
        return pltpu.make_async_copy(held[i], targets[i], o_sem.at[i])

    turned = small[...].astype(f32).T
    gains[...] = turned[experts : experts + 8]
    leave(6).start()

    def step(t, carried):
        at = pl.ds(pl.multiple_of(t * 64, 64), 64)
        normed, _ = row_norm(tokens[at, :].astype(f32))
        h1[at, :] = (normed * gains[0:1, :]).astype(bf16)
        return carried

    lax.fori_loop(0, rows // 64, step, 0)
    loads[0].wait()
    kv = dot(h1[...], wqkv[:, q_width:])
    for j in range(kv_heads):
        at = slice(j * head, (j + 1) * head)
        keyval[c, :, at] = turn(kv[:, at], cosine[...], sine[...]).astype(bf16)
    keyval[c, :, kv_width:] = kv[:, kv_width:].astype(bf16)

    def give(i):
        return remote(keyval.at[c], keyval.at[c], send.at[i - 1], recv.at[i - 1], others[i - 1], e)

    for i in range(1, size):
        @pl.when(c + i < size)
        def _():
            give(i).start()

    for j in range(1, size):
        @pl.when(j > c)
        def _():
            keyval[j] = jnp.zeros((rows, 2 * kv_width), bf16)

    pair = 2 * head

    def project(t, carried):
        at = pl.ds(pl.multiple_of(t * pair, pair), pair)
        q = dot(h1[...], wqkv[:, at])
        for j in range(2):
            queries[2 * t + j] = turn(q[:, j * head : (j + 1) * head], cosine[...], sine[...]).astype(bf16)
        return carried

    lax.fori_loop(0, heads // 2, project, 0)
    leave(0).start()
    if hop:
        early.pump(2)
    for i in range(1, size):
        @pl.when(c - i >= 0)
        def _():
            give(i).wait_recv()
    leave(1).start()

    keys_count = size * rows
    scaling = 1.0 / math.sqrt(head)
    lane = lax.broadcasted_iota(jnp.int32, (rows, 128), 1)

    def one_head(j):
        h = j // groups
        keys = keyval[:, :, pl.ds(pl.multiple_of(h * head, head), head)].reshape(keys_count, head)
        values = keyval[:, :, pl.ds(pl.multiple_of(kv_width + h * head, head), head)].reshape(keys_count, head)
        place = lax.broadcasted_iota(jnp.int32, (rows, keys_count), 1)
        row = c * rows + lax.broadcasted_iota(jnp.int32, (rows, keys_count), 0)
        scores = jnp.where(place <= row, dot_nt(queries[j], keys) * scaling, NEG)
        peak = jnp.max(scores, -1, keepdims=True)
        raised = jnp.exp(scores - peak)
        total = jnp.sum(raised, -1, keepdims=True)
        probs = (raised * (1.0 / total)).astype(bf16)
        return dot(probs, values), peak + jnp.log(total)

    def two_heads(t, stats):
        found = [one_head(2 * t + i) for i in range(2)]
        mixed[:, pl.ds(pl.multiple_of(t * pair, pair), pair)] = jnp.concatenate(
            [block for block, _ in found], 1
        ).astype(bf16)
        for i, (_, value) in enumerate(found):
            stats = jnp.where(lane == 2 * t + i, value, stats)
        return stats

    lse[...] = lax.fori_loop(0, heads // 2, two_heads, jnp.zeros((rows, 128), f32))
    leave(2).start()
    leave(3).start()
    if hop:
        late.pump(2, onward=False)
    loads[1].wait()

    def outward(t, carried):
        at = pl.ds(pl.multiple_of(t * 256, 256), 256)
        mid[:, at] = tokens[:, at].astype(f32) + dot(mixed[...], wout[:, at])
        return carried

    lax.fori_loop(0, width // 256, outward, 0)
    leave(4).start()

    def last(t, carried):
        at = pl.ds(pl.multiple_of(t * 64, 64), 64)
        normed, _ = row_norm(mid[at, :])
        hidden[at, :] = (normed * gains[1:2, :]).astype(bf16)
        return carried

    lax.fori_loop(0, rows // 64, last, 0)
    leave(5).start()
    if hop:
        early.pump(3, onward=False)
        early.finish([1, 2], [2, 3])
        late.finish([1], [2])
    for i in range(7):
        leave(i).wait()
    for i in range(1, size):
        @pl.when(c + i < size)
        def _():
            give(i).wait_send()


def attend(hop, experts, tokens, small, cosine, sine, qkv_full, out_full, rows_all, collective_id):
    size, line = lax.axis_size("ctx"), lax.axis_size("exp") // 2
    rows, width = tokens.shape
    f32, bf16 = jnp.float32, jnp.bfloat16
    dma = pltpu.SemaphoreType.DMA
    vmem = pl.BlockSpec(memory_space=pltpu.VMEM)
    shape = jax.ShapeDtypeStruct
    made = (
        shape((QUERY_HEADS, rows, HEAD_WIDTH), bf16),
        shape((size, rows, 2 * KEY_VALUE_HEADS * HEAD_WIDTH), bf16),
        shape((rows, QUERY_HEADS * HEAD_WIDTH), bf16),
        shape((rows, 128), f32),
        shape((rows, width), f32),
        shape((rows, width), bf16),
        shape((8, width), f32),
    )
    return pl.pallas_call(
        functools.partial(attend_kernel, size, line, hop, experts, QUERY_HEADS, KEY_VALUE_HEADS),
        out_shape=made + (shape(rows_all.shape, bf16),),
        in_specs=[vmem] * 4 + [ANY] * 3,
        out_specs=(ANY,) * 8,
        input_output_aliases={6: 7},
        scratch_shapes=[pltpu.VMEM(one.shape, one.dtype) for one in made]
        + [
            pltpu.VMEM(qkv_full.shape, bf16),
            pltpu.VMEM(out_full.shape, bf16),
            pltpu.VMEM((rows, width), bf16),
            dma((2,)),
            dma((size - 1,)),
            dma((size - 1,)),
            dma((7,)),
        ]
        + (Gathering.scratch(line) * 2 if hop else []),
        compiler_params=pltpu.CompilerParams(
            collective_id=collective_id, has_side_effects=True, vmem_limit_bytes=62 << 20
        ),
        name="attend",
    )(tokens, small, cosine, sine, qkv_full, out_full, rows_all)


def halves(values):
    coarse = values.astype(jnp.bfloat16)
    return coarse, (values - coarse.astype(jnp.float32)).astype(jnp.bfloat16)


def backward_kernel(size, line, heads, kv_heads, experts, fused, *refs):
    back_part, out_part, grads, early_first, early_back, early_out, tokens, mid, final, marks, small, gains = refs[:12]
    queries, keyval, mixed, lse, cosine, sine, qkv_hbm, out_hbm, output, grad_tokens = refs[12:22]
    (dense_out, dense_q, dense_kv), refs = refs[22:25], refs[25:]
    if fused:
        totals, total_out, total_q, total_kv, land_one, land_two = refs[:6]
        landing, refs = refs[6:16], refs[16:]
        tmp = refs[0]
        sum_refs, refs = [refs[1 + 7 * i : 8 + 7 * i] for i in range(5)], refs[36:]
        total_scratch, refs = refs[:8], refs[8:]
        share_out, share_q, share_kv, refs = refs[:7], refs[7:14], refs[14:21], refs[21:]
    else:
        came, out_sum = back_part, out_part
    wqkv, wout, probs, d_scores, d_mixed, d_att, d_mid, h1, h2, dq, dkv, kv_part, kv_other, stage = refs[:14]
    w_sem, kv_send, kv_recv, s_sem = refs[14:]
    f32, bf16 = jnp.float32, jnp.bfloat16
    c, e = lax.axis_index("ctx"), lax.axis_index("exp")
    p, k = e // 2, e % 2
    rows, width = tokens.shape
    head = HEAD_WIDTH
    groups = heads // kv_heads
    q_width, kv_width = heads * head, kv_heads * head
    scaling = 1.0 / math.sqrt(head)
    keys_count = size * rows
    n = 2 * line
    shard = dense_out.shape[1]

    loads = [
        pltpu.make_async_copy(qkv_hbm, wqkv, w_sem.at[0]),
        pltpu.make_async_copy(out_hbm, wout, w_sem.at[1]),
    ]
    others = [lax.rem(c + i, size) for i in range(1, size)]
    column = [(p > 0, c, e - 2), (p < line - 1, c, e + 2), (True, c, e + 1 - 2 * k)]
    greet((column if fused else []) + [(True, there, e) for there in others])
    ticked = []

    def tick():
        if fused and len(ticked) < experts_total.ticks:
            experts_total.tick(len(ticked))
            ticked.append(1)

    if fused:
        experts_total = Totals(
            grads, early_first, *total_scratch[3:5], totals, land_one, land_two, total_scratch[:3], total_scratch[5:]
        )
        experts_total.begin()
        sums = [
            Summing(
                line, part, landing[2 * i], landing[2 * i + 1], sum_refs[i][0], tmp, sum_refs[i][1:],
                (early_back, early_out, None, None, None)[i],
            )
            for i, part in enumerate((back_part, out_part, dense_out, dense_q, dense_kv))
        ]
        back, outs, dense_outs, dense_qs, dense_kvs = sums
        came, out_sum = back.result(), outs.result()
        sharing_out = Sharing(dense_outs.result(), total_out, share_out[:4], share_out[4:])
        sharing_q = Sharing(dense_qs.result(), total_q, share_q[:4], share_q[4:])
        sharing_kv = Sharing(dense_kvs.result(), total_kv, share_kv[:4], share_kv[4:])
        back.begin()
    for copy in loads:
        copy.start()

    lane = lax.broadcasted_iota(jnp.int32, (rows, 128), 1)

    def keys_of(h):
        return keyval[:, :, pl.ds(pl.multiple_of(h * head, head), head)].reshape(keys_count, head)

    def values_of(h):
        return keyval[:, :, pl.ds(pl.multiple_of(kv_width + h * head, head), head)].reshape(keys_count, head)

    def again(j, carried):
        place = lax.broadcasted_iota(jnp.int32, (rows, keys_count), 1)
        row = c * rows + lax.broadcasted_iota(jnp.int32, (rows, keys_count), 0)
        scores = dot_nt(queries[j], keys_of(j // groups)) * scaling
        level = jnp.sum(jnp.where(lane == j, lse[...], 0.0), -1, keepdims=True)
        probs[j] = jnp.exp(jnp.where(place <= row, scores - level, NEG)).astype(bf16)
        return carried

    def norms(t, carried):
        at = pl.ds(pl.multiple_of(t * 64, 64), 64)
        normed, _ = row_norm(mid[at, :])
        h2[at, :] = (normed * gains[1:2, :]).astype(bf16)
        normed, _ = row_norm(tokens[at, :].astype(f32))
        h1[at, :] = (normed * gains[0:1, :]).astype(bf16)
        return carried

    bounds = [heads * i // max(1, line - 1) for i in range(line)]
    for i, d in enumerate(range(line - 1, 0, -1)):
        if fused and i > 0:
            back.step(d)
        if i == 0:
            lax.fori_loop(0, rows // 64, norms, 0)
        lax.fori_loop(bounds[i], bounds[i + 1], again, 0)
        tick()
        if fused and d == 2:
            outs.begin()
            tick()
    if fused:
        back.step(0)
        tick()

    logits = jnp.where(marks[...].astype(f32) > 0.5, dot(h2[...], small[...]), NEG)
    raised = jnp.exp(logits - jnp.max(logits, -1, keepdims=True))
    gates = raised / jnp.sum(raised, -1, keepdims=True)
    extra = came[:, width:].astype(f32)
    grad_gates = extra + pltpu.roll(extra, extra.shape[1] // 2, 1)
    grad_logits = gates * (grad_gates - jnp.sum(gates * grad_gates, -1, keepdims=True))
    logits_hi, logits_lo = halves(grad_logits)
    grad_small = dot_tn(h2[...], logits_hi) + dot_tn(h2[...], logits_lo)

    def second_norm(t, total):
        at = pl.ds(pl.multiple_of(t * 32, 32), 32)
        normed, inverse = row_norm(mid[at, :])
        low, high = halves(grad_logits_ref[at, :])
        grad_h2 = came[at, :width].astype(f32) + dot_nt(low, small[...]) + dot_nt(high, small[...])
        total = total + jnp.sum(grad_h2 * normed, 0, keepdims=True)
        scaled = grad_h2 * gains[1:2, :]
        grad = final[at, :].astype(f32) + inverse * (scaled - normed * jnp.mean(scaled * normed, -1, keepdims=True))
        d_mid[at, :] = grad
        d_att[at, :] = grad.astype(bf16)
        return total

    grad_logits_ref = dkv.at[:, 0:128]
    dkv[:, 0:128] = grad_logits
    gain_two = lax.fori_loop(0, rows // 32, second_norm, jnp.zeros((1, width), f32))

    loads[1].wait()

    def mixing(t, carried):
        at = pl.ds(pl.multiple_of(t * 256, 256), 256)
        block = dot_nt(d_att[...], wout[at, :]).astype(bf16)
        for i in range(2):
            d_mixed[2 * t + i] = block[:, i * head : (i + 1) * head]
        return carried

    lax.fori_loop(0, q_width // 256, mixing, 0)
    if fused and line > 2:
        outs.step(line - 2)
    tick()

    def gradients(left, right, dense, column, count):
        def store(t):
            return pltpu.make_async_copy(
                stage.at[lax.rem(t, 2)],
                dense.at[:, :, pl.ds(pl.multiple_of(column + t * 256, 128), 256)],
                s_sem.at[lax.rem(t, 2)],
            )

        def one(t, carried):
            @pl.when(t >= 2)
            def _():
                store(t - 2).wait()

            product = dot_tn(left[...], right[:, pl.ds(pl.multiple_of(t * 256, 256), 256)])
            stage[lax.rem(t, 2)] = product.astype(bf16).reshape(n, shard, 256)
            store(t).start()
            return carried

        lax.fori_loop(0, count, one, 0)
        for t in range(max(0, count - 2), count):
            store(jnp.int32(t)).wait()

    gradients(mixed, d_att, dense_out, 0, width // 256)
    if fused:
        dense_outs.begin()
        tick()
        for d in range(line - 3, 0, -1):
            outs.step(d)

    def per_head(j, carried):
        grad_probs = dot_nt(d_mixed[j], values_of(j // groups))
        weights_now = probs[j].astype(f32)
        inner = jnp.sum(weights_now * grad_probs, -1, keepdims=True)
        grad = (weights_now * (grad_probs - inner) * scaling).astype(bf16)
        d_scores[lax.rem(j, groups)] = grad
        back_q = dot(grad, keys_of(j // groups))
        dq[:, pl.ds(pl.multiple_of(j * head, head), head)] = turn(back_q, cosine[...], -sine[...]).astype(bf16)
        return carried

    for h in range(kv_heads):
        lax.fori_loop(h * groups, (h + 1) * groups, per_head, 0)
        these = slice(h * groups, (h + 1) * groups)
        grad_keys = dot_tn(
            d_scores[...].reshape(groups * rows, keys_count), queries[these].reshape(groups * rows, head)
        )
        grad_values = dot_tn(
            probs[these].reshape(groups * rows, keys_count), d_mixed[these].reshape(groups * rows, head)
        )
        kv_part[:, :, h * head : (h + 1) * head] = grad_keys.astype(bf16).reshape(size, rows, head)
        at = kv_width + h * head
        kv_part[:, :, at : at + head] = grad_values.astype(bf16).reshape(size, rows, head)
        if h == 0 and fused:
            tick()
            outs.step(0)

    def give(i):
        there = lax.rem(c + size - i, size)
        return remote(kv_part.at[there], kv_other.at[i - 1], kv_send.at[i - 1], kv_recv.at[i - 1], there, e)

    for i in range(1, size):
        @pl.when(c - i >= 0)
        def _():
            give(i).start()

    tick()
    if fused and line > 2:
        dense_outs.step(line - 2)
    gradients(h1, dq, dense_q, 0, q_width // 256)
    if fused:
        dense_qs.begin()
    tick()

    own = kv_part[c].astype(f32)
    dkv[...] = own
    for i in range(1, size):
        @pl.when(c + i < size)
        def _():
            give(i).wait_recv()
            dkv[...] += kv_other[i - 1].astype(f32)
    for j in range(kv_heads):
        at = slice(j * head, (j + 1) * head)
        dkv[:, at] = turn(dkv[:, at], cosine[...], -sine[...])
    dq[:, q_width:] = dkv[...].astype(bf16)
    dkv_low = dq.at[:, q_width:]
    gradients(h1, dkv_low, dense_kv, 0, 2 * kv_width // 256)
    if fused:
        for d in range(line - 3, 0, -1):
            dense_outs.step(d)
    loads[0].wait()

    def inputs(t, total):
        at = pl.ds(pl.multiple_of(t * 128, 128), 128)
        grad_h1 = dot_nt(dq[at, :], wqkv[...])
        normed, inverse = row_norm(tokens[at, :].astype(f32))
        total = total + jnp.sum(grad_h1 * normed, 0, keepdims=True)
        scaled = grad_h1 * gains[0:1, :]
        grad_tokens[at, :] = d_mid[at, :] + inverse * (
            scaled - normed * jnp.mean(scaled * normed, -1, keepdims=True)
        )
        return total

    gain_one = lax.fori_loop(0, rows // 128, inputs, jnp.zeros((1, width), f32))
    sub = lax.broadcasted_iota(jnp.int32, (128, width), 0)
    gain_rows = jnp.where(sub == experts, gain_one, jnp.where(sub == experts + 1, gain_two, 0.0))
    grad_small = (grad_small + gain_rows.T).astype(bf16).reshape(n, shard, 128)
    stage[0, :, :, 0:128] = grad_small
    small_store = pltpu.make_async_copy(
        stage.at[0, :, :, 0:128], dense_kv.at[:, :, 2 * kv_width :], s_sem.at[0]
    )
    small_store.start()
    small_store.wait()
    tick()
    if fused:
        dense_kvs.begin()

    def finish(t, carried):
        at = pl.ds(pl.multiple_of(t * 64, 64), 64)
        output[at, :] = (mid[at, :] + out_sum[at, :].astype(f32)).astype(bf16)
        return carried

    lax.fori_loop(0, rows // 64, finish, 0)
    if fused:
        dense_outs.step(0)
        sharing_out.begin()
        tick()
        for d in range(line - 2, -1, -1):
            dense_qs.step(d)
            if d == 0:
                sharing_q.begin()
            tick()
            if d == line - 2:
                sharing_out.second()
            dense_kvs.step(d)
            if d == line - 3:
                sharing_out.third()
        sharing_kv.begin()
        sharing_q.second()
        sharing_out.fourth()
        tick()
        sharing_kv.second()
        sharing_q.third()
        while len(ticked) < experts_total.ticks:
            tick()
        sharing_kv.third()
        sharing_q.fourth()
        sharing_kv.fourth()
        for one in sums:
            one.end()
        sharing_out.end()
        sharing_q.end()
        sharing_kv.end()
        experts_total.end()
    for i in range(1, size):
        @pl.when(c - i >= 0)
        def _():
            give(i).wait_send()


def backward(experts, shard, back_part, out_part, grads, early, tokens, mid, final, marks, small, gains, queries, keyval, mixed, lse,
             cosine, sine, qkv_full, out_full, collective_id):
    size, n = lax.axis_size("ctx"), lax.axis_size("exp")
    line = n // 2
    rows, width = tokens.shape
    heads, kv_heads, head = QUERY_HEADS, KEY_VALUE_HEADS, HEAD_WIDTH
    kv_both = 2 * kv_heads * head
    keys_count = size * rows
    f32, bf16 = jnp.float32, jnp.bfloat16
    dma = pltpu.SemaphoreType.DMA
    vmem = pl.BlockSpec(memory_space=pltpu.VMEM)
    shape = jax.ShapeDtypeStruct
    fused = planned(size, n, shard)
    dense_widths = (width, heads * head, kv_both + small.shape[1])
    shapes = [
        shape((rows, width), bf16),
        shape((rows, width), f32),
        *(shape((n, shard, wide), bf16) for wide in dense_widths),
    ]
    summing = []
    if fused:
        deep = grads.shape[0] // Totals.count
        shapes += [
            shape(grads.shape, bf16),
            *(shape((shard, wide), bf16) for wide in dense_widths),
        ]
        shapes += Totals.landing(deep, grads.shape[1])
        summed = [(rows, back_part.shape[2]), (rows, width)] + [(shard, wide) for wide in dense_widths]
        for high, wide in summed:
            shapes += Summing.landing(line, high, wide)
        widest = max(wide for _, wide in summed)
        summing = [
            pltpu.VMEM((2, rows, widest), bf16),
        ]
        for high, wide in summed:
            summing += Summing.scratch(line, high, wide)
        summing += Totals.scratch(deep, grads.shape[1])
        for wide in dense_widths:
            summing += Sharing.scratch(shard, wide)
    else:
        back_part = lax.psum_scatter(back_part, "exp", scatter_dimension=0)
        out_part = lax.psum_scatter(out_part, "exp", scatter_dimension=0)
    found = pl.pallas_call(
        functools.partial(backward_kernel, size, line, heads, kv_heads, experts, fused),
        out_shape=tuple(shapes),
        in_specs=[ANY if fused else vmem] * 2 + [ANY] * 4 + [vmem] * 12 + [ANY] * 2,
        out_specs=(vmem, vmem) + (ANY,) * (len(shapes) - 2),
        scratch_shapes=summing
        + [
            pltpu.VMEM(qkv_full.shape, bf16),
            pltpu.VMEM(out_full.shape, bf16),
            pltpu.VMEM((heads, rows, keys_count), bf16),
            pltpu.VMEM((heads // kv_heads, rows, keys_count), bf16),
            pltpu.VMEM((heads, rows, head), bf16),
            pltpu.VMEM((rows, width), bf16),
            pltpu.VMEM((rows, width), f32),
            pltpu.VMEM((rows, width), bf16),
            pltpu.VMEM((rows, width), bf16),
            pltpu.VMEM((rows, heads * head + kv_both), bf16),
            pltpu.VMEM((rows, kv_both), f32),
            pltpu.VMEM((size, rows, kv_both), bf16),
            pltpu.VMEM((size - 1, rows, kv_both), bf16),
            pltpu.VMEM((2, n, shard, 256), bf16),
            dma((2,)),
            dma((size - 1,)),
            dma((size - 1,)),
            dma((2,)),
        ],
        compiler_params=pltpu.CompilerParams(
            collective_id=collective_id, has_side_effects=True, vmem_limit_bytes=62 << 20
        ),
        name="backward",
    )(back_part, out_part, grads, *early, tokens, mid, final, marks, small, gains, queries, keyval, mixed, lse, cosine, sine,
      qkv_full, out_full)
    if fused:
        return found[:2] + found[5:9]
    dense = tuple(lax.psum_scatter(part, "exp", scatter_dimension=0) for part in found[2:5])
    return found[:2] + (lax.psum(grads, "ctx"),) + tuple(lax.psum(part, "ctx") for part in dense)


def widen_kernel(total, *refs):
    dense, (gate, up, down), dense_to, held, refs = refs[:3], refs[3:6], refs[6:9], refs[9], refs[10:]
    held_dense, wide, wide_dense, (in_sem, out_sem, dense_in, dense_done) = refs[:3], refs[3], refs[4:7], refs[7:]
    f32 = jnp.float32
    high = held.shape[1]
    blocks, slots = held.shape[0], wide.shape[0]
    per, tall = blocks // 3, gate.shape[1] // high

    def load(i):
        return pltpu.make_async_copy(total.at[pl.ds(i * high, high)], held.at[i], in_sem.at[i])

    def store(i):
        n, at = i // per, i % per
        if n < 2:
            target = (gate, up)[n].at[at // tall, pl.ds(at % tall * high, high)]
        else:
            target = down.at[at // tall, :, pl.ds(at % tall * high, high)]
        return pltpu.make_async_copy(wide.at[i % slots], target, out_sem.at[i % slots])

    small_in = [
        pltpu.make_async_copy(src, dst, dense_in.at[i])
        for i, (src, dst) in enumerate(zip(dense, held_dense))
    ]
    small_done = [
        pltpu.make_async_copy(src, dst, dense_done.at[i])
        for i, (src, dst) in enumerate(zip(wide_dense, dense_to))
    ]
    load(0).start()
    for copy in small_in:
        copy.start()
    for i in range(1, blocks):
        load(i).start()
    for i in range(blocks):
        load(i).wait()
        if i >= slots:
            store(i - slots).wait()
        wide[i % slots] = held[i].astype(f32)
        store(i).start()
        if i == 0:
            for copy in small_in:
                copy.wait()
            for src, dst in zip(held_dense, wide_dense):
                dst[...] = src[:, : dst.shape[1]].astype(f32)
            for copy in small_done:
                copy.start()
    for i in range(max(0, blocks - slots), blocks):
        store(i).wait()
    for copy in small_done:
        copy.wait()


def widen(total, parts, local, width, units, kv_both):
    f32 = jnp.float32
    blocks, slots = total.shape[0] // units, 4
    shape = jax.ShapeDtypeStruct
    dma = pltpu.SemaphoreType.DMA
    dense = [parts[0].shape, parts[1].shape, (parts[2].shape[0], kv_both)]
    return pl.pallas_call(
        widen_kernel,
        out_shape=(
            shape((local, width, units), f32),
            shape((local, width, units), f32),
            shape((local, units, width), f32),
            *(shape(one, f32) for one in dense),
        ),
        in_specs=[ANY] * 4,
        out_specs=(ANY,) * 6,
        scratch_shapes=[
            pltpu.VMEM((blocks, units, units), total.dtype),
            *(pltpu.VMEM(one.shape, one.dtype) for one in parts),
            pltpu.VMEM((slots, units, units), f32),
            *(pltpu.VMEM(one, f32) for one in dense),
            dma((blocks,)),
            dma((slots,)),
            dma((3,)),
            dma((3,)),
        ],
        compiler_params=pltpu.CompilerParams(vmem_limit_bytes=56 << 20),
        name="widen",
    )(total, *parts)


def rope_tables(first_row, row_count, head_size):
    half_size = head_size // 2
    frequency = ROPE_BASE ** (-jnp.arange(half_size, dtype=jnp.float32) * (2.0 / head_size))
    places = (first_row + jnp.arange(row_count, dtype=jnp.int32)).astype(jnp.float32)
    angles = places[:, None] * frequency[None, :]
    cosine = jnp.cos(angles)
    sine = jnp.sin(angles)
    return (jnp.concatenate([cosine, cosine], 1), jnp.concatenate([-sine, sine], 1))


def ein(spec, a, b):
    return jnp.einsum(spec, a, b, preferred_element_type=jnp.float32)


def shards(
    tokens,
    routes,
    gain_attn,
    w_query,
    key_value_weight,
    w_out,
    gain_ffn,
    w_router,
    w_gate,
    w_up,
    w_down,
    cotangent,
):
    f32 = jnp.float32
    bf16 = jnp.bfloat16
    rows, width = tokens.shape[1:]
    ctx_size, exp_size = lax.axis_size("ctx"), lax.axis_size("exp")
    ctx_index, exp_index = lax.axis_index("ctx"), lax.axis_index("exp")
    local_experts = w_gate.shape[0]
    experts = local_experts * exp_size
    top = routes.shape[2]
    capacity = 2 * rows * top // experts
    shard_rows = w_query.shape[0]
    heads, kv_heads, head = QUERY_HEADS, KEY_VALUE_HEADS, HEAD_WIDTH
    groups = heads // kv_heads
    q_width, kv_width = heads * head, kv_heads * head
    scaling = 1.0 / math.sqrt(head)
    first_row = ctx_index * rows

    named_own = jnp.max((routes[0][:, :, None] == jnp.arange(128, dtype=jnp.int32)).astype(bf16), axis=1)
    lane = lax.broadcasted_iota(jnp.int32, (shard_rows, 128), 1)
    gains_wide = [lax.broadcast_in_dim(gain, (shard_rows, 128), (0,)) for gain in (gain_attn, gain_ffn)]
    small = lax.pad(w_router, jnp.zeros((), bf16), ((0, 0, 0), (0, 128 - experts, 0)))
    small = jnp.where(lane == experts, gains_wide[0], jnp.where(lane == experts + 1, gains_wide[1], small))
    qkv_full, out_full, small_full, named, rows_all = gather_weights(
        (w_query, key_value_weight, w_out, small), named_own, cotangent[0], 1
    )

    cosine, sine = rope_tables(first_row, rows, head)
    hops = planned(ctx_size, exp_size, shard_rows)
    queries, keyval, mixed, lse, resid_mid, hidden_two, gains, rows_all = attend(
        hops, experts, tokens[0], small_full, cosine, sine, qkv_full, out_full, rows_all, 2
    )

    _, out_part, back_part, grads, _, *early = expert_pass(
        hops and exp_size > 6, hops, capacity, hidden_two, cotangent[0], rows_all, named, small_full, w_gate, w_up, w_down, 3
    )
    output, grad_input, grads, *dense = backward(
        experts, shard_rows, back_part, out_part, grads, early or [grads] * 3, tokens[0], resid_mid, cotangent[0], named_own, small_full, gains,
        queries, keyval, mixed, lse, cosine, sine, qkv_full, out_full, 4
    )
    small_total = dense[2][:, 2 * kv_width :].astype(f32)
    grad_gate, grad_up, grad_down, grad_out, grad_query, grad_keyval = widen(
        grads, dense, local_experts, width, w_gate.shape[2], 2 * kv_width
    )
    return (
        output[None],
        grad_input[None],
        small_total[:, experts],
        grad_query,
        grad_keyval,
        grad_out,
        small_total[:, experts + 1],
        small_total[:, :experts],
        grad_gate,
        grad_up,
        grad_down,
    )


def solution(mesh):
    rows, wide, deep = P("exp", "ctx", None), P("exp", None), P("exp", None, None)
    flat = P("exp")
    return jax.shard_map(
        shards,
        mesh=mesh,
        in_specs=(rows, rows, flat, wide, wide, wide, flat, wide, deep, deep, deep, rows),
        out_specs=(rows, rows, flat, wide, wide, wide, flat, wide, deep, deep, deep),
        check_vma=False,
    )
```
